32 devices in a mesh: inp: 4 (over y, x), freq: 8 (over z, core).
Axes of the slice: x: 2, y: 2, z: 4, core: 2. Of those that a mesh axis runs over, the one named last changes fastest.
Arguments:
- volts: bfloat16 [16, 2, 2048, 1024], P('freq', None, 'inp'), parts along dimension 0, may hold values from -6 to 6
- position_input: int32 [8, 256], P('inp'), may hold values from 0 to 255, each once within a row
- tile_group: int32 [8, 3, 2], P('inp'), may hold values from 0 to 31
Outputs:
- stacked: float32 [32, 16, 2, 511], P('inp', 'freq'), parts along dimension 1
The draws below stay inside these ranges and needn't reach their ends.
There are 8 independent parts, one for each index of `freq`. The reference program is written for one: setup_inputs(seed, part) draws one part's arguments, and reference() takes and returns one part's arrays. A program takes and returns all parts, laid end to end along the dimension named above; an argument that names none is the same for every part. Nothing has to cross between parts.
Inputs may be any that keep to these rules, and one draw needn't show every extreme that they name: `position_input`: each row holds every position's input index within the block once. `tile_group`: entry [a, l, b] names the row group of the tile of block a with the b-th block of the device at level l of block a's device.
All inputs are finite; a program needn't handle non-finite values.
Results may differ from the reference program's by a relative error of at most 0.0003.
Values may be sent and summed in bfloat16 or wider, within the bound.
No kernel may reach another device: no remote copies, remote signals or barrier semaphores. Data moves between devices by JAX's collectives and lax.ppermute only.
A program may use at most 192 MiB of HBM per device.

```python
import math
import jax
import jax.numpy as jnp
import numpy as np
from jax import lax

B = 256
BLK_DEV = 2
SAMPLES = 1024
F_DEV = 2
LEVELS = 2
NBLK = 8
INPUTS = 2048
ROWGROUPS = 32
DIFFS = 511
N_INP = 4


def with_ends(entries, stream_key, low, largest):
    shape = entries.shape
    spot = [jax.random.randint(jax.random.fold_in(stream_key, axis), (), 0, shape[axis]) for axis in range(len(shape))]
    entries = entries.at[tuple(spot)].set(low)
    longest = shape.index(max(shape))
    spot[longest] = (spot[longest] + 1) % shape[longest]
    return entries.at[tuple(spot)].set(largest)


def shard_levels(rng, dims, pieces, smallest, high):
    factor_of = 1.0
    for axis_at, blocks in pieces:
        heights = jax.random.uniform(jax.random.fold_in(jax.random.fold_in(rng, 6), axis_at), (blocks,), jnp.float32, smallest / len(pieces), high / len(pieces))
        factor_of = factor_of * jnp.repeat(jnp.exp(heights), dims[axis_at] // blocks).reshape((-1,) + (1,) * (len(dims) - 1 - axis_at))
    return factor_of


def rank_table(number_of, skew):
    loads = [(1 << 20) // math.isqrt(grade ** skew) + 1 for grade in range(1, number_of + 1)]
    deviation = 1 + sum(loads) // (1 << 30)
    return np.cumsum(np.array([max(1, weight // deviation) for weight in loads]))


def ranked_ids(key, dims, count, slope):
    grid = rank_table(count, slope)
    pick = jax.random.randint(jax.random.fold_in(key, 1), dims, 0, int(grid[count - 1]))
    standing = jnp.searchsorted(jnp.asarray(grid, jnp.int32), pick, side="right")
    return jax.random.permutation(jax.random.fold_in(key, 2), count)[standing].astype(jnp.int32)


def normal_values(key, extent, width, limit, cuts=(), kind=jnp.bfloat16):
    values = width * jax.random.normal(key, extent, jnp.float32)
    if cuts:
        values = values * shard_levels(key, extent, cuts, -0.22, 0.18)
    return jnp.clip(values, -limit, limit).astype(kind)


def setup_inputs(seed: int = 0, part: int = 0) -> dict:
    key_list = jax.random.split(jax.random.key(seed), 4)
    part_splits = jax.random.split(jax.random.fold_in(key_list[3], part), 4)
    return {
        "volts": normal_values(part_splits[0], (F_DEV, 2, INPUTS, SAMPLES), 1.0, 6.0, ((2, 4),)),
        "position_input": jax.vmap(lambda own: jax.random.permutation(own, B))(jax.random.split(key_list[1], NBLK)).reshape((NBLK, B)).astype(jnp.int32),
        "tile_group": with_ends(ranked_ids(key_list[2], (NBLK, LEVELS + 1, BLK_DEV), ROWGROUPS, 2), jax.random.fold_in(key_list[2], 3), 0, ROWGROUPS - 1).astype(jnp.int32),
    }


def diagonals(tile_block):
    tile_width = tile_block.shape[-1]
    lead = tile_block.shape[:-2]
    flipped = jnp.flip(tile_block, axis=-2)
    padded = jnp.pad(flipped, [(0, 0)] * len(lead) + [(0, 0), (0, tile_width)])
    flattened = padded.reshape(lead + (2 * tile_width * tile_width,))
    flattened = flattened[..., : tile_width * (2 * tile_width - 1)]
    sheared = flattened.reshape(lead + (tile_width, 2 * tile_width - 1))
    return jnp.sum(sheared, axis=-2)


def cross_tiles(own_panel, partner_panel):
    own_f = own_panel.astype(jnp.float32)
    partner_f = partner_panel.astype(jnp.float32)
    high = lax.Precision.HIGHEST
    real_part = jnp.einsum("fps,fqs->fpq", own_f[:, 0], partner_f[:, 0], precision=high) + jnp.einsum("fps,fqs->fpq", own_f[:, 1], partner_f[:, 1], precision=high)
    imag_part = jnp.einsum("fps,fqs->fpq", own_f[:, 1], partner_f[:, 0], precision=high) - jnp.einsum("fps,fqs->fpq", own_f[:, 0], partner_f[:, 1], precision=high)
    return real_part, imag_part


def stack_round(real_part, imag_part, own_round, blocks, tile_width, samples):
    stacked_parts = jnp.stack([real_part, imag_part], axis=1) * (1.0 / samples)
    channels = stacked_parts.shape[0]
    tile_view = stacked_parts.reshape(channels, 2, blocks, tile_width, blocks, tile_width).transpose(0, 1, 2, 4, 3, 5)
    lag_sums = diagonals(tile_view)
    if own_round:
        diffs = 2 * tile_width - 1
        center = (jnp.arange(diffs) == tile_width - 1).astype(jnp.float32)
        keep_mask = 1.0 - jnp.eye(blocks, dtype=jnp.float32)[:, :, None] * center[None, None, :]
        lag_sums = lag_sums * keep_mask
    return lag_sums


def reference(volts, position_input, tile_group):
    blocks_all, tile_width = position_input.shape
    offsets = tile_width * jnp.arange(blocks_all)[:, None]
    index_list = (position_input + offsets).reshape(-1).astype(jnp.int32)
    ordered = jnp.take(volts, index_list, axis=2)
    channels = volts.shape[0]
    samples = volts.shape[3]
    row_count = BLK_DEV * tile_width
    stacked = jnp.zeros((ROWGROUPS, channels, 2, DIFFS), jnp.float32)
    group_range = jnp.arange(ROWGROUPS).astype(jnp.int32)
    for device in range(N_INP):
        own_panel = ordered[:, :, device * row_count:(device + 1) * row_count]
        partners = [device] + [device ^ (1 << bit_index) for bit_index in range(LEVELS)]
        for level_index in range(LEVELS + 1):
            partner = partners[level_index]
            partner_panel = ordered[:, :, partner * row_count:(partner + 1) * row_count]
            real_part, imag_part = cross_tiles(own_panel, partner_panel)
            lag_sums = stack_round(real_part, imag_part, level_index == 0, BLK_DEV, tile_width, samples)
            group_ids = tile_group[device * BLK_DEV:(device + 1) * BLK_DEV, level_index, :].reshape(-1).astype(jnp.int32)
            one_hot = (group_ids[:, None] == group_range[None, :]).astype(jnp.float32)
            flat_sums = lag_sums.reshape(channels, 2, BLK_DEV * BLK_DEV, DIFFS)
            stacked = stacked + jnp.einsum("ng,fcne->gfce", one_hot, flat_sums, precision=lax.Precision.HIGHEST)
    return stacked
```

```python
import functools

import jax
import jax.numpy as jnp
from jax import lax
from jax.experimental import pallas as pl
from jax.experimental.pallas import tpu as pltpu
from jax.sharding import PartitionSpec as P

RG_DEV = 8
ANY = pl.BlockSpec(memory_space=pl.ANY)
WHOLE = pl.BlockSpec(memory_space=pltpu.VMEM)


def xor_permute(x, axis, distance):
    return lax.ppermute(x, axis, [(i, i ^ distance) for i in range(lax.axis_size(axis))])


def parity(index, levels):
    bits = index & 1
    for level in range(1, levels):
        bits = bits ^ ((index >> level) & 1)
    return bits


def order_matrix(position_row):
    width = position_row.shape[-1]
    by_position = jnp.transpose(jnp.broadcast_to(position_row, (width, width)))
    inputs = lax.broadcasted_iota(jnp.int32, (width, width), 1)
    return (by_position == inputs).astype(jnp.float32).astype(jnp.bfloat16)


def product(x, y):
    return lax.dot_general(x, y, (((1,), (1,)), ((), ())), preferred_element_type=jnp.float32)


def lag_rows(tiles):
    count, width, _ = tiles.shape
    half = width // 2
    low, high = tiles[:, :half], tiles[:, half:]
    sheared = jnp.concatenate(
        [
            high[:, :, :half],
            high[:, :, half:] + low[:, :, :half],
            low[:, :, half:],
            jnp.zeros((count, half, half), jnp.float32),
        ],
        axis=2,
    )
    rows = half
    while rows > 8:
        rows //= 2
        upper = sheared[:, :rows].reshape(count * rows, 2 * width)
        upper = pltpu.roll(upper, rows, 1).reshape(count, rows, 2 * width)
        sheared = upper + sheared[:, rows:]
    flat = sheared.reshape(count * rows, 2 * width)
    sublane = lax.broadcasted_iota(jnp.int32, flat.shape, 0) % 8
    while rows > 1:
        rows //= 2
        flat = jnp.where((sublane & rows) == 0, pltpu.roll(flat, rows, 1), flat)
    return jnp.sum(flat.reshape(count, 8, 2 * width), axis=1)


def tile_lags(x_re, x_im, y_re, y_im):
    real_part = product(x_re, y_re) + product(x_im, y_im)
    imag_part = product(x_im, y_re) - product(x_re, y_im)
    return lag_rows(jnp.stack([real_part, imag_part])) * (1.0 / x_re.shape[1])


def split_bf16(x):
    first = x.astype(jnp.bfloat16)
    rest = x - first.astype(jnp.float32)
    second = rest.astype(jnp.bfloat16)
    third = (rest - second.astype(jnp.float32)).astype(jnp.bfloat16)
    return first, second, third


def conjugate_lags(lags):
    count, width = lags.shape
    flip = (
        lax.broadcasted_iota(jnp.int32, (width, width), 0)
        + lax.broadcasted_iota(jnp.int32, (width, width), 1)
        == width - 2
    )
    flip = flip.astype(jnp.float32).astype(jnp.bfloat16)
    parts = jnp.dot(
        jnp.concatenate(split_bf16(lags), axis=0), flip, preferred_element_type=jnp.float32
    )
    turned = parts[:count] + parts[count : 2 * count] + parts[2 * count :]
    odd = lax.broadcasted_iota(jnp.int32, turned.shape, 0) % 2 == 1
    return jnp.where(odd, -turned, turned)


def group_sums(target_row, lags, rows):
    count = lags.shape[0]
    pick = lax.broadcasted_iota(jnp.int32, (rows, count), 0) == target_row
    pick = pick.astype(jnp.float32).astype(jnp.bfloat16)
    total = None
    for part in split_bf16(lags):
        term = jnp.dot(pick, part, preferred_element_type=jnp.float32)
        total = term if total is None else total + term
    return total


def send_kernel(levels, block, position_ref, volts_ref, out_ref, raw, ordered, in_sem, out_sem):
    other = 1 - parity(lax.axis_index("inp"), levels)
    width = raw.shape[1]
    loads = [
        pltpu.make_async_copy(
            volts_ref.at[other, c, pl.ds(block * width, width)], raw.at[c], in_sem.at[c]
        )
        for c in range(2)
    ]
    for load in loads:
        load.start()
    order = order_matrix(position_ref[block : block + 1, :])
    stores = []
    for c in range(2):
        loads[c].wait()
        ordered[c] = jnp.dot(order, raw[c], preferred_element_type=jnp.float32).astype(jnp.bfloat16)
        store = pltpu.make_async_copy(ordered.at[c], out_ref.at[c], out_sem.at[c])
        store.start()
        stores.append(store)
    for store in stores:
        store.wait()


def order_to_send(position_input, volts, block, levels):
    width = position_input.shape[1]
    samples = volts.shape[3]
    return pl.pallas_call(
        functools.partial(send_kernel, levels, block),
        out_shape=jax.ShapeDtypeStruct((2, width, samples), jnp.bfloat16),
        in_specs=[WHOLE, ANY],
        out_specs=ANY,
        scratch_shapes=[
            pltpu.VMEM((2, width, samples), jnp.bfloat16),
            pltpu.VMEM((2, width, samples), jnp.bfloat16),
            pltpu.SemaphoreType.DMA((2,)),
            pltpu.SemaphoreType.DMA((2,)),
        ],
        compiler_params=pltpu.CompilerParams(vmem_limit_bytes=16 << 20),
        cost_estimate=pl.CostEstimate(
            flops=4 * width * width * samples, bytes_accessed=8 * width * samples, transcendentals=0
        ),
        name="order_to_send",
    )(position_input, volts)


def own_kernel(levels, blocks, position_ref, volts_ref, *refs):
    sent = refs[:blocks]
    panel_ref, lags_ref, raw, panels, in_sem, sent_sem, out_sem = refs[blocks:]
    mine = parity(lax.axis_index("inp"), levels)
    width = raw.shape[2]
    loads = [
        [
            pltpu.make_async_copy(
                volts_ref.at[mine, c, pl.ds(b * width, width)], raw.at[b, c], in_sem.at[b, c]
            )
            for c in range(2)
        ]
        for b in range(blocks)
    ]
    others = [
        pltpu.make_async_copy(sent[b], panels.at[1, b], sent_sem.at[b]) for b in range(blocks)
    ]
    for b in range(blocks):
        for c in range(2):
            loads[b][c].start()
    for other in others:
        other.start()
    stores = []
    for b in range(blocks):
        order = order_matrix(position_ref[b : b + 1, :])
        for c in range(2):
            loads[b][c].wait()
            panels[0, b, c] = jnp.dot(
                order, raw[b, c], preferred_element_type=jnp.float32
            ).astype(jnp.bfloat16)
        store = pltpu.make_async_copy(panels.at[0, b], panel_ref.at[b], out_sem.at[b])
        store.start()
        stores.append(store)
    for other in others:
        other.wait()

    def one_tile(index, carry):
        channel = index // (blocks * blocks)
        a = index // blocks % blocks
        b = index % blocks
        lags = tile_lags(
            panels[channel, a, 0], panels[channel, a, 1], panels[channel, b, 0], panels[channel, b, 1]
        )
        center = lax.broadcasted_iota(jnp.int32, lags.shape, 1) == width - 1
        lags_ref[index] = jnp.where(jnp.logical_and(center, a == b), 0.0, lags)
        return carry

    lax.fori_loop(0, 2 * blocks * blocks, one_tile, 0)
    for store in stores:
        store.wait()


def own_level(position_input, volts, sent, levels):
    blocks, width = position_input.shape
    samples = volts.shape[3]
    return pl.pallas_call(
        functools.partial(own_kernel, levels, blocks),
        out_shape=(
            jax.ShapeDtypeStruct((blocks, 2, width, samples), jnp.bfloat16),
            jax.ShapeDtypeStruct((2 * blocks * blocks, 2, 2 * width), jnp.float32),
        ),
        in_specs=[WHOLE, ANY] + [ANY] * blocks,
        out_specs=(ANY, WHOLE),
        scratch_shapes=[
            pltpu.VMEM((blocks, 2, width, samples), jnp.bfloat16),
            pltpu.VMEM((2, blocks, 2, width, samples), jnp.bfloat16),
            pltpu.SemaphoreType.DMA((blocks, 2)),
            pltpu.SemaphoreType.DMA((blocks,)),
            pltpu.SemaphoreType.DMA((blocks,)),
        ],
        compiler_params=pltpu.CompilerParams(vmem_limit_bytes=32 << 20),
        cost_estimate=pl.CostEstimate(
            flops=16 * blocks * blocks * width * width * samples,
            bytes_accessed=12 * blocks * width * samples,
            transcendentals=0,
        ),
        name="own_level",
    )(position_input, volts, *sent)


def pair_lags(blocks, levels, panel, partners, panel_sem, partner_sem, panel_ref, partner_refs):
    loads = [
        pltpu.make_async_copy(partner_refs[level], partners.at[level], partner_sem.at[level])
        for level in range(levels)
    ]
    own_loads = [
        pltpu.make_async_copy(panel_ref.at[a], panel.at[a], panel_sem.at[a]) for a in range(blocks)
    ]
    loads[0].start()
    for own_load in own_loads:
        own_load.start()
    for load in loads[1:]:
        load.start()
    rows = []
    for level in range(levels):
        loads[level].wait()
        for a in range(blocks):
            if level == 0:
                own_loads[a].wait()
            rows.append(
                tile_lags(panel[a, 0], panel[a, 1], partners[level, 0], partners[level, 1])
            )
    lags = jnp.concatenate(rows, axis=0)
    return jnp.concatenate([lags, conjugate_lags(lags)], axis=0)


def first_kernel(blocks, levels, out_rows, target_ref, own_ref, panel_ref, *refs):
    partner_refs = refs[:levels]
    sums_ref, panel, partners, panel_sem, partner_sem = refs[levels:]
    lags = pair_lags(
        blocks, levels, panel, partners, panel_sem, partner_sem, panel_ref, partner_refs
    )
    own = own_ref[...]
    lags = jnp.concatenate([own, lags], axis=0)
    sums_ref[...] = group_sums(target_ref[...], lags, out_rows)


def last_kernel(blocks, levels, out_rows, target_ref, sums_ref, panel_ref, *refs):
    partner_refs = refs[:levels]
    out_refs = refs[levels:-4]
    panel, partners, panel_sem, partner_sem = refs[-4:]
    lags = pair_lags(
        blocks, levels, panel, partners, panel_sem, partner_sem, panel_ref, partner_refs
    )
    sums = sums_ref[...] + group_sums(target_ref[...], lags, out_rows)
    share = out_rows // len(out_refs)
    for place, out_ref in enumerate(out_refs):
        out_ref[...] = sums[place * share : (place + 1) * share]


def pair_call(kernel, targets, before, panel, partners, out_shapes, out_rows, name):
    blocks, _, width, samples = panel.shape
    levels = len(partners)
    return pl.pallas_call(
        functools.partial(kernel, blocks, levels, out_rows),
        out_shape=out_shapes,
        in_specs=[WHOLE, WHOLE, ANY] + [ANY] * levels,
        out_specs=jax.tree.map(lambda _: WHOLE, out_shapes),
        scratch_shapes=[
            pltpu.VMEM((blocks, 2, width, samples), jnp.bfloat16),
            pltpu.VMEM((levels, 2, width, samples), jnp.bfloat16),
            pltpu.SemaphoreType.DMA((blocks,)),
            pltpu.SemaphoreType.DMA((levels,)),
        ],
        compiler_params=pltpu.CompilerParams(vmem_limit_bytes=32 << 20),
        cost_estimate=pl.CostEstimate(
            flops=8 * levels * blocks * width * width * samples,
            bytes_accessed=4 * (blocks + levels) * width * samples,
            transcendentals=0,
        ),
        name=name,
    )(targets, before, panel, *partners)


def on_device(volts, position_input, tile_group):
    blocks, width = position_input.shape
    devices = lax.axis_size("inp")
    levels = devices.bit_length() - 1
    me = lax.axis_index("inp")
    mine = parity(me, levels)

    arrived = []
    sent = []
    for b in range(blocks):
        sent.append(order_to_send(position_input, volts, b, levels))
        arrived.append([xor_permute(sent[b], "inp", 1 << level) for level in range(levels)])

    all_groups = lax.all_gather(tile_group, "inp", axis=0, tiled=True)
    all_groups = all_groups.reshape(devices, blocks, levels + 1, blocks)

    def targets(groups, channel):
        groups = groups.reshape(-1).astype(jnp.int32)
        channel = jnp.broadcast_to(channel, groups.shape).astype(jnp.int32)
        place = ((groups // RG_DEV) ^ me) * RG_DEV + groups % RG_DEV
        return (place * 4 + channel * 2)[:, None] + jnp.arange(2, dtype=jnp.int32)[None, :]

    own_groups = jnp.concatenate([tile_group[:, 0].reshape(-1)] * 2)
    own_channel = jnp.repeat(jnp.stack([mine, 1 - mine]), blocks * blocks)
    own_targets = targets(own_groups, own_channel).reshape(-1)
    partner_groups = jnp.stack(
        [
            lax.dynamic_index_in_dim(all_groups, me ^ (1 << level), 0, keepdims=False)[:, level + 1]
            for level in range(levels)
        ]
    )
    forward = tile_group[:, 1:]
    pair_targets = [
        jnp.concatenate(
            [
                targets(forward[:, :, b].T, mine).reshape(-1),
                targets(partner_groups[:, b, :], mine).reshape(-1),
            ]
        )
        for b in range(blocks)
    ]

    panel, own_lags = own_level(position_input, volts, sent, levels)
    own_lags = own_lags.reshape(-1, 2 * width)
    out_rows = devices * RG_DEV * 4
    sums = pair_call(
        first_kernel,
        jnp.concatenate([own_targets, pair_targets[0]])[None, :],
        own_lags,
        panel,
        arrived[0],
        jax.ShapeDtypeStruct((out_rows, 2 * width), jnp.float32),
        out_rows,
        "pairs_first",
    )
    parts = pair_call(
        last_kernel,
        pair_targets[1][None, :],
        sums,
        panel,
        arrived[1],
        tuple(jax.ShapeDtypeStruct((RG_DEV * 4, 2 * width), jnp.float32) for _ in range(devices)),
        out_rows,
        "pairs_last",
    )
    total = parts[0]
    for distance in range(1, devices):
        total = total + xor_permute(parts[distance], "inp", distance)
    return total.reshape(RG_DEV, 2, 2, 2 * width)[..., : 2 * width - 1]


def solution(mesh):
    return jax.shard_map(
        on_device,
        mesh=mesh,
        in_specs=(P("freq", None, "inp", None), P("inp", None), P("inp", None, None)),
        out_specs=P("inp", "freq", None, None),
        check_vma=False,
    )
```

```python
import functools

import jax
import jax.numpy as jnp
from jax import lax
from jax.experimental import pallas as pl
from jax.experimental.pallas import tpu as pltpu
from jax.sharding import PartitionSpec as P

RG_DEV = 8
HBM = pl.BlockSpec(memory_space=pltpu.HBM)
WHOLE = pl.BlockSpec(memory_space=pltpu.VMEM)


def xor_permute(x, axis, distance):
    return lax.ppermute(x, axis, [(i, i ^ distance) for i in range(lax.axis_size(axis))])


def parity(index, levels):
    bits = index & 1
    for level in range(1, levels):
        bits = bits ^ ((index >> level) & 1)
    return bits


def order_matrix(position_row):
    width = position_row.shape[-1]
    by_position = jnp.transpose(jnp.broadcast_to(position_row, (width, width)))
    inputs = lax.broadcasted_iota(jnp.int32, (width, width), 1)
    return (by_position == inputs).astype(jnp.float32).astype(jnp.bfloat16)


def product(x, y):
    return lax.dot_general(x, y, (((1,), (1,)), ((), ())), preferred_element_type=jnp.float32)


def lag_rows(tiles):
    count, width, _ = tiles.shape
    half = width // 2
    low, high = tiles[:, :half], tiles[:, half:]
    sheared = jnp.concatenate(
        [
            high[:, :, :half],
            high[:, :, half:] + low[:, :, :half],
            low[:, :, half:],
            jnp.zeros((count, half, half), jnp.float32),
        ],
        axis=2,
    )
    rows = half
    while rows > 8:
        rows //= 2
        upper = sheared[:, :rows].reshape(count * rows, 2 * width)
        upper = pltpu.roll(upper, rows, 1).reshape(count, rows, 2 * width)
        sheared = upper + sheared[:, rows:]
    flat = sheared.reshape(count * rows, 2 * width)
    sublane = lax.broadcasted_iota(jnp.int32, flat.shape, 0) % 8
    while rows > 1:
        rows //= 2
        flat = jnp.where((sublane & rows) == 0, pltpu.roll(flat, rows, 1), flat)
    return jnp.sum(flat.reshape(count, 8, 2 * width), axis=1)


def tile_lags(x_re, x_im, y_re, y_im, samples):
    real_part = product(x_re, y_re) + product(x_im, y_im)
    imag_part = product(x_im, y_re) - product(x_re, y_im)
    return lag_rows(jnp.stack([real_part, imag_part])) * (1.0 / samples)


def split_bf16(x):
    first = x.astype(jnp.bfloat16)
    rest = x - first.astype(jnp.float32)
    second = rest.astype(jnp.bfloat16)
    third = (rest - second.astype(jnp.float32)).astype(jnp.bfloat16)
    return first, second, third


def conjugate_lags(lags):
    count, width = lags.shape
    flip = (
        lax.broadcasted_iota(jnp.int32, (width, width), 0)
        + lax.broadcasted_iota(jnp.int32, (width, width), 1)
        == width - 2
    )
    flip = flip.astype(jnp.float32).astype(jnp.bfloat16)
    parts = jnp.dot(
        jnp.concatenate(split_bf16(lags), axis=0), flip, preferred_element_type=jnp.float32
    )
    turned = parts[:count] + parts[count : 2 * count] + parts[2 * count :]
    odd = lax.broadcasted_iota(jnp.int32, turned.shape, 0) % 2 == 1
    return jnp.where(odd, -turned, turned)


def group_sums(target_row, lags, rows):
    count = lags.shape[0]
    pick = lax.broadcasted_iota(jnp.int32, (rows, count), 0) == target_row
    pick = pick.astype(jnp.float32).astype(jnp.bfloat16)
    total = None
    for part in split_bf16(lags):
        term = jnp.dot(pick, part, preferred_element_type=jnp.float32)
        total = term if total is None else total + term
    return total


def send_kernel(levels, block, cuts, position_ref, volts_ref, *refs):
    out_refs, (position, raw, position_sem, in_sem) = refs[: len(cuts)], refs[len(cuts) :]
    other = 1 - parity(lax.axis_index("inp"), levels)
    width = raw.shape[1]
    load_position = pltpu.make_async_copy(position_ref, position, position_sem)
    load_position.start()
    loads = [
        pltpu.make_async_copy(
            volts_ref.at[other, c, pl.ds(block * width, width)], raw.at[c], in_sem.at[c]
        )
        for c in range(2)
    ]
    for load in loads:
        load.start()
    load_position.wait()
    order = order_matrix(position[block : block + 1, :])
    for c in range(2):
        loads[c].wait()
        for (first, last), out_ref in zip(cuts, out_refs):
            out_ref[c] = jnp.dot(
                order, raw[c, :, first:last], preferred_element_type=jnp.float32
            ).astype(jnp.bfloat16)


def order_to_send(position_input, volts, block, cuts, levels):
    blocks, width = position_input.shape
    samples = volts.shape[3]
    return pl.pallas_call(
        functools.partial(send_kernel, levels, block, cuts),
        out_shape=[
            jax.ShapeDtypeStruct((2, width, last - first), jnp.bfloat16) for first, last in cuts
        ],
        in_specs=[HBM, HBM],
        out_specs=[WHOLE] * len(cuts),
        scratch_shapes=[
            pltpu.VMEM((blocks, width), jnp.int32),
            pltpu.VMEM((2, width, samples), jnp.bfloat16),
            pltpu.SemaphoreType.DMA(()),
            pltpu.SemaphoreType.DMA((2,)),
        ],
        compiler_params=pltpu.CompilerParams(vmem_limit_bytes=12 << 20),
        cost_estimate=pl.CostEstimate(
            flops=4 * width * width * samples, bytes_accessed=8 * width * samples, transcendentals=0
        ),
        name="order_to_send",
    )(pltpu.with_memory_space_constraint(position_input, pltpu.HBM), volts)


def own_kernel(levels, out_rows, target_ref, position_ref, volts_ref, *refs):
    panel_ref, sums_ref, raw, other_panel, lags_ref, in_sem = refs
    blocks, _, width, _ = panel_ref.shape
    mine = parity(lax.axis_index("inp"), levels)
    channels = (mine, 1 - mine)
    loads = [
        [
            [
                pltpu.make_async_copy(
                    volts_ref.at[channels[f], c, pl.ds(b * width, width)],
                    raw.at[f, b, c],
                    in_sem.at[f, b, c],
                )
                for c in range(2)
            ]
            for b in range(blocks)
        ]
        for f in range(2)
    ]
    for f in range(2):
        for b in range(blocks):
            for c in range(2):
                loads[f][b][c].start()
    orders = [order_matrix(position_ref[b : b + 1, :]) for b in range(blocks)]
    for f, panel in enumerate((panel_ref, other_panel)):
        for b in range(blocks):
            for c in range(2):
                loads[f][b][c].wait()
                panel[b, c] = jnp.dot(
                    orders[b], raw[f, b, c], preferred_element_type=jnp.float32
                ).astype(jnp.bfloat16)

        def one_tile(index, carry, panel=panel, f=f):
            a = index // blocks
            b = index % blocks
            lags = tile_lags(panel[a, 0], panel[a, 1], panel[b, 0], panel[b, 1], panel.shape[3])
            center = lax.broadcasted_iota(jnp.int32, lags.shape, 1) == width - 1
            lags_ref[f * blocks * blocks + index] = jnp.where(
                jnp.logical_and(center, a == b), 0.0, lags
            )
            return carry

        lax.fori_loop(0, blocks * blocks, one_tile, 0)
    lags = jnp.concatenate([lags_ref[i] for i in range(2 * blocks * blocks)], axis=0)
    sums_ref[...] = group_sums(target_ref[...], lags, out_rows)


def own_level(targets, position_input, volts, levels, out_rows):
    blocks, width = position_input.shape
    samples = volts.shape[3]
    return pl.pallas_call(
        functools.partial(own_kernel, levels, out_rows),
        out_shape=(
            jax.ShapeDtypeStruct((blocks, 2, width, samples), jnp.bfloat16),
            jax.ShapeDtypeStruct((out_rows, 2 * width), jnp.float32),
        ),
        in_specs=[WHOLE, WHOLE, HBM],
        out_specs=(WHOLE, WHOLE),
        scratch_shapes=[
            pltpu.VMEM((2, blocks, 2, width, samples), jnp.bfloat16),
            pltpu.VMEM((blocks, 2, width, samples), jnp.bfloat16),
            pltpu.VMEM((2 * blocks * blocks, 2, 2 * width), jnp.float32),
            pltpu.SemaphoreType.DMA((2, blocks, 2)),
        ],
        compiler_params=pltpu.CompilerParams(vmem_limit_bytes=24 << 20),
        cost_estimate=pl.CostEstimate(
            flops=16 * blocks * blocks * width * width * samples,
            bytes_accessed=12 * blocks * width * samples,
            transcendentals=0,
        ),
        name="own_level",
    )(targets, position_input, volts)


def pair_kernel(levels, cut, target_ref, sums_ref, panel_ref, *refs):
    partner_refs, out_refs = refs[:levels], refs[levels:]
    blocks = panel_ref.shape[0]
    first, last = cut
    rows = [
        tile_lags(
            panel_ref[a, 0, :, first:last],
            panel_ref[a, 1, :, first:last],
            partner_ref[0],
            partner_ref[1],
            panel_ref.shape[3],
        )
        for partner_ref in partner_refs
        for a in range(blocks)
    ]
    lags = jnp.concatenate(rows, axis=0)
    lags = jnp.concatenate([lags, conjugate_lags(lags)], axis=0)
    sums = sums_ref[...] + group_sums(target_ref[...], lags, sums_ref.shape[0])
    share = sums.shape[0] // len(out_refs)
    for place, out_ref in enumerate(out_refs):
        out_ref[...] = sums[place * share : (place + 1) * share]


def pair_level(targets, sums, panel, partners, cut, shares):
    blocks, _, width, _ = panel.shape
    levels = len(partners)
    length = cut[1] - cut[0]
    share = jax.ShapeDtypeStruct((sums.shape[0] // shares, sums.shape[1]), jnp.float32)
    return pl.pallas_call(
        functools.partial(pair_kernel, levels, cut),
        out_shape=[share] * shares,
        in_specs=[WHOLE] * (3 + levels),
        out_specs=[WHOLE] * shares,
        compiler_params=pltpu.CompilerParams(vmem_limit_bytes=24 << 20),
        cost_estimate=pl.CostEstimate(
            flops=8 * levels * blocks * width * width * length,
            bytes_accessed=4 * (blocks + levels) * width * length,
            transcendentals=0,
        ),
        name="pair_level",
    )(targets, sums, panel, *partners)


def on_device(volts, position_input, tile_group):
    blocks, width = position_input.shape
    samples = volts.shape[3]
    devices = lax.axis_size("inp")
    levels = devices.bit_length() - 1
    me = lax.axis_index("inp")
    mine = parity(me, levels)
    out_rows = devices * RG_DEV * 4

    def target_rows(groups, owner, channel):
        place = ((groups // RG_DEV) ^ owner) * RG_DEV + groups % RG_DEV
        return (place * 4 + channel * 2)[..., None] + jnp.arange(2, dtype=jnp.int32)

    volts = pltpu.with_memory_space_constraint(volts, pltpu.HBM)
    pieces = []
    cuts_of = [[(0, samples)]] * (blocks - 1) + [[(0, samples // 2), (samples // 2, samples)]]
    turned = []
    for b in range(blocks):
        sent = order_to_send(position_input, volts, b, cuts_of[b], levels)
        for cut, piece in zip(cuts_of[b], sent):
            arrived = [xor_permute(piece, "inp", 1 << level) for level in range(levels)]
            pieces.append((b, cut, arrived))
        if b == 0:
            turned = [
                xor_permute(
                    target_rows(tile_group[:, level + 1], me ^ (1 << level), 1 - mine).reshape(
                        blocks, -1
                    ),
                    "inp",
                    1 << level,
                )
                for level in range(levels)
            ]

    own_targets = jnp.concatenate(
        [target_rows(tile_group[:, 0], me, channel).reshape(1, -1) for channel in (mine, 1 - mine)],
        axis=1,
    )
    panel, sums = own_level(own_targets, position_input, volts, levels, out_rows)
    forward = target_rows(tile_group[:, 1:], me, mine)
    for number, (b, cut, arrived) in enumerate(pieces):
        targets = jnp.concatenate(
            [forward[:, level, b].reshape(1, -1) for level in range(levels)]
            + [turned[level][b : b + 1] for level in range(levels)],
            axis=1,
        )
        last = number == len(pieces) - 1
        parts = pair_level(targets, sums, panel, arrived, cut, devices if last else 1)
        sums = parts[0]
    total = parts[0]
    for distance in range(1, devices):
        total = total + xor_permute(parts[distance], "inp", distance)
    return total.reshape(RG_DEV, 2, 2, 2 * width)[..., : 2 * width - 1]


def solution(mesh):
    return jax.shard_map(
        on_device,
        mesh=mesh,
        in_specs=(P("freq", None, "inp", None), P("inp", None), P("inp", None, None)),
        out_specs=P("inp", "freq", None, None),
        check_vma=False,
    )
```

```python
import functools

import jax
import jax.numpy as jnp
from jax import lax
from jax.experimental import pallas as pl
from jax.experimental.pallas import tpu as pltpu
from jax.sharding import PartitionSpec as P

RG_DEV = 8
GROUP_ROWS = 16
HBM = pl.BlockSpec(memory_space=pltpu.HBM)
WHOLE = pl.BlockSpec(memory_space=pltpu.VMEM)


def xor_permute(x, axis, distance):
    return lax.ppermute(x, axis, [(i, i ^ distance) for i in range(lax.axis_size(axis))])


def parity(index, levels):
    bits = index & 1
    for level in range(1, levels):
        bits = bits ^ ((index >> level) & 1)
    return bits


def order_matrix(position_row):
    width = position_row.shape[-1]
    by_position = jnp.transpose(jnp.broadcast_to(position_row, (width, width)))
    inputs = lax.broadcasted_iota(jnp.int32, (width, width), 1)
    return (by_position == inputs).astype(jnp.float32).astype(jnp.bfloat16)


def product(x, y):
    return lax.dot_general(x, y, (((1,), (1,)), ((), ())), preferred_element_type=jnp.float32)


def lag_rows(tiles):
    count, width, _ = tiles.shape
    half = width // 2
    low, high = tiles[:, :half], tiles[:, half:]
    sheared = jnp.concatenate(
        [
            high[:, :, :half],
            high[:, :, half:] + low[:, :, :half],
            low[:, :, half:],
            jnp.zeros((count, half, half), jnp.float32),
        ],
        axis=2,
    )
    rows = half
    while rows > 8:
        rows //= 2
        upper = sheared[:, :rows].reshape(count * rows, 2 * width)
        upper = pltpu.roll(upper, rows, 1).reshape(count, rows, 2 * width)
        sheared = upper + sheared[:, rows:]
    flat = sheared.reshape(count * rows, 2 * width)
    sublane = lax.broadcasted_iota(jnp.int32, flat.shape, 0) % 8
    while rows > 1:
        rows //= 2
        flat = jnp.where((sublane & rows) == 0, pltpu.roll(flat, rows, 1), flat)
    return jnp.sum(flat.reshape(count, 8, 2 * width), axis=1)


def tile_lags(x_re, x_im, y_re, y_im, samples):
    real_part = product(x_re, y_re) + product(x_im, y_im)
    imag_part = product(x_im, y_re) - product(x_re, y_im)
    return lag_rows(jnp.stack([real_part, imag_part])) * (1.0 / samples)


def split_bf16(x):
    first = x.astype(jnp.bfloat16)
    rest = x - first.astype(jnp.float32)
    second = rest.astype(jnp.bfloat16)
    third = (rest - second.astype(jnp.float32)).astype(jnp.bfloat16)
    return first, second, third


def conjugate_lags(lags):
    count, width = lags.shape
    flip = (
        lax.broadcasted_iota(jnp.int32, (width, width), 0)
        + lax.broadcasted_iota(jnp.int32, (width, width), 1)
        == width - 2
    )
    flip = flip.astype(jnp.float32).astype(jnp.bfloat16)
    parts = jnp.dot(
        jnp.concatenate(split_bf16(lags), axis=0), flip, preferred_element_type=jnp.float32
    )
    turned = parts[:count] + parts[count : 2 * count] + parts[2 * count :]
    odd = lax.broadcasted_iota(jnp.int32, turned.shape, 0) % 2 == 1
    return jnp.where(odd, -turned, turned)


def group_sums(target_row, lags, rows):
    count = lags.shape[0]
    pick = lax.broadcasted_iota(jnp.int32, (rows, count), 0) == target_row
    pick = pick.astype(jnp.float32).astype(jnp.bfloat16)
    total = None
    for part in split_bf16(lags):
        term = jnp.dot(pick, part, preferred_element_type=jnp.float32)
        total = term if total is None else total + term
    return total


def send_kernel(levels, pieces, with_groups, position_ref, volts_ref, *refs):
    if with_groups:
        group_ref, refs = refs[0], refs[1:]
    out_refs, refs = refs[: len(pieces)], refs[len(pieces) :]
    position, raw, position_sem, in_sem = refs[:4]
    other = 1 - parity(lax.axis_index("inp"), levels)
    width = position.shape[1]
    load_position = pltpu.make_async_copy(position_ref, position, position_sem)
    load_position.start()
    if with_groups:
        groups, group_sem = refs[4:]
        load_groups = pltpu.make_async_copy(group_ref, groups, group_sem)
        load_groups.start()
    blocks = sorted({block for block, _, _ in pieces})
    spans = [
        (
            min(first for b, first, _ in pieces if b == block),
            max(last for b, _, last in pieces if b == block),
        )
        for block in blocks
    ]
    loads = [
        [
            pltpu.make_async_copy(
                volts_ref.at[other, c, pl.ds(block * width, width), pl.ds(first, last - first)],
                raw.at[i, c, :, pl.ds(first, last - first)],
                in_sem.at[i, c],
            )
            for c in range(2)
        ]
        for i, (block, (first, last)) in enumerate(zip(blocks, spans))
    ]
    for load in loads:
        load[0].start()
        load[1].start()
    load_position.wait()
    orders = [order_matrix(position[block : block + 1, :]) for block in blocks]
    for i, block in enumerate(blocks):
        for c in range(2):
            loads[i][c].wait()
            for (b, first, last), out_ref in zip(pieces, out_refs):
                if b == block:
                    out_ref[c * width : (c + 1) * width, :] = jnp.dot(
                        orders[i], raw[i, c, :, first:last], preferred_element_type=jnp.float32
                    ).astype(jnp.bfloat16)
    if with_groups:
        load_groups.wait()
        out_refs[0][2 * width :, :] = jnp.zeros(
            (GROUP_ROWS, out_refs[0].shape[1]), jnp.bfloat16
        )
        rows = jnp.concatenate([groups[b] for b in range(groups.shape[0])], axis=0)
        lines, lanes = rows.shape
        rows = jnp.pad(rows, ((0, GROUP_ROWS - lines), (0, 128 - lanes)))
        out_refs[0][2 * width :, :128] = rows.astype(jnp.float32).astype(jnp.bfloat16)


def order_to_send(position_input, volts, groups, pieces, levels):
    width = position_input.shape[1]
    samples = volts.shape[3]
    count = len({block for block, _, _ in pieces})
    total = sum(last - first for _, first, last in pieces)
    with_groups = groups is not None
    extra = [GROUP_ROWS if with_groups else 0] + [0] * (len(pieces) - 1)
    inputs = [position_input, volts] + ([groups] if with_groups else [])
    scratch = [
        pltpu.VMEM(position_input.shape, jnp.int32),
        pltpu.VMEM((count, 2, width, samples), jnp.bfloat16),
        pltpu.SemaphoreType.DMA(()),
        pltpu.SemaphoreType.DMA((count, 2)),
    ]
    if with_groups:
        scratch += [pltpu.VMEM(groups.shape, jnp.int32), pltpu.SemaphoreType.DMA(())]
    return pl.pallas_call(
        functools.partial(send_kernel, levels, pieces, with_groups),
        out_shape=[
            jax.ShapeDtypeStruct((2 * width + more, last - first), jnp.bfloat16)
            for (_, first, last), more in zip(pieces, extra)
        ],
        in_specs=[HBM] * len(inputs),
        out_specs=[WHOLE] * len(pieces),
        scratch_shapes=scratch,
        compiler_params=pltpu.CompilerParams(vmem_limit_bytes=16 << 20),
        cost_estimate=pl.CostEstimate(
            flops=4 * width * width * total, bytes_accessed=8 * width * total, transcendentals=0
        ),
        name="order_to_send",
    )(*[pltpu.with_memory_space_constraint(x, pltpu.HBM) for x in inputs])


def own_kernel(levels, out_rows, target_ref, position_ref, volts_ref, *refs):
    panel_ref, sums_ref, raw, other_panel, lags_ref, in_sem = refs
    blocks, _, width, _ = panel_ref.shape
    mine = parity(lax.axis_index("inp"), levels)
    channels = (mine, 1 - mine)
    loads = [
        [
            [
                pltpu.make_async_copy(
                    volts_ref.at[channels[f], c, pl.ds(b * width, width)],
                    raw.at[f, b, c],
                    in_sem.at[f, b, c],
                )
                for c in range(2)
            ]
            for b in range(blocks)
        ]
        for f in range(2)
    ]
    for f in range(2):
        for b in range(blocks):
            for c in range(2):
                loads[f][b][c].start()
    orders = [order_matrix(position_ref[b : b + 1, :]) for b in range(blocks)]
    for f, panel in enumerate((panel_ref, other_panel)):
        for b in range(blocks):
            for c in range(2):
                loads[f][b][c].wait()
                panel[b, c] = jnp.dot(
                    orders[b], raw[f, b, c], preferred_element_type=jnp.float32
                ).astype(jnp.bfloat16)

        def one_tile(index, carry, panel=panel, f=f):
            a = index // blocks
            b = index % blocks
            lags = tile_lags(panel[a, 0], panel[a, 1], panel[b, 0], panel[b, 1], panel.shape[3])
            center = lax.broadcasted_iota(jnp.int32, lags.shape, 1) == width - 1
            lags_ref[f * blocks * blocks + index] = jnp.where(
                jnp.logical_and(center, a == b), 0.0, lags
            )
            return carry

        lax.fori_loop(0, blocks * blocks, one_tile, 0)
    lags = jnp.concatenate([lags_ref[i] for i in range(2 * blocks * blocks)], axis=0)
    sums_ref[...] = group_sums(target_ref[...], lags, out_rows)


def own_level(targets, position_input, volts, levels, out_rows):
    blocks, width = position_input.shape
    samples = volts.shape[3]
    return pl.pallas_call(
        functools.partial(own_kernel, levels, out_rows),
        out_shape=(
            jax.ShapeDtypeStruct((blocks, 2, width, samples), jnp.bfloat16),
            jax.ShapeDtypeStruct((out_rows, 2 * width), jnp.float32),
        ),
        in_specs=[WHOLE, WHOLE, HBM],
        out_specs=(WHOLE, WHOLE),
        scratch_shapes=[
            pltpu.VMEM((2, blocks, 2, width, samples), jnp.bfloat16),
            pltpu.VMEM((blocks, 2, width, samples), jnp.bfloat16),
            pltpu.VMEM((2 * blocks * blocks, 2, 2 * width), jnp.float32),
            pltpu.SemaphoreType.DMA((2, blocks, 2)),
        ],
        compiler_params=pltpu.CompilerParams(vmem_limit_bytes=24 << 20),
        cost_estimate=pl.CostEstimate(
            flops=16 * blocks * blocks * width * width * samples,
            bytes_accessed=12 * blocks * width * samples,
            transcendentals=0,
        ),
        name="own_level",
    )(targets, position_input, pltpu.with_memory_space_constraint(volts, pltpu.HBM))


def pair_kernel(levels, spans, target_ref, sums_ref, panel_ref, *refs):
    partner_refs, out_refs = refs[: levels * len(spans)], refs[levels * len(spans) :]
    blocks, _, width, samples = panel_ref.shape
    rows = []
    for level in range(levels):
        for a in range(blocks):
            real_part, imag_part = 0.0, 0.0
            for i, (first, last) in enumerate(spans):
                partner = partner_refs[level * len(spans) + i]
                x_re, x_im = panel_ref[a, 0, :, first:last], panel_ref[a, 1, :, first:last]
                y_re, y_im = partner[:width], partner[width : 2 * width]
                real_part = real_part + (product(x_re, y_re) + product(x_im, y_im))
                imag_part = imag_part + (product(x_im, y_re) - product(x_re, y_im))
            rows.append(lag_rows(jnp.stack([real_part, imag_part])) * (1.0 / samples))
    lags = jnp.concatenate(rows, axis=0)
    lags = jnp.concatenate([lags, conjugate_lags(lags)], axis=0)
    sums = sums_ref[...] + group_sums(target_ref[...], lags, sums_ref.shape[0])
    share = sums.shape[0] // len(out_refs)
    for place, out_ref in enumerate(out_refs):
        out_ref[...] = sums[place * share : (place + 1) * share]


def pair_level(targets, sums, panel, arrived, spans, shares):
    blocks, _, width, _ = panel.shape
    levels = len(arrived)
    length = sum(last - first for first, last in spans)
    share = jax.ShapeDtypeStruct((sums.shape[0] // shares, sums.shape[1]), jnp.float32)
    partners = [piece for level in arrived for piece in level]
    return pl.pallas_call(
        functools.partial(pair_kernel, levels, spans),
        out_shape=[share] * shares,
        in_specs=[WHOLE] * (3 + len(partners)),
        out_specs=[WHOLE] * shares,
        compiler_params=pltpu.CompilerParams(vmem_limit_bytes=24 << 20),
        cost_estimate=pl.CostEstimate(
            flops=8 * levels * blocks * width * width * length,
            bytes_accessed=4 * (blocks + levels) * width * length,
            transcendentals=0,
        ),
        name="pair_level",
    )(targets, sums, panel, *partners)


def on_device(volts, position_input, tile_group):
    blocks, width = position_input.shape
    samples = volts.shape[3]
    devices = lax.axis_size("inp")
    levels = devices.bit_length() - 1
    me = lax.axis_index("inp")
    mine = parity(me, levels)
    out_rows = devices * RG_DEV * 4

    def target_rows(groups, channel):
        place = ((groups // RG_DEV) ^ me) * RG_DEV + groups % RG_DEV
        return (place * 4 + channel * 2)[..., None] + jnp.arange(2, dtype=jnp.int32)

    first_cut, last_cut = samples // 4, samples - samples // 4
    head = [(0, 0, first_cut)]
    rest = [(0, first_cut, samples), (1, 0, last_cut), (1, last_cut, samples)]
    by_block = tile_group.transpose(0, 2, 1)
    sent = order_to_send(position_input, volts, by_block, head, levels)
    partner_of = [functools.partial(xor_permute, axis="inp", distance=1 << l) for l in range(levels)]
    head_arrived = [send(sent[0]) for send in partner_of]
    sent = order_to_send(position_input, volts, None, rest, levels)
    rest_arrived = [[send(piece) for send in partner_of] for piece in sent]

    own_targets = jnp.concatenate(
        [target_rows(tile_group[:, 0], channel).reshape(1, -1) for channel in (mine, 1 - mine)],
        axis=1,
    )
    panel, sums = own_level(own_targets, position_input, volts, levels, out_rows)
    forward = target_rows(tile_group[:, 1:], mine)
    turned = [
        target_rows(
            piece[2 * width : 2 * width + blocks * blocks, level + 1].astype(jnp.int32), mine
        ).reshape(blocks, -1)
        for level, piece in enumerate(head_arrived)
    ]
    targets = [
        jnp.concatenate(
            [forward[:, level, b].reshape(1, -1) for level in range(levels)]
            + [turned[level][b : b + 1] for level in range(levels)],
            axis=1,
        )
        for b in range(blocks)
    ]
    steps = [
        (0, [head[0], rest[0]], list(zip(head_arrived, rest_arrived[0]))),
        (1, [rest[1]], [[piece] for piece in rest_arrived[1]]),
        (1, [rest[2]], [[piece] for piece in rest_arrived[2]]),
    ]
    for number, (b, pieces, arrived) in enumerate(steps):
        shares = devices if number == len(steps) - 1 else 1
        spans = [(first, last) for _, first, last in pieces]
        parts = pair_level(targets[b], sums, panel, arrived, spans, shares)
        sums = parts[0]
    total = parts[0]
    for distance in range(1, devices):
        total = total + xor_permute(parts[distance], "inp", distance)
    return total.reshape(RG_DEV, 2, 2, 2 * width)[..., : 2 * width - 1]


def solution(mesh):
    return jax.shard_map(
        on_device,
        mesh=mesh,
        in_specs=(P("freq", None, "inp", None), P("inp", None), P("inp", None, None)),
        out_specs=P("inp", "freq", None, None),
        check_vma=False,
    )
```

```python
import functools

import jax
import jax.numpy as jnp
from jax import lax
from jax.experimental import pallas as pl
from jax.experimental.pallas import tpu as pltpu
from jax.sharding import PartitionSpec as P

RG_DEV = 8
GROUP_ROWS = 16
HBM = pl.BlockSpec(memory_space=pltpu.HBM)
WHOLE = pl.BlockSpec(memory_space=pltpu.VMEM)


def xor_permute(x, axis, distance):
    return lax.ppermute(x, axis, [(i, i ^ distance) for i in range(lax.axis_size(axis))])


def parity(index, levels):
    bits = index & 1
    for level in range(1, levels):
        bits = bits ^ ((index >> level) & 1)
    return bits


def order_matrix(position_row):
    width = position_row.shape[-1]
    by_position = jnp.transpose(jnp.broadcast_to(position_row, (width, width)))
    inputs = lax.broadcasted_iota(jnp.int32, (width, width), 1)
    return (by_position == inputs).astype(jnp.float32).astype(jnp.bfloat16)


def product(x, y):
    return lax.dot_general(x, y, (((1,), (1,)), ((), ())), preferred_element_type=jnp.float32)


def lag_rows(tiles):
    count, width, _ = tiles.shape
    half = width // 2
    low, high = tiles[:, :half], tiles[:, half:]
    sheared = jnp.concatenate(
        [
            high[:, :, :half],
            high[:, :, half:] + low[:, :, :half],
            low[:, :, half:],
            jnp.zeros((count, half, half), jnp.float32),
        ],
        axis=2,
    )
    rows = half
    while rows > 8:
        rows //= 2
        upper = sheared[:, :rows].reshape(count * rows, 2 * width)
        upper = pltpu.roll(upper, rows, 1).reshape(count, rows, 2 * width)
        sheared = upper + sheared[:, rows:]
    flat = sheared.reshape(count * rows, 2 * width)
    sublane = lax.broadcasted_iota(jnp.int32, flat.shape, 0) % 8
    while rows > 1:
        rows //= 2
        flat = jnp.where((sublane & rows) == 0, pltpu.roll(flat, rows, 1), flat)
    return jnp.sum(flat.reshape(count, 8, 2 * width), axis=1)


def tile_lags(x_re, x_im, y_re, y_im, samples):
    real_part = product(x_re, y_re) + product(x_im, y_im)
    imag_part = product(x_im, y_re) - product(x_re, y_im)
    return lag_rows(jnp.stack([real_part, imag_part])) * (1.0 / samples)


def split_bf16(x):
    first = x.astype(jnp.bfloat16)
    rest = x - first.astype(jnp.float32)
    second = rest.astype(jnp.bfloat16)
    third = (rest - second.astype(jnp.float32)).astype(jnp.bfloat16)
    return first, second, third


def conjugate_lags(lags):
    count, width = lags.shape
    flip = (
        lax.broadcasted_iota(jnp.int32, (width, width), 0)
        + lax.broadcasted_iota(jnp.int32, (width, width), 1)
        == width - 2
    )
    flip = flip.astype(jnp.float32).astype(jnp.bfloat16)
    parts = jnp.dot(
        jnp.concatenate(split_bf16(lags), axis=0), flip, preferred_element_type=jnp.float32
    )
    turned = parts[:count] + parts[count : 2 * count] + parts[2 * count :]
    odd = lax.broadcasted_iota(jnp.int32, turned.shape, 0) % 2 == 1
    return jnp.where(odd, -turned, turned)


def group_sums(target_row, lags, rows):
    count = lags.shape[0]
    pick = lax.broadcasted_iota(jnp.int32, (rows, count), 0) == target_row
    pick = pick.astype(jnp.float32).astype(jnp.bfloat16)
    total = None
    for part in split_bf16(lags):
        term = jnp.dot(pick, part, preferred_element_type=jnp.float32)
        total = term if total is None else total + term
    return total


def send_kernel(levels, pieces, with_groups, position_ref, volts_ref, *refs):
    if with_groups:
        group_ref, refs = refs[0], refs[1:]
    out_refs, refs = refs[: len(pieces)], refs[len(pieces) :]
    position, raw, position_sem, in_sem = refs[:4]
    other = 1 - parity(lax.axis_index("inp"), levels)
    width = position.shape[1]
    load_position = pltpu.make_async_copy(position_ref, position, position_sem)
    load_position.start()
    if with_groups:
        groups, group_sem = refs[4:]
        load_groups = pltpu.make_async_copy(group_ref, groups, group_sem)
        load_groups.start()
    blocks = sorted({block for block, _, _ in pieces})
    spans = [
        (
            min(first for b, first, _ in pieces if b == block),
            max(last for b, _, last in pieces if b == block),
        )
        for block in blocks
    ]
    loads = [
        [
            pltpu.make_async_copy(
                volts_ref.at[other, c, pl.ds(block * width, width), pl.ds(first, last - first)],
                raw.at[i, c, :, pl.ds(first, last - first)],
                in_sem.at[i, c],
            )
            for c in range(2)
        ]
        for i, (block, (first, last)) in enumerate(zip(blocks, spans))
    ]
    for load in loads:
        load[0].start()
        load[1].start()
    load_position.wait()
    orders = [order_matrix(position[block : block + 1, :]) for block in blocks]
    for i, block in enumerate(blocks):
        for c in range(2):
            loads[i][c].wait()
            for (b, first, last), out_ref in zip(pieces, out_refs):
                if b == block:
                    out_ref[c * width : (c + 1) * width, :] = jnp.dot(
                        orders[i], raw[i, c, :, first:last], preferred_element_type=jnp.float32
                    ).astype(jnp.bfloat16)
    if with_groups:
        load_groups.wait()
        out_refs[0][2 * width :, :] = jnp.zeros(
            (GROUP_ROWS, out_refs[0].shape[1]), jnp.bfloat16
        )
        rows = jnp.concatenate([groups[b] for b in range(groups.shape[0])], axis=0)
        lines, lanes = rows.shape
        rows = jnp.pad(rows, ((0, GROUP_ROWS - lines), (0, 128 - lanes)))
        out_refs[0][2 * width :, :128] = rows.astype(jnp.float32).astype(jnp.bfloat16)


def order_to_send(position_input, volts, groups, pieces, levels):
    width = position_input.shape[1]
    samples = volts.shape[3]
    count = len({block for block, _, _ in pieces})
    total = sum(last - first for _, first, last in pieces)
    with_groups = groups is not None
    extra = [GROUP_ROWS if with_groups else 0] + [0] * (len(pieces) - 1)
    inputs = [position_input, volts] + ([groups] if with_groups else [])
    scratch = [
        pltpu.VMEM(position_input.shape, jnp.int32),
        pltpu.VMEM((count, 2, width, samples), jnp.bfloat16),
        pltpu.SemaphoreType.DMA(()),
        pltpu.SemaphoreType.DMA((count, 2)),
    ]
    if with_groups:
        scratch += [pltpu.VMEM(groups.shape, jnp.int32), pltpu.SemaphoreType.DMA(())]
    return pl.pallas_call(
        functools.partial(send_kernel, levels, pieces, with_groups),
        out_shape=[
            jax.ShapeDtypeStruct((2 * width + more, last - first), jnp.bfloat16)
            for (_, first, last), more in zip(pieces, extra)
        ],
        in_specs=[HBM] * len(inputs),
        out_specs=[WHOLE] * len(pieces),
        scratch_shapes=scratch,
        compiler_params=pltpu.CompilerParams(vmem_limit_bytes=16 << 20),
        cost_estimate=pl.CostEstimate(
            flops=4 * width * width * total, bytes_accessed=8 * width * total, transcendentals=0
        ),
        name="order_to_send",
    )(*[pltpu.with_memory_space_constraint(x, pltpu.HBM) for x in inputs])


def own_kernel(levels, out_rows, target_ref, position_ref, volts_ref, *refs):
    panel_ref, sums_ref, raw, other_panel, lags_ref, in_sem = refs
    blocks, _, width, _ = panel_ref.shape
    mine = parity(lax.axis_index("inp"), levels)
    channels = (mine, 1 - mine)
    loads = [
        [
            [
                pltpu.make_async_copy(
                    volts_ref.at[channels[f], c, pl.ds(b * width, width)],
                    raw.at[f, b, c],
                    in_sem.at[f, b, c],
                )
                for c in range(2)
            ]
            for b in range(blocks)
        ]
        for f in range(2)
    ]
    for f in range(2):
        for b in range(blocks):
            for c in range(2):
                loads[f][b][c].start()
    orders = [order_matrix(position_ref[b : b + 1, :]) for b in range(blocks)]
    for f, panel in enumerate((panel_ref, other_panel)):
        for b in range(blocks):
            for c in range(2):
                loads[f][b][c].wait()
                panel[b, c] = jnp.dot(
                    orders[b], raw[f, b, c], preferred_element_type=jnp.float32
                ).astype(jnp.bfloat16)

        def one_tile(index, carry, panel=panel, f=f):
            a = index // blocks
            b = index % blocks
            lags = tile_lags(panel[a, 0], panel[a, 1], panel[b, 0], panel[b, 1], panel.shape[3])
            center = lax.broadcasted_iota(jnp.int32, lags.shape, 1) == width - 1
            lags_ref[f * blocks * blocks + index] = jnp.where(
                jnp.logical_and(center, a == b), 0.0, lags
            )
            return carry

        lax.fori_loop(0, blocks * blocks, one_tile, 0)
    lags = jnp.concatenate([lags_ref[i] for i in range(2 * blocks * blocks)], axis=0)
    sums_ref[...] = group_sums(target_ref[...], lags, out_rows)


def own_level(targets, position_input, volts, levels, out_rows):
    blocks, width = position_input.shape
    samples = volts.shape[3]
    return pl.pallas_call(
        functools.partial(own_kernel, levels, out_rows),
        out_shape=(
            jax.ShapeDtypeStruct((blocks, 2, width, samples), jnp.bfloat16),
            jax.ShapeDtypeStruct((out_rows, 2 * width), jnp.float32),
        ),
        in_specs=[WHOLE, WHOLE, HBM],
        out_specs=(WHOLE, WHOLE),
        scratch_shapes=[
            pltpu.VMEM((2, blocks, 2, width, samples), jnp.bfloat16),
            pltpu.VMEM((blocks, 2, width, samples), jnp.bfloat16),
            pltpu.VMEM((2 * blocks * blocks, 2, 2 * width), jnp.float32),
            pltpu.SemaphoreType.DMA((2, blocks, 2)),
        ],
        compiler_params=pltpu.CompilerParams(vmem_limit_bytes=24 << 20),
        cost_estimate=pl.CostEstimate(
            flops=16 * blocks * blocks * width * width * samples,
            bytes_accessed=12 * blocks * width * samples,
            transcendentals=0,
        ),
        name="own_level",
    )(targets, position_input, pltpu.with_memory_space_constraint(volts, pltpu.HBM))


def pair_kernel(levels, spans, target_ref, sums_ref, panel_ref, *refs):
    partner_refs, out_ref = refs[:-1], refs[-1]
    blocks, _, width, samples = panel_ref.shape
    rows = []
    for level in range(levels):
        for a in range(blocks):
            real_part, imag_part = 0.0, 0.0
            for i, (first, last) in enumerate(spans):
                partner = partner_refs[level * len(spans) + i]
                x_re, x_im = panel_ref[a, 0, :, first:last], panel_ref[a, 1, :, first:last]
                y_re, y_im = partner[:width], partner[width : 2 * width]
                real_part = real_part + (product(x_re, y_re) + product(x_im, y_im))
                imag_part = imag_part + (product(x_im, y_re) - product(x_re, y_im))
            rows.append(lag_rows(jnp.stack([real_part, imag_part])) * (1.0 / samples))
    lags = jnp.concatenate(rows, axis=0)
    lags = jnp.concatenate([lags, conjugate_lags(lags)], axis=0)
    out_ref[...] = sums_ref[...] + group_sums(target_ref[...], lags, sums_ref.shape[0])


def pair_level(targets, sums, panel, arrived, spans):
    blocks, _, width, _ = panel.shape
    levels = len(arrived)
    length = sum(last - first for first, last in spans)
    partners = [piece for level in arrived for piece in level]
    return pl.pallas_call(
        functools.partial(pair_kernel, levels, spans),
        out_shape=jax.ShapeDtypeStruct(sums.shape, jnp.float32),
        in_specs=[WHOLE] * (3 + len(partners)),
        out_specs=WHOLE,
        compiler_params=pltpu.CompilerParams(vmem_limit_bytes=24 << 20),
        cost_estimate=pl.CostEstimate(
            flops=8 * levels * blocks * width * width * length,
            bytes_accessed=4 * (blocks + levels) * width * length,
            transcendentals=0,
        ),
        name="pair_level",
    )(targets, sums, panel, *partners)


def on_device(volts, position_input, tile_group):
    blocks, width = position_input.shape
    samples = volts.shape[3]
    devices = lax.axis_size("inp")
    levels = devices.bit_length() - 1
    me = lax.axis_index("inp")
    mine = parity(me, levels)
    out_rows = devices * RG_DEV * 4

    def target_rows(groups, channel):
        return (groups * 4 + channel * 2)[..., None] + jnp.arange(2, dtype=jnp.int32)

    first_cut, last_cut = samples // 4, samples - samples // 4
    head = [(0, 0, first_cut)]
    rest = [(0, first_cut, samples), (1, 0, last_cut), (1, last_cut, samples)]
    by_block = tile_group.transpose(0, 2, 1)
    sent = order_to_send(position_input, volts, by_block, head, levels)
    partner_of = [functools.partial(xor_permute, axis="inp", distance=1 << l) for l in range(levels)]
    head_arrived = [send(sent[0]) for send in partner_of]
    sent = order_to_send(position_input, volts, None, rest, levels)
    rest_arrived = [[send(piece) for send in partner_of] for piece in sent]

    own_targets = jnp.concatenate(
        [target_rows(tile_group[:, 0], channel).reshape(1, -1) for channel in (mine, 1 - mine)],
        axis=1,
    )
    panel, sums = own_level(own_targets, position_input, volts, levels, out_rows)
    forward = target_rows(tile_group[:, 1:], mine)
    turned = [
        target_rows(
            piece[2 * width : 2 * width + blocks * blocks, level + 1].astype(jnp.int32), mine
        ).reshape(blocks, -1)
        for level, piece in enumerate(head_arrived)
    ]
    targets = [
        jnp.concatenate(
            [forward[:, level, b].reshape(1, -1) for level in range(levels)]
            + [turned[level][b : b + 1] for level in range(levels)],
            axis=1,
        )
        for b in range(blocks)
    ]
    steps = [
        (0, [head[0], rest[0]], list(zip(head_arrived, rest_arrived[0]))),
        (1, [rest[1]], [[piece] for piece in rest_arrived[1]]),
        (1, [rest[2]], [[piece] for piece in rest_arrived[2]]),
    ]
    for b, pieces, arrived in steps:
        spans = [(first, last) for _, first, last in pieces]
        sums = pair_level(targets[b], sums, panel, arrived, spans)
    parts = sums.reshape(devices, RG_DEV * 4, 2 * width)
    parts = lax.all_to_all(parts, "inp", split_axis=0, concat_axis=0)
    total = parts[0]
    for device in range(1, devices):
        total = total + parts[device]
    return total.reshape(RG_DEV, 2, 2, 2 * width)[..., : 2 * width - 1]


def solution(mesh):
    return jax.shard_map(
        on_device,
        mesh=mesh,
        in_specs=(P("freq", None, "inp", None), P("inp", None), P("inp", None, None)),
        out_specs=P("inp", "freq", None, None),
        check_vma=False,
    )
```

```python
import functools

import jax
import jax.numpy as jnp
from jax import lax
from jax.experimental import pallas as pl
from jax.experimental.pallas import tpu as pltpu
from jax.sharding import PartitionSpec as P

RG_DEV = 8
GROUP_ROWS = 16
HBM = pl.BlockSpec(memory_space=pltpu.HBM)
WHOLE = pl.BlockSpec(memory_space=pltpu.VMEM)


def xor_permute(x, axis, distance):
    return lax.ppermute(x, axis, [(i, i ^ distance) for i in range(lax.axis_size(axis))])


def parity(index, levels):
    bits = index & 1
    for level in range(1, levels):
        bits = bits ^ ((index >> level) & 1)
    return bits


def order_matrix(position_row):
    width = position_row.shape[-1]
    by_position = jnp.transpose(jnp.broadcast_to(position_row, (width, width)))
    inputs = lax.broadcasted_iota(jnp.int32, (width, width), 1)
    return (by_position == inputs).astype(jnp.float32).astype(jnp.bfloat16)


def product(x, y):
    return lax.dot_general(x, y, (((1,), (1,)), ((), ())), preferred_element_type=jnp.float32)


def lag_rows(tiles):
    count, width, _ = tiles.shape
    half = width // 2
    low, high = tiles[:, :half], tiles[:, half:]
    sheared = jnp.concatenate(
        [
            high[:, :, :half],
            high[:, :, half:] + low[:, :, :half],
            low[:, :, half:],
            jnp.zeros((count, half, half), jnp.float32),
        ],
        axis=2,
    )
    rows = half
    while rows > 8:
        rows //= 2
        upper = sheared[:, :rows].reshape(count * rows, 2 * width)
        upper = pltpu.roll(upper, rows, 1).reshape(count, rows, 2 * width)
        sheared = upper + sheared[:, rows:]
    flat = sheared.reshape(count * rows, 2 * width)
    sublane = lax.broadcasted_iota(jnp.int32, flat.shape, 0) % 8
    while rows > 1:
        rows //= 2
        flat = jnp.where((sublane & rows) == 0, pltpu.roll(flat, rows, 1), flat)
    return jnp.sum(flat.reshape(count, 8, 2 * width), axis=1)


def tile_lags(x_re, x_im, y_re, y_im, samples):
    real_part = product(x_re, y_re) + product(x_im, y_im)
    imag_part = product(x_im, y_re) - product(x_re, y_im)
    return lag_rows(jnp.stack([real_part, imag_part])) * (1.0 / samples)


def split_rows(x):
    first = x.astype(jnp.bfloat16).astype(jnp.float32)
    rest = x - first
    second = rest.astype(jnp.bfloat16).astype(jnp.float32)
    return jnp.concatenate([first, second, rest - second], axis=0)


def conjugate_lags(lags):
    count, width = lags.shape
    lanes = 128
    flip = (
        lax.broadcasted_iota(jnp.int32, (lanes, lanes), 0)
        + lax.broadcasted_iota(jnp.int32, (lanes, lanes), 1)
        == lanes - 1
    )
    flip = flip.astype(jnp.float32).astype(jnp.bfloat16)
    terms = split_rows(lags)
    spans = range(0, width, lanes)
    terms = jnp.concatenate([terms[:, first : first + lanes] for first in spans], axis=0)
    terms = jnp.dot(terms.astype(jnp.bfloat16), flip, preferred_element_type=jnp.float32)
    turned = []
    for i in reversed(range(len(spans))):
        part = terms[3 * count * i : 3 * count * (i + 1)]
        turned.append(part[:count] + part[count : 2 * count] + part[2 * count :])
    turned = pltpu.roll(jnp.concatenate(turned, axis=1), width - 1, 1)
    odd = lax.broadcasted_iota(jnp.int32, turned.shape, 0) % 2 == 1
    return jnp.where(odd, -turned, turned)


def group_sums(targets, lags, rows):
    pick = lax.broadcasted_iota(jnp.int32, (rows, targets.shape[1]), 0) == targets
    pick = pick.astype(jnp.float32).astype(jnp.bfloat16)
    terms = split_rows(lags).astype(jnp.bfloat16)
    return jnp.dot(pick, terms, preferred_element_type=jnp.float32)


def columns(piece):
    spans, start = [], 0
    for _, first, last in piece:
        spans.append((start, start + last - first))
        start += last - first
    return spans


def piece_shape(piece, width, more):
    return jax.ShapeDtypeStruct((2 * width + more, columns(piece)[-1][1]), jnp.bfloat16)


def send_kernel(levels, pieces, with_groups, position_ref, volts_ref, *refs):
    if with_groups:
        group_ref, refs = refs[0], refs[1:]
    out_refs, refs = refs[: len(pieces)], refs[len(pieces) :]
    position, raw, position_sem, in_sem = refs[:4]
    other = 1 - parity(lax.axis_index("inp"), levels)
    width = position.shape[1]
    load_position = pltpu.make_async_copy(position_ref, position, position_sem)
    load_position.start()
    if with_groups:
        groups, group_sem = refs[4:]
        load_groups = pltpu.make_async_copy(group_ref, groups, group_sem)
        load_groups.start()
    parts = [segment for piece in pieces for segment in piece]
    blocks = sorted({block for block, _, _ in parts})
    spans = [
        (
            min(first for b, first, _ in parts if b == block),
            max(last for b, _, last in parts if b == block),
        )
        for block in blocks
    ]
    loads = [
        [
            pltpu.make_async_copy(
                volts_ref.at[other, c, pl.ds(block * width, width), pl.ds(first, last - first)],
                raw.at[i, c, :, pl.ds(first, last - first)],
                in_sem.at[i, c],
            )
            for c in range(2)
        ]
        for i, (block, (first, last)) in enumerate(zip(blocks, spans))
    ]
    for load in loads:
        load[0].start()
        load[1].start()
    load_position.wait()
    orders = [order_matrix(position[block : block + 1, :]) for block in blocks]
    for i, block in enumerate(blocks):
        for c in range(2):
            loads[i][c].wait()
            for piece, out_ref in zip(pieces, out_refs):
                for (b, first, last), (start, end) in zip(piece, columns(piece)):
                    if b == block:
                        out_ref[c * width : (c + 1) * width, start:end] = jnp.dot(
                            orders[i], raw[i, c, :, first:last], preferred_element_type=jnp.float32
                        ).astype(jnp.bfloat16)
    if with_groups:
        load_groups.wait()
        out_refs[0][2 * width :, :] = jnp.zeros(
            (GROUP_ROWS, out_refs[0].shape[1]), jnp.bfloat16
        )
        rows = jnp.concatenate([groups[b] for b in range(groups.shape[0])], axis=0)
        lines, lanes = rows.shape
        rows = jnp.pad(rows, ((0, GROUP_ROWS - lines), (0, 128 - lanes)))
        out_refs[0][2 * width :, :128] = rows.astype(jnp.float32).astype(jnp.bfloat16)


def order_to_send(position_input, volts, groups, pieces, levels):
    width = position_input.shape[1]
    samples = volts.shape[3]
    count = len({block for piece in pieces for block, _, _ in piece})
    total = sum(columns(piece)[-1][1] for piece in pieces)
    with_groups = groups is not None
    extra = [GROUP_ROWS if with_groups else 0] + [0] * (len(pieces) - 1)
    inputs = [position_input, volts] + ([groups] if with_groups else [])
    scratch = [
        pltpu.VMEM(position_input.shape, jnp.int32),
        pltpu.VMEM((count, 2, width, samples), jnp.bfloat16),
        pltpu.SemaphoreType.DMA(()),
        pltpu.SemaphoreType.DMA((count, 2)),
    ]
    if with_groups:
        scratch += [pltpu.VMEM(groups.shape, jnp.int32), pltpu.SemaphoreType.DMA(())]
    return pl.pallas_call(
        functools.partial(send_kernel, levels, pieces, with_groups),
        out_shape=[piece_shape(piece, width, more) for piece, more in zip(pieces, extra)],
        in_specs=[HBM] * len(inputs),
        out_specs=[WHOLE] * len(pieces),
        scratch_shapes=scratch,
        compiler_params=pltpu.CompilerParams(vmem_limit_bytes=16 << 20),
        cost_estimate=pl.CostEstimate(
            flops=4 * width * width * total, bytes_accessed=8 * width * total, transcendentals=0
        ),
        name="order_to_send",
    )(*[pltpu.with_memory_space_constraint(x, pltpu.HBM) for x in inputs])


def own_kernel(levels, out_rows, pieces, target_ref, position_ref, volts_ref, *refs):
    panel_ref, sums_ref, *piece_refs, raw, other_panel, lags_ref, in_sem = refs
    blocks, _, width, _ = panel_ref.shape
    mine = parity(lax.axis_index("inp"), levels)
    channels = (mine, 1 - mine)
    loads = [
        [
            [
                pltpu.make_async_copy(
                    volts_ref.at[channels[f], c, pl.ds(b * width, width)],
                    raw.at[f, b, c],
                    in_sem.at[f, b, c],
                )
                for c in range(2)
            ]
            for b in range(blocks)
        ]
        for f in range(2)
    ]
    for f in range(2):
        for b in range(blocks):
            for c in range(2):
                loads[f][b][c].start()
    orders = [order_matrix(position_ref[b : b + 1, :]) for b in range(blocks)]
    for f, panel in enumerate((panel_ref, other_panel)):
        for b in range(blocks):
            for c in range(2):
                loads[f][b][c].wait()
                panel[b, c] = jnp.dot(
                    orders[b], raw[f, b, c], preferred_element_type=jnp.float32
                ).astype(jnp.bfloat16)

        def one_tile(index, carry, panel=panel, f=f):
            a = index // blocks
            b = index % blocks
            lags = tile_lags(panel[a, 0], panel[a, 1], panel[b, 0], panel[b, 1], panel.shape[3])
            center = lax.broadcasted_iota(jnp.int32, lags.shape, 1) == width - 1
            lags_ref[f * blocks * blocks + index] = jnp.where(
                jnp.logical_and(center, a == b), 0.0, lags
            )
            return carry

        lax.fori_loop(0, blocks * blocks, one_tile, 0)
    tiles = blocks * blocks
    lags = jnp.concatenate([lags_ref[i] for i in range(tiles)], axis=0)
    sums_ref[...] = group_sums(target_ref[...], lags, out_rows)
    lags = jnp.concatenate([lags_ref[tiles + i] for i in range(tiles)], axis=0)
    for piece, piece_ref in zip(pieces, piece_refs):
        for (block, first, last), (start, end) in zip(piece, columns(piece)):
            for c in range(2):
                piece_ref[c * width : (c + 1) * width, start:end] = other_panel[
                    block, c, :, first:last
                ]
    high = lags.astype(jnp.bfloat16).astype(jnp.float32)
    terms = jnp.concatenate([high, lags - high], axis=0).astype(jnp.bfloat16)
    beyond = piece_refs[0].shape[1] - 2 * width
    piece_refs[0][2 * width :, : 2 * width] = terms
    piece_refs[0][2 * width :, 2 * width :] = jnp.zeros((terms.shape[0], beyond), jnp.bfloat16)


def own_level(targets, position_input, volts, pieces, levels, out_rows):
    blocks, width = position_input.shape
    samples = volts.shape[3]
    extra = [4 * blocks * blocks] + [0] * (len(pieces) - 1)
    return pl.pallas_call(
        functools.partial(own_kernel, levels, out_rows, pieces),
        out_shape=(
            jax.ShapeDtypeStruct((blocks, 2, width, samples), jnp.bfloat16),
            jax.ShapeDtypeStruct((out_rows, 2 * width), jnp.float32),
            *[piece_shape(piece, width, more) for piece, more in zip(pieces, extra)],
        ),
        in_specs=[WHOLE, WHOLE, HBM],
        out_specs=(WHOLE,) * (2 + len(pieces)),
        scratch_shapes=[
            pltpu.VMEM((2, blocks, 2, width, samples), jnp.bfloat16),
            pltpu.VMEM((blocks, 2, width, samples), jnp.bfloat16),
            pltpu.VMEM((2 * blocks * blocks, 2, 2 * width), jnp.float32),
            pltpu.SemaphoreType.DMA((2, blocks, 2)),
        ],
        compiler_params=pltpu.CompilerParams(vmem_limit_bytes=16 << 20),
        cost_estimate=pl.CostEstimate(
            flops=16 * blocks * blocks * width * width * samples,
            bytes_accessed=12 * blocks * width * samples,
            transcendentals=0,
        ),
        name="own_level",
    )(targets, position_input, pltpu.with_memory_space_constraint(volts, pltpu.HBM))


def pair_kernel(levels, pieces, more, target_ref, sums_ref, panel_ref, *refs):
    count = levels * len(pieces)
    partner_refs, out_refs = refs[:count], refs[count:]
    _, _, width, samples = panel_ref.shape
    rows = []
    for block in sorted({block for piece in pieces for block, _, _ in piece}):
        for level in range(levels):
            for a in range(panel_ref.shape[0]):
                real_part, imag_part = 0.0, 0.0
                for i, piece in enumerate(pieces):
                    partner = partner_refs[level * len(pieces) + i]
                    for (b, first, last), (start, end) in zip(piece, columns(piece)):
                        if b != block:
                            continue
                        x_re, x_im = panel_ref[a, 0, :, first:last], panel_ref[a, 1, :, first:last]
                        y_re = partner[:width, start:end]
                        y_im = partner[width : 2 * width, start:end]
                        real_part = real_part + (product(x_re, y_re) + product(x_im, y_im))
                        imag_part = imag_part + (product(x_im, y_re) - product(x_re, y_im))
                rows.append(lag_rows(jnp.stack([real_part, imag_part])) * (1.0 / samples))
    lags = jnp.concatenate(rows, axis=0)
    lags = [lags, conjugate_lags(lags)]
    if more:
        terms = partner_refs[0][2 * width :, : 2 * width].astype(jnp.float32)
        lags.append(terms[: terms.shape[0] // 2] + terms[terms.shape[0] // 2 :])
    lags = jnp.concatenate(lags, axis=0)
    sums = sums_ref[...] + group_sums(target_ref[...], lags, sums_ref.shape[0])
    share = sums.shape[0] // len(out_refs)
    for place, out_ref in enumerate(out_refs):
        out_ref[...] = sums[place * share : (place + 1) * share]


def pair_level(targets, sums, panel, arrived, more, pieces, shares):
    blocks, _, width, _ = panel.shape
    levels = len(arrived)
    length = sum(columns(piece)[-1][1] for piece in pieces)
    share = jax.ShapeDtypeStruct((sums.shape[0] // shares, sums.shape[1]), jnp.float32)
    partners = [piece for level in arrived for piece in level]
    targets = jnp.concatenate(targets * 3)[None, :]
    return pl.pallas_call(
        functools.partial(pair_kernel, levels, pieces, more),
        out_shape=[share] * shares,
        in_specs=[WHOLE] * (3 + len(partners)),
        out_specs=[WHOLE] * shares,
        compiler_params=pltpu.CompilerParams(vmem_limit_bytes=16 << 20),
        cost_estimate=pl.CostEstimate(
            flops=8 * levels * blocks * width * width * length,
            bytes_accessed=4 * (blocks + levels) * width * length,
            transcendentals=0,
        ),
        name="pair_level",
    )(targets, sums, panel, *partners)


def finish_kernel(levels, *refs):
    part_refs, out_ref = refs[:-1], refs[-1]
    mine = parity(lax.axis_index("inp"), levels)
    groups, _, _, lags = out_ref.shape
    sums = [None, None]
    for distance, part_ref in enumerate(part_refs):
        side = distance.bit_count() % 2
        sums[side] = part_ref[...] if sums[side] is None else sums[side] + part_ref[...]
    for f in range(2):
        total = jnp.where(mine == f, sums[0], sums[1])
        for g in range(groups):
            out_ref[g, f] = total[2 * g : 2 * g + 2, :lags]


def finish(parts, levels, lags):
    return pl.pallas_call(
        functools.partial(finish_kernel, levels),
        out_shape=jax.ShapeDtypeStruct((RG_DEV, 2, 2, lags), jnp.float32),
        in_specs=[WHOLE] * len(parts),
        out_specs=WHOLE,
        compiler_params=pltpu.CompilerParams(vmem_limit_bytes=8 << 20),
        name="finish",
    )(*parts)


def on_device(volts, position_input, tile_group):
    blocks, width = position_input.shape
    samples = volts.shape[3]
    devices = lax.axis_size("inp")
    levels = devices.bit_length() - 1
    me = lax.axis_index("inp")
    out_rows = devices * RG_DEV * 2

    def target_rows(groups):
        place = ((groups // RG_DEV) ^ me) * RG_DEV + groups % RG_DEV
        return (place[..., None] * 2 + jnp.arange(2, dtype=jnp.int32)).reshape(-1)

    eighth = samples // 8
    head = [[(0, 0, 2 * eighth)]]
    rest = [[(0, 2 * eighth, samples), (1, 0, 2 * eighth)]]
    tail = [[(1, 2 * eighth, 7 * eighth)], [(1, 7 * eighth, samples)]]
    by_block = tile_group.transpose(0, 2, 1)
    partner_of = [functools.partial(xor_permute, axis="inp", distance=1 << l) for l in range(levels)]
    sent = order_to_send(position_input, volts, by_block, head, levels)
    head_arrived = [send(sent[0]) for send in partner_of]
    sent = order_to_send(position_input, volts, None, rest, levels)
    rest_arrived = [[send(piece) for send in partner_of] for piece in sent]
    own_targets = jnp.concatenate([target_rows(tile_group[:, 0])] * 3)[None, :]
    panel, sums, *sent = own_level(own_targets, position_input, volts, tail, levels, out_rows)
    tail_arrived = [[send(piece) for send in partner_of] for piece in sent]
    partner_groups = [
        piece[2 * width : 2 * width + blocks * blocks, : levels + 1]
        .astype(jnp.int32)
        .reshape(blocks, blocks, levels + 1)
        for piece in head_arrived
    ]
    forward = [
        [target_rows(tile_group[:, level + 1, b]) for level in range(levels)] for b in range(blocks)
    ]
    turned = [
        [target_rows(partner_groups[level][b, :, level + 1]) for level in range(levels)]
        for b in range(blocks)
    ]
    both = forward[0] + forward[1] + turned[0] + turned[1]
    second = forward[1] + turned[1]
    own_neighbour = [target_rows(partner_groups[0][:, :, 0])]
    steps = [
        (both, head + rest, list(zip(head_arrived, rest_arrived[0])), False),
        (second + own_neighbour, tail[:1], [[piece] for piece in tail_arrived[0]], True),
        (second, tail[1:], [[piece] for piece in tail_arrived[1]], False),
    ]
    for number, (rows, pieces, arrived, more) in enumerate(steps):
        shares = devices if number == len(steps) - 1 else 1
        parts = pair_level(rows, sums, panel, arrived, more, pieces, shares)
        sums = parts[0]
    parts = [parts[0]] + [
        xor_permute(parts[distance], "inp", distance) for distance in range(1, devices)
    ]
    return finish(parts, levels, 2 * width - 1)


def solution(mesh):
    return jax.shard_map(
        on_device,
        mesh=mesh,
        in_specs=(P("freq", None, "inp", None), P("inp", None), P("inp", None, None)),
        out_specs=P("inp", "freq", None, None),
        check_vma=False,
    )
```

```python
import functools

import jax
import jax.numpy as jnp
from jax import lax
from jax.experimental import pallas as pl
from jax.experimental.pallas import tpu as pltpu
from jax.sharding import PartitionSpec as P

RG_DEV = 8
GROUP_ROWS = 16
HBM = pl.BlockSpec(memory_space=pltpu.HBM)
WHOLE = pl.BlockSpec(memory_space=pltpu.VMEM)


def xor_permute(x, axis, distance):
    return lax.ppermute(x, axis, [(i, i ^ distance) for i in range(lax.axis_size(axis))])


def parity(index, levels):
    bits = index & 1
    for level in range(1, levels):
        bits = bits ^ ((index >> level) & 1)
    return bits


def order_matrix(position_row):
    width = position_row.shape[-1]
    by_position = jnp.transpose(jnp.broadcast_to(position_row, (width, width)))
    inputs = lax.broadcasted_iota(jnp.int32, (width, width), 1)
    return (by_position == inputs).astype(jnp.float32).astype(jnp.bfloat16)


def product(x, y):
    return lax.dot_general(x, y, (((1,), (1,)), ((), ())), preferred_element_type=jnp.float32)


def lag_rows(tiles):
    count, width, _ = tiles.shape
    half = width // 2
    low, high = tiles[:, :half], tiles[:, half:]
    sheared = jnp.concatenate(
        [
            high[:, :, :half],
            high[:, :, half:] + low[:, :, :half],
            low[:, :, half:],
            jnp.zeros((count, half, half), jnp.float32),
        ],
        axis=2,
    )
    rows = half
    while rows > 8:
        rows //= 2
        upper = sheared[:, :rows].reshape(count * rows, 2 * width)
        upper = pltpu.roll(upper, rows, 1).reshape(count, rows, 2 * width)
        sheared = upper + sheared[:, rows:]
    flat = sheared.reshape(count * rows, 2 * width)
    sublane = lax.broadcasted_iota(jnp.int32, flat.shape, 0) % 8
    while rows > 1:
        rows //= 2
        flat = jnp.where((sublane & rows) == 0, pltpu.roll(flat, rows, 1), flat)
    return jnp.sum(flat.reshape(count, 8, 2 * width), axis=1)


def tile_lags(x_re, x_im, y_re, y_im, samples):
    real_part = product(x_re, y_re) + product(x_im, y_im)
    imag_part = product(x_im, y_re) - product(x_re, y_im)
    return lag_rows(jnp.stack([real_part, imag_part])) * (1.0 / samples)


def split_rows(x):
    first = x.astype(jnp.bfloat16).astype(jnp.float32)
    rest = x - first
    second = rest.astype(jnp.bfloat16).astype(jnp.float32)
    return jnp.concatenate([first, second, rest - second], axis=0)


def conjugate_lags(lags):
    count, width = lags.shape
    lanes = 128
    flip = (
        lax.broadcasted_iota(jnp.int32, (lanes, lanes), 0)
        + lax.broadcasted_iota(jnp.int32, (lanes, lanes), 1)
        == lanes - 1
    )
    flip = flip.astype(jnp.float32).astype(jnp.bfloat16)
    terms = split_rows(lags)
    spans = range(0, width, lanes)
    terms = jnp.concatenate([terms[:, first : first + lanes] for first in spans], axis=0)
    terms = jnp.dot(terms.astype(jnp.bfloat16), flip, preferred_element_type=jnp.float32)
    turned = []
    for i in reversed(range(len(spans))):
        part = terms[3 * count * i : 3 * count * (i + 1)]
        turned.append(part[:count] + part[count : 2 * count] + part[2 * count :])
    turned = pltpu.roll(jnp.concatenate(turned, axis=1), width - 1, 1)
    odd = lax.broadcasted_iota(jnp.int32, turned.shape, 0) % 2 == 1
    return jnp.where(odd, -turned, turned)


def group_block(groups):
    rows = jnp.concatenate([groups[b] for b in range(groups.shape[0])], axis=0)
    lines, lanes = rows.shape
    return jnp.pad(rows, ((0, GROUP_ROWS - lines), (0, 128 - lanes)))


def target_rows(groups):
    me = lax.axis_index("inp")
    bits = RG_DEV.bit_length() - 1
    return (((groups >> bits) ^ me) << (bits + 1)) + ((groups & (RG_DEV - 1)) << 1)


def pick_matrix(entries, rows):
    count = len(entries)
    shape = (rows, 3 * count)
    row = lax.broadcasted_iota(jnp.int32, shape, 0)
    column = lax.broadcasted_iota(jnp.int32, shape, 1) % count
    pick = jnp.zeros(shape, jnp.float32)
    for j, (targets, line, lane, part) in enumerate(entries):
        target = jnp.broadcast_to(targets[line : line + 1, lane : lane + 1] + part, shape)
        pick = jnp.where(jnp.logical_and(column == j, row == target), 1.0, pick)
    return pick.astype(jnp.bfloat16)


def pick_matrices(groups, heads, blocks, out_rows):
    own = target_rows(group_block(groups))
    others = [target_rows(head.astype(jnp.float32).astype(jnp.int32)) for head in heads]
    levels = range(len(heads))

    def entries(b):
        order = [(level, a, p) for level in levels for a in range(blocks) for p in range(2)]
        forward = [(own, a * blocks + b, level + 1, p) for level, a, p in order]
        turned = [(others[level], b * blocks + a, level + 1, p) for level, a, p in order]
        return forward, turned

    forward, turned = zip(*[entries(b) for b in range(blocks)])
    tiles = [(line, part) for line in range(blocks * blocks) for part in range(2)]
    return [
        pick_matrix(columns, out_rows)
        for columns in (
            [(own, line, 0, part) for line, part in tiles],
            [entry for side in (forward, turned) for block in side for entry in block],
            forward[-1] + turned[-1],
            [(others[0], line, 0, part) for line, part in tiles],
        )
    ]


def group_sums(pick, lags):
    terms = split_rows(lags).astype(jnp.bfloat16)
    return jnp.dot(pick, terms, preferred_element_type=jnp.float32)


def columns(piece):
    spans, start = [], 0
    for _, first, last in piece:
        spans.append((start, start + last - first))
        start += last - first
    return spans


def piece_shape(piece, width, more):
    return jax.ShapeDtypeStruct((2 * width + more, columns(piece)[-1][1]), jnp.bfloat16)


def send_kernel(levels, pieces, with_groups, position_ref, volts_ref, *refs):
    if with_groups:
        group_ref, refs = refs[0], refs[1:]
    out_refs, refs = refs[: len(pieces)], refs[len(pieces) :]
    position, raw, position_sem, in_sem = refs[:4]
    other = 1 - parity(lax.axis_index("inp"), levels)
    width = position.shape[1]
    load_position = pltpu.make_async_copy(position_ref, position, position_sem)
    load_position.start()
    if with_groups:
        groups, group_sem = refs[4:]
        load_groups = pltpu.make_async_copy(group_ref, groups, group_sem)
        load_groups.start()
    parts = [segment for piece in pieces for segment in piece]
    blocks = sorted({block for block, _, _ in parts})
    spans = [
        (
            min(first for b, first, _ in parts if b == block),
            max(last for b, _, last in parts if b == block),
        )
        for block in blocks
    ]
    loads = [
        [
            pltpu.make_async_copy(
                volts_ref.at[other, c, pl.ds(block * width, width), pl.ds(first, last - first)],
                raw.at[i, c, :, pl.ds(first, last - first)],
                in_sem.at[i, c],
            )
            for c in range(2)
        ]
        for i, (block, (first, last)) in enumerate(zip(blocks, spans))
    ]
    for load in loads:
        load[0].start()
        load[1].start()
    load_position.wait()
    orders = [order_matrix(position[block : block + 1, :]) for block in blocks]
    for i, block in enumerate(blocks):
        for c in range(2):
            loads[i][c].wait()
            for piece, out_ref in zip(pieces, out_refs):
                for (b, first, last), (start, end) in zip(piece, columns(piece)):
                    if b == block:
                        out_ref[c * width : (c + 1) * width, start:end] = jnp.dot(
                            orders[i], raw[i, c, :, first:last], preferred_element_type=jnp.float32
                        ).astype(jnp.bfloat16)
    if with_groups:
        load_groups.wait()
        out_refs[0][2 * width :, :] = jnp.zeros(
            (GROUP_ROWS, out_refs[0].shape[1]), jnp.bfloat16
        )
        rows = group_block(groups[...])
        out_refs[0][2 * width :, :128] = rows.astype(jnp.float32).astype(jnp.bfloat16)


def order_to_send(position_input, volts, groups, pieces, levels):
    width = position_input.shape[1]
    samples = volts.shape[3]
    count = len({block for piece in pieces for block, _, _ in piece})
    total = sum(columns(piece)[-1][1] for piece in pieces)
    with_groups = groups is not None
    extra = [GROUP_ROWS if with_groups else 0] + [0] * (len(pieces) - 1)
    inputs = [position_input, volts] + ([groups] if with_groups else [])
    scratch = [
        pltpu.VMEM(position_input.shape, jnp.int32),
        pltpu.VMEM((count, 2, width, samples), jnp.bfloat16),
        pltpu.SemaphoreType.DMA(()),
        pltpu.SemaphoreType.DMA((count, 2)),
    ]
    if with_groups:
        scratch += [pltpu.VMEM(groups.shape, jnp.int32), pltpu.SemaphoreType.DMA(())]
    return pl.pallas_call(
        functools.partial(send_kernel, levels, pieces, with_groups),
        out_shape=[piece_shape(piece, width, more) for piece, more in zip(pieces, extra)],
        in_specs=[HBM] * len(inputs),
        out_specs=[WHOLE] * len(pieces),
        scratch_shapes=scratch,
        compiler_params=pltpu.CompilerParams(vmem_limit_bytes=16 << 20),
        cost_estimate=pl.CostEstimate(
            flops=4 * width * width * total, bytes_accessed=8 * width * total, transcendentals=0
        ),
        name="order_to_send",
    )(*[pltpu.with_memory_space_constraint(x, pltpu.HBM) for x in inputs])


def own_kernel(levels, pieces, group_ref, position_ref, volts_ref, *refs):
    head_refs, refs = refs[:levels], refs[levels:]
    panel_ref, sums_ref, *refs, raw, other_panel, lags_ref, in_sem = refs
    pick_refs, piece_refs = refs[:3], refs[3:]
    blocks, _, width, _ = panel_ref.shape
    mine = parity(lax.axis_index("inp"), levels)
    channels = (mine, 1 - mine)
    loads = [
        [
            [
                pltpu.make_async_copy(
                    volts_ref.at[channels[f], c, pl.ds(b * width, width)],
                    raw.at[f, b, c],
                    in_sem.at[f, b, c],
                )
                for c in range(2)
            ]
            for b in range(blocks)
        ]
        for f in range(2)
    ]
    for f in range(2):
        for b in range(blocks):
            for c in range(2):
                loads[f][b][c].start()
    orders = [order_matrix(position_ref[b : b + 1, :]) for b in range(blocks)]
    for f, panel in enumerate((panel_ref, other_panel)):
        for b in range(blocks):
            for c in range(2):
                loads[f][b][c].wait()
                panel[b, c] = jnp.dot(
                    orders[b], raw[f, b, c], preferred_element_type=jnp.float32
                ).astype(jnp.bfloat16)

        def one_tile(index, carry, panel=panel, f=f):
            a = index // blocks
            b = index % blocks
            lags = tile_lags(panel[a, 0], panel[a, 1], panel[b, 0], panel[b, 1], panel.shape[3])
            center = lax.broadcasted_iota(jnp.int32, lags.shape, 1) == width - 1
            lags_ref[f * blocks * blocks + index] = jnp.where(
                jnp.logical_and(center, a == b), 0.0, lags
            )
            return carry

        lax.fori_loop(0, blocks * blocks, one_tile, 0)
    tiles = blocks * blocks
    lags = jnp.concatenate([lags_ref[i] for i in range(tiles)], axis=0)
    heads = [head_ref[2 * width :, :128] for head_ref in head_refs]
    own_pick, *picks = pick_matrices(group_ref[...], heads, blocks, sums_ref.shape[0])
    for pick_ref, pick in zip(pick_refs, picks):
        pick_ref[...] = pick
    sums_ref[...] = group_sums(own_pick, lags)
    lags = jnp.concatenate([lags_ref[tiles + i] for i in range(tiles)], axis=0)
    for piece, piece_ref in zip(pieces, piece_refs):
        for (block, first, last), (start, end) in zip(piece, columns(piece)):
            for c in range(2):
                piece_ref[c * width : (c + 1) * width, start:end] = other_panel[
                    block, c, :, first:last
                ]
    high = lags.astype(jnp.bfloat16).astype(jnp.float32)
    terms = jnp.concatenate([high, lags - high], axis=0).astype(jnp.bfloat16)
    beyond = piece_refs[0].shape[1] - 2 * width
    piece_refs[0][2 * width :, : 2 * width] = terms
    piece_refs[0][2 * width :, 2 * width :] = jnp.zeros((terms.shape[0], beyond), jnp.bfloat16)


def own_level(groups, position_input, volts, heads, pieces, out_rows):
    levels = len(heads)
    blocks, width = position_input.shape
    samples = volts.shape[3]
    extra = [4 * blocks * blocks] + [0] * (len(pieces) - 1)
    counts = (4 * levels * blocks * blocks, 4 * levels * blocks, 2 * blocks * blocks)
    return pl.pallas_call(
        functools.partial(own_kernel, levels, pieces),
        out_shape=(
            jax.ShapeDtypeStruct((blocks, 2, width, samples), jnp.bfloat16),
            jax.ShapeDtypeStruct((out_rows, 2 * width), jnp.float32),
            *[jax.ShapeDtypeStruct((out_rows, 3 * n), jnp.bfloat16) for n in counts],
            *[piece_shape(piece, width, more) for piece, more in zip(pieces, extra)],
        ),
        in_specs=[WHOLE, WHOLE, HBM] + [WHOLE] * levels,
        out_specs=(WHOLE,) * (2 + len(counts) + len(pieces)),
        scratch_shapes=[
            pltpu.VMEM((2, blocks, 2, width, samples), jnp.bfloat16),
            pltpu.VMEM((blocks, 2, width, samples), jnp.bfloat16),
            pltpu.VMEM((2 * blocks * blocks, 2, 2 * width), jnp.float32),
            pltpu.SemaphoreType.DMA((2, blocks, 2)),
        ],
        compiler_params=pltpu.CompilerParams(vmem_limit_bytes=16 << 20),
        cost_estimate=pl.CostEstimate(
            flops=16 * blocks * blocks * width * width * samples,
            bytes_accessed=12 * blocks * width * samples,
            transcendentals=0,
        ),
        name="own_level",
    )(groups, position_input, pltpu.with_memory_space_constraint(volts, pltpu.HBM), *heads)


def pair_lags(levels, pieces, panel_ref, partner_refs):
    _, _, width, samples = panel_ref.shape
    rows = []
    for block in sorted({block for piece in pieces for block, _, _ in piece}):
        for level in range(levels):
            for a in range(panel_ref.shape[0]):
                real_part, imag_part = 0.0, 0.0
                for i, piece in enumerate(pieces):
                    partner = partner_refs[level * len(pieces) + i]
                    for (b, first, last), (start, end) in zip(piece, columns(piece)):
                        if b != block:
                            continue
                        x_re, x_im = panel_ref[a, 0, :, first:last], panel_ref[a, 1, :, first:last]
                        y_re = partner[:width, start:end]
                        y_im = partner[width : 2 * width, start:end]
                        real_part = real_part + (product(x_re, y_re) + product(x_im, y_im))
                        imag_part = imag_part + (product(x_im, y_re) - product(x_re, y_im))
                rows.append(lag_rows(jnp.stack([real_part, imag_part])) * (1.0 / samples))
    lags = jnp.concatenate(rows, axis=0)
    return jnp.concatenate([lags, conjugate_lags(lags)], axis=0)


def first_kernel(levels, pieces, pick_ref, sums_ref, panel_ref, *refs):
    partner_refs, out_ref = refs[:-1], refs[-1]
    lags = pair_lags(levels, pieces, panel_ref, partner_refs)
    out_ref[...] = sums_ref[...] + group_sums(pick_ref[...], lags)


def next_kernel(levels, pieces, pick_ref, neighbour_ref, sums_ref, panel_ref, *refs):
    partner_refs, out_ref = refs[:-1], refs[-1]
    width = panel_ref.shape[2]
    lags = pair_lags(levels, pieces, panel_ref, partner_refs)
    terms = partner_refs[0][2 * width :, : 2 * width].astype(jnp.float32)
    half = terms.shape[0] // 2
    sums = sums_ref[...] + group_sums(neighbour_ref[...], terms[:half] + terms[half:])
    out_ref[...] = sums + group_sums(pick_ref[...], lags)


def last_kernel(levels, pieces, pick_ref, sums_ref, panel_ref, *refs):
    count = levels * len(pieces)
    partner_refs, out_refs = refs[:count], refs[count:]
    lags = pair_lags(levels, pieces, panel_ref, partner_refs)
    sums = sums_ref[...] + group_sums(pick_ref[...], lags)
    share = sums.shape[0] // len(out_refs)
    for place, out_ref in enumerate(out_refs):
        out_ref[...] = sums[place * share : (place + 1) * share]


def pair_call(kernel, before, panel, arrived, pieces, out_shapes):
    blocks, _, width, _ = panel.shape
    levels = len(arrived)
    length = sum(columns(piece)[-1][1] for piece in pieces)
    inputs = [*before, panel, *[piece for level in arrived for piece in level]]
    return pl.pallas_call(
        functools.partial(kernel, levels, pieces),
        out_shape=out_shapes,
        in_specs=[WHOLE] * len(inputs),
        out_specs=[WHOLE] * len(out_shapes),
        compiler_params=pltpu.CompilerParams(vmem_limit_bytes=16 << 20),
        cost_estimate=pl.CostEstimate(
            flops=8 * levels * blocks * width * width * length,
            bytes_accessed=4 * (blocks + levels) * width * length,
            transcendentals=0,
        ),
        name=kernel.__name__,
    )(*inputs)


def finish_kernel(levels, *refs):
    part_refs, out_ref = refs[:-1], refs[-1]
    mine = parity(lax.axis_index("inp"), levels)
    groups, _, _, lags = out_ref.shape
    sums = [None, None]
    for distance, part_ref in enumerate(part_refs):
        side = distance.bit_count() % 2
        sums[side] = part_ref[...] if sums[side] is None else sums[side] + part_ref[...]
    for f in range(2):
        total = jnp.where(mine == f, sums[0], sums[1])
        for g in range(groups):
            out_ref[g, f] = total[2 * g : 2 * g + 2, :lags]


def finish(parts, levels, lags):
    return pl.pallas_call(
        functools.partial(finish_kernel, levels),
        out_shape=jax.ShapeDtypeStruct((RG_DEV, 2, 2, lags), jnp.float32),
        in_specs=[WHOLE] * len(parts),
        out_specs=WHOLE,
        compiler_params=pltpu.CompilerParams(vmem_limit_bytes=8 << 20),
        name="finish",
    )(*parts)


def on_device(volts, position_input, tile_group):
    blocks, width = position_input.shape
    samples = volts.shape[3]
    devices = lax.axis_size("inp")
    levels = devices.bit_length() - 1
    out_rows = devices * RG_DEV * 2
    eighth = samples // 8
    head = [[(0, 0, 2 * eighth)]]
    rest = [[(0, 2 * eighth, samples), (1, 0, 2 * eighth)]]
    tail = [[(1, 2 * eighth, 7 * eighth)], [(1, 7 * eighth, samples)]]
    by_block = tile_group.transpose(0, 2, 1)
    partner_of = [functools.partial(xor_permute, axis="inp", distance=1 << l) for l in range(levels)]
    sent = order_to_send(position_input, volts, by_block, head, levels)
    head_arrived = [send(sent[0]) for send in partner_of]
    sent = order_to_send(position_input, volts, None, rest, levels)
    rest_arrived = [[send(piece) for send in partner_of] for piece in sent]
    panel, sums, both, second, neighbour, *sent = own_level(
        by_block, position_input, volts, head_arrived, tail, out_rows
    )
    tail_arrived = [[send(piece) for send in partner_of] for piece in sent]

    lags_all = jax.ShapeDtypeStruct(sums.shape, jnp.float32)
    (sums,) = pair_call(
        first_kernel,
        [both, sums],
        panel,
        list(zip(head_arrived, rest_arrived[0])),
        head + rest,
        [lags_all],
    )
    (sums,) = pair_call(
        next_kernel,
        [second, neighbour, sums],
        panel,
        [[piece] for piece in tail_arrived[0]],
        tail[:1],
        [lags_all],
    )
    share = jax.ShapeDtypeStruct((out_rows // devices, 2 * width), jnp.float32)
    parts = pair_call(
        last_kernel,
        [second, sums],
        panel,
        [[piece] for piece in tail_arrived[1]],
        tail[1:],
        [share] * devices,
    )
    parts = [parts[0]] + [
        xor_permute(parts[distance], "inp", distance) for distance in range(1, devices)
    ]
    return finish(parts, levels, 2 * width - 1)


def solution(mesh):
    return jax.shard_map(
        on_device,
        mesh=mesh,
        in_specs=(P("freq", None, "inp", None), P("inp", None), P("inp", None, None)),
        out_specs=P("inp", "freq", None, None),
        check_vma=False,
    )
```

```python
import functools

import jax
import jax.numpy as jnp
from jax import lax
from jax.experimental import pallas as pl
from jax.experimental.pallas import tpu as pltpu
from jax.sharding import PartitionSpec as P

RG_DEV = 8
GROUP_ROWS = 16
HBM = pl.BlockSpec(memory_space=pltpu.HBM)
WHOLE = pl.BlockSpec(memory_space=pltpu.VMEM)


def xor_permute(x, axis, distance):
    return lax.ppermute(x, axis, [(i, i ^ distance) for i in range(lax.axis_size(axis))])


def parity(index, levels):
    bits = index & 1
    for level in range(1, levels):
        bits = bits ^ ((index >> level) & 1)
    return bits


def order_matrix(position_row):
    width = position_row.shape[-1]
    by_position = jnp.transpose(jnp.broadcast_to(position_row, (width, width)))
    inputs = lax.broadcasted_iota(jnp.int32, (width, width), 1)
    return (by_position == inputs).astype(jnp.float32).astype(jnp.bfloat16)


def product(x, y):
    return lax.dot_general(x, y, (((1,), (1,)), ((), ())), preferred_element_type=jnp.float32)


def lag_rows(tiles):
    count, width, _ = tiles.shape
    half = width // 2
    low, high = tiles[:, :half], tiles[:, half:]
    sheared = jnp.concatenate(
        [
            high[:, :, :half],
            high[:, :, half:] + low[:, :, :half],
            low[:, :, half:],
            jnp.zeros((count, half, half), jnp.float32),
        ],
        axis=2,
    )
    rows = half
    while rows > 8:
        rows //= 2
        upper = sheared[:, :rows].reshape(count * rows, 2 * width)
        upper = pltpu.roll(upper, rows, 1).reshape(count, rows, 2 * width)
        sheared = upper + sheared[:, rows:]
    flat = sheared.reshape(count * rows, 2 * width)
    sublane = lax.broadcasted_iota(jnp.int32, flat.shape, 0) % 8
    while rows > 1:
        rows //= 2
        flat = jnp.where((sublane & rows) == 0, pltpu.roll(flat, rows, 1), flat)
    return jnp.sum(flat.reshape(count, 8, 2 * width), axis=1)


def tile_lags(x_re, x_im, y_re, y_im, samples):
    real_part = product(x_re, y_re) + product(x_im, y_im)
    imag_part = product(x_im, y_re) - product(x_re, y_im)
    return lag_rows(jnp.stack([real_part, imag_part])) * (1.0 / samples)


def split_rows(x):
    first = x.astype(jnp.bfloat16).astype(jnp.float32)
    rest = x - first
    second = rest.astype(jnp.bfloat16).astype(jnp.float32)
    return jnp.concatenate([first, second, rest - second], axis=0)


def conjugate_lags(lags):
    count, width = lags.shape
    lanes = 128
    flip = (
        lax.broadcasted_iota(jnp.int32, (lanes, lanes), 0)
        + lax.broadcasted_iota(jnp.int32, (lanes, lanes), 1)
        == lanes - 1
    )
    flip = flip.astype(jnp.float32).astype(jnp.bfloat16)
    terms = split_rows(lags)
    spans = range(0, width, lanes)
    terms = jnp.concatenate([terms[:, first : first + lanes] for first in spans], axis=0)
    terms = jnp.dot(terms.astype(jnp.bfloat16), flip, preferred_element_type=jnp.float32)
    turned = []
    for i in reversed(range(len(spans))):
        part = terms[3 * count * i : 3 * count * (i + 1)]
        turned.append(part[:count] + part[count : 2 * count] + part[2 * count :])
    turned = pltpu.roll(jnp.concatenate(turned, axis=1), width - 1, 1)
    odd = lax.broadcasted_iota(jnp.int32, turned.shape, 0) % 2 == 1
    return jnp.where(odd, -turned, turned)


def group_block(groups):
    rows = jnp.concatenate([groups[b] for b in range(groups.shape[0])], axis=0)
    lines, lanes = rows.shape
    return jnp.pad(rows, ((0, GROUP_ROWS - lines), (0, 128 - lanes)))


def target_rows(groups):
    me = lax.axis_index("inp")
    bits = RG_DEV.bit_length() - 1
    return (((groups >> bits) ^ me) << (bits + 2)) + ((groups & (RG_DEV - 1)) << 2)


def pick_matrix(entries, rows):
    count = len(entries)
    shape = (rows, 3 * count)
    row = lax.broadcasted_iota(jnp.int32, shape, 0)
    column = lax.broadcasted_iota(jnp.int32, shape, 1) % count
    pick = jnp.zeros(shape, jnp.float32)
    for j, (targets, line, lane, part) in enumerate(entries):
        target = jnp.broadcast_to(targets[line : line + 1, lane : lane + 1] + part, shape)
        pick = jnp.where(jnp.logical_and(column == j, row == target), 1.0, pick)
    return pick.astype(jnp.bfloat16)


def pick_matrices(groups, heads, blocks, out_rows, mine):
    own = target_rows(group_block(groups))
    others = [target_rows(head.astype(jnp.float32).astype(jnp.int32)) for head in heads]
    parts = [2 * mine, 2 * mine + 1]

    def entries(b):
        order = [(level, a, p) for level in range(len(heads)) for a in range(blocks) for p in parts]
        forward = [(own, a * blocks + b, level + 1, p) for level, a, p in order]
        turned = [(others[level], b * blocks + a, level + 1, p) for level, a, p in order]
        return forward, turned

    forward, turned = zip(*[entries(b) for b in range(blocks)])
    both_channels = parts + [2 - 2 * mine, 3 - 2 * mine]
    tiles = [
        (own, line, 0, part)
        for channel in (both_channels[:2], both_channels[2:])
        for line in range(blocks * blocks)
        for part in channel
    ]
    pairs = [entry for side in (forward, turned) for block in side for entry in block]
    return [pick_matrix(columns, out_rows) for columns in (tiles, pairs, forward[-1] + turned[-1])]


def group_sums(pick, lags):
    terms = split_rows(lags).astype(jnp.bfloat16)
    return jnp.dot(pick, terms, preferred_element_type=jnp.float32)


def columns(piece):
    spans, start = [], 0
    for _, first, last in piece:
        spans.append((start, start + last - first))
        start += last - first
    return spans


def piece_shape(piece, width, more):
    return jax.ShapeDtypeStruct((2 * width + more, columns(piece)[-1][1]), jnp.bfloat16)


def send_kernel(levels, pieces, with_groups, position_ref, volts_ref, *refs):
    if with_groups:
        group_ref, refs = refs[0], refs[1:]
    out_refs, refs = refs[: len(pieces)], refs[len(pieces) :]
    position, raw, position_sem, in_sem = refs[:4]
    other = 1 - parity(lax.axis_index("inp"), levels)
    width = position.shape[1]
    load_position = pltpu.make_async_copy(position_ref, position, position_sem)
    load_position.start()
    if with_groups:
        groups, group_sem = refs[4:]
        load_groups = pltpu.make_async_copy(group_ref, groups, group_sem)
        load_groups.start()
    parts = [segment for piece in pieces for segment in piece]
    blocks = sorted({block for block, _, _ in parts})
    spans = [
        (
            min(first for b, first, _ in parts if b == block),
            max(last for b, _, last in parts if b == block),
        )
        for block in blocks
    ]
    loads = [
        [
            pltpu.make_async_copy(
                volts_ref.at[other, c, pl.ds(block * width, width), pl.ds(first, last - first)],
                raw.at[i, c, :, pl.ds(first, last - first)],
                in_sem.at[i, c],
            )
            for c in range(2)
        ]
        for i, (block, (first, last)) in enumerate(zip(blocks, spans))
    ]
    for load in loads:
        load[0].start()
        load[1].start()
    load_position.wait()
    orders = [order_matrix(position[block : block + 1, :]) for block in blocks]
    for i, block in enumerate(blocks):
        for c in range(2):
            loads[i][c].wait()
            for piece, out_ref in zip(pieces, out_refs):
                for (b, first, last), (start, end) in zip(piece, columns(piece)):
                    if b == block:
                        out_ref[c * width : (c + 1) * width, start:end] = jnp.dot(
                            orders[i], raw[i, c, :, first:last], preferred_element_type=jnp.float32
                        ).astype(jnp.bfloat16)
    if with_groups:
        load_groups.wait()
        out_refs[0][2 * width :, :] = jnp.zeros(
            (GROUP_ROWS, out_refs[0].shape[1]), jnp.bfloat16
        )
        rows = group_block(groups[...])
        out_refs[0][2 * width :, :128] = rows.astype(jnp.float32).astype(jnp.bfloat16)


def order_to_send(position_input, volts, groups, pieces, levels):
    width = position_input.shape[1]
    samples = volts.shape[3]
    count = len({block for piece in pieces for block, _, _ in piece})
    total = sum(columns(piece)[-1][1] for piece in pieces)
    with_groups = groups is not None
    extra = [GROUP_ROWS if with_groups else 0] + [0] * (len(pieces) - 1)
    inputs = [position_input, volts] + ([groups] if with_groups else [])
    scratch = [
        pltpu.VMEM(position_input.shape, jnp.int32),
        pltpu.VMEM((count, 2, width, samples), jnp.bfloat16),
        pltpu.SemaphoreType.DMA(()),
        pltpu.SemaphoreType.DMA((count, 2)),
    ]
    if with_groups:
        scratch += [pltpu.VMEM(groups.shape, jnp.int32), pltpu.SemaphoreType.DMA(())]
    return pl.pallas_call(
        functools.partial(send_kernel, levels, pieces, with_groups),
        out_shape=[piece_shape(piece, width, more) for piece, more in zip(pieces, extra)],
        in_specs=[HBM] * len(inputs),
        out_specs=[WHOLE] * len(pieces),
        scratch_shapes=scratch,
        compiler_params=pltpu.CompilerParams(vmem_limit_bytes=16 << 20),
        cost_estimate=pl.CostEstimate(
            flops=4 * width * width * total, bytes_accessed=8 * width * total, transcendentals=0
        ),
        name="order_to_send",
    )(*[pltpu.with_memory_space_constraint(x, pltpu.HBM) for x in inputs])


def own_kernel(levels, pieces, group_ref, position_ref, volts_ref, *refs):
    head_refs, refs = refs[:levels], refs[levels:]
    panel_ref, sums_ref, *refs, raw, other_panel, lags_ref, in_sem = refs
    pick_refs, piece_refs = refs[:2], refs[2:]
    blocks, _, width, _ = panel_ref.shape
    mine = parity(lax.axis_index("inp"), levels)
    channels = (mine, 1 - mine)
    loads = [
        [
            [
                pltpu.make_async_copy(
                    volts_ref.at[channels[f], c, pl.ds(b * width, width)],
                    raw.at[f, b, c],
                    in_sem.at[f, b, c],
                )
                for c in range(2)
            ]
            for b in range(blocks)
        ]
        for f in range(2)
    ]
    for f in range(2):
        for b in range(blocks):
            for c in range(2):
                loads[f][b][c].start()
    orders = [order_matrix(position_ref[b : b + 1, :]) for b in range(blocks)]
    for f, panel in enumerate((panel_ref, other_panel)):
        for b in range(blocks):
            for c in range(2):
                loads[f][b][c].wait()
                panel[b, c] = jnp.dot(
                    orders[b], raw[f, b, c], preferred_element_type=jnp.float32
                ).astype(jnp.bfloat16)

        def one_tile(index, carry, panel=panel, f=f):
            a = index // blocks
            b = index % blocks
            lags = tile_lags(panel[a, 0], panel[a, 1], panel[b, 0], panel[b, 1], panel.shape[3])
            center = lax.broadcasted_iota(jnp.int32, lags.shape, 1) == width - 1
            lags_ref[f * blocks * blocks + index] = jnp.where(
                jnp.logical_and(center, a == b), 0.0, lags
            )
            return carry

        lax.fori_loop(0, blocks * blocks, one_tile, 0)
    lags = jnp.concatenate([lags_ref[i] for i in range(2 * blocks * blocks)], axis=0)
    heads = [head_ref[2 * width :, :128] for head_ref in head_refs]
    own_pick, *picks = pick_matrices(group_ref[...], heads, blocks, sums_ref.shape[0], mine)
    for pick_ref, pick in zip(pick_refs, picks):
        pick_ref[...] = pick
    sums_ref[...] = group_sums(own_pick, lags)
    for piece, piece_ref in zip(pieces, piece_refs):
        for (block, first, last), (start, end) in zip(piece, columns(piece)):
            for c in range(2):
                piece_ref[c * width : (c + 1) * width, start:end] = other_panel[
                    block, c, :, first:last
                ]


def own_level(groups, position_input, volts, heads, pieces, out_rows):
    levels = len(heads)
    blocks, width = position_input.shape
    samples = volts.shape[3]
    counts = (4 * levels * blocks * blocks, 4 * levels * blocks)
    return pl.pallas_call(
        functools.partial(own_kernel, levels, pieces),
        out_shape=(
            jax.ShapeDtypeStruct((blocks, 2, width, samples), jnp.bfloat16),
            jax.ShapeDtypeStruct((out_rows, 2 * width), jnp.float32),
            *[jax.ShapeDtypeStruct((out_rows, 3 * n), jnp.bfloat16) for n in counts],
            *[piece_shape(piece, width, 0) for piece in pieces],
        ),
        in_specs=[WHOLE, WHOLE, HBM] + [WHOLE] * levels,
        out_specs=(WHOLE,) * (2 + len(counts) + len(pieces)),
        scratch_shapes=[
            pltpu.VMEM((2, blocks, 2, width, samples), jnp.bfloat16),
            pltpu.VMEM((blocks, 2, width, samples), jnp.bfloat16),
            pltpu.VMEM((2 * blocks * blocks, 2, 2 * width), jnp.float32),
            pltpu.SemaphoreType.DMA((2, blocks, 2)),
        ],
        compiler_params=pltpu.CompilerParams(vmem_limit_bytes=16 << 20),
        cost_estimate=pl.CostEstimate(
            flops=16 * blocks * blocks * width * width * samples,
            bytes_accessed=12 * blocks * width * samples,
            transcendentals=0,
        ),
        name="own_level",
    )(groups, position_input, pltpu.with_memory_space_constraint(volts, pltpu.HBM), *heads)


def pair_lags(levels, pieces, panel_ref, partner_refs):
    _, _, width, samples = panel_ref.shape
    rows = []
    for block in sorted({block for piece in pieces for block, _, _ in piece}):
        for level in range(levels):
            for a in range(panel_ref.shape[0]):
                real_part, imag_part = 0.0, 0.0
                for i, piece in enumerate(pieces):
                    partner = partner_refs[level * len(pieces) + i]
                    for (b, first, last), (start, end) in zip(piece, columns(piece)):
                        if b != block:
                            continue
                        x_re, x_im = panel_ref[a, 0, :, first:last], panel_ref[a, 1, :, first:last]
                        y_re = partner[:width, start:end]
                        y_im = partner[width : 2 * width, start:end]
                        real_part = real_part + (product(x_re, y_re) + product(x_im, y_im))
                        imag_part = imag_part + (product(x_im, y_re) - product(x_re, y_im))
                rows.append(lag_rows(jnp.stack([real_part, imag_part])) * (1.0 / samples))
    lags = jnp.concatenate(rows, axis=0)
    return jnp.concatenate([lags, conjugate_lags(lags)], axis=0)


def pair_kernel(levels, pieces, pick_ref, sums_ref, panel_ref, *refs):
    count = levels * len(pieces)
    partner_refs, out_refs = refs[:count], refs[count:]
    lags = pair_lags(levels, pieces, panel_ref, partner_refs)
    sums = sums_ref[...] + group_sums(pick_ref[...], lags)
    share = sums.shape[0] // len(out_refs)
    for place, out_ref in enumerate(out_refs):
        out_ref[...] = sums[place * share : (place + 1) * share]


def pair_call(pick, sums, panel, arrived, pieces, shares):
    blocks, _, width, _ = panel.shape
    levels = len(arrived)
    length = sum(columns(piece)[-1][1] for piece in pieces)
    share = jax.ShapeDtypeStruct((sums.shape[0] // shares, sums.shape[1]), jnp.float32)
    inputs = [pick, sums, panel, *[piece for level in arrived for piece in level]]
    return pl.pallas_call(
        functools.partial(pair_kernel, levels, pieces),
        out_shape=[share] * shares,
        in_specs=[WHOLE] * len(inputs),
        out_specs=[WHOLE] * shares,
        compiler_params=pltpu.CompilerParams(vmem_limit_bytes=16 << 20),
        cost_estimate=pl.CostEstimate(
            flops=8 * levels * blocks * width * width * length,
            bytes_accessed=4 * (blocks + levels) * width * length,
            transcendentals=0,
        ),
        name="pair_level",
    )(*inputs)


def finish_kernel(*refs):
    part_refs, out_ref = refs[:-1], refs[-1]
    groups, channels, parts, lags = out_ref.shape
    total = part_refs[0][...]
    for part_ref in part_refs[1:]:
        total = total + part_ref[...]
    for g in range(groups):
        for f in range(channels):
            row = (g * channels + f) * parts
            out_ref[g, f] = total[row : row + parts, :lags]


def finish(parts, lags):
    return pl.pallas_call(
        finish_kernel,
        out_shape=jax.ShapeDtypeStruct((RG_DEV, 2, 2, lags), jnp.float32),
        in_specs=[WHOLE] * len(parts),
        out_specs=WHOLE,
        compiler_params=pltpu.CompilerParams(vmem_limit_bytes=8 << 20),
        name="finish",
    )(*parts)


def on_device(volts, position_input, tile_group):
    blocks, width = position_input.shape
    samples = volts.shape[3]
    devices = lax.axis_size("inp")
    levels = devices.bit_length() - 1
    out_rows = devices * RG_DEV * 4
    eighth = samples // 8
    head = [[(0, 0, 2 * eighth)]]
    rest = [[(0, 2 * eighth, samples), (1, 0, 2 * eighth)]]
    tail = [[(1, 2 * eighth, 7 * eighth)], [(1, 7 * eighth, samples)]]
    by_block = tile_group.transpose(0, 2, 1)
    partner_of = [functools.partial(xor_permute, axis="inp", distance=1 << l) for l in range(levels)]
    sent = order_to_send(position_input, volts, by_block, head, levels)
    head_arrived = [send(sent[0]) for send in partner_of]
    sent = order_to_send(position_input, volts, None, rest, levels)
    rest_arrived = [[send(piece) for send in partner_of] for piece in sent]
    panel, sums, both, second, *sent = own_level(
        by_block, position_input, volts, head_arrived, tail, out_rows
    )
    tail_arrived = [[send(piece) for send in partner_of] for piece in sent]

    first_arrived = list(zip(head_arrived, rest_arrived[0]))
    (sums,) = pair_call(both, sums, panel, first_arrived, head + rest, 1)
    (sums,) = pair_call(second, sums, panel, [[x] for x in tail_arrived[0]], tail[:1], 1)
    parts = pair_call(second, sums, panel, [[x] for x in tail_arrived[1]], tail[1:], devices)
    parts = [
        xor_permute(parts[distance], "inp", distance) for distance in reversed(range(1, devices))
    ] + [parts[0]]
    return finish(parts, 2 * width - 1)


def solution(mesh):
    return jax.shard_map(
        on_device,
        mesh=mesh,
        in_specs=(P("freq", None, "inp", None), P("inp", None), P("inp", None, None)),
        out_specs=P("inp", "freq", None, None),
        check_vma=False,
    )
```

```python
import functools

import jax
import jax.numpy as jnp
from jax import lax
from jax.experimental import pallas as pl
from jax.experimental.pallas import tpu as pltpu
from jax.sharding import PartitionSpec as P

RG_DEV = 8
GROUP_ROWS = 16
HBM = pl.BlockSpec(memory_space=pltpu.HBM)
WHOLE = pl.BlockSpec(memory_space=pltpu.VMEM)


def xor_permute(x, axis, distance):
    return lax.ppermute(x, axis, [(i, i ^ distance) for i in range(lax.axis_size(axis))])


def parity(index, levels):
    bits = index & 1
    for level in range(1, levels):
        bits = bits ^ ((index >> level) & 1)
    return bits


def order_matrix(position_row):
    width = position_row.shape[-1]
    by_position = jnp.transpose(jnp.broadcast_to(position_row, (width, width)))
    inputs = lax.broadcasted_iota(jnp.int32, (width, width), 1)
    return (by_position == inputs).astype(jnp.float32).astype(jnp.bfloat16)


def product(x, y):
    return lax.dot_general(x, y, (((1,), (1,)), ((), ())), preferred_element_type=jnp.float32)


def lag_rows(tiles):
    count, width, _ = tiles.shape
    half = width // 2
    low, high = tiles[:, :half], tiles[:, half:]
    sheared = jnp.concatenate(
        [
            high[:, :, :half],
            high[:, :, half:] + low[:, :, :half],
            low[:, :, half:],
            jnp.zeros((count, half, half), jnp.float32),
        ],
        axis=2,
    )
    rows = half
    while rows > 8:
        rows //= 2
        upper = sheared[:, :rows].reshape(count * rows, 2 * width)
        upper = pltpu.roll(upper, rows, 1).reshape(count, rows, 2 * width)
        sheared = upper + sheared[:, rows:]
    flat = sheared.reshape(count * rows, 2 * width)
    sublane = lax.broadcasted_iota(jnp.int32, flat.shape, 0) % 8
    while rows > 1:
        rows //= 2
        flat = jnp.where((sublane & rows) == 0, pltpu.roll(flat, rows, 1), flat)
    return jnp.sum(flat.reshape(count, 8, 2 * width), axis=1)


def tile_lags(x_re, x_im, y_re, y_im, samples):
    real_part = product(x_re, y_re) + product(x_im, y_im)
    imag_part = product(x_im, y_re) - product(x_re, y_im)
    return lag_rows(jnp.stack([real_part, imag_part])) * (1.0 / samples)


def split_rows(x):
    first = x.astype(jnp.bfloat16).astype(jnp.float32)
    rest = x - first
    second = rest.astype(jnp.bfloat16).astype(jnp.float32)
    return jnp.concatenate([first, second, rest - second], axis=0)


def conjugate_lags(lags):
    count, width = lags.shape
    lanes = 128
    flip = (
        lax.broadcasted_iota(jnp.int32, (lanes, lanes), 0)
        + lax.broadcasted_iota(jnp.int32, (lanes, lanes), 1)
        == lanes - 1
    )
    flip = flip.astype(jnp.float32).astype(jnp.bfloat16)
    terms = split_rows(lags)
    spans = range(0, width, lanes)
    terms = jnp.concatenate([terms[:, first : first + lanes] for first in spans], axis=0)
    terms = jnp.dot(terms.astype(jnp.bfloat16), flip, preferred_element_type=jnp.float32)
    turned = []
    for i in reversed(range(len(spans))):
        part = terms[3 * count * i : 3 * count * (i + 1)]
        turned.append(part[:count] + part[count : 2 * count] + part[2 * count :])
    turned = pltpu.roll(jnp.concatenate(turned, axis=1), width - 1, 1)
    odd = lax.broadcasted_iota(jnp.int32, turned.shape, 0) % 2 == 1
    return jnp.where(odd, -turned, turned)


def group_block(groups):
    rows = jnp.concatenate([groups[b] for b in range(groups.shape[0])], axis=0)
    lines, lanes = rows.shape
    return jnp.pad(rows, ((0, GROUP_ROWS - lines), (0, 128 - lanes)))


def target_rows(groups):
    me = lax.axis_index("inp")
    bits = RG_DEV.bit_length() - 1
    return (((groups >> bits) ^ me) << (bits + 2)) + ((groups & (RG_DEV - 1)) << 2)


def pick_matrix(entries, rows):
    count = len(entries)
    shape = (rows, 3 * count)
    row = lax.broadcasted_iota(jnp.int32, shape, 0)
    column = lax.broadcasted_iota(jnp.int32, shape, 1) % count
    pick = jnp.zeros(shape, jnp.float32)
    for j, (targets, line, lane, part) in enumerate(entries):
        target = jnp.broadcast_to(targets[line : line + 1, lane : lane + 1] + part, shape)
        pick = jnp.where(jnp.logical_and(column == j, row == target), 1.0, pick)
    return pick.astype(jnp.bfloat16)


def pick_matrices(groups, heads, blocks, out_rows, mine):
    own = target_rows(group_block(groups))
    others = [target_rows(head.astype(jnp.float32).astype(jnp.int32)) for head in heads]
    parts = [2 * mine, 2 * mine + 1]

    def entries(b):
        order = [(level, a, p) for level in range(len(heads)) for a in range(blocks) for p in parts]
        forward = [(own, a * blocks + b, level + 1, p) for level, a, p in order]
        turned = [(others[level], b * blocks + a, level + 1, p) for level, a, p in order]
        return forward, turned

    forward, turned = zip(*[entries(b) for b in range(blocks)])
    both_channels = parts + [2 - 2 * mine, 3 - 2 * mine]
    tiles = [
        (own, line, 0, part)
        for channel in (both_channels[:2], both_channels[2:])
        for line in range(blocks * blocks)
        for part in channel
    ]
    pairs = [entry for side in (forward, turned) for block in side for entry in block]
    return [pick_matrix(columns, out_rows) for columns in (tiles, pairs, forward[-1] + turned[-1])]


def group_sums(pick, lags):
    terms = split_rows(lags).astype(jnp.bfloat16)
    return jnp.dot(pick, terms, preferred_element_type=jnp.float32)


def columns(piece):
    spans, start = [], 0
    for _, first, last in piece:
        spans.append((start, start + last - first))
        start += last - first
    return spans


def piece_shape(piece, width, more):
    return jax.ShapeDtypeStruct((2 * width + more, columns(piece)[-1][1]), jnp.bfloat16)


def send_kernel(levels, pieces, with_groups, position_ref, volts_ref, extra_ref, *refs):
    out_refs, refs = refs[: len(pieces)], refs[len(pieces) :]
    position, raw, position_sem, in_sem = refs[:4]
    other = 1 - parity(lax.axis_index("inp"), levels)
    width = position.shape[1]
    load_position = pltpu.make_async_copy(position_ref, position, position_sem)
    load_position.start()
    if with_groups:
        groups, group_sem = refs[4:]
        load_groups = pltpu.make_async_copy(extra_ref, groups, group_sem)
        load_groups.start()
    parts = [segment for piece in pieces for segment in piece]
    blocks = sorted({block for block, _, _ in parts})
    spans = [
        (
            min(first for b, first, _ in parts if b == block),
            max(last for b, _, last in parts if b == block),
        )
        for block in blocks
    ]
    loads = [
        [
            pltpu.make_async_copy(
                volts_ref.at[other, c, pl.ds(block * width, width), pl.ds(first, last - first)],
                raw.at[i, c, :, pl.ds(first, last - first)],
                in_sem.at[i, c],
            )
            for c in range(2)
        ]
        for i, (block, (first, last)) in enumerate(zip(blocks, spans))
    ]
    for load in loads:
        load[0].start()
        load[1].start()
    load_position.wait()
    orders = [order_matrix(position[block : block + 1, :]) for block in blocks]
    for i, block in enumerate(blocks):
        for c in range(2):
            loads[i][c].wait()
            for piece, out_ref in zip(pieces, out_refs):
                for (b, first, last), (start, end) in zip(piece, columns(piece)):
                    if b == block:
                        out_ref[c * width : (c + 1) * width, start:end] = jnp.dot(
                            orders[i], raw[i, c, :, first:last], preferred_element_type=jnp.float32
                        ).astype(jnp.bfloat16)
    if with_groups:
        load_groups.wait()
        out_refs[0][2 * width :, :] = jnp.zeros(
            (GROUP_ROWS, out_refs[0].shape[1]), jnp.bfloat16
        )
        rows = group_block(groups[...])
        out_refs[0][2 * width :, :128] = rows.astype(jnp.float32).astype(jnp.bfloat16)


def order_to_send(position_input, volts, groups, before, pieces, levels):
    width = position_input.shape[1]
    samples = volts.shape[3]
    count = len({block for piece in pieces for block, _, _ in piece})
    total = sum(columns(piece)[-1][1] for piece in pieces)
    with_groups = groups is not None
    extra = [GROUP_ROWS if with_groups else 0] + [0] * (len(pieces) - 1)
    inputs = [pltpu.with_memory_space_constraint(x, pltpu.HBM) for x in (position_input, volts)]
    if with_groups:
        inputs.append(pltpu.with_memory_space_constraint(groups, pltpu.HBM))
    else:
        inputs.append(before)
    scratch = [
        pltpu.VMEM(position_input.shape, jnp.int32),
        pltpu.VMEM((count, 2, width, samples), jnp.bfloat16),
        pltpu.SemaphoreType.DMA(()),
        pltpu.SemaphoreType.DMA((count, 2)),
    ]
    if with_groups:
        scratch += [pltpu.VMEM(groups.shape, jnp.int32), pltpu.SemaphoreType.DMA(())]
    return pl.pallas_call(
        functools.partial(send_kernel, levels, pieces, with_groups),
        out_shape=[piece_shape(piece, width, more) for piece, more in zip(pieces, extra)],
        in_specs=[HBM, HBM, HBM if with_groups else pl.BlockSpec(memory_space=pl.ANY)],
        out_specs=[WHOLE] * len(pieces),
        scratch_shapes=scratch,
        compiler_params=pltpu.CompilerParams(vmem_limit_bytes=16 << 20),
        cost_estimate=pl.CostEstimate(
            flops=4 * width * width * total, bytes_accessed=8 * width * total, transcendentals=0
        ),
        name="order_to_send",
    )(*inputs)


def own_kernel(levels, pieces, last, group_ref, position_ref, volts_ref, *refs):
    head_refs, refs = refs[:levels], refs[levels:]
    panel_ref, sums_ref, *refs, raw, other_panel, lags_ref, in_sem = refs
    pick_refs, piece_refs, (last_ref, last_panel_ref) = refs[:2], refs[2:-2], refs[-2:]
    blocks, _, width, _ = panel_ref.shape
    mine = parity(lax.axis_index("inp"), levels)
    channels = (mine, 1 - mine)
    loads = [
        [
            [
                pltpu.make_async_copy(
                    volts_ref.at[channels[f], c, pl.ds(b * width, width)],
                    raw.at[f, b, c],
                    in_sem.at[f, b, c],
                )
                for c in range(2)
            ]
            for b in range(blocks)
        ]
        for f in range(2)
    ]
    for f in range(2):
        for b in range(blocks):
            for c in range(2):
                loads[f][b][c].start()
    orders = [order_matrix(position_ref[b : b + 1, :]) for b in range(blocks)]
    for f, panel in enumerate((panel_ref, other_panel)):
        for b in range(blocks):
            for c in range(2):
                loads[f][b][c].wait()
                panel[b, c] = jnp.dot(
                    orders[b], raw[f, b, c], preferred_element_type=jnp.float32
                ).astype(jnp.bfloat16)

        def one_tile(index, carry, panel=panel, f=f):
            a = index // blocks
            b = index % blocks
            lags = tile_lags(panel[a, 0], panel[a, 1], panel[b, 0], panel[b, 1], panel.shape[3])
            center = lax.broadcasted_iota(jnp.int32, lags.shape, 1) == width - 1
            lags_ref[f * blocks * blocks + index] = jnp.where(
                jnp.logical_and(center, a == b), 0.0, lags
            )
            return carry

        lax.fori_loop(0, blocks * blocks, one_tile, 0)
    lags = jnp.concatenate([lags_ref[i] for i in range(2 * blocks * blocks)], axis=0)
    heads = [head_ref[2 * width :, :128] for head_ref in head_refs]
    own_pick, *picks = pick_matrices(group_ref[...], heads, blocks, sums_ref.shape[0], mine)
    for pick_ref, pick in zip(pick_refs, picks):
        pick_ref[...] = pick
    sums_ref[...] = group_sums(own_pick, lags)
    for piece, piece_ref in zip(pieces, piece_refs):
        for (block, first, _), (start, end) in zip(piece, columns(piece)):
            for c in range(2):
                piece_ref[c * width : (c + 1) * width, start:end] = other_panel[
                    block, c, :, first:end - start + first
                ]
    block, first, end = last
    depth = end - first
    for c in range(2):
        last_ref[:, c * depth : (c + 1) * depth] = other_panel[block, c, :, first:end]
    for a in range(blocks):
        real_part, imag_part = panel_ref[a, 0, :, first:end], panel_ref[a, 1, :, first:end]
        last_panel_ref[a, :width, :depth] = real_part
        last_panel_ref[a, :width, depth:] = imag_part
        last_panel_ref[a, width:, :depth] = imag_part
        last_panel_ref[a, width:, depth:] = -real_part


def own_level(groups, position_input, volts, heads, pieces, last, out_rows):
    levels = len(heads)
    blocks, width = position_input.shape
    samples = volts.shape[3]
    counts = (4 * levels * blocks * blocks, 4 * levels * blocks)
    depth = last[2] - last[1]
    return pl.pallas_call(
        functools.partial(own_kernel, levels, pieces, last),
        out_shape=(
            jax.ShapeDtypeStruct((blocks, 2, width, samples), jnp.bfloat16),
            jax.ShapeDtypeStruct((out_rows, 2 * width), jnp.float32),
            *[jax.ShapeDtypeStruct((out_rows, 3 * n), jnp.bfloat16) for n in counts],
            *[piece_shape(piece, width, 0) for piece in pieces],
            jax.ShapeDtypeStruct((width, 2 * depth), jnp.bfloat16),
            jax.ShapeDtypeStruct((blocks, 2 * width, 2 * depth), jnp.bfloat16),
        ),
        in_specs=[WHOLE, WHOLE, HBM] + [WHOLE] * levels,
        out_specs=(WHOLE,) * (4 + len(counts) + len(pieces)),
        scratch_shapes=[
            pltpu.VMEM((2, blocks, 2, width, samples), jnp.bfloat16),
            pltpu.VMEM((blocks, 2, width, samples), jnp.bfloat16),
            pltpu.VMEM((2 * blocks * blocks, 2, 2 * width), jnp.float32),
            pltpu.SemaphoreType.DMA((2, blocks, 2)),
        ],
        compiler_params=pltpu.CompilerParams(vmem_limit_bytes=16 << 20),
        cost_estimate=pl.CostEstimate(
            flops=64 * blocks * blocks * width * width * samples,
            bytes_accessed=12 * blocks * width * samples,
            transcendentals=0,
        ),
        name="own_level",
    )(groups, position_input, pltpu.with_memory_space_constraint(volts, pltpu.HBM), *heads)


def pair_lags(levels, pieces, panel_ref, partner_refs):
    _, _, width, samples = panel_ref.shape
    rows = []
    for block in sorted({block for piece in pieces for block, _, _ in piece}):
        for level in range(levels):
            for a in range(panel_ref.shape[0]):
                real_part, imag_part = 0.0, 0.0
                for i, piece in enumerate(pieces):
                    partner = partner_refs[level * len(pieces) + i]
                    for (b, first, last), (start, end) in zip(piece, columns(piece)):
                        if b != block:
                            continue
                        x_re, x_im = panel_ref[a, 0, :, first:last], panel_ref[a, 1, :, first:last]
                        y_re = partner[:width, start:end]
                        y_im = partner[width : 2 * width, start:end]
                        real_part = real_part + (product(x_re, y_re) + product(x_im, y_im))
                        imag_part = imag_part + (product(x_im, y_re) - product(x_re, y_im))
                rows.append(lag_rows(jnp.stack([real_part, imag_part])) * (1.0 / samples))
    lags = jnp.concatenate(rows, axis=0)
    return jnp.concatenate([lags, conjugate_lags(lags)], axis=0)


def add_lags(rows, pick_ref, sums_ref):
    lags = jnp.concatenate(rows, axis=0)
    lags = jnp.concatenate([lags, conjugate_lags(lags)], axis=0)
    return sums_ref[...] + group_sums(pick_ref[...], lags)


def pair_kernel(levels, pieces, pick_ref, sums_ref, panel_ref, *refs):
    partner_refs, out_ref = refs[:-1], refs[-1]
    _, _, width, samples = panel_ref.shape
    rows = []
    for block in sorted({block for piece in pieces for block, _, _ in piece}):
        for level in range(levels):
            for a in range(panel_ref.shape[0]):
                real_part, imag_part = 0.0, 0.0
                for i, piece in enumerate(pieces):
                    partner = partner_refs[level * len(pieces) + i]
                    for (b, first, last), (start, end) in zip(piece, columns(piece)):
                        if b != block:
                            continue
                        x_re, x_im = panel_ref[a, 0, :, first:last], panel_ref[a, 1, :, first:last]
                        y_re = partner[:width, start:end]
                        y_im = partner[width : 2 * width, start:end]
                        real_part = real_part + (product(x_re, y_re) + product(x_im, y_im))
                        imag_part = imag_part + (product(x_im, y_re) - product(x_re, y_im))
                rows.append(lag_rows(jnp.stack([real_part, imag_part])) * (1.0 / samples))
    out_ref[...] = add_lags(rows, pick_ref, sums_ref)


def last_kernel(levels, samples, pick_ref, sums_ref, panel_ref, *refs):
    partner_refs, out_refs = refs[:levels], refs[levels:]
    blocks, rows_both, _ = panel_ref.shape
    width = rows_both // 2
    rows = []
    for partner_ref in partner_refs:
        for a in range(blocks):
            tiles = product(panel_ref[a], partner_ref[...]).reshape(2, width, width)
            rows.append(lag_rows(tiles) * (1.0 / samples))
    sums = add_lags(rows, pick_ref, sums_ref)
    share = sums.shape[0] // len(out_refs)
    for place, out_ref in enumerate(out_refs):
        out_ref[...] = sums[place * share : (place + 1) * share]


def pair_call(kernel, inputs, work, out_shape):
    return pl.pallas_call(
        kernel,
        out_shape=out_shape,
        in_specs=[WHOLE] * len(inputs),
        out_specs=[WHOLE] * len(out_shape),
        compiler_params=pltpu.CompilerParams(vmem_limit_bytes=16 << 20),
        cost_estimate=pl.CostEstimate(flops=work, bytes_accessed=4 << 20, transcendentals=0),
        name="pair_level",
    )(*inputs)


def finish_kernel(*refs):
    part_refs, out_ref = refs[:-1], refs[-1]
    groups, channels, parts, lags = out_ref.shape
    total = part_refs[0][...]
    for part_ref in part_refs[1:]:
        total = total + part_ref[...]
    for g in range(groups):
        for f in range(channels):
            row = (g * channels + f) * parts
            out_ref[g, f] = total[row : row + parts, :lags]


def finish(parts, lags):
    return pl.pallas_call(
        finish_kernel,
        out_shape=jax.ShapeDtypeStruct((RG_DEV, 2, 2, lags), jnp.float32),
        in_specs=[WHOLE] * len(parts),
        out_specs=WHOLE,
        compiler_params=pltpu.CompilerParams(vmem_limit_bytes=8 << 20),
        name="finish",
    )(*parts)


def on_device(volts, position_input, tile_group):
    blocks, width = position_input.shape
    samples = volts.shape[3]
    devices = lax.axis_size("inp")
    levels = devices.bit_length() - 1
    out_rows = devices * RG_DEV * 4
    eighth = samples // 8
    head = [[(0, 0, 2 * eighth)]]
    rest = [[(0, 2 * eighth, samples), (1, 0, 2 * eighth)]]
    tail = [[(1, 2 * eighth, 6 * eighth)]]
    last = (1, 6 * eighth, samples)
    by_block = tile_group.transpose(0, 2, 1)
    partner_of = [functools.partial(xor_permute, axis="inp", distance=1 << l) for l in range(levels)]
    sent = order_to_send(position_input, volts, by_block, None, head, levels)
    head_arrived = [send(sent[0]) for send in partner_of]
    sent = order_to_send(position_input, volts, None, sent[0], rest, levels)
    rest_arrived = [[send(piece) for send in partner_of] for piece in sent]
    panel, sums, both, second, *sent, last_panel = own_level(
        by_block, position_input, volts, head_arrived, tail, last, out_rows
    )
    tail_arrived = [[send(piece) for send in partner_of] for piece in sent]

    whole = jax.ShapeDtypeStruct(sums.shape, jnp.float32)
    share = jax.ShapeDtypeStruct((out_rows // devices, 2 * width), jnp.float32)
    flops = 8 * levels * blocks * width * width
    arrived = [piece for pair in zip(head_arrived, rest_arrived[0]) for piece in pair]
    (sums,) = pair_call(
        functools.partial(pair_kernel, levels, head + rest),
        [both, sums, panel, *arrived],
        flops * 10 * eighth,
        [whole],
    )
    (sums,) = pair_call(
        functools.partial(pair_kernel, levels, tail),
        [second, sums, panel, *tail_arrived[0]],
        flops * 4 * eighth,
        [whole],
    )
    parts = pair_call(
        functools.partial(last_kernel, levels, samples),
        [second, sums, last_panel, *tail_arrived[1]],
        flops * 2 * eighth,
        [share] * devices,
    )
    parts = [
        xor_permute(parts[distance], "inp", distance) for distance in reversed(range(1, devices))
    ] + [parts[0]]
    return finish(parts, 2 * width - 1)


def solution(mesh):
    return jax.shard_map(
        on_device,
        mesh=mesh,
        in_specs=(P("freq", None, "inp", None), P("inp", None), P("inp", None, None)),
        out_specs=P("inp", "freq", None, None),
        check_vma=False,
    )
```

```python
import functools

import jax
import jax.numpy as jnp
from jax import lax
from jax.experimental import pallas as pl
from jax.experimental.pallas import tpu as pltpu
from jax.sharding import PartitionSpec as P

RG_DEV = 8
GROUP_ROWS = 16
HBM = pl.BlockSpec(memory_space=pltpu.HBM)
WHOLE = pl.BlockSpec(memory_space=pltpu.VMEM)


def xor_permute(x, axis, distance):
    return lax.ppermute(x, axis, [(i, i ^ distance) for i in range(lax.axis_size(axis))])


def parity(index, levels):
    bits = index & 1
    for level in range(1, levels):
        bits = bits ^ ((index >> level) & 1)
    return bits


def order_matrix(position_row):
    width = position_row.shape[-1]
    by_position = jnp.transpose(jnp.broadcast_to(position_row, (width, width)))
    inputs = lax.broadcasted_iota(jnp.int32, (width, width), 1)
    return (by_position == inputs).astype(jnp.float32).astype(jnp.bfloat16)


def product(x, y):
    return lax.dot_general(x, y, (((1,), (1,)), ((), ())), preferred_element_type=jnp.float32)


def lag_rows(tiles):
    count, width, _ = tiles.shape
    half = width // 2
    low, high = tiles[:, :half], tiles[:, half:]
    sheared = jnp.concatenate(
        [
            high[:, :, :half],
            high[:, :, half:] + low[:, :, :half],
            low[:, :, half:],
            jnp.zeros((count, half, half), jnp.float32),
        ],
        axis=2,
    )
    rows = half
    while rows > 8:
        rows //= 2
        upper = sheared[:, :rows].reshape(count * rows, 2 * width)
        upper = pltpu.roll(upper, rows, 1).reshape(count, rows, 2 * width)
        sheared = upper + sheared[:, rows:]
    flat = sheared.reshape(count * rows, 2 * width)
    sublane = lax.broadcasted_iota(jnp.int32, flat.shape, 0) % 8
    while rows > 1:
        rows //= 2
        flat = jnp.where((sublane & rows) == 0, pltpu.roll(flat, rows, 1), flat)
    return jnp.sum(flat.reshape(count, 8, 2 * width), axis=1)


def tile_lags(x_re, x_im, y_re, y_im, samples):
    real_part = product(x_re, y_re) + product(x_im, y_im)
    imag_part = product(x_im, y_re) - product(x_re, y_im)
    return lag_rows(jnp.stack([real_part, imag_part])) * (1.0 / samples)


def split_rows(x):
    first = x.astype(jnp.bfloat16).astype(jnp.float32)
    rest = x - first
    second = rest.astype(jnp.bfloat16).astype(jnp.float32)
    return jnp.concatenate([first, second, rest - second], axis=0)


def conjugate_lags(lags):
    count, width = lags.shape
    lanes = 128
    flip = (
        lax.broadcasted_iota(jnp.int32, (lanes, lanes), 0)
        + lax.broadcasted_iota(jnp.int32, (lanes, lanes), 1)
        == lanes - 1
    )
    flip = flip.astype(jnp.float32).astype(jnp.bfloat16)
    terms = split_rows(lags)
    spans = range(0, width, lanes)
    terms = jnp.concatenate([terms[:, first : first + lanes] for first in spans], axis=0)
    terms = jnp.dot(terms.astype(jnp.bfloat16), flip, preferred_element_type=jnp.float32)
    turned = []
    for i in reversed(range(len(spans))):
        part = terms[3 * count * i : 3 * count * (i + 1)]
        turned.append(part[:count] + part[count : 2 * count] + part[2 * count :])
    turned = pltpu.roll(jnp.concatenate(turned, axis=1), width - 1, 1)
    odd = lax.broadcasted_iota(jnp.int32, turned.shape, 0) % 2 == 1
    return jnp.where(odd, -turned, turned)


def group_block(groups):
    rows = jnp.concatenate([groups[b] for b in range(groups.shape[0])], axis=0)
    lines, lanes = rows.shape
    return jnp.pad(rows, ((0, GROUP_ROWS - lines), (0, 128 - lanes)))


def target_rows(groups):
    me = lax.axis_index("inp")
    bits = RG_DEV.bit_length() - 1
    return (((groups >> bits) ^ me) << (bits + 1)) + ((groups & (RG_DEV - 1)) << 1)


def pick_matrix(entries, rows):
    count = len(entries)
    shape = (rows, 3 * count)
    row = lax.broadcasted_iota(jnp.int32, shape, 0)
    column = lax.broadcasted_iota(jnp.int32, shape, 1) % count
    pick = jnp.zeros(shape, jnp.float32)
    for j, (targets, line, lane, part) in enumerate(entries):
        target = jnp.broadcast_to(targets[line : line + 1, lane : lane + 1] + part, shape)
        pick = jnp.where(jnp.logical_and(column == j, row == target), 1.0, pick)
    return pick.astype(jnp.bfloat16)


def pick_matrices(groups, heads, blocks, out_rows):
    own = target_rows(group_block(groups))
    others = [target_rows(head.astype(jnp.float32).astype(jnp.int32)) for head in heads]
    tiles = [(line, part) for line in range(blocks * blocks) for part in range(2)]
    columns = [
        [(own, line, 0, part) for line, part in tiles],
        [(others[-1], line, 0, part) for line, part in tiles],
    ]
    levels = range(len(heads))

    def pairs(block_set, level_set):
        order = [
            (b, level, a, part)
            for b in block_set
            for level in level_set
            for a in range(blocks)
            for part in range(2)
        ]
        forward = [(own, a * blocks + b, level + 1, part) for b, level, a, part in order]
        turned = [(others[level], b * blocks + a, level + 1, part) for b, level, a, part in order]
        return forward + turned

    columns.append(pairs(range(blocks), levels))
    columns.append(pairs([blocks - 1], levels))
    columns += [pairs([blocks - 1], [level]) for level in levels]
    return [pick_matrix(entries, out_rows) for entries in columns]


def group_sums(pick, lags):
    terms = split_rows(lags).astype(jnp.bfloat16)
    return jnp.dot(pick, terms, preferred_element_type=jnp.float32)


def columns(piece):
    spans, start = [], 0
    for _, first, last in piece:
        spans.append((start, start + last - first))
        start += last - first
    return spans


def piece_shape(piece, width, more):
    return jax.ShapeDtypeStruct((2 * width + more, columns(piece)[-1][1]), jnp.bfloat16)


def send_kernel(levels, pieces, with_groups, position_ref, volts_ref, extra_ref, *refs):
    out_refs, refs = refs[: len(pieces)], refs[len(pieces) :]
    position, raw, position_sem, in_sem = refs[:4]
    other = 1 - parity(lax.axis_index("inp"), levels)
    width = position.shape[1]
    load_position = pltpu.make_async_copy(position_ref, position, position_sem)
    load_position.start()
    if with_groups:
        groups, group_sem = refs[4:]
        load_groups = pltpu.make_async_copy(extra_ref, groups, group_sem)
        load_groups.start()
    parts = [segment for piece in pieces for segment in piece]
    blocks = sorted({block for block, _, _ in parts})
    spans = [
        (
            min(first for b, first, _ in parts if b == block),
            max(last for b, _, last in parts if b == block),
        )
        for block in blocks
    ]
    loads = [
        [
            pltpu.make_async_copy(
                volts_ref.at[other, c, pl.ds(block * width, width), pl.ds(first, last - first)],
                raw.at[i, c, :, pl.ds(first, last - first)],
                in_sem.at[i, c],
            )
            for c in range(2)
        ]
        for i, (block, (first, last)) in enumerate(zip(blocks, spans))
    ]
    for load in loads:
        load[0].start()
        load[1].start()
    load_position.wait()
    orders = [order_matrix(position[block : block + 1, :]) for block in blocks]
    for i, block in enumerate(blocks):
        for c in range(2):
            loads[i][c].wait()
            for piece, out_ref in zip(pieces, out_refs):
                for (b, first, last), (start, end) in zip(piece, columns(piece)):
                    if b == block:
                        out_ref[c * width : (c + 1) * width, start:end] = jnp.dot(
                            orders[i], raw[i, c, :, first:last], preferred_element_type=jnp.float32
                        ).astype(jnp.bfloat16)
    if with_groups:
        load_groups.wait()
        out_refs[0][2 * width :, :] = jnp.zeros(
            (GROUP_ROWS, out_refs[0].shape[1]), jnp.bfloat16
        )
        rows = group_block(groups[...])
        out_refs[0][2 * width :, :128] = rows.astype(jnp.float32).astype(jnp.bfloat16)


def order_to_send(position_input, volts, groups, before, pieces, levels):
    width = position_input.shape[1]
    samples = volts.shape[3]
    count = len({block for piece in pieces for block, _, _ in piece})
    total = sum(columns(piece)[-1][1] for piece in pieces)
    with_groups = groups is not None
    extra = [GROUP_ROWS if with_groups else 0] + [0] * (len(pieces) - 1)
    inputs = [pltpu.with_memory_space_constraint(x, pltpu.HBM) for x in (position_input, volts)]
    if with_groups:
        inputs.append(pltpu.with_memory_space_constraint(groups, pltpu.HBM))
    else:
        inputs.append(before)
    scratch = [
        pltpu.VMEM(position_input.shape, jnp.int32),
        pltpu.VMEM((count, 2, width, samples), jnp.bfloat16),
        pltpu.SemaphoreType.DMA(()),
        pltpu.SemaphoreType.DMA((count, 2)),
    ]
    if with_groups:
        scratch += [pltpu.VMEM(groups.shape, jnp.int32), pltpu.SemaphoreType.DMA(())]
    return pl.pallas_call(
        functools.partial(send_kernel, levels, pieces, with_groups),
        out_shape=[piece_shape(piece, width, more) for piece, more in zip(pieces, extra)],
        in_specs=[HBM, HBM, HBM if with_groups else pl.BlockSpec(memory_space=pl.ANY)],
        out_specs=[WHOLE] * len(pieces),
        scratch_shapes=scratch,
        compiler_params=pltpu.CompilerParams(vmem_limit_bytes=16 << 20),
        cost_estimate=pl.CostEstimate(
            flops=4 * width * width * total, bytes_accessed=8 * width * total, transcendentals=0
        ),
        name="order_to_send",
    )(*inputs)


def own_kernel(levels, piece, last, group_ref, position_ref, volts_ref, *refs):
    head_refs, refs = refs[:levels], refs[levels:]
    panel_ref, sums_ref, *refs, raw, other_panel, lags_ref, in_sem = refs
    pick_refs, (more_ref, piece_ref, last_ref, last_panel_ref) = refs[:-4], refs[-4:]
    blocks, _, width, _ = panel_ref.shape
    mine = parity(lax.axis_index("inp"), levels)
    channels = (mine, 1 - mine)
    loads = [
        [
            [
                pltpu.make_async_copy(
                    volts_ref.at[channels[f], c, pl.ds(b * width, width)],
                    raw.at[f, b, c],
                    in_sem.at[f, b, c],
                )
                for c in range(2)
            ]
            for b in range(blocks)
        ]
        for f in range(2)
    ]
    for f in range(2):
        for b in range(blocks):
            for c in range(2):
                loads[f][b][c].start()
    orders = [order_matrix(position_ref[b : b + 1, :]) for b in range(blocks)]
    for f, panel in enumerate((panel_ref, other_panel)):
        for b in range(blocks):
            for c in range(2):
                loads[f][b][c].wait()
                panel[b, c] = jnp.dot(
                    orders[b], raw[f, b, c], preferred_element_type=jnp.float32
                ).astype(jnp.bfloat16)

        def one_tile(index, carry, panel=panel, f=f):
            a = index // blocks
            b = index % blocks
            lags = tile_lags(panel[a, 0], panel[a, 1], panel[b, 0], panel[b, 1], panel.shape[3])
            center = lax.broadcasted_iota(jnp.int32, lags.shape, 1) == width - 1
            lags_ref[f * blocks * blocks + index] = jnp.where(
                jnp.logical_and(center, a == b), 0.0, lags
            )
            return carry

        lax.fori_loop(0, blocks * blocks, one_tile, 0)
    tiles = blocks * blocks
    lags = jnp.concatenate([lags_ref[i] for i in range(tiles)], axis=0)
    heads = [head_ref[2 * width :, :128] for head_ref in head_refs]
    own_pick, *picks = pick_matrices(group_ref[...], heads, blocks, sums_ref.shape[0])
    for pick_ref, pick in zip(pick_refs, picks):
        pick_ref[...] = pick
    sums_ref[...] = group_sums(own_pick, lags)
    for (block, first, end), (start, stop) in zip(piece, columns(piece)):
        for c in range(2):
            rows = other_panel[block, c, :, first:end]
            piece_ref[c * width : (c + 1) * width, start:stop] = rows
            more_ref[c * width : (c + 1) * width, start:stop] = rows
    lags = jnp.concatenate([lags_ref[tiles + i] for i in range(tiles)], axis=0)
    high = lags.astype(jnp.bfloat16).astype(jnp.float32)
    terms = jnp.concatenate([high, lags - high], axis=0).astype(jnp.bfloat16)
    more_ref[2 * width :, :] = terms
    block, first, end = last
    depth = end - first
    for c in range(2):
        last_ref[:, c * depth : (c + 1) * depth] = other_panel[block, c, :, first:end]
    for a in range(blocks):
        real_part, imag_part = panel_ref[a, 0, :, first:end], panel_ref[a, 1, :, first:end]
        last_panel_ref[a, :width, :depth] = real_part
        last_panel_ref[a, :width, depth:] = imag_part
        last_panel_ref[a, width:, :depth] = imag_part
        last_panel_ref[a, width:, depth:] = -real_part


def own_level(groups, position_input, volts, heads, piece, last, out_rows):
    levels = len(heads)
    blocks, width = position_input.shape
    samples = volts.shape[3]
    tiles = 2 * blocks * blocks
    counts = [tiles, 2 * levels * tiles, 2 * levels * tiles // blocks] + [4 * blocks] * levels
    depth = last[2] - last[1]
    return pl.pallas_call(
        functools.partial(own_kernel, levels, piece, last),
        out_shape=(
            jax.ShapeDtypeStruct((blocks, 2, width, samples), jnp.bfloat16),
            jax.ShapeDtypeStruct((out_rows, 2 * width), jnp.float32),
            *[jax.ShapeDtypeStruct((out_rows, 3 * n), jnp.bfloat16) for n in counts],
            piece_shape(piece, width, 2 * tiles),
            piece_shape(piece, width, 0),
            jax.ShapeDtypeStruct((width, 2 * depth), jnp.bfloat16),
            jax.ShapeDtypeStruct((blocks, 2 * width, 2 * depth), jnp.bfloat16),
        ),
        in_specs=[WHOLE, WHOLE, HBM] + [WHOLE] * levels,
        out_specs=(WHOLE,) * (6 + len(counts)),
        scratch_shapes=[
            pltpu.VMEM((2, blocks, 2, width, samples), jnp.bfloat16),
            pltpu.VMEM((blocks, 2, width, samples), jnp.bfloat16),
            pltpu.VMEM((2 * blocks * blocks, 2, 2 * width), jnp.float32),
            pltpu.SemaphoreType.DMA((2, blocks, 2)),
        ],
        compiler_params=pltpu.CompilerParams(vmem_limit_bytes=16 << 20),
        cost_estimate=pl.CostEstimate(
            flops=64 * blocks * blocks * width * width * samples,
            bytes_accessed=12 * blocks * width * samples,
            transcendentals=0,
        ),
        name="own_level",
    )(groups, position_input, pltpu.with_memory_space_constraint(volts, pltpu.HBM), *heads)


def add_lags(rows, pick_ref, sums_ref):
    lags = jnp.concatenate(rows, axis=0)
    lags = jnp.concatenate([lags, conjugate_lags(lags)], axis=0)
    return sums_ref[...] + group_sums(pick_ref[...], lags)


def pair_kernel(levels, pieces, pick_ref, sums_ref, panel_ref, *refs):
    count = levels * len(pieces)
    partner_refs, more_refs, out_ref = refs[:count], refs[count:-1], refs[-1]
    _, _, width, samples = panel_ref.shape
    rows = []
    for block in sorted({block for piece in pieces for block, _, _ in piece}):
        for level in range(levels):
            for a in range(panel_ref.shape[0]):
                real_part, imag_part = 0.0, 0.0
                for i, piece in enumerate(pieces):
                    partner = partner_refs[level * len(pieces) + i]
                    for (b, first, last), (start, end) in zip(piece, columns(piece)):
                        if b != block:
                            continue
                        x_re, x_im = panel_ref[a, 0, :, first:last], panel_ref[a, 1, :, first:last]
                        y_re = partner[:width, start:end]
                        y_im = partner[width : 2 * width, start:end]
                        real_part = real_part + (product(x_re, y_re) + product(x_im, y_im))
                        imag_part = imag_part + (product(x_im, y_re) - product(x_re, y_im))
                rows.append(lag_rows(jnp.stack([real_part, imag_part])) * (1.0 / samples))
    sums = add_lags(rows, pick_ref, sums_ref)
    for more_ref in more_refs:
        terms = partner_refs[-1][2 * width :, :].astype(jnp.float32)
        half = terms.shape[0] // 2
        sums = sums + group_sums(more_ref[...], terms[:half] + terms[half:])
    out_ref[...] = sums


def last_kernel(samples, pick_ref, sums_ref, panel_ref, partner_ref, *out_refs):
    blocks, rows_both, _ = panel_ref.shape
    width = rows_both // 2
    rows = []
    for a in range(blocks):
        tiles = product(panel_ref[a], partner_ref[...]).reshape(2, width, width)
        rows.append(lag_rows(tiles) * (1.0 / samples))
    sums = add_lags(rows, pick_ref, sums_ref)
    share = sums.shape[0] // len(out_refs)
    for place, out_ref in enumerate(out_refs):
        out_ref[...] = sums[place * share : (place + 1) * share]


def pair_call(kernel, inputs, work, out_shape):
    return pl.pallas_call(
        kernel,
        out_shape=out_shape,
        in_specs=[WHOLE] * len(inputs),
        out_specs=[WHOLE] * len(out_shape),
        compiler_params=pltpu.CompilerParams(vmem_limit_bytes=16 << 20),
        cost_estimate=pl.CostEstimate(flops=work, bytes_accessed=4 << 20, transcendentals=0),
        name="pair_level",
    )(*inputs)


def finish_kernel(levels, *refs):
    part_refs, out_ref = refs[:-1], refs[-1]
    mine = parity(lax.axis_index("inp"), levels)
    groups, channels, parts, lags = out_ref.shape
    sums = [None, None]
    for distance, part_ref in enumerate(reversed(part_refs)):
        side = distance.bit_count() % 2
        sums[side] = part_ref[...] if sums[side] is None else sums[side] + part_ref[...]
    for f in range(channels):
        total = jnp.where(mine == f, sums[0], sums[1])
        for g in range(groups):
            out_ref[g, f] = total[g * parts : (g + 1) * parts, :lags]


def finish(parts, levels, lags):
    return pl.pallas_call(
        functools.partial(finish_kernel, levels),
        out_shape=jax.ShapeDtypeStruct((RG_DEV, 2, 2, lags), jnp.float32),
        in_specs=[WHOLE] * len(parts),
        out_specs=WHOLE,
        compiler_params=pltpu.CompilerParams(vmem_limit_bytes=8 << 20),
        name="finish",
    )(*parts)


def on_device(volts, position_input, tile_group):
    blocks, width = position_input.shape
    samples = volts.shape[3]
    devices = lax.axis_size("inp")
    levels = devices.bit_length() - 1
    out_rows = devices * RG_DEV * 2
    eighth = samples // 8
    head = [[(0, 0, 2 * eighth)]]
    rest = [[(0, 2 * eighth, samples), (1, 0, 2 * eighth)]]
    tail = [(1, 2 * eighth, 6 * eighth)]
    last = (1, 6 * eighth, samples)
    by_block = tile_group.transpose(0, 2, 1)
    partner_of = [functools.partial(xor_permute, axis="inp", distance=1 << l) for l in range(levels)]
    sent = order_to_send(position_input, volts, by_block, None, head, levels)
    head_arrived = [send(sent[0]) for send in partner_of]
    sent = order_to_send(position_input, volts, None, sent[0], rest, levels)
    rest_arrived = [[send(piece) for send in partner_of] for piece in sent]
    panel, sums, neighbour, both, second, *picks, more, piece, last_piece, last_panel = own_level(
        by_block, position_input, volts, head_arrived, tail, last, out_rows
    )
    tail_arrived = [send(piece) for send in partner_of[:-1]] + [partner_of[-1](more)]
    last_arrived = [send(last_piece) for send in partner_of]

    whole = jax.ShapeDtypeStruct(sums.shape, jnp.float32)
    share = jax.ShapeDtypeStruct((out_rows // devices, 2 * width), jnp.float32)
    flops = 8 * levels * blocks * width * width
    arrived = [piece for pair in zip(head_arrived, rest_arrived[0]) for piece in pair]
    (sums,) = pair_call(
        functools.partial(pair_kernel, levels, head + rest),
        [both, sums, panel, *arrived],
        flops * 10 * eighth,
        [whole],
    )
    (sums,) = pair_call(
        functools.partial(pair_kernel, levels, [tail]),
        [second, sums, panel, *tail_arrived, neighbour],
        flops * 4 * eighth,
        [whole],
    )
    for level in reversed(range(levels)):
        parts = pair_call(
            functools.partial(last_kernel, samples),
            [picks[level], sums, last_panel, last_arrived[level]],
            flops * 2 * eighth // levels,
            [share] * devices if level == 0 else [whole],
        )
        sums = parts[0]
    parts = [
        xor_permute(parts[distance], "inp", distance) for distance in reversed(range(1, devices))
    ] + [parts[0]]
    return finish(parts, levels, 2 * width - 1)


def solution(mesh):
    return jax.shard_map(
        on_device,
        mesh=mesh,
        in_specs=(P("freq", None, "inp", None), P("inp", None), P("inp", None, None)),
        out_specs=P("inp", "freq", None, None),
        check_vma=False,
    )
```

```python
import functools

import jax
import jax.numpy as jnp
from jax import lax
from jax.experimental import pallas as pl
from jax.experimental.pallas import tpu as pltpu
from jax.sharding import PartitionSpec as P

RG_DEV = 8
GROUP_ROWS = 16
HBM = pl.BlockSpec(memory_space=pltpu.HBM)
WHOLE = pl.BlockSpec(memory_space=pltpu.VMEM)


def xor_permute(x, axis, distance):
    return lax.ppermute(x, axis, [(i, i ^ distance) for i in range(lax.axis_size(axis))])


def parity(index, levels):
    bits = index & 1
    for level in range(1, levels):
        bits = bits ^ ((index >> level) & 1)
    return bits


def order_matrix(position_row):
    width = position_row.shape[-1]
    by_position = jnp.transpose(jnp.broadcast_to(position_row, (width, width)))
    inputs = lax.broadcasted_iota(jnp.int32, (width, width), 1)
    return (by_position == inputs).astype(jnp.float32).astype(jnp.bfloat16)


def product(x, y):
    return lax.dot_general(x, y, (((1,), (1,)), ((), ())), preferred_element_type=jnp.float32)


def lag_rows(tiles):
    count, width, _ = tiles.shape
    half = width // 2
    low, high = tiles[:, :half], tiles[:, half:]
    sheared = jnp.concatenate(
        [
            high[:, :, :half],
            high[:, :, half:] + low[:, :, :half],
            low[:, :, half:],
            jnp.zeros((count, half, half), jnp.float32),
        ],
        axis=2,
    )
    rows = half
    while rows > 8:
        rows //= 2
        upper = sheared[:, :rows].reshape(count * rows, 2 * width)
        upper = pltpu.roll(upper, rows, 1).reshape(count, rows, 2 * width)
        sheared = upper + sheared[:, rows:]
    flat = sheared.reshape(count * rows, 2 * width)
    sublane = lax.broadcasted_iota(jnp.int32, flat.shape, 0) % 8
    while rows > 1:
        rows //= 2
        flat = jnp.where((sublane & rows) == 0, pltpu.roll(flat, rows, 1), flat)
    return jnp.sum(flat.reshape(count, 8, 2 * width), axis=1)


def tile_lags(x_re, x_im, y_re, y_im, samples):
    real_part = product(x_re, y_re) + product(x_im, y_im)
    imag_part = product(x_im, y_re) - product(x_re, y_im)
    return lag_rows(jnp.stack([real_part, imag_part])) * (1.0 / samples)


def split_rows(x):
    first = x.astype(jnp.bfloat16).astype(jnp.float32)
    rest = x - first
    second = rest.astype(jnp.bfloat16).astype(jnp.float32)
    return jnp.concatenate([first, second, rest - second], axis=0)


def conjugate_lags(lags):
    count, width = lags.shape
    lanes = 128
    flip = (
        lax.broadcasted_iota(jnp.int32, (lanes, lanes), 0)
        + lax.broadcasted_iota(jnp.int32, (lanes, lanes), 1)
        == lanes - 1
    )
    flip = flip.astype(jnp.float32).astype(jnp.bfloat16)
    terms = split_rows(lags)
    spans = range(0, width, lanes)
    terms = jnp.concatenate([terms[:, first : first + lanes] for first in spans], axis=0)
    terms = jnp.dot(terms.astype(jnp.bfloat16), flip, preferred_element_type=jnp.float32)
    turned = []
    for i in reversed(range(len(spans))):
        part = terms[3 * count * i : 3 * count * (i + 1)]
        turned.append(part[:count] + part[count : 2 * count] + part[2 * count :])
    turned = pltpu.roll(jnp.concatenate(turned, axis=1), width - 1, 1)
    odd = lax.broadcasted_iota(jnp.int32, turned.shape, 0) % 2 == 1
    return jnp.where(odd, -turned, turned)


def group_block(groups):
    rows = jnp.concatenate([groups[b] for b in range(groups.shape[0])], axis=0)
    lines, lanes = rows.shape
    return jnp.pad(rows, ((0, GROUP_ROWS - lines), (0, 128 - lanes)))


def target_rows(groups):
    me = lax.axis_index("inp")
    bits = RG_DEV.bit_length() - 1
    return (((groups >> bits) ^ me) << (bits + 1)) + ((groups & (RG_DEV - 1)) << 1)


def pick_matrix(entries, rows):
    count = len(entries)
    shape = (rows, 3 * count)
    row = lax.broadcasted_iota(jnp.int32, shape, 0)
    column = lax.broadcasted_iota(jnp.int32, shape, 1) % count
    pick = jnp.zeros(shape, jnp.float32)
    for j, (targets, line, lane, part) in enumerate(entries):
        target = jnp.broadcast_to(targets[line : line + 1, lane : lane + 1] + part, shape)
        pick = jnp.where(jnp.logical_and(column == j, row == target), 1.0, pick)
    return pick.astype(jnp.bfloat16)


def pick_matrices(groups, heads, blocks, out_rows):
    own = target_rows(group_block(groups))
    others = [target_rows(head.astype(jnp.float32).astype(jnp.int32)) for head in heads]
    tiles = [(line, part) for line in range(blocks * blocks) for part in range(2)]
    columns = [
        [(own, line, 0, part) for line, part in tiles],
        [(others[-1], line, 0, part) for line, part in tiles],
    ]
    levels = range(len(heads))

    def pairs(block_set, level_set):
        order = [
            (b, level, a, part)
            for b in block_set
            for level in level_set
            for a in range(blocks)
            for part in range(2)
        ]
        forward = [(own, a * blocks + b, level + 1, part) for b, level, a, part in order]
        turned = [(others[level], b * blocks + a, level + 1, part) for b, level, a, part in order]
        return forward + turned

    columns.append(pairs(range(blocks), levels))
    columns.append(pairs([blocks - 1], levels))
    columns += [pairs([blocks - 1], [level]) for level in levels]
    return [pick_matrix(entries, out_rows) for entries in columns]


def group_sums(pick, lags):
    terms = split_rows(lags).astype(jnp.bfloat16)
    return jnp.dot(pick, terms, preferred_element_type=jnp.float32)


def columns(piece):
    spans, start = [], 0
    for _, first, last in piece:
        spans.append((start, start + last - first))
        start += last - first
    return spans


def piece_shape(piece, width, more):
    return jax.ShapeDtypeStruct((2 * width + more, columns(piece)[-1][1]), jnp.bfloat16)


def load_piece(piece, other, width, volts_ref, raw, in_sem):
    blocks = sorted({block for block, _, _ in piece})
    loads = []
    for i, block in enumerate(blocks):
        start = min(first for b, first, _ in piece if b == block)
        end = max(last for b, _, last in piece if b == block)
        for c in range(2):
            load = pltpu.make_async_copy(
                volts_ref.at[other, c, pl.ds(block * width, width), pl.ds(start, end - start)],
                raw.at[i, c, :, pl.ds(start, end - start)],
                in_sem.at[i, c],
            )
            load.start()
            loads.append((i, block, c, load))
    return loads


def order_piece(piece, loads, position, raw, out_ref):
    width = position.shape[1]
    orders = {
        block: order_matrix(position[block : block + 1, :]) for block in sorted({l[1] for l in loads})
    }
    for i, block, c, load in loads:
        load.wait()
        for (b, first, last), (start, end) in zip(piece, columns(piece)):
            if b == block:
                out_ref[c * width : (c + 1) * width, start:end] = jnp.dot(
                    orders[block], raw[i, c, :, first:last], preferred_element_type=jnp.float32
                ).astype(jnp.bfloat16)


def order_and_store(rest, loads, position, raw, ordered, rest_ref, out_sem):
    order_piece(rest, loads, position, raw, ordered)
    store = pltpu.make_async_copy(ordered, rest_ref, out_sem)
    store.start()
    store.wait()


def on_odd_core():
    return lax.axis_index("freq") % 2 == 1


def head_kernel(levels, head, rest, position_ref, volts_ref, group_ref, *refs):
    head_ref, rest_ref, position, groups, *refs = refs
    raw, rest_raw, ordered, small_sem, in_sem, rest_sem, out_sem = refs
    other = 1 - parity(lax.axis_index("inp"), levels)
    width = position.shape[1]
    load_position = pltpu.make_async_copy(position_ref, position, small_sem.at[0])
    load_position.start()
    load_groups = pltpu.make_async_copy(group_ref, groups, small_sem.at[1])
    load_groups.start()
    loads = load_piece(head, other, width, volts_ref, raw, in_sem)
    load_position.wait()

    @pl.when(on_odd_core())
    def _():
        rest_loads = load_piece(rest, other, width, volts_ref, rest_raw, rest_sem)
        order_and_store(rest, rest_loads, position, rest_raw, ordered, rest_ref, out_sem)

    order_piece(head, loads, position, raw, head_ref)
    load_groups.wait()
    head_ref[2 * width :, :] = jnp.zeros((GROUP_ROWS, head_ref.shape[1]), jnp.bfloat16)
    rows = group_block(groups[...])
    head_ref[2 * width :, :128] = rows.astype(jnp.float32).astype(jnp.bfloat16)


def rest_kernel(levels, rest, position_ref, volts_ref, _, rest_ref, position, raw, ordered, *sems):
    position_sem, rest_sem, out_sem = sems
    other = 1 - parity(lax.axis_index("inp"), levels)

    @pl.when(jnp.logical_not(on_odd_core()))
    def _():
        load_position = pltpu.make_async_copy(position_ref, position, position_sem)
        load_position.start()
        loads = load_piece(rest, other, position.shape[1], volts_ref, raw, rest_sem)
        load_position.wait()
        order_and_store(rest, loads, position, raw, ordered, rest_ref, out_sem)


def order_to_send(position_input, volts, groups, head, rest, levels):
    blocks, width = position_input.shape
    samples = volts.shape[3]
    in_hbm = [pltpu.with_memory_space_constraint(x, pltpu.HBM) for x in (position_input, volts)]
    any_space = pl.BlockSpec(memory_space=pl.ANY)
    head_shape, rest_shape = piece_shape(head, width, GROUP_ROWS), piece_shape(rest, width, 0)
    position = pltpu.VMEM(position_input.shape, jnp.int32)
    rest_scratch = [
        pltpu.VMEM((blocks, 2, width, samples), jnp.bfloat16),
        pltpu.VMEM(rest_shape.shape, jnp.bfloat16),
    ]
    semaphore = pltpu.SemaphoreType.DMA
    params = pltpu.CompilerParams(vmem_limit_bytes=16 << 20)
    flops = 4 * width * width * columns(rest)[-1][1]
    cost = pl.CostEstimate(flops=flops, bytes_accessed=2 << 20, transcendentals=0)
    sent, second = pl.pallas_call(
        functools.partial(head_kernel, levels, head, rest),
        out_shape=[head_shape, rest_shape],
        in_specs=[HBM] * 3,
        out_specs=[WHOLE, any_space],
        scratch_shapes=[
            position,
            pltpu.VMEM(groups.shape, jnp.int32),
            pltpu.VMEM((1, 2, width, samples), jnp.bfloat16),
            *rest_scratch,
            semaphore((2,)),
            semaphore((1, 2)),
            semaphore((blocks, 2)),
            semaphore(()),
        ],
        compiler_params=params,
        cost_estimate=cost,
        name="order_head",
    )(*in_hbm, pltpu.with_memory_space_constraint(groups, pltpu.HBM))
    second = pl.pallas_call(
        functools.partial(rest_kernel, levels, rest),
        out_shape=rest_shape,
        in_specs=[HBM, HBM, any_space],
        out_specs=any_space,
        scratch_shapes=[
            position,
            *rest_scratch,
            semaphore(()),
            semaphore((blocks, 2)),
            semaphore(()),
        ],
        input_output_aliases={2: 0},
        compiler_params=params,
        cost_estimate=cost,
        name="order_rest",
    )(*in_hbm, second)
    return sent, second


def own_kernel(levels, piece, last, group_ref, position_ref, volts_ref, *refs):
    head_refs, refs = refs[:levels], refs[levels:]
    panel_ref, sums_ref, *refs, raw, other_panel, lags_ref, in_sem = refs
    pick_refs, (more_ref, piece_ref, last_ref, last_panel_ref) = refs[:-4], refs[-4:]
    blocks, _, width, _ = panel_ref.shape
    mine = parity(lax.axis_index("inp"), levels)
    channels = (mine, 1 - mine)
    loads = [
        [
            [
                pltpu.make_async_copy(
                    volts_ref.at[channels[f], c, pl.ds(b * width, width)],
                    raw.at[f, b, c],
                    in_sem.at[f, b, c],
                )
                for c in range(2)
            ]
            for b in range(blocks)
        ]
        for f in range(2)
    ]
    for f in range(2):
        for b in range(blocks):
            for c in range(2):
                loads[f][b][c].start()
    orders = [order_matrix(position_ref[b : b + 1, :]) for b in range(blocks)]
    for f, panel in enumerate((panel_ref, other_panel)):
        for b in range(blocks):
            for c in range(2):
                loads[f][b][c].wait()
                panel[b, c] = jnp.dot(
                    orders[b], raw[f, b, c], preferred_element_type=jnp.float32
                ).astype(jnp.bfloat16)

        def one_tile(index, carry, panel=panel, f=f):
            a = index // blocks
            b = index % blocks
            lags = tile_lags(panel[a, 0], panel[a, 1], panel[b, 0], panel[b, 1], panel.shape[3])
            center = lax.broadcasted_iota(jnp.int32, lags.shape, 1) == width - 1
            lags_ref[f * blocks * blocks + index] = jnp.where(
                jnp.logical_and(center, a == b), 0.0, lags
            )
            return carry

        lax.fori_loop(0, blocks * blocks, one_tile, 0)
    tiles = blocks * blocks
    lags = jnp.concatenate([lags_ref[i] for i in range(tiles)], axis=0)
    heads = [head_ref[2 * width :, :128] for head_ref in head_refs]
    own_pick, *picks = pick_matrices(group_ref[...], heads, blocks, sums_ref.shape[0])
    for pick_ref, pick in zip(pick_refs, picks):
        pick_ref[...] = pick
    sums_ref[...] = group_sums(own_pick, lags)
    for (block, first, end), (start, stop) in zip(piece, columns(piece)):
        for c in range(2):
            rows = other_panel[block, c, :, first:end]
            piece_ref[c * width : (c + 1) * width, start:stop] = rows
            more_ref[c * width : (c + 1) * width, start:stop] = rows
    lags = jnp.concatenate([lags_ref[tiles + i] for i in range(tiles)], axis=0)
    high = lags.astype(jnp.bfloat16).astype(jnp.float32)
    terms = jnp.concatenate([high, lags - high], axis=0).astype(jnp.bfloat16)
    more_ref[2 * width :, :] = terms
    block, first, end = last
    depth = end - first
    for c in range(2):
        last_ref[:, c * depth : (c + 1) * depth] = other_panel[block, c, :, first:end]
    for a in range(blocks):
        real_part, imag_part = panel_ref[a, 0, :, first:end], panel_ref[a, 1, :, first:end]
        last_panel_ref[a, :width, :depth] = real_part
        last_panel_ref[a, :width, depth:] = imag_part
        last_panel_ref[a, width:, :depth] = imag_part
        last_panel_ref[a, width:, depth:] = -real_part


def own_level(groups, position_input, volts, heads, piece, last, out_rows):
    levels = len(heads)
    blocks, width = position_input.shape
    samples = volts.shape[3]
    tiles = 2 * blocks * blocks
    counts = [tiles, 2 * levels * tiles, 2 * levels * tiles // blocks] + [4 * blocks] * levels
    depth = last[2] - last[1]
    return pl.pallas_call(
        functools.partial(own_kernel, levels, piece, last),
        out_shape=(
            jax.ShapeDtypeStruct((blocks, 2, width, samples), jnp.bfloat16),
            jax.ShapeDtypeStruct((out_rows, 2 * width), jnp.float32),
            *[jax.ShapeDtypeStruct((out_rows, 3 * n), jnp.bfloat16) for n in counts],
            piece_shape(piece, width, 2 * tiles),
            piece_shape(piece, width, 0),
            jax.ShapeDtypeStruct((width, 2 * depth), jnp.bfloat16),
            jax.ShapeDtypeStruct((blocks, 2 * width, 2 * depth), jnp.bfloat16),
        ),
        in_specs=[WHOLE, WHOLE, HBM] + [WHOLE] * levels,
        out_specs=(WHOLE,) * (6 + len(counts)),
        scratch_shapes=[
            pltpu.VMEM((2, blocks, 2, width, samples), jnp.bfloat16),
            pltpu.VMEM((blocks, 2, width, samples), jnp.bfloat16),
            pltpu.VMEM((2 * blocks * blocks, 2, 2 * width), jnp.float32),
            pltpu.SemaphoreType.DMA((2, blocks, 2)),
        ],
        compiler_params=pltpu.CompilerParams(vmem_limit_bytes=16 << 20),
        cost_estimate=pl.CostEstimate(
            flops=64 * blocks * blocks * width * width * samples,
            bytes_accessed=12 * blocks * width * samples,
            transcendentals=0,
        ),
        name="own_level",
    )(groups, position_input, pltpu.with_memory_space_constraint(volts, pltpu.HBM), *heads)


def add_lags(rows, pick_ref, sums_ref):
    lags = jnp.concatenate(rows, axis=0)
    lags = jnp.concatenate([lags, conjugate_lags(lags)], axis=0)
    return sums_ref[...] + group_sums(pick_ref[...], lags)


def pair_kernel(levels, pieces, pick_ref, sums_ref, panel_ref, *refs):
    count = levels * len(pieces)
    partner_refs, more_refs, out_ref = refs[:count], refs[count:-1], refs[-1]
    _, _, width, samples = panel_ref.shape
    rows = []
    for block in sorted({block for piece in pieces for block, _, _ in piece}):
        for level in range(levels):
            for a in range(panel_ref.shape[0]):
                real_part, imag_part = 0.0, 0.0
                for i, piece in enumerate(pieces):
                    partner = partner_refs[level * len(pieces) + i]
                    for (b, first, last), (start, end) in zip(piece, columns(piece)):
                        if b != block:
                            continue
                        x_re, x_im = panel_ref[a, 0, :, first:last], panel_ref[a, 1, :, first:last]
                        y_re = partner[:width, start:end]
                        y_im = partner[width : 2 * width, start:end]
                        real_part = real_part + (product(x_re, y_re) + product(x_im, y_im))
                        imag_part = imag_part + (product(x_im, y_re) - product(x_re, y_im))
                rows.append(lag_rows(jnp.stack([real_part, imag_part])) * (1.0 / samples))
    sums = add_lags(rows, pick_ref, sums_ref)
    for more_ref in more_refs:
        terms = partner_refs[-1][2 * width :, :].astype(jnp.float32)
        half = terms.shape[0] // 2
        sums = sums + group_sums(more_ref[...], terms[:half] + terms[half:])
    out_ref[...] = sums


def last_kernel(samples, pick_ref, sums_ref, panel_ref, partner_ref, *out_refs):
    blocks, rows_both, _ = panel_ref.shape
    width = rows_both // 2
    rows = []
    for a in range(blocks):
        tiles = product(panel_ref[a], partner_ref[...]).reshape(2, width, width)
        rows.append(lag_rows(tiles) * (1.0 / samples))
    sums = add_lags(rows, pick_ref, sums_ref)
    share = sums.shape[0] // len(out_refs)
    for place, out_ref in enumerate(out_refs):
        out_ref[...] = sums[place * share : (place + 1) * share]


def pair_call(kernel, inputs, work, out_shape):
    return pl.pallas_call(
        kernel,
        out_shape=out_shape,
        in_specs=[WHOLE] * len(inputs),
        out_specs=[WHOLE] * len(out_shape),
        compiler_params=pltpu.CompilerParams(vmem_limit_bytes=16 << 20),
        cost_estimate=pl.CostEstimate(flops=work, bytes_accessed=4 << 20, transcendentals=0),
        name="pair_level",
    )(*inputs)


def finish_kernel(levels, *refs):
    part_refs, out_ref = refs[:-1], refs[-1]
    mine = parity(lax.axis_index("inp"), levels)
    groups, channels, parts, lags = out_ref.shape
    sums = [None, None]
    for distance, part_ref in enumerate(reversed(part_refs)):
        side = distance.bit_count() % 2
        sums[side] = part_ref[...] if sums[side] is None else sums[side] + part_ref[...]
    for f in range(channels):
        total = jnp.where(mine == f, sums[0], sums[1])
        for g in range(groups):
            out_ref[g, f] = total[g * parts : (g + 1) * parts, :lags]


def finish(parts, levels, lags):
    return pl.pallas_call(
        functools.partial(finish_kernel, levels),
        out_shape=jax.ShapeDtypeStruct((RG_DEV, 2, 2, lags), jnp.float32),
        in_specs=[WHOLE] * len(parts),
        out_specs=WHOLE,
        compiler_params=pltpu.CompilerParams(vmem_limit_bytes=8 << 20),
        name="finish",
    )(*parts)


def on_device(volts, position_input, tile_group):
    blocks, width = position_input.shape
    samples = volts.shape[3]
    devices = lax.axis_size("inp")
    levels = devices.bit_length() - 1
    out_rows = devices * RG_DEV * 2
    eighth = samples // 8
    head = [(0, 0, 3 * eighth)]
    rest = [(0, 3 * eighth, samples), (1, 0, 2 * eighth)]
    tail = [(1, 2 * eighth, 6 * eighth)]
    last = (1, 6 * eighth, samples)
    by_block = tile_group.transpose(0, 2, 1)
    partner_of = [functools.partial(xor_permute, axis="inp", distance=1 << l) for l in range(levels)]
    sent, second = order_to_send(position_input, volts, by_block, head, rest, levels)
    head_arrived = [send(sent) for send in partner_of]
    rest_arrived = [send(second) for send in partner_of]
    panel, sums, neighbour, both, second, *picks, more, piece, last_piece, last_panel = own_level(
        by_block, position_input, volts, head_arrived, tail, last, out_rows
    )
    tail_arrived = [send(piece) for send in partner_of[:-1]] + [partner_of[-1](more)]
    last_arrived = [send(last_piece) for send in partner_of]

    whole = jax.ShapeDtypeStruct(sums.shape, jnp.float32)
    share = jax.ShapeDtypeStruct((out_rows // devices, 2 * width), jnp.float32)
    flops = 8 * levels * blocks * width * width
    arrived = [piece for pair in zip(head_arrived, rest_arrived) for piece in pair]
    (sums,) = pair_call(
        functools.partial(pair_kernel, levels, [head, rest]),
        [both, sums, panel, *arrived],
        flops * 10 * eighth,
        [whole],
    )
    (sums,) = pair_call(
        functools.partial(pair_kernel, levels, [tail]),
        [second, sums, panel, *tail_arrived, neighbour],
        flops * 4 * eighth,
        [whole],
    )
    for level in reversed(range(levels)):
        parts = pair_call(
            functools.partial(last_kernel, samples),
            [picks[level], sums, last_panel, last_arrived[level]],
            flops * 2 * eighth // levels,
            [share] * devices if level == 0 else [whole],
        )
        sums = parts[0]
    parts = [
        xor_permute(parts[distance], "inp", distance) for distance in reversed(range(1, devices))
    ] + [parts[0]]
    return finish(parts, levels, 2 * width - 1)


def solution(mesh):
    return jax.shard_map(
        on_device,
        mesh=mesh,
        in_specs=(P("freq", None, "inp", None), P("inp", None), P("inp", None, None)),
        out_specs=P("inp", "freq", None, None),
        check_vma=False,
    )
```

```python
import functools

import jax
import jax.numpy as jnp
from jax import lax
from jax.experimental import pallas as pl
from jax.experimental.pallas import tpu as pltpu
from jax.sharding import PartitionSpec as P

RG_DEV = 8
GROUP_ROWS = 16
HBM = pl.BlockSpec(memory_space=pltpu.HBM)
WHOLE = pl.BlockSpec(memory_space=pltpu.VMEM)


def xor_permute(x, axis, distance):
    return lax.ppermute(x, axis, [(i, i ^ distance) for i in range(lax.axis_size(axis))])


def parity(index, levels):
    bits = index & 1
    for level in range(1, levels):
        bits = bits ^ ((index >> level) & 1)
    return bits


def order_matrix(position_row):
    width = position_row.shape[-1]
    by_position = jnp.transpose(jnp.broadcast_to(position_row, (width, width)))
    inputs = lax.broadcasted_iota(jnp.int32, (width, width), 1)
    return (by_position == inputs).astype(jnp.float32).astype(jnp.bfloat16)


def product(x, y):
    return lax.dot_general(x, y, (((1,), (1,)), ((), ())), preferred_element_type=jnp.float32)


def lag_rows(tiles):
    count, width, _ = tiles.shape
    half = width // 2
    low, high = tiles[:, :half], tiles[:, half:]
    sheared = jnp.concatenate(
        [
            high[:, :, :half],
            high[:, :, half:] + low[:, :, :half],
            low[:, :, half:],
            jnp.zeros((count, half, half), jnp.float32),
        ],
        axis=2,
    )
    rows = half
    while rows > 8:
        rows //= 2
        upper = sheared[:, :rows].reshape(count * rows, 2 * width)
        upper = pltpu.roll(upper, rows, 1).reshape(count, rows, 2 * width)
        sheared = upper + sheared[:, rows:]
    flat = sheared.reshape(count * rows, 2 * width)
    sublane = lax.broadcasted_iota(jnp.int32, flat.shape, 0) % 8
    while rows > 1:
        rows //= 2
        flat = jnp.where((sublane & rows) == 0, pltpu.roll(flat, rows, 1), flat)
    return jnp.sum(flat.reshape(count, 8, 2 * width), axis=1)


def tile_lags(x_re, x_im, y_re, y_im, samples):
    real_part = product(x_re, y_re) + product(x_im, y_im)
    imag_part = product(x_im, y_re) - product(x_re, y_im)
    return lag_rows(jnp.stack([real_part, imag_part])) * (1.0 / samples)


def split_rows(x):
    first = x.astype(jnp.bfloat16).astype(jnp.float32)
    rest = x - first
    second = rest.astype(jnp.bfloat16).astype(jnp.float32)
    return jnp.concatenate([first, second, rest - second], axis=0)


def anti_identity(size):
    place = lax.broadcasted_iota(jnp.int32, (size, size), 0) + lax.broadcasted_iota(
        jnp.int32, (size, size), 1
    )
    return (place == size - 1).astype(jnp.float32).astype(jnp.bfloat16)


def turn_lags(terms):
    count, width = terms.shape
    lanes = 128
    spans = range(0, width, lanes)
    terms = jnp.concatenate([terms[:, first : first + lanes] for first in spans], axis=0)
    terms = jnp.dot(
        terms.astype(jnp.bfloat16), anti_identity(lanes), preferred_element_type=jnp.float32
    )
    blocks = [terms[count * i : count * (i + 1)] for i in reversed(range(len(spans)))]
    return pltpu.roll(jnp.concatenate(blocks, axis=1), width - 1, 1)


def conjugate_lags(lags):
    count = lags.shape[0]
    turned = turn_lags(split_rows(lags))
    turned = turned[:count] + turned[count : 2 * count] + turned[2 * count :]
    odd = lax.broadcasted_iota(jnp.int32, turned.shape, 0) % 2 == 1
    return jnp.where(odd, -turned, turned)


def sheared_eights(tiles):
    count, width, _ = tiles.shape
    half = width // 2
    low, high = tiles[:, :half], tiles[:, half:]
    sheared = jnp.concatenate(
        [
            low[:, :, :half],
            low[:, :, half:] + high[:, :, :half],
            high[:, :, half:],
            jnp.zeros((count, half, half), jnp.float32),
        ],
        axis=2,
    )
    rows = half
    while rows > 8:
        rows //= 2
        lower = sheared[:, rows:].reshape(count * rows, 2 * width)
        lower = pltpu.roll(lower, rows, 1).reshape(count, rows, 2 * width)
        sheared = sheared[:, :rows] + lower
    return [pltpu.roll(sheared[i], 0, 1, stride=1, stride_axis=0) for i in range(count)]


def group_block(groups, columns=128):
    rows = jnp.concatenate([groups[b] for b in range(groups.shape[0])], axis=0)
    lines, lanes = rows.shape
    return jnp.pad(rows, ((0, GROUP_ROWS - lines), (0, columns - lanes)))


def target_rows(groups):
    me = lax.axis_index("inp")
    bits = RG_DEV.bit_length() - 1
    return (((groups >> bits) ^ me) << (bits + 2)) + ((groups & (RG_DEV - 1)) << 2)


def pick_matrix(entries, rows, repeat=1, sides=1):
    count = len(entries) // sides
    side = 3 * count * repeat
    shape = (rows, sides * side)
    row = lax.broadcasted_iota(jnp.int32, shape, 0)
    column = lax.broadcasted_iota(jnp.int32, shape, 1)
    entry = column // side * count + column % side % (count * repeat) // repeat
    pick = jnp.zeros(shape, jnp.float32)
    for j, (targets, line, lane, part, sign) in enumerate(entries):
        target = jnp.broadcast_to(targets[line : line + 1, lane : lane + 1] + part, shape)
        pick = jnp.where(jnp.logical_and(entry == j, row == target), sign, pick)
    return pick.astype(jnp.bfloat16)


def pick_matrices(groups, heads, blocks, out_rows, mine):
    own = target_rows(group_block(groups))
    others = [target_rows(head.astype(jnp.float32).astype(jnp.int32)) for head in heads]
    parts = [2 * mine, 2 * mine + 1]

    def pairs(b):
        order = [(level, a, p) for level in range(len(heads)) for a in range(blocks) for p in range(2)]
        forward = [(own, a * blocks + b, level + 1, parts[p], 1.0) for level, a, p in order]
        turned = [(others[level], b * blocks + a, level + 1, parts[p], 1.0) for level, a, p in order]
        return forward, turned

    forward, turned = zip(*[pairs(b) for b in range(blocks)])
    both_channels = [parts, [2 - 2 * mine, 3 - 2 * mine]]
    tiles = [
        (own, line, 0, part, 1.0)
        for channel in both_channels
        for line in range(blocks * blocks)
        for part in channel
    ]
    both = [entry for side in (forward, turned) for block in side for entry in block]
    signed = [entry[:4] + (-1.0 if i % 2 else 1.0,) for i, entry in enumerate(turned[-1])]
    return [
        pick_matrix(tiles, out_rows),
        pick_matrix(both, out_rows),
        pick_matrix(forward[-1] + turned[-1], out_rows),
        pick_matrix(forward[-1] + signed, out_rows, repeat=8, sides=2),
    ]


def group_sums(pick, lags):
    terms = split_rows(lags).astype(jnp.bfloat16)
    return jnp.dot(pick, terms, preferred_element_type=jnp.float32)


def columns(piece):
    spans, start = [], 0
    for _, first, last in piece:
        spans.append((start, start + last - first))
        start += last - first
    return spans


def piece_shape(piece, width, more):
    return jax.ShapeDtypeStruct((2 * width + more, columns(piece)[-1][1]), jnp.bfloat16)


def load_piece(piece, other, width, volts_ref, raw, in_sem):
    blocks = sorted({block for block, _, _ in piece})
    loads = []
    for i, block in enumerate(blocks):
        start = min(first for b, first, _ in piece if b == block)
        end = max(last for b, _, last in piece if b == block)
        for c in range(2):
            load = pltpu.make_async_copy(
                volts_ref.at[other, c, pl.ds(block * width, width), pl.ds(start, end - start)],
                raw.at[i, c, :, pl.ds(start, end - start)],
                in_sem.at[i, c],
            )
            load.start()
            loads.append((i, block, c, load))
    return loads


def order_piece(piece, loads, position, raw, out_ref):
    width = position.shape[1]
    orders = {
        block: order_matrix(position[block : block + 1, :]) for block in sorted({l[1] for l in loads})
    }
    for i, block, c, load in loads:
        load.wait()
        for (b, first, last), (start, end) in zip(piece, columns(piece)):
            if b == block:
                out_ref[c * width : (c + 1) * width, start:end] = jnp.dot(
                    orders[block], raw[i, c, :, first:last], preferred_element_type=jnp.float32
                ).astype(jnp.bfloat16)


def head_kernel(levels, piece, position_ref, volts_ref, group_ref, head_ref, *scratch):
    position, groups, small_sem, in_sem = scratch
    other = 1 - parity(lax.axis_index("inp"), levels)
    width = position.shape[1]
    ((block, first, last),) = piece
    smalls = [
        pltpu.make_async_copy(position_ref, position, small_sem.at[0]),
        pltpu.make_async_copy(group_ref, groups, small_sem.at[1]),
    ]
    loads = [
        pltpu.make_async_copy(
            volts_ref.at[other, c, pl.ds(block * width, width), pl.ds(first, last - first)],
            head_ref.at[pl.ds(c * width, width), :],
            in_sem.at[c],
        )
        for c in range(2)
    ]
    for copy in smalls + loads:
        copy.start()
    for copy in smalls:
        copy.wait()
    rows = group_block(groups[...], last - first)
    line = lax.broadcasted_iota(jnp.int32, rows.shape, 0)
    own_row = jnp.broadcast_to(position[block : block + 1, :], rows.shape)
    rows = jnp.where(line == groups.shape[0] ** 2, own_row, rows)
    head_ref[2 * width :, :] = rows.astype(jnp.float32).astype(jnp.bfloat16)
    for copy in loads:
        copy.wait()


def rest_kernel(levels, piece, position_ref, volts_ref, _, out_ref, position, raw, small_sem, in_sem):
    other = 1 - parity(lax.axis_index("inp"), levels)
    load_position = pltpu.make_async_copy(position_ref, position, small_sem)
    load_position.start()
    loads = load_piece(piece, other, position.shape[1], volts_ref, raw, in_sem)
    load_position.wait()
    order_piece(piece, loads, position, raw, out_ref)


def early_pieces(position_input, volts, groups, head, rest, levels):
    blocks, width = position_input.shape
    samples = volts.shape[3]
    assert columns(head)[-1][1] == width
    in_hbm = [pltpu.with_memory_space_constraint(x, pltpu.HBM) for x in (position_input, volts)]
    position = pltpu.VMEM(position_input.shape, jnp.int32)
    semaphore = pltpu.SemaphoreType.DMA
    sent = pl.pallas_call(
        functools.partial(head_kernel, levels, head),
        out_shape=piece_shape(head, width, GROUP_ROWS),
        in_specs=[HBM] * 3,
        out_specs=WHOLE,
        scratch_shapes=[
            position,
            pltpu.VMEM(groups.shape, jnp.int32),
            semaphore((2,)),
            semaphore((2,)),
        ],
        compiler_params=pltpu.CompilerParams(vmem_limit_bytes=8 << 20),
        cost_estimate=pl.CostEstimate(flops=0, bytes_accessed=1 << 20, transcendentals=0),
        name="first_piece",
    )(*in_hbm, pltpu.with_memory_space_constraint(groups, pltpu.HBM))
    second = pl.pallas_call(
        functools.partial(rest_kernel, levels, rest),
        out_shape=piece_shape(rest, width, 0),
        in_specs=[HBM, HBM, pl.BlockSpec(memory_space=pl.ANY)],
        out_specs=WHOLE,
        scratch_shapes=[
            position,
            pltpu.VMEM((blocks, 2, width, samples), jnp.bfloat16),
            semaphore(()),
            semaphore((blocks, 2)),
        ],
        compiler_params=pltpu.CompilerParams(vmem_limit_bytes=16 << 20),
        cost_estimate=pl.CostEstimate(
            flops=4 * width * width * columns(rest)[-1][1],
            bytes_accessed=4 << 20,
            transcendentals=0,
        ),
        name="second_piece",
    )(*in_hbm, sent)
    return sent, second


def own_kernel(levels, pieces, last, group_ref, position_ref, volts_ref, *refs):
    head_refs, refs = refs[:levels], refs[levels:]
    panel_ref, sums_ref, *refs, raw, other_panel, lags_ref, in_sem = refs
    pick_refs, ordered_refs, refs = refs[:3], refs[3 : 3 + levels], refs[3 + levels :]
    piece_refs, (last_ref, last_panel_ref) = refs[:-2], refs[-2:]
    blocks, _, width, _ = panel_ref.shape
    mine = parity(lax.axis_index("inp"), levels)
    channels = (mine, 1 - mine)
    loads = [
        [
            [
                pltpu.make_async_copy(
                    volts_ref.at[channels[f], c, pl.ds(b * width, width)],
                    raw.at[f, b, c],
                    in_sem.at[f, b, c],
                )
                for c in range(2)
            ]
            for b in range(blocks)
        ]
        for f in range(2)
    ]
    for f in range(2):
        for b in range(blocks):
            for c in range(2):
                loads[f][b][c].start()
    orders = [order_matrix(position_ref[b : b + 1, :]) for b in range(blocks)]
    for f, panel in enumerate((panel_ref, other_panel)):
        for b in range(blocks):
            for c in range(2):
                loads[f][b][c].wait()
                panel[b, c] = jnp.dot(
                    orders[b], raw[f, b, c], preferred_element_type=jnp.float32
                ).astype(jnp.bfloat16)

        def one_tile(index, carry, panel=panel, f=f):
            a = index // blocks
            b = index % blocks
            lags = tile_lags(panel[a, 0], panel[a, 1], panel[b, 0], panel[b, 1], panel.shape[3])
            center = lax.broadcasted_iota(jnp.int32, lags.shape, 1) == width - 1
            lags_ref[f * blocks * blocks + index] = jnp.where(
                jnp.logical_and(center, a == b), 0.0, lags
            )
            return carry

        lax.fori_loop(0, blocks * blocks, one_tile, 0)
    lags = jnp.concatenate([lags_ref[i] for i in range(2 * blocks * blocks)], axis=0)
    heads = [head_ref[2 * width :, :] for head_ref in head_refs]
    for head, head_ref, ordered_ref in zip(heads, head_refs, ordered_refs):
        positions = head.astype(jnp.float32).astype(jnp.int32)[blocks**2 : blocks**2 + 1]
        order = order_matrix(positions)
        for c in range(2):
            rows = head_ref[c * width : (c + 1) * width, :]
            rows = jnp.dot(order, rows, preferred_element_type=jnp.float32)
            ordered_ref[c * width : (c + 1) * width, :] = rows.astype(jnp.bfloat16)
    own_pick, *picks = pick_matrices(group_ref[...], heads, blocks, sums_ref.shape[0], mine)
    for pick_ref, pick in zip(pick_refs, picks):
        pick_ref[...] = pick
    sums_ref[...] = group_sums(own_pick, lags)
    for piece, piece_ref in zip(pieces, piece_refs):
        for (block, first, _), (start, end) in zip(piece, columns(piece)):
            for c in range(2):
                piece_ref[c * width : (c + 1) * width, start:end] = other_panel[
                    block, c, :, first:end - start + first
                ]
    block, first, end = last
    depth = end - first
    for c in range(2):
        last_ref[:, c * depth : (c + 1) * depth] = other_panel[block, c, :, first:end]
    turn = anti_identity(width)
    for a in range(blocks):
        real_part, imag_part = [
            jnp.dot(turn, panel_ref[a, c, :, first:end], preferred_element_type=jnp.float32)
            for c in range(2)
        ]
        last_panel_ref[a, :width, :depth] = real_part.astype(jnp.bfloat16)
        last_panel_ref[a, :width, depth:] = imag_part.astype(jnp.bfloat16)
        last_panel_ref[a, width:, :depth] = imag_part.astype(jnp.bfloat16)
        last_panel_ref[a, width:, depth:] = (-real_part).astype(jnp.bfloat16)


def own_level(groups, position_input, volts, heads, pieces, last, out_rows):
    levels = len(heads)
    blocks, width = position_input.shape
    samples = volts.shape[3]
    pairs = 4 * levels * blocks
    counts = (3 * pairs * blocks, 3 * pairs, 3 * pairs * 8)
    depth = last[2] - last[1]
    return pl.pallas_call(
        functools.partial(own_kernel, levels, pieces, last),
        out_shape=(
            jax.ShapeDtypeStruct((blocks, 2, width, samples), jnp.bfloat16),
            jax.ShapeDtypeStruct((out_rows, 2 * width), jnp.float32),
            *[jax.ShapeDtypeStruct((out_rows, n), jnp.bfloat16) for n in counts],
            *[jax.ShapeDtypeStruct((2 * width, head.shape[1]), jnp.bfloat16) for head in heads],
            *[piece_shape(piece, width, 0) for piece in pieces],
            jax.ShapeDtypeStruct((width, 2 * depth), jnp.bfloat16),
            jax.ShapeDtypeStruct((blocks, 2 * width, 2 * depth), jnp.bfloat16),
        ),
        in_specs=[WHOLE, WHOLE, HBM] + [WHOLE] * levels,
        out_specs=(WHOLE,) * (4 + len(counts) + levels + len(pieces)),
        scratch_shapes=[
            pltpu.VMEM((2, blocks, 2, width, samples), jnp.bfloat16),
            pltpu.VMEM((blocks, 2, width, samples), jnp.bfloat16),
            pltpu.VMEM((2 * blocks * blocks, 2, 2 * width), jnp.float32),
            pltpu.SemaphoreType.DMA((2, blocks, 2)),
        ],
        compiler_params=pltpu.CompilerParams(vmem_limit_bytes=16 << 20),
        cost_estimate=pl.CostEstimate(
            flops=64 * blocks * blocks * width * width * samples,
            bytes_accessed=12 * blocks * width * samples,
            transcendentals=0,
        ),
        name="own_level",
    )(groups, position_input, pltpu.with_memory_space_constraint(volts, pltpu.HBM), *heads)


def add_lags(rows, pick_ref, sums_ref):
    lags = jnp.concatenate(rows, axis=0)
    lags = jnp.concatenate([lags, conjugate_lags(lags)], axis=0)
    return sums_ref[...] + group_sums(pick_ref[...], lags)


def pair_kernel(levels, pieces, pick_ref, sums_ref, panel_ref, *refs):
    partner_refs, out_ref = refs[:-1], refs[-1]
    _, _, width, samples = panel_ref.shape
    rows = []
    for block in sorted({block for piece in pieces for block, _, _ in piece}):
        for level in range(levels):
            for a in range(panel_ref.shape[0]):
                real_part, imag_part = 0.0, 0.0
                for i, piece in enumerate(pieces):
                    partner = partner_refs[level * len(pieces) + i]
                    for (b, first, last), (start, end) in zip(piece, columns(piece)):
                        if b != block:
                            continue
                        x_re, x_im = panel_ref[a, 0, :, first:last], panel_ref[a, 1, :, first:last]
                        y_re = partner[:width, start:end]
                        y_im = partner[width : 2 * width, start:end]
                        real_part = real_part + (product(x_re, y_re) + product(x_im, y_im))
                        imag_part = imag_part + (product(x_im, y_re) - product(x_re, y_im))
                rows.append(lag_rows(jnp.stack([real_part, imag_part])) * (1.0 / samples))
    out_ref[...] = add_lags(rows, pick_ref, sums_ref)


def last_kernel(levels, samples, pick_ref, sums_ref, panel_ref, *refs):
    partner_refs, out_refs = refs[:levels], refs[levels:]
    blocks, rows_both, _ = panel_ref.shape
    width = rows_both // 2
    rows = []
    for partner_ref in partner_refs:
        for a in range(blocks):
            tiles = product(panel_ref[a], partner_ref[...]).reshape(2, width, width)
            rows += sheared_eights(tiles)
    terms = split_rows(jnp.concatenate(rows, axis=0) * (1.0 / samples))
    terms = jnp.concatenate([terms, turn_lags(terms)], axis=0).astype(jnp.bfloat16)
    sums = sums_ref[...] + jnp.dot(pick_ref[...], terms, preferred_element_type=jnp.float32)
    share = sums.shape[0] // len(out_refs)
    for place, out_ref in enumerate(out_refs):
        out_ref[...] = sums[place * share : (place + 1) * share]


def pair_call(kernel, inputs, work, out_shape):
    return pl.pallas_call(
        kernel,
        out_shape=out_shape,
        in_specs=[WHOLE] * len(inputs),
        out_specs=[WHOLE] * len(out_shape),
        compiler_params=pltpu.CompilerParams(vmem_limit_bytes=16 << 20),
        cost_estimate=pl.CostEstimate(flops=work, bytes_accessed=4 << 20, transcendentals=0),
        name="pair_level",
    )(*inputs)


def finish_kernel(*refs):
    part_refs, out_ref = refs[:-1], refs[-1]
    groups, channels, parts, lags = out_ref.shape
    total = part_refs[0][...]
    for part_ref in part_refs[1:]:
        total = total + part_ref[...]
    for g in range(groups):
        for f in range(channels):
            row = (g * channels + f) * parts
            out_ref[g, f] = total[row : row + parts, :lags]


def finish(parts, lags):
    return pl.pallas_call(
        finish_kernel,
        out_shape=jax.ShapeDtypeStruct((RG_DEV, 2, 2, lags), jnp.float32),
        in_specs=[WHOLE] * len(parts),
        out_specs=WHOLE,
        compiler_params=pltpu.CompilerParams(vmem_limit_bytes=8 << 20),
        name="finish",
    )(*parts)


def on_device(volts, position_input, tile_group):
    blocks, width = position_input.shape
    samples = volts.shape[3]
    devices = lax.axis_size("inp")
    levels = devices.bit_length() - 1
    out_rows = devices * RG_DEV * 4
    eighth = samples // 8
    head = [(0, 0, 2 * eighth)]
    rest = [(0, 2 * eighth, samples), (1, 0, 2 * eighth)]
    tail = [[(1, 2 * eighth, 6 * eighth)]]
    last = (1, 6 * eighth, samples)
    by_block = tile_group.transpose(0, 2, 1)
    partner_of = [functools.partial(xor_permute, axis="inp", distance=1 << l) for l in range(levels)]
    sent, second = early_pieces(position_input, volts, by_block, head, rest, levels)
    head_arrived = [send(sent) for send in partner_of]
    rest_arrived = [send(second) for send in partner_of]
    panel, sums, both, single, eights, *sent = own_level(
        by_block, position_input, volts, head_arrived, tail, last, out_rows
    )
    head_ordered, (*sent, last_panel) = sent[:levels], sent[levels:]
    tail_arrived = [[send(piece) for send in partner_of] for piece in sent]

    whole = jax.ShapeDtypeStruct(sums.shape, jnp.float32)
    share = jax.ShapeDtypeStruct((out_rows // devices, 2 * width), jnp.float32)
    flops = 8 * levels * blocks * width * width
    arrived = [piece for pair in zip(head_ordered, rest_arrived) for piece in pair]
    (sums,) = pair_call(
        functools.partial(pair_kernel, levels, [head, rest]),
        [both, sums, panel, *arrived],
        flops * 10 * eighth,
        [whole],
    )
    (sums,) = pair_call(
        functools.partial(pair_kernel, levels, tail),
        [single, sums, panel, *tail_arrived[0]],
        flops * 4 * eighth,
        [whole],
    )
    parts = pair_call(
        functools.partial(last_kernel, levels, samples),
        [eights, sums, last_panel, *tail_arrived[1]],
        flops * 2 * eighth,
        [share] * devices,
    )
    parts = [
        xor_permute(parts[distance], "inp", distance) for distance in reversed(range(1, devices))
    ] + [parts[0]]
    return finish(parts, 2 * width - 1)


def solution(mesh):
    return jax.shard_map(
        on_device,
        mesh=mesh,
        in_specs=(P("freq", None, "inp", None), P("inp", None), P("inp", None, None)),
        out_specs=P("inp", "freq", None, None),
        check_vma=False,
    )
```

```python
import functools

import jax
import jax.numpy as jnp
from jax import lax
from jax.experimental import pallas as pl
from jax.experimental.pallas import tpu as pltpu
from jax.sharding import PartitionSpec as P

RG_DEV = 8
GROUP_ROWS = 16
HBM = pl.BlockSpec(memory_space=pltpu.HBM)
WHOLE = pl.BlockSpec(memory_space=pltpu.VMEM)


def xor_permute(x, axis, distance):
    return lax.ppermute(x, axis, [(i, i ^ distance) for i in range(lax.axis_size(axis))])


def parity(index, levels):
    bits = index & 1
    for level in range(1, levels):
        bits = bits ^ ((index >> level) & 1)
    return bits


def order_matrix(position_row):
    width = position_row.shape[-1]
    by_position = jnp.transpose(jnp.broadcast_to(position_row, (width, width)))
    inputs = lax.broadcasted_iota(jnp.int32, (width, width), 1)
    return (by_position == inputs).astype(jnp.float32).astype(jnp.bfloat16)


def product(x, y):
    return lax.dot_general(x, y, (((1,), (1,)), ((), ())), preferred_element_type=jnp.float32)


def lag_rows(tiles):
    count, width, _ = tiles.shape
    half = width // 2
    low, high = tiles[:, :half], tiles[:, half:]
    sheared = jnp.concatenate(
        [
            high[:, :, :half],
            high[:, :, half:] + low[:, :, :half],
            low[:, :, half:],
            jnp.zeros((count, half, half), jnp.float32),
        ],
        axis=2,
    )
    rows = half
    while rows > 8:
        rows //= 2
        upper = sheared[:, :rows].reshape(count * rows, 2 * width)
        upper = pltpu.roll(upper, rows, 1).reshape(count, rows, 2 * width)
        sheared = upper + sheared[:, rows:]
    flat = sheared.reshape(count * rows, 2 * width)
    sublane = lax.broadcasted_iota(jnp.int32, flat.shape, 0) % 8
    while rows > 1:
        rows //= 2
        flat = jnp.where((sublane & rows) == 0, pltpu.roll(flat, rows, 1), flat)
    return jnp.sum(flat.reshape(count, 8, 2 * width), axis=1)


def tile_lags(x_re, x_im, y_re, y_im, samples):
    real_part = product(x_re, y_re) + product(x_im, y_im)
    imag_part = product(x_im, y_re) - product(x_re, y_im)
    return lag_rows(jnp.stack([real_part, imag_part])) * (1.0 / samples)


def split_rows(x):
    first = x.astype(jnp.bfloat16).astype(jnp.float32)
    rest = x - first
    second = rest.astype(jnp.bfloat16).astype(jnp.float32)
    return jnp.concatenate([first, second, rest - second], axis=0)


def anti_identity(size):
    place = lax.broadcasted_iota(jnp.int32, (size, size), 0) + lax.broadcasted_iota(
        jnp.int32, (size, size), 1
    )
    return (place == size - 1).astype(jnp.float32).astype(jnp.bfloat16)


def turn_lags(terms):
    count, width = terms.shape
    lanes = 128
    spans = range(0, width, lanes)
    terms = jnp.concatenate([terms[:, first : first + lanes] for first in spans], axis=0)
    terms = jnp.dot(
        terms.astype(jnp.bfloat16), anti_identity(lanes), preferred_element_type=jnp.float32
    )
    blocks = [terms[count * i : count * (i + 1)] for i in reversed(range(len(spans)))]
    return pltpu.roll(jnp.concatenate(blocks, axis=1), width - 1, 1)


def conjugate_lags(lags):
    count = lags.shape[0]
    turned = turn_lags(split_rows(lags))
    turned = turned[:count] + turned[count : 2 * count] + turned[2 * count :]
    odd = lax.broadcasted_iota(jnp.int32, turned.shape, 0) % 2 == 1
    return jnp.where(odd, -turned, turned)


def sheared_eights(tiles):
    count, width, _ = tiles.shape
    half = width // 2
    low, high = tiles[:, :half], tiles[:, half:]
    sheared = jnp.concatenate(
        [
            low[:, :, :half],
            low[:, :, half:] + high[:, :, :half],
            high[:, :, half:],
            jnp.zeros((count, half, half), jnp.float32),
        ],
        axis=2,
    )
    rows = half
    while rows > 8:
        rows //= 2
        lower = sheared[:, rows:].reshape(count * rows, 2 * width)
        lower = pltpu.roll(lower, rows, 1).reshape(count, rows, 2 * width)
        sheared = sheared[:, :rows] + lower
    return [pltpu.roll(sheared[i], 0, 1, stride=1, stride_axis=0) for i in range(count)]


def group_block(groups, columns=128):
    rows = jnp.concatenate([groups[b] for b in range(groups.shape[0])], axis=0)
    lines, lanes = rows.shape
    return jnp.pad(rows, ((0, GROUP_ROWS - lines), (0, columns - lanes)))


def target_rows(groups):
    return groups << 1


def pick_matrix(entries, rows, repeat=1, sides=1):
    count = len(entries) // sides
    side = 3 * count * repeat
    shape = (rows, sides * side)
    row = lax.broadcasted_iota(jnp.int32, shape, 0)
    column = lax.broadcasted_iota(jnp.int32, shape, 1)
    entry = column // side * count + column % side % (count * repeat) // repeat
    pick = jnp.zeros(shape, jnp.float32)
    for j, (targets, line, lane, part, sign) in enumerate(entries):
        target = jnp.broadcast_to(targets[line : line + 1, lane : lane + 1] + part, shape)
        pick = jnp.where(jnp.logical_and(entry == j, row == target), sign, pick)
    return pick.astype(jnp.bfloat16)


def pick_matrices(groups, heads, blocks, out_rows):
    own = target_rows(group_block(groups))
    others = [target_rows(head.astype(jnp.float32).astype(jnp.int32)) for head in heads]

    def pairs(b):
        order = [(level, a, p) for level in range(len(heads)) for a in range(blocks) for p in range(2)]
        forward = [(own, a * blocks + b, level + 1, p, 1.0) for level, a, p in order]
        turned = [(others[level], b * blocks + a, level + 1, p, 1.0) for level, a, p in order]
        return forward, turned

    forward, turned = zip(*[pairs(b) for b in range(blocks)])
    tiles = [
        [(targets, line, 0, p, 1.0) for line in range(blocks * blocks) for p in range(2)]
        for targets in (own, others[-1])
    ]
    both = [entry for side in (forward, turned) for block in side for entry in block]
    signed = [entry[:4] + (-1.0 if i % 2 else 1.0,) for i, entry in enumerate(turned[-1])]
    return [
        pick_matrix(tiles[0], out_rows),
        pick_matrix(tiles[1], out_rows),
        pick_matrix(both, out_rows),
        pick_matrix(forward[-1] + turned[-1], out_rows),
        pick_matrix(forward[-1] + signed, out_rows, repeat=8, sides=2),
    ]


def group_sums(pick, lags):
    terms = split_rows(lags).astype(jnp.bfloat16)
    return jnp.dot(pick, terms, preferred_element_type=jnp.float32)


def columns(piece):
    spans, start = [], 0
    for _, first, last in piece:
        spans.append((start, start + last - first))
        start += last - first
    return spans


def piece_shape(piece, width, more):
    return jax.ShapeDtypeStruct((2 * width + more, columns(piece)[-1][1]), jnp.bfloat16)


def load_piece(piece, other, width, volts_ref, raw, in_sem):
    blocks = sorted({block for block, _, _ in piece})
    loads = []
    for i, block in enumerate(blocks):
        start = min(first for b, first, _ in piece if b == block)
        end = max(last for b, _, last in piece if b == block)
        for c in range(2):
            load = pltpu.make_async_copy(
                volts_ref.at[other, c, pl.ds(block * width, width), pl.ds(start, end - start)],
                raw.at[i, c, :, pl.ds(start, end - start)],
                in_sem.at[i, c],
            )
            load.start()
            loads.append((i, block, c, load))
    return loads


def order_piece(piece, loads, position, raw, out_ref):
    width = position.shape[1]
    orders = {
        block: order_matrix(position[block : block + 1, :]) for block in sorted({l[1] for l in loads})
    }
    for i, block, c, load in loads:
        load.wait()
        for (b, first, last), (start, end) in zip(piece, columns(piece)):
            if b == block:
                out_ref[c * width : (c + 1) * width, start:end] = jnp.dot(
                    orders[block], raw[i, c, :, first:last], preferred_element_type=jnp.float32
                ).astype(jnp.bfloat16)


def head_kernel(levels, piece, position_ref, volts_ref, group_ref, head_ref, *scratch):
    position, groups, small_sem, in_sem = scratch
    other = 1 - parity(lax.axis_index("inp"), levels)
    width = position.shape[1]
    ((block, first, last),) = piece
    smalls = [
        pltpu.make_async_copy(position_ref, position, small_sem.at[0]),
        pltpu.make_async_copy(group_ref, groups, small_sem.at[1]),
    ]
    loads = [
        pltpu.make_async_copy(
            volts_ref.at[other, c, pl.ds(block * width, width), pl.ds(first, last - first)],
            head_ref.at[pl.ds(c * width, width), :],
            in_sem.at[c],
        )
        for c in range(2)
    ]
    for copy in smalls + loads:
        copy.start()
    for copy in smalls:
        copy.wait()
    rows = group_block(groups[...], last - first)
    line = lax.broadcasted_iota(jnp.int32, rows.shape, 0)
    own_row = jnp.broadcast_to(position[block : block + 1, :], rows.shape)
    rows = jnp.where(line == groups.shape[0] ** 2, own_row, rows)
    head_ref[2 * width :, :] = rows.astype(jnp.float32).astype(jnp.bfloat16)
    for copy in loads:
        copy.wait()


def rest_kernel(levels, piece, position_ref, volts_ref, _, out_ref, position, raw, small_sem, in_sem):
    other = 1 - parity(lax.axis_index("inp"), levels)
    load_position = pltpu.make_async_copy(position_ref, position, small_sem)
    load_position.start()
    loads = load_piece(piece, other, position.shape[1], volts_ref, raw, in_sem)
    load_position.wait()
    order_piece(piece, loads, position, raw, out_ref)


def early_pieces(position_input, volts, groups, head, rest, levels):
    blocks, width = position_input.shape
    samples = volts.shape[3]
    assert columns(head)[-1][1] == width
    in_hbm = [pltpu.with_memory_space_constraint(x, pltpu.HBM) for x in (position_input, volts)]
    position = pltpu.VMEM(position_input.shape, jnp.int32)
    semaphore = pltpu.SemaphoreType.DMA
    sent = pl.pallas_call(
        functools.partial(head_kernel, levels, head),
        out_shape=piece_shape(head, width, GROUP_ROWS),
        in_specs=[HBM] * 3,
        out_specs=WHOLE,
        scratch_shapes=[
            position,
            pltpu.VMEM(groups.shape, jnp.int32),
            semaphore((2,)),
            semaphore((2,)),
        ],
        compiler_params=pltpu.CompilerParams(vmem_limit_bytes=8 << 20),
        cost_estimate=pl.CostEstimate(flops=0, bytes_accessed=1 << 20, transcendentals=0),
        name="first_piece",
    )(*in_hbm, pltpu.with_memory_space_constraint(groups, pltpu.HBM))
    second = pl.pallas_call(
        functools.partial(rest_kernel, levels, rest),
        out_shape=piece_shape(rest, width, 0),
        in_specs=[HBM, HBM, pl.BlockSpec(memory_space=pl.ANY)],
        out_specs=WHOLE,
        scratch_shapes=[
            position,
            pltpu.VMEM((blocks, 2, width, samples), jnp.bfloat16),
            semaphore(()),
            semaphore((blocks, 2)),
        ],
        compiler_params=pltpu.CompilerParams(vmem_limit_bytes=16 << 20),
        cost_estimate=pl.CostEstimate(
            flops=4 * width * width * columns(rest)[-1][1],
            bytes_accessed=4 << 20,
            transcendentals=0,
        ),
        name="second_piece",
    )(*in_hbm, sent)
    return sent, second


def own_kernel(levels, piece, last, group_ref, position_ref, volts_ref, *refs):
    head_refs, refs = refs[:levels], refs[levels:]
    panel_ref, sums_ref, *refs, raw, other_panel, lags_ref, in_sem = refs
    pick_refs, ordered_refs, refs = refs[:4], refs[4 : 4 + levels], refs[4 + levels :]
    more_ref, piece_ref, last_ref, last_panel_ref = refs
    blocks, _, width, _ = panel_ref.shape
    mine = parity(lax.axis_index("inp"), levels)
    channels = (mine, 1 - mine)
    loads = [
        [
            [
                pltpu.make_async_copy(
                    volts_ref.at[channels[f], c, pl.ds(b * width, width)],
                    raw.at[f, b, c],
                    in_sem.at[f, b, c],
                )
                for c in range(2)
            ]
            for b in range(blocks)
        ]
        for f in range(2)
    ]
    for f in range(2):
        for b in range(blocks):
            for c in range(2):
                loads[f][b][c].start()
    orders = [order_matrix(position_ref[b : b + 1, :]) for b in range(blocks)]
    for f, panel in enumerate((panel_ref, other_panel)):
        for b in range(blocks):
            for c in range(2):
                loads[f][b][c].wait()
                panel[b, c] = jnp.dot(
                    orders[b], raw[f, b, c], preferred_element_type=jnp.float32
                ).astype(jnp.bfloat16)

        def one_tile(index, carry, panel=panel, f=f):
            a = index // blocks
            b = index % blocks
            lags = tile_lags(panel[a, 0], panel[a, 1], panel[b, 0], panel[b, 1], panel.shape[3])
            center = lax.broadcasted_iota(jnp.int32, lags.shape, 1) == width - 1
            lags_ref[f * blocks * blocks + index] = jnp.where(
                jnp.logical_and(center, a == b), 0.0, lags
            )
            return carry

        lax.fori_loop(0, blocks * blocks, one_tile, 0)
    tiles = blocks * blocks
    lags = jnp.concatenate([lags_ref[i] for i in range(tiles)], axis=0)
    heads = [head_ref[2 * width :, :] for head_ref in head_refs]
    for head, head_ref, ordered_ref in zip(heads, head_refs, ordered_refs):
        positions = head.astype(jnp.float32).astype(jnp.int32)[blocks**2 : blocks**2 + 1]
        order = order_matrix(positions)
        for c in range(2):
            rows = head_ref[c * width : (c + 1) * width, :]
            rows = jnp.dot(order, rows, preferred_element_type=jnp.float32)
            ordered_ref[c * width : (c + 1) * width, :] = rows.astype(jnp.bfloat16)
    own_pick, *picks = pick_matrices(group_ref[...], heads, blocks, sums_ref.shape[0])
    for pick_ref, pick in zip(pick_refs, picks):
        pick_ref[...] = pick
    sums_ref[...] = group_sums(own_pick, lags)
    for (block, first, end), (start, stop) in zip(piece, columns(piece)):
        for c in range(2):
            rows = other_panel[block, c, :, first:end]
            piece_ref[c * width : (c + 1) * width, start:stop] = rows
            more_ref[c * width : (c + 1) * width, start:stop] = rows
    lags = jnp.concatenate([lags_ref[tiles + i] for i in range(tiles)], axis=0)
    high = lags.astype(jnp.bfloat16).astype(jnp.float32)
    terms = jnp.concatenate([high, lags - high], axis=0)
    more_ref[2 * width :, :] = terms.astype(jnp.bfloat16)
    block, first, end = last
    depth = end - first
    for c in range(2):
        last_ref[:, c * depth : (c + 1) * depth] = other_panel[block, c, :, first:end]
    turn = anti_identity(width)
    for a in range(blocks):
        real_part, imag_part = [
            jnp.dot(turn, panel_ref[a, c, :, first:end], preferred_element_type=jnp.float32)
            for c in range(2)
        ]
        last_panel_ref[a, :width, :depth] = real_part.astype(jnp.bfloat16)
        last_panel_ref[a, :width, depth:] = imag_part.astype(jnp.bfloat16)
        last_panel_ref[a, width:, :depth] = imag_part.astype(jnp.bfloat16)
        last_panel_ref[a, width:, depth:] = (-real_part).astype(jnp.bfloat16)


def own_level(groups, position_input, volts, heads, piece, last, out_rows):
    levels = len(heads)
    blocks, width = position_input.shape
    samples = volts.shape[3]
    pairs = 4 * levels * blocks
    tiles = 2 * blocks * blocks
    counts = (3 * tiles, 3 * pairs * blocks, 3 * pairs, 3 * pairs * 8)
    depth = last[2] - last[1]
    return pl.pallas_call(
        functools.partial(own_kernel, levels, piece, last),
        out_shape=(
            jax.ShapeDtypeStruct((blocks, 2, width, samples), jnp.bfloat16),
            jax.ShapeDtypeStruct((out_rows, 2 * width), jnp.float32),
            *[jax.ShapeDtypeStruct((out_rows, n), jnp.bfloat16) for n in counts],
            *[jax.ShapeDtypeStruct((2 * width, head.shape[1]), jnp.bfloat16) for head in heads],
            piece_shape(piece, width, 2 * tiles),
            piece_shape(piece, width, 0),
            jax.ShapeDtypeStruct((width, 2 * depth), jnp.bfloat16),
            jax.ShapeDtypeStruct((blocks, 2 * width, 2 * depth), jnp.bfloat16),
        ),
        in_specs=[WHOLE, WHOLE, HBM] + [WHOLE] * levels,
        out_specs=(WHOLE,) * (6 + len(counts) + levels),
        scratch_shapes=[
            pltpu.VMEM((2, blocks, 2, width, samples), jnp.bfloat16),
            pltpu.VMEM((blocks, 2, width, samples), jnp.bfloat16),
            pltpu.VMEM((2 * blocks * blocks, 2, 2 * width), jnp.float32),
            pltpu.SemaphoreType.DMA((2, blocks, 2)),
        ],
        compiler_params=pltpu.CompilerParams(vmem_limit_bytes=16 << 20),
        cost_estimate=pl.CostEstimate(
            flops=64 * blocks * blocks * width * width * samples,
            bytes_accessed=12 * blocks * width * samples,
            transcendentals=0,
        ),
        name="own_level",
    )(groups, position_input, pltpu.with_memory_space_constraint(volts, pltpu.HBM), *heads)


def add_lags(rows, pick_ref, sums_ref):
    lags = jnp.concatenate(rows, axis=0)
    lags = jnp.concatenate([lags, conjugate_lags(lags)], axis=0)
    return sums_ref[...] + group_sums(pick_ref[...], lags)


def pair_kernel(levels, pieces, pick_ref, sums_ref, panel_ref, *refs):
    count = levels * len(pieces)
    partner_refs, more_refs, out_ref = refs[:count], refs[count:-1], refs[-1]
    _, _, width, samples = panel_ref.shape
    rows = []
    for block in sorted({block for piece in pieces for block, _, _ in piece}):
        for level in range(levels):
            for a in range(panel_ref.shape[0]):
                real_part, imag_part = 0.0, 0.0
                for i, piece in enumerate(pieces):
                    partner = partner_refs[level * len(pieces) + i]
                    for (b, first, last), (start, end) in zip(piece, columns(piece)):
                        if b != block:
                            continue
                        x_re, x_im = panel_ref[a, 0, :, first:last], panel_ref[a, 1, :, first:last]
                        y_re = partner[:width, start:end]
                        y_im = partner[width : 2 * width, start:end]
                        real_part = real_part + (product(x_re, y_re) + product(x_im, y_im))
                        imag_part = imag_part + (product(x_im, y_re) - product(x_re, y_im))
                rows.append(lag_rows(jnp.stack([real_part, imag_part])) * (1.0 / samples))
    sums = add_lags(rows, pick_ref, sums_ref)
    for more_ref in more_refs:
        terms = partner_refs[-1][2 * width :, :].astype(jnp.float32)
        half = terms.shape[0] // 2
        sums = sums + group_sums(more_ref[...], terms[:half] + terms[half:])
    out_ref[...] = sums


def last_kernel(levels, samples, pick_ref, sums_ref, panel_ref, *refs):
    partner_refs, out_ref = refs[:-1], refs[-1]
    blocks, rows_both, _ = panel_ref.shape
    width = rows_both // 2
    rows = []
    for partner_ref in partner_refs:
        for a in range(blocks):
            tiles = product(panel_ref[a], partner_ref[...]).reshape(2, width, width)
            rows += sheared_eights(tiles)
    terms = split_rows(jnp.concatenate(rows, axis=0) * (1.0 / samples))
    terms = jnp.concatenate([terms, turn_lags(terms)], axis=0).astype(jnp.bfloat16)
    out_ref[...] = sums_ref[...] + jnp.dot(
        pick_ref[...], terms, preferred_element_type=jnp.float32
    )


def pair_call(kernel, inputs, work):
    return pl.pallas_call(
        kernel,
        out_shape=jax.ShapeDtypeStruct(inputs[1].shape, jnp.float32),
        in_specs=[WHOLE] * len(inputs),
        out_specs=WHOLE,
        compiler_params=pltpu.CompilerParams(vmem_limit_bytes=16 << 20),
        cost_estimate=pl.CostEstimate(flops=work, bytes_accessed=4 << 20, transcendentals=0),
        name="pair_level",
    )(*inputs)


def finish_kernel(part_ref, out_ref):
    groups, channels, parts, lags = out_ref.shape
    sums = [None] * channels
    for device in range(part_ref.shape[0]):
        f = device.bit_count() % 2
        sums[f] = part_ref[device] if sums[f] is None else sums[f] + part_ref[device]
    for f in range(channels):
        for g in range(groups):
            out_ref[g, f] = sums[f][g * parts : (g + 1) * parts, :lags]


def finish(parts, lags):
    return pl.pallas_call(
        finish_kernel,
        out_shape=jax.ShapeDtypeStruct((RG_DEV, 2, 2, lags), jnp.float32),
        in_specs=[WHOLE],
        out_specs=WHOLE,
        compiler_params=pltpu.CompilerParams(vmem_limit_bytes=8 << 20),
        name="finish",
    )(parts)


def on_device(volts, position_input, tile_group):
    blocks, width = position_input.shape
    samples = volts.shape[3]
    devices = lax.axis_size("inp")
    levels = devices.bit_length() - 1
    out_rows = devices * RG_DEV * 2
    eighth = samples // 8
    head = [(0, 0, 2 * eighth)]
    rest = [(0, 2 * eighth, samples), (1, 0, 2 * eighth)]
    tail = [(1, 2 * eighth, 6 * eighth)]
    last = (1, 6 * eighth, samples)
    by_block = tile_group.transpose(0, 2, 1)
    partner_of = [functools.partial(xor_permute, axis="inp", distance=1 << l) for l in range(levels)]
    sent, second = early_pieces(position_input, volts, by_block, head, rest, levels)
    head_arrived = [send(sent) for send in partner_of]
    rest_arrived = [send(second) for send in partner_of]
    panel, sums, neighbour, both, single, eights, *sent = own_level(
        by_block, position_input, volts, head_arrived, tail, last, out_rows
    )
    head_ordered, (more, piece, last_piece, last_panel) = sent[:levels], sent[levels:]
    tail_arrived = [send(piece) for send in partner_of[:-1]] + [partner_of[-1](more)]
    last_arrived = [send(last_piece) for send in partner_of]

    flops = 8 * levels * blocks * width * width
    arrived = [piece for pair in zip(head_ordered, rest_arrived) for piece in pair]
    sums = pair_call(
        functools.partial(pair_kernel, levels, [head, rest]),
        [both, sums, panel, *arrived],
        flops * 10 * eighth,
    )
    sums = pair_call(
        functools.partial(pair_kernel, levels, [tail]),
        [single, sums, panel, *tail_arrived, neighbour],
        flops * 4 * eighth,
    )
    sums = pair_call(
        functools.partial(last_kernel, levels, samples),
        [eights, sums, last_panel, *last_arrived],
        flops * 2 * eighth,
    )
    parts = sums.reshape(devices, -1, 2 * width)
    return finish(lax.all_to_all(parts, "inp", 0, 0), 2 * width - 1)


def solution(mesh):
    return jax.shard_map(
        on_device,
        mesh=mesh,
        in_specs=(P("freq", None, "inp", None), P("inp", None), P("inp", None, None)),
        out_specs=P("inp", "freq", None, None),
        check_vma=False,
    )
```

```python
import functools

import jax
import jax.numpy as jnp
from jax import lax
from jax.experimental import pallas as pl
from jax.experimental.pallas import tpu as pltpu
from jax.sharding import PartitionSpec as P

RG_DEV = 8
GROUP_ROWS = 16
HBM = pl.BlockSpec(memory_space=pltpu.HBM)
WHOLE = pl.BlockSpec(memory_space=pltpu.VMEM)


def xor_permute(x, axis, distance):
    return lax.ppermute(x, axis, [(i, i ^ distance) for i in range(lax.axis_size(axis))])


def parity(index, levels):
    bits = index & 1
    for level in range(1, levels):
        bits = bits ^ ((index >> level) & 1)
    return bits


def order_matrix(position_row):
    width = position_row.shape[-1]
    by_position = jnp.transpose(jnp.broadcast_to(position_row, (width, width)))
    inputs = lax.broadcasted_iota(jnp.int32, (width, width), 1)
    return (by_position == inputs).astype(jnp.float32).astype(jnp.bfloat16)


def product(x, y):
    return lax.dot_general(x, y, (((1,), (1,)), ((), ())), preferred_element_type=jnp.float32)


def lag_rows(tiles):
    count, width, _ = tiles.shape
    half = width // 2
    low, high = tiles[:, :half], tiles[:, half:]
    sheared = jnp.concatenate(
        [
            high[:, :, :half],
            high[:, :, half:] + low[:, :, :half],
            low[:, :, half:],
            jnp.zeros((count, half, half), jnp.float32),
        ],
        axis=2,
    )
    rows = half
    while rows > 8:
        rows //= 2
        upper = sheared[:, :rows].reshape(count * rows, 2 * width)
        upper = pltpu.roll(upper, rows, 1).reshape(count, rows, 2 * width)
        sheared = upper + sheared[:, rows:]
    flat = sheared.reshape(count * rows, 2 * width)
    sublane = lax.broadcasted_iota(jnp.int32, flat.shape, 0) % 8
    while rows > 1:
        rows //= 2
        flat = jnp.where((sublane & rows) == 0, pltpu.roll(flat, rows, 1), flat)
    return jnp.sum(flat.reshape(count, 8, 2 * width), axis=1)


def tile_lags(x_re, x_im, y_re, y_im, samples):
    real_part = product(x_re, y_re) + product(x_im, y_im)
    imag_part = product(x_im, y_re) - product(x_re, y_im)
    return lag_rows(jnp.stack([real_part, imag_part])) * (1.0 / samples)


def split_rows(x):
    first = x.astype(jnp.bfloat16).astype(jnp.float32)
    rest = x - first
    second = rest.astype(jnp.bfloat16).astype(jnp.float32)
    return jnp.concatenate([first, second, rest - second], axis=0)


def anti_identity(size):
    place = lax.broadcasted_iota(jnp.int32, (size, size), 0) + lax.broadcasted_iota(
        jnp.int32, (size, size), 1
    )
    return (place == size - 1).astype(jnp.float32).astype(jnp.bfloat16)


def turn_lags(terms):
    count, width = terms.shape
    lanes = 128
    spans = range(0, width, lanes)
    terms = jnp.concatenate([terms[:, first : first + lanes] for first in spans], axis=0)
    terms = jnp.dot(
        terms.astype(jnp.bfloat16), anti_identity(lanes), preferred_element_type=jnp.float32
    )
    blocks = [terms[count * i : count * (i + 1)] for i in reversed(range(len(spans)))]
    return pltpu.roll(jnp.concatenate(blocks, axis=1), width - 1, 1)


def conjugate_lags(lags):
    count = lags.shape[0]
    turned = turn_lags(split_rows(lags))
    turned = turned[:count] + turned[count : 2 * count] + turned[2 * count :]
    odd = lax.broadcasted_iota(jnp.int32, turned.shape, 0) % 2 == 1
    return jnp.where(odd, -turned, turned)


def sheared_eights(tiles):
    count, width, _ = tiles.shape
    half = width // 2
    low, high = tiles[:, :half], tiles[:, half:]
    sheared = jnp.concatenate(
        [
            low[:, :, :half],
            low[:, :, half:] + high[:, :, :half],
            high[:, :, half:],
            jnp.zeros((count, half, half), jnp.float32),
        ],
        axis=2,
    )
    rows = half
    while rows > 8:
        rows //= 2
        lower = sheared[:, rows:].reshape(count * rows, 2 * width)
        lower = pltpu.roll(lower, rows, 1).reshape(count, rows, 2 * width)
        sheared = sheared[:, :rows] + lower
    return [pltpu.roll(sheared[i], 0, 1, stride=1, stride_axis=0) for i in range(count)]


def group_block(groups, columns=128):
    rows = jnp.concatenate([groups[b] for b in range(groups.shape[0])], axis=0)
    lines, lanes = rows.shape
    return jnp.pad(rows, ((0, GROUP_ROWS - lines), (0, columns - lanes)))


def target_rows(groups):
    me = lax.axis_index("inp")
    bits = RG_DEV.bit_length() - 1
    return (((groups >> bits) ^ me) << (bits + 1)) + ((groups & (RG_DEV - 1)) << 1)


def pick_matrix(entries, rows, repeat=1, sides=1):
    count = len(entries) // sides
    side = 3 * count * repeat
    shape = (rows, sides * side)
    row = lax.broadcasted_iota(jnp.int32, shape, 0)
    column = lax.broadcasted_iota(jnp.int32, shape, 1)
    entry = column // side * count + column % side % (count * repeat) // repeat
    pick = jnp.zeros(shape, jnp.float32)
    for j, (targets, line, lane, part, sign) in enumerate(entries):
        target = jnp.broadcast_to(targets[line : line + 1, lane : lane + 1] + part, shape)
        pick = jnp.where(jnp.logical_and(entry == j, row == target), sign, pick)
    return pick.astype(jnp.bfloat16)


def pick_matrices(groups, heads, blocks, out_rows):
    own = target_rows(group_block(groups))
    others = [target_rows(head.astype(jnp.float32).astype(jnp.int32)) for head in heads]

    def pairs(b):
        order = [(level, a, p) for level in range(len(heads)) for a in range(blocks) for p in range(2)]
        forward = [(own, a * blocks + b, level + 1, p, 1.0) for level, a, p in order]
        turned = [(others[level], b * blocks + a, level + 1, p, 1.0) for level, a, p in order]
        return forward, turned

    forward, turned = zip(*[pairs(b) for b in range(blocks)])
    tiles = [
        [(targets, line, 0, p, 1.0) for line in range(blocks * blocks) for p in range(2)]
        for targets in (own, others[-1])
    ]
    both = [entry for side in (forward, turned) for block in side for entry in block]
    signed = [entry[:4] + (-1.0 if i % 2 else 1.0,) for i, entry in enumerate(turned[-1])]
    by_tile = [forward[-1][i : i + 2] + signed[i : i + 2] for i in range(0, len(signed), 2)]
    return [
        pick_matrix(tiles[0], out_rows),
        pick_matrix(tiles[1], out_rows),
        pick_matrix(both, out_rows),
        pick_matrix(forward[-1] + turned[-1], out_rows),
        jnp.stack([pick_matrix(entries, out_rows, repeat=8, sides=2) for entries in by_tile]),
    ]


def group_sums(pick, lags):
    terms = split_rows(lags).astype(jnp.bfloat16)
    return jnp.dot(pick, terms, preferred_element_type=jnp.float32)


def columns(piece):
    spans, start = [], 0
    for _, first, last in piece:
        spans.append((start, start + last - first))
        start += last - first
    return spans


def piece_shape(piece, width, more):
    return jax.ShapeDtypeStruct((2 * width + more, columns(piece)[-1][1]), jnp.bfloat16)


def load_piece(piece, other, width, volts_ref, raw, in_sem):
    blocks = sorted({block for block, _, _ in piece})
    loads = []
    for i, block in enumerate(blocks):
        start = min(first for b, first, _ in piece if b == block)
        end = max(last for b, _, last in piece if b == block)
        for c in range(2):
            load = pltpu.make_async_copy(
                volts_ref.at[other, c, pl.ds(block * width, width), pl.ds(start, end - start)],
                raw.at[i, c, :, pl.ds(start, end - start)],
                in_sem.at[i, c],
            )
            load.start()
            loads.append((i, block, c, load))
    return loads


def order_piece(piece, loads, position, raw, out_ref):
    width = position.shape[1]
    orders = {
        block: order_matrix(position[block : block + 1, :]) for block in sorted({l[1] for l in loads})
    }
    for i, block, c, load in loads:
        load.wait()
        for (b, first, last), (start, end) in zip(piece, columns(piece)):
            if b == block:
                out_ref[c * width : (c + 1) * width, start:end] = jnp.dot(
                    orders[block], raw[i, c, :, first:last], preferred_element_type=jnp.float32
                ).astype(jnp.bfloat16)


def head_kernel(levels, piece, position_ref, volts_ref, group_ref, head_ref, *scratch):
    position, groups, small_sem, in_sem = scratch
    other = 1 - parity(lax.axis_index("inp"), levels)
    width = position.shape[1]
    ((block, first, last),) = piece
    smalls = [
        pltpu.make_async_copy(position_ref, position, small_sem.at[0]),
        pltpu.make_async_copy(group_ref, groups, small_sem.at[1]),
    ]
    loads = [
        pltpu.make_async_copy(
            volts_ref.at[other, c, pl.ds(block * width, width), pl.ds(first, last - first)],
            head_ref.at[pl.ds(c * width, width), :],
            in_sem.at[c],
        )
        for c in range(2)
    ]
    for copy in smalls + loads:
        copy.start()
    for copy in smalls:
        copy.wait()
    rows = group_block(groups[...], last - first)
    line = lax.broadcasted_iota(jnp.int32, rows.shape, 0)
    own_row = jnp.broadcast_to(position[block : block + 1, :], rows.shape)
    rows = jnp.where(line == groups.shape[0] ** 2, own_row, rows)
    head_ref[2 * width :, :] = rows.astype(jnp.float32).astype(jnp.bfloat16)
    for copy in loads:
        copy.wait()


def rest_kernel(levels, piece, position_ref, volts_ref, _, out_ref, position, raw, small_sem, in_sem):
    other = 1 - parity(lax.axis_index("inp"), levels)
    load_position = pltpu.make_async_copy(position_ref, position, small_sem)
    load_position.start()
    loads = load_piece(piece, other, position.shape[1], volts_ref, raw, in_sem)
    load_position.wait()
    order_piece(piece, loads, position, raw, out_ref)


def early_pieces(position_input, volts, groups, head, rest, levels):
    blocks, width = position_input.shape
    samples = volts.shape[3]
    assert columns(head)[-1][1] == width
    in_hbm = [pltpu.with_memory_space_constraint(x, pltpu.HBM) for x in (position_input, volts)]
    position = pltpu.VMEM(position_input.shape, jnp.int32)
    semaphore = pltpu.SemaphoreType.DMA
    sent = pl.pallas_call(
        functools.partial(head_kernel, levels, head),
        out_shape=piece_shape(head, width, GROUP_ROWS),
        in_specs=[HBM] * 3,
        out_specs=WHOLE,
        scratch_shapes=[
            position,
            pltpu.VMEM(groups.shape, jnp.int32),
            semaphore((2,)),
            semaphore((2,)),
        ],
        compiler_params=pltpu.CompilerParams(vmem_limit_bytes=8 << 20),
        cost_estimate=pl.CostEstimate(flops=0, bytes_accessed=1 << 20, transcendentals=0),
        name="first_piece",
    )(*in_hbm, pltpu.with_memory_space_constraint(groups, pltpu.HBM))
    second = pl.pallas_call(
        functools.partial(rest_kernel, levels, rest),
        out_shape=piece_shape(rest, width, 0),
        in_specs=[HBM, HBM, pl.BlockSpec(memory_space=pl.ANY)],
        out_specs=WHOLE,
        scratch_shapes=[
            position,
            pltpu.VMEM((blocks, 2, width, samples), jnp.bfloat16),
            semaphore(()),
            semaphore((blocks, 2)),
        ],
        compiler_params=pltpu.CompilerParams(vmem_limit_bytes=16 << 20),
        cost_estimate=pl.CostEstimate(
            flops=4 * width * width * columns(rest)[-1][1],
            bytes_accessed=4 << 20,
            transcendentals=0,
        ),
        name="second_piece",
    )(*in_hbm, sent)
    return sent, second


def own_kernel(levels, piece, last, group_ref, position_ref, volts_ref, *refs):
    head_refs, refs = refs[:levels], refs[levels:]
    panel_ref, sums_ref, *refs, raw, other_panel, lags_ref, in_sem = refs
    pick_refs, ordered_refs, refs = refs[:4], refs[4 : 4 + levels], refs[4 + levels :]
    more_ref, piece_ref, last_ref, last_panel_ref = refs
    blocks, _, width, _ = panel_ref.shape
    mine = parity(lax.axis_index("inp"), levels)
    channels = (mine, 1 - mine)
    loads = [
        [
            [
                pltpu.make_async_copy(
                    volts_ref.at[channels[f], c, pl.ds(b * width, width)],
                    raw.at[f, b, c],
                    in_sem.at[f, b, c],
                )
                for c in range(2)
            ]
            for b in range(blocks)
        ]
        for f in range(2)
    ]
    for f in range(2):
        for b in range(blocks):
            for c in range(2):
                loads[f][b][c].start()
    orders = [order_matrix(position_ref[b : b + 1, :]) for b in range(blocks)]
    for f, panel in enumerate((panel_ref, other_panel)):
        for b in range(blocks):
            for c in range(2):
                loads[f][b][c].wait()
                panel[b, c] = jnp.dot(
                    orders[b], raw[f, b, c], preferred_element_type=jnp.float32
                ).astype(jnp.bfloat16)

        def one_tile(index, carry, panel=panel, f=f):
            a = index // blocks
            b = index % blocks
            lags = tile_lags(panel[a, 0], panel[a, 1], panel[b, 0], panel[b, 1], panel.shape[3])
            center = lax.broadcasted_iota(jnp.int32, lags.shape, 1) == width - 1
            lags_ref[f * blocks * blocks + index] = jnp.where(
                jnp.logical_and(center, a == b), 0.0, lags
            )
            return carry

        lax.fori_loop(0, blocks * blocks, one_tile, 0)
    tiles = blocks * blocks
    lags = jnp.concatenate([lags_ref[i] for i in range(tiles)], axis=0)
    heads = [head_ref[2 * width :, :] for head_ref in head_refs]
    for head, head_ref, ordered_ref in zip(heads, head_refs, ordered_refs):
        positions = head.astype(jnp.float32).astype(jnp.int32)[blocks**2 : blocks**2 + 1]
        order = order_matrix(positions)
        for c in range(2):
            rows = head_ref[c * width : (c + 1) * width, :]
            rows = jnp.dot(order, rows, preferred_element_type=jnp.float32)
            ordered_ref[c * width : (c + 1) * width, :] = rows.astype(jnp.bfloat16)
    own_pick, *picks = pick_matrices(group_ref[...], heads, blocks, sums_ref.shape[0])
    for pick_ref, pick in zip(pick_refs, picks):
        pick_ref[...] = pick
    sums_ref[...] = group_sums(own_pick, lags)
    for (block, first, end), (start, stop) in zip(piece, columns(piece)):
        for c in range(2):
            rows = other_panel[block, c, :, first:end]
            piece_ref[c * width : (c + 1) * width, start:stop] = rows
            more_ref[c * width : (c + 1) * width, start:stop] = rows
    lags = jnp.concatenate([lags_ref[tiles + i] for i in range(tiles)], axis=0)
    high = lags.astype(jnp.bfloat16).astype(jnp.float32)
    terms = jnp.concatenate([high, lags - high], axis=0)
    more_ref[2 * width :, :] = terms.astype(jnp.bfloat16)
    block, first, end = last
    depth = end - first
    for c in range(2):
        last_ref[:, c * depth : (c + 1) * depth] = other_panel[block, c, :, first:end]
    turn = anti_identity(width)
    for a in range(blocks):
        real_part, imag_part = [
            jnp.dot(turn, panel_ref[a, c, :, first:end], preferred_element_type=jnp.float32)
            for c in range(2)
        ]
        last_panel_ref[a, :width, :depth] = real_part.astype(jnp.bfloat16)
        last_panel_ref[a, :width, depth:] = imag_part.astype(jnp.bfloat16)
        last_panel_ref[a, width:, :depth] = imag_part.astype(jnp.bfloat16)
        last_panel_ref[a, width:, depth:] = (-real_part).astype(jnp.bfloat16)


def own_level(groups, position_input, volts, heads, piece, last, out_rows):
    levels = len(heads)
    blocks, width = position_input.shape
    samples = volts.shape[3]
    pairs = 4 * levels * blocks
    tiles = 2 * blocks * blocks
    counts = (3 * tiles, 3 * pairs * blocks, 3 * pairs)
    depth = last[2] - last[1]
    return pl.pallas_call(
        functools.partial(own_kernel, levels, piece, last),
        out_shape=(
            jax.ShapeDtypeStruct((blocks, 2, width, samples), jnp.bfloat16),
            jax.ShapeDtypeStruct((out_rows, 2 * width), jnp.float32),
            *[jax.ShapeDtypeStruct((out_rows, n), jnp.bfloat16) for n in counts],
            jax.ShapeDtypeStruct((levels * blocks, out_rows, 96), jnp.bfloat16),
            *[jax.ShapeDtypeStruct((2 * width, head.shape[1]), jnp.bfloat16) for head in heads],
            piece_shape(piece, width, 2 * tiles),
            piece_shape(piece, width, 0),
            jax.ShapeDtypeStruct((width, 2 * depth), jnp.bfloat16),
            jax.ShapeDtypeStruct((blocks, 2 * width, 2 * depth), jnp.bfloat16),
        ),
        in_specs=[WHOLE, WHOLE, HBM] + [WHOLE] * levels,
        out_specs=(WHOLE,) * (7 + len(counts) + levels),
        scratch_shapes=[
            pltpu.VMEM((2, blocks, 2, width, samples), jnp.bfloat16),
            pltpu.VMEM((blocks, 2, width, samples), jnp.bfloat16),
            pltpu.VMEM((2 * blocks * blocks, 2, 2 * width), jnp.float32),
            pltpu.SemaphoreType.DMA((2, blocks, 2)),
        ],
        compiler_params=pltpu.CompilerParams(vmem_limit_bytes=16 << 20),
        cost_estimate=pl.CostEstimate(
            flops=64 * blocks * blocks * width * width * samples,
            bytes_accessed=12 * blocks * width * samples,
            transcendentals=0,
        ),
        name="own_level",
    )(groups, position_input, pltpu.with_memory_space_constraint(volts, pltpu.HBM), *heads)


def add_lags(rows, pick_ref, sums_ref):
    lags = jnp.concatenate(rows, axis=0)
    lags = jnp.concatenate([lags, conjugate_lags(lags)], axis=0)
    return sums_ref[...] + group_sums(pick_ref[...], lags)


def pair_kernel(levels, pieces, pick_ref, sums_ref, panel_ref, *refs):
    count = levels * len(pieces)
    partner_refs, more_refs, out_ref = refs[:count], refs[count:-1], refs[-1]
    _, _, width, samples = panel_ref.shape
    rows = []
    for block in sorted({block for piece in pieces for block, _, _ in piece}):
        for level in range(levels):
            for a in range(panel_ref.shape[0]):
                real_part, imag_part = 0.0, 0.0
                for i, piece in enumerate(pieces):
                    partner = partner_refs[level * len(pieces) + i]
                    for (b, first, last), (start, end) in zip(piece, columns(piece)):
                        if b != block:
                            continue
                        x_re, x_im = panel_ref[a, 0, :, first:last], panel_ref[a, 1, :, first:last]
                        y_re = partner[:width, start:end]
                        y_im = partner[width : 2 * width, start:end]
                        real_part = real_part + (product(x_re, y_re) + product(x_im, y_im))
                        imag_part = imag_part + (product(x_im, y_re) - product(x_re, y_im))
                rows.append(lag_rows(jnp.stack([real_part, imag_part])) * (1.0 / samples))
    sums = add_lags(rows, pick_ref, sums_ref)
    for more_ref in more_refs:
        terms = partner_refs[-1][2 * width :, :].astype(jnp.float32)
        half = terms.shape[0] // 2
        sums = sums + group_sums(more_ref[...], terms[:half] + terms[half:])
    out_ref[...] = sums


def last_kernel(levels, samples, pick_ref, sums_ref, panel_ref, *refs):
    partner_refs, out_refs = refs[:levels], refs[levels:]
    blocks, rows_both, _ = panel_ref.shape
    width = rows_both // 2
    sums = sums_ref[...]
    for level, partner_ref in enumerate(partner_refs):
        for a in range(blocks):
            tiles = product(panel_ref[a], partner_ref[...]).reshape(2, width, width)
            rows = jnp.concatenate(sheared_eights(tiles), axis=0) * (1.0 / samples)
            terms = split_rows(rows)
            terms = jnp.concatenate([terms, turn_lags(terms)], axis=0).astype(jnp.bfloat16)
            pick = pick_ref[level * blocks + a]
            sums = sums + jnp.dot(pick, terms, preferred_element_type=jnp.float32)
    share = sums.shape[0] // len(out_refs)
    for place, out_ref in enumerate(out_refs):
        out_ref[...] = sums[place * share : (place + 1) * share]


def pair_call(kernel, inputs, work, shares=1):
    rows, width = inputs[1].shape
    return pl.pallas_call(
        kernel,
        out_shape=[jax.ShapeDtypeStruct((rows // shares, width), jnp.float32)] * shares,
        in_specs=[WHOLE] * len(inputs),
        out_specs=[WHOLE] * shares,
        compiler_params=pltpu.CompilerParams(vmem_limit_bytes=16 << 20),
        cost_estimate=pl.CostEstimate(flops=work, bytes_accessed=4 << 20, transcendentals=0),
        name="pair_level",
    )(*inputs)


def finish_kernel(levels, *refs):
    part_refs, out_ref = refs[:-1], refs[-1]
    mine = parity(lax.axis_index("inp"), levels)
    groups, channels, parts, lags = out_ref.shape
    sums = [None, None]
    for distance, part_ref in enumerate(reversed(part_refs)):
        side = distance.bit_count() % 2
        sums[side] = part_ref[...] if sums[side] is None else sums[side] + part_ref[...]
    for f in range(channels):
        total = jnp.where(mine == f, sums[0], sums[1])
        for g in range(groups):
            out_ref[g, f] = total[g * parts : (g + 1) * parts, :lags]


def finish(parts, levels, lags):
    return pl.pallas_call(
        functools.partial(finish_kernel, levels),
        out_shape=jax.ShapeDtypeStruct((RG_DEV, 2, 2, lags), jnp.float32),
        in_specs=[WHOLE] * len(parts),
        out_specs=WHOLE,
        compiler_params=pltpu.CompilerParams(vmem_limit_bytes=8 << 20),
        name="finish",
    )(*parts)


def on_device(volts, position_input, tile_group):
    blocks, width = position_input.shape
    samples = volts.shape[3]
    devices = lax.axis_size("inp")
    levels = devices.bit_length() - 1
    out_rows = devices * RG_DEV * 2
    eighth = samples // 8
    head = [(0, 0, 2 * eighth)]
    rest = [(0, 2 * eighth, samples), (1, 0, 2 * eighth)]
    tail = [(1, 2 * eighth, 6 * eighth)]
    last = (1, 6 * eighth, samples)
    by_block = tile_group.transpose(0, 2, 1)
    partner_of = [functools.partial(xor_permute, axis="inp", distance=1 << l) for l in range(levels)]
    sent, second = early_pieces(position_input, volts, by_block, head, rest, levels)
    head_arrived = [send(sent) for send in partner_of]
    rest_arrived = [send(second) for send in partner_of]
    panel, sums, neighbour, both, single, eights, *sent = own_level(
        by_block, position_input, volts, head_arrived, tail, last, out_rows
    )
    head_ordered, (more, piece, last_piece, last_panel) = sent[:levels], sent[levels:]
    tail_arrived = [send(piece) for send in partner_of[:-1]] + [partner_of[-1](more)]
    last_arrived = [send(last_piece) for send in partner_of]

    flops = 8 * levels * blocks * width * width
    arrived = [piece for pair in zip(head_ordered, rest_arrived) for piece in pair]
    (sums,) = pair_call(
        functools.partial(pair_kernel, levels, [head, rest]),
        [both, sums, panel, *arrived],
        flops * 10 * eighth,
    )
    (sums,) = pair_call(
        functools.partial(pair_kernel, levels, [tail]),
        [single, sums, panel, *tail_arrived, neighbour],
        flops * 4 * eighth,
    )
    parts = pair_call(
        functools.partial(last_kernel, levels, samples),
        [eights, sums, last_panel, *last_arrived],
        flops * 2 * eighth,
        devices,
    )
    parts = [
        xor_permute(parts[distance], "inp", distance) for distance in reversed(range(1, devices))
    ] + [parts[0]]
    return finish(parts, levels, 2 * width - 1)


def solution(mesh):
    return jax.shard_map(
        on_device,
        mesh=mesh,
        in_specs=(P("freq", None, "inp", None), P("inp", None), P("inp", None, None)),
        out_specs=P("inp", "freq", None, None),
        check_vma=False,
    )
```

```python
import functools

import jax
import jax.numpy as jnp
from jax import lax
from jax.experimental import pallas as pl
from jax.experimental.pallas import tpu as pltpu
from jax.sharding import PartitionSpec as P

RG_DEV = 8
GROUP_ROWS = 16
HBM = pl.BlockSpec(memory_space=pltpu.HBM)
WHOLE = pl.BlockSpec(memory_space=pltpu.VMEM)


def xor_permute(x, axis, distance):
    return lax.ppermute(x, axis, [(i, i ^ distance) for i in range(lax.axis_size(axis))])


def parity(index, levels):
    bits = index & 1
    for level in range(1, levels):
        bits = bits ^ ((index >> level) & 1)
    return bits


def order_matrix(position_row):
    width = position_row.shape[-1]
    by_position = jnp.transpose(jnp.broadcast_to(position_row, (width, width)))
    inputs = lax.broadcasted_iota(jnp.int32, (width, width), 1)
    return (by_position == inputs).astype(jnp.float32).astype(jnp.bfloat16)


def product(x, y):
    return lax.dot_general(x, y, (((1,), (1,)), ((), ())), preferred_element_type=jnp.float32)


def lag_rows(tiles):
    count, width, _ = tiles.shape
    half = width // 2
    low, high = tiles[:, :half], tiles[:, half:]
    sheared = jnp.concatenate(
        [
            high[:, :, :half],
            high[:, :, half:] + low[:, :, :half],
            low[:, :, half:],
            jnp.zeros((count, half, half), jnp.float32),
        ],
        axis=2,
    )
    rows = half
    while rows > 8:
        rows //= 2
        upper = sheared[:, :rows].reshape(count * rows, 2 * width)
        upper = pltpu.roll(upper, rows, 1).reshape(count, rows, 2 * width)
        sheared = upper + sheared[:, rows:]
    flat = sheared.reshape(count * rows, 2 * width)
    sublane = lax.broadcasted_iota(jnp.int32, flat.shape, 0) % 8
    while rows > 1:
        rows //= 2
        flat = jnp.where((sublane & rows) == 0, pltpu.roll(flat, rows, 1), flat)
    return jnp.sum(flat.reshape(count, 8, 2 * width), axis=1)


def tile_lags(x_re, x_im, y_re, y_im, samples):
    real_part = product(x_re, y_re) + product(x_im, y_im)
    imag_part = product(x_im, y_re) - product(x_re, y_im)
    return lag_rows(jnp.stack([real_part, imag_part])) * (1.0 / samples)


def split_rows(x):
    first = x.astype(jnp.bfloat16).astype(jnp.float32)
    rest = x - first
    second = rest.astype(jnp.bfloat16).astype(jnp.float32)
    return jnp.concatenate([first, second, rest - second], axis=0)


def anti_identity(size):
    place = lax.broadcasted_iota(jnp.int32, (size, size), 0) + lax.broadcasted_iota(
        jnp.int32, (size, size), 1
    )
    return (place == size - 1).astype(jnp.float32).astype(jnp.bfloat16)


def turn_lags(terms):
    count, width = terms.shape
    lanes = 128
    spans = range(0, width, lanes)
    terms = jnp.concatenate([terms[:, first : first + lanes] for first in spans], axis=0)
    terms = jnp.dot(
        terms.astype(jnp.bfloat16), anti_identity(lanes), preferred_element_type=jnp.float32
    )
    blocks = [terms[count * i : count * (i + 1)] for i in reversed(range(len(spans)))]
    return pltpu.roll(jnp.concatenate(blocks, axis=1), width - 1, 1)


def conjugate_lags(lags):
    count = lags.shape[0]
    turned = turn_lags(split_rows(lags))
    turned = turned[:count] + turned[count : 2 * count] + turned[2 * count :]
    odd = lax.broadcasted_iota(jnp.int32, turned.shape, 0) % 2 == 1
    return jnp.where(odd, -turned, turned)


def sheared_eights(tiles):
    count, width, _ = tiles.shape
    half = width // 2
    low, high = tiles[:, :half], tiles[:, half:]
    sheared = jnp.concatenate(
        [
            low[:, :, :half],
            low[:, :, half:] + high[:, :, :half],
            high[:, :, half:],
            jnp.zeros((count, half, half), jnp.float32),
        ],
        axis=2,
    )
    rows = half
    while rows > 8:
        rows //= 2
        lower = sheared[:, rows:].reshape(count * rows, 2 * width)
        lower = pltpu.roll(lower, rows, 1).reshape(count, rows, 2 * width)
        sheared = sheared[:, :rows] + lower
    return [pltpu.roll(sheared[i], 0, 1, stride=1, stride_axis=0) for i in range(count)]


def group_block(groups, columns=128):
    rows = jnp.concatenate([groups[b] for b in range(groups.shape[0])], axis=0)
    lines, lanes = rows.shape
    return jnp.pad(rows, ((0, GROUP_ROWS - lines), (0, columns - lanes)))


def target_rows(groups):
    me = lax.axis_index("inp")
    bits = RG_DEV.bit_length() - 1
    return (((groups >> bits) ^ me) << (bits + 1)) + ((groups & (RG_DEV - 1)) << 1)


def pick_matrix(entries, rows, repeat=1, sides=1):
    count = len(entries) // sides
    side = 3 * count * repeat
    shape = (rows, sides * side)
    row = lax.broadcasted_iota(jnp.int32, shape, 0)
    column = lax.broadcasted_iota(jnp.int32, shape, 1)
    entry = column // side * count + column % side % (count * repeat) // repeat
    pick = jnp.zeros(shape, jnp.float32)
    for j, (targets, line, lane, part, sign) in enumerate(entries):
        target = jnp.broadcast_to(targets[line : line + 1, lane : lane + 1] + part, shape)
        pick = jnp.where(jnp.logical_and(entry == j, row == target), sign, pick)
    return pick.astype(jnp.bfloat16)


def pick_matrices(groups, heads, blocks, out_rows):
    own = target_rows(group_block(groups))
    others = [target_rows(head.astype(jnp.float32).astype(jnp.int32)) for head in heads]

    def pairs(b):
        order = [(level, a, p) for level in range(len(heads)) for a in range(blocks) for p in range(2)]
        forward = [(own, a * blocks + b, level + 1, p, 1.0) for level, a, p in order]
        turned = [(others[level], b * blocks + a, level + 1, p, 1.0) for level, a, p in order]
        return forward, turned

    forward, turned = zip(*[pairs(b) for b in range(blocks)])
    tiles = [
        [(targets, line, 0, p, 1.0) for line in range(blocks * blocks) for p in range(2)]
        for targets in (own, others[-1])
    ]
    both = [entry for side in (forward, turned) for block in side for entry in block]
    signed = [entry[:4] + (-1.0 if i % 2 else 1.0,) for i, entry in enumerate(turned[-1])]
    return [
        pick_matrix(tiles[0], out_rows),
        pick_matrix(tiles[1], out_rows),
        pick_matrix(both, out_rows),
        pick_matrix(forward[-1] + turned[-1], out_rows),
        pick_matrix(forward[-1] + signed, out_rows, repeat=8, sides=2),
    ]


def group_sums(pick, lags):
    terms = split_rows(lags).astype(jnp.bfloat16)
    return jnp.dot(pick, terms, preferred_element_type=jnp.float32)


def columns(piece):
    spans, start = [], 0
    for _, first, last in piece:
        spans.append((start, start + last - first))
        start += last - first
    return spans


def piece_shape(piece, width, more):
    return jax.ShapeDtypeStruct((2 * width + more, columns(piece)[-1][1]), jnp.bfloat16)


def load_piece(piece, other, width, volts_ref, raw, in_sem):
    blocks = sorted({block for block, _, _ in piece})
    loads = []
    for i, block in enumerate(blocks):
        start = min(first for b, first, _ in piece if b == block)
        end = max(last for b, _, last in piece if b == block)
        for c in range(2):
            load = pltpu.make_async_copy(
                volts_ref.at[other, c, pl.ds(block * width, width), pl.ds(start, end - start)],
                raw.at[i, c, :, pl.ds(start, end - start)],
                in_sem.at[i, c],
            )
            load.start()
            loads.append((i, block, c, load))
    return loads


def order_piece(piece, loads, position, raw, out_ref):
    width = position.shape[1]
    orders = {
        block: order_matrix(position[block : block + 1, :]) for block in sorted({l[1] for l in loads})
    }
    for i, block, c, load in loads:
        load.wait()
        for (b, first, last), (start, end) in zip(piece, columns(piece)):
            if b == block:
                out_ref[c * width : (c + 1) * width, start:end] = jnp.dot(
                    orders[block], raw[i, c, :, first:last], preferred_element_type=jnp.float32
                ).astype(jnp.bfloat16)


def head_kernel(levels, piece, position_ref, volts_ref, group_ref, head_ref, *scratch):
    position, groups, small_sem, in_sem = scratch
    other = 1 - parity(lax.axis_index("inp"), levels)
    width = position.shape[1]
    ((block, first, last),) = piece
    smalls = [
        pltpu.make_async_copy(position_ref, position, small_sem.at[0]),
        pltpu.make_async_copy(group_ref, groups, small_sem.at[1]),
    ]
    loads = [
        pltpu.make_async_copy(
            volts_ref.at[other, c, pl.ds(block * width, width), pl.ds(first, last - first)],
            head_ref.at[pl.ds(c * width, width), :],
            in_sem.at[c],
        )
        for c in range(2)
    ]
    for copy in smalls + loads:
        copy.start()
    for copy in smalls:
        copy.wait()
    rows = group_block(groups[...], last - first)
    line = lax.broadcasted_iota(jnp.int32, rows.shape, 0)
    own_row = jnp.broadcast_to(position[block : block + 1, :], rows.shape)
    rows = jnp.where(line == groups.shape[0] ** 2, own_row, rows)
    head_ref[2 * width :, :] = rows.astype(jnp.float32).astype(jnp.bfloat16)
    for copy in loads:
        copy.wait()


def rest_kernel(levels, piece, position_ref, volts_ref, _, out_ref, position, raw, small_sem, in_sem):
    other = 1 - parity(lax.axis_index("inp"), levels)
    load_position = pltpu.make_async_copy(position_ref, position, small_sem)
    load_position.start()
    loads = load_piece(piece, other, position.shape[1], volts_ref, raw, in_sem)
    load_position.wait()
    order_piece(piece, loads, position, raw, out_ref)


def early_pieces(position_input, volts, groups, head, rest, levels):
    blocks, width = position_input.shape
    samples = volts.shape[3]
    assert columns(head)[-1][1] == width
    in_hbm = [pltpu.with_memory_space_constraint(x, pltpu.HBM) for x in (position_input, volts)]
    position = pltpu.VMEM(position_input.shape, jnp.int32)
    semaphore = pltpu.SemaphoreType.DMA
    sent = pl.pallas_call(
        functools.partial(head_kernel, levels, head),
        out_shape=piece_shape(head, width, GROUP_ROWS),
        in_specs=[HBM] * 3,
        out_specs=WHOLE,
        scratch_shapes=[
            position,
            pltpu.VMEM(groups.shape, jnp.int32),
            semaphore((2,)),
            semaphore((2,)),
        ],
        compiler_params=pltpu.CompilerParams(vmem_limit_bytes=8 << 20),
        cost_estimate=pl.CostEstimate(flops=0, bytes_accessed=1 << 20, transcendentals=0),
        name="first_piece",
    )(*in_hbm, pltpu.with_memory_space_constraint(groups, pltpu.HBM))
    second = pl.pallas_call(
        functools.partial(rest_kernel, levels, rest),
        out_shape=piece_shape(rest, width, 0),
        in_specs=[HBM, HBM, pl.BlockSpec(memory_space=pl.ANY)],
        out_specs=WHOLE,
        scratch_shapes=[
            position,
            pltpu.VMEM((blocks, 2, width, samples), jnp.bfloat16),
            semaphore(()),
            semaphore((blocks, 2)),
        ],
        compiler_params=pltpu.CompilerParams(vmem_limit_bytes=16 << 20),
        cost_estimate=pl.CostEstimate(
            flops=4 * width * width * columns(rest)[-1][1],
            bytes_accessed=4 << 20,
            transcendentals=0,
        ),
        name="second_piece",
    )(*in_hbm, sent)
    return sent, second


def own_kernel(levels, piece, last, group_ref, position_ref, volts_ref, *refs):
    head_refs, refs = refs[:levels], refs[levels:]
    panel_ref, sums_ref, *refs, raw, other_panel, lags_ref, in_sem = refs
    pick_refs, ordered_refs, refs = refs[:4], refs[4 : 4 + levels], refs[4 + levels :]
    more_ref, piece_ref, last_ref, last_panel_ref = refs
    blocks, _, width, _ = panel_ref.shape
    mine = parity(lax.axis_index("inp"), levels)
    channels = (mine, 1 - mine)
    loads = [
        [
            [
                pltpu.make_async_copy(
                    volts_ref.at[channels[f], c, pl.ds(b * width, width)],
                    raw.at[f, b, c],
                    in_sem.at[f, b, c],
                )
                for c in range(2)
            ]
            for b in range(blocks)
        ]
        for f in range(2)
    ]
    for f in range(2):
        for b in range(blocks):
            for c in range(2):
                loads[f][b][c].start()
    orders = [order_matrix(position_ref[b : b + 1, :]) for b in range(blocks)]
    for f, panel in enumerate((panel_ref, other_panel)):
        for b in range(blocks):
            for c in range(2):
                loads[f][b][c].wait()
                panel[b, c] = jnp.dot(
                    orders[b], raw[f, b, c], preferred_element_type=jnp.float32
                ).astype(jnp.bfloat16)

        def one_tile(index, carry, panel=panel, f=f):
            a = index // blocks
            b = index % blocks
            lags = tile_lags(panel[a, 0], panel[a, 1], panel[b, 0], panel[b, 1], panel.shape[3])
            center = lax.broadcasted_iota(jnp.int32, lags.shape, 1) == width - 1
            lags_ref[f * blocks * blocks + index] = jnp.where(
                jnp.logical_and(center, a == b), 0.0, lags
            )
            return carry

        lax.fori_loop(0, blocks * blocks, one_tile, 0)
    tiles = blocks * blocks
    lags = jnp.concatenate([lags_ref[i] for i in range(tiles)], axis=0)
    heads = [head_ref[2 * width :, :] for head_ref in head_refs]
    for head, head_ref, ordered_ref in zip(heads, head_refs, ordered_refs):
        positions = head.astype(jnp.float32).astype(jnp.int32)[blocks**2 : blocks**2 + 1]
        order = order_matrix(positions)
        for c in range(2):
            rows = head_ref[c * width : (c + 1) * width, :]
            rows = jnp.dot(order, rows, preferred_element_type=jnp.float32)
            ordered_ref[c * width : (c + 1) * width, :] = rows.astype(jnp.bfloat16)
    own_pick, *picks = pick_matrices(group_ref[...], heads, blocks, sums_ref.shape[0])
    for pick_ref, pick in zip(pick_refs, picks):
        pick_ref[...] = pick
    sums_ref[...] = group_sums(own_pick, lags)
    for (block, first, end), (start, stop) in zip(piece, columns(piece)):
        for c in range(2):
            rows = other_panel[block, c, :, first:end]
            piece_ref[c * width : (c + 1) * width, start:stop] = rows
            more_ref[c * width : (c + 1) * width, start:stop] = rows
    lags = jnp.concatenate([lags_ref[tiles + i] for i in range(tiles)], axis=0)
    high = lags.astype(jnp.bfloat16).astype(jnp.float32)
    terms = jnp.concatenate([high, lags - high], axis=0)
    more_ref[2 * width :, :] = terms.astype(jnp.bfloat16)
    block, first, end = last
    depth = end - first
    for c in range(2):
        last_ref[:, c * depth : (c + 1) * depth] = other_panel[block, c, :, first:end]
    turn = anti_identity(width)
    for a in range(blocks):
        real_part, imag_part = [
            jnp.dot(turn, panel_ref[a, c, :, first:end], preferred_element_type=jnp.float32)
            for c in range(2)
        ]
        last_panel_ref[a, :width, :depth] = real_part.astype(jnp.bfloat16)
        last_panel_ref[a, :width, depth:] = imag_part.astype(jnp.bfloat16)
        last_panel_ref[a, width:, :depth] = imag_part.astype(jnp.bfloat16)
        last_panel_ref[a, width:, depth:] = (-real_part).astype(jnp.bfloat16)


def own_level(groups, position_input, volts, heads, piece, last, out_rows):
    levels = len(heads)
    blocks, width = position_input.shape
    samples = volts.shape[3]
    pairs = 4 * levels * blocks
    tiles = 2 * blocks * blocks
    counts = (3 * tiles, 3 * pairs * blocks, 3 * pairs, 3 * pairs * 8)
    depth = last[2] - last[1]
    return pl.pallas_call(
        functools.partial(own_kernel, levels, piece, last),
        out_shape=(
            jax.ShapeDtypeStruct((blocks, 2, width, samples), jnp.bfloat16),
            jax.ShapeDtypeStruct((out_rows, 2 * width), jnp.float32),
            *[jax.ShapeDtypeStruct((out_rows, n), jnp.bfloat16) for n in counts],
            *[jax.ShapeDtypeStruct((2 * width, head.shape[1]), jnp.bfloat16) for head in heads],
            piece_shape(piece, width, 2 * tiles),
            piece_shape(piece, width, 0),
            jax.ShapeDtypeStruct((width, 2 * depth), jnp.bfloat16),
            jax.ShapeDtypeStruct((blocks, 2 * width, 2 * depth), jnp.bfloat16),
        ),
        in_specs=[WHOLE, WHOLE, HBM] + [WHOLE] * levels,
        out_specs=(WHOLE,) * (6 + len(counts) + levels),
        scratch_shapes=[
            pltpu.VMEM((2, blocks, 2, width, samples), jnp.bfloat16),
            pltpu.VMEM((blocks, 2, width, samples), jnp.bfloat16),
            pltpu.VMEM((2 * blocks * blocks, 2, 2 * width), jnp.float32),
            pltpu.SemaphoreType.DMA((2, blocks, 2)),
        ],
        compiler_params=pltpu.CompilerParams(vmem_limit_bytes=16 << 20),
        cost_estimate=pl.CostEstimate(
            flops=64 * blocks * blocks * width * width * samples,
            bytes_accessed=12 * blocks * width * samples,
            transcendentals=0,
        ),
        name="own_level",
    )(groups, position_input, pltpu.with_memory_space_constraint(volts, pltpu.HBM), *heads)


def add_lags(rows, pick_ref, sums_ref):
    lags = jnp.concatenate(rows, axis=0)
    lags = jnp.concatenate([lags, conjugate_lags(lags)], axis=0)
    return sums_ref[...] + group_sums(pick_ref[...], lags)


def pair_kernel(levels, pieces, pick_ref, sums_ref, panel_ref, *refs):
    count = levels * len(pieces)
    partner_refs, more_refs, out_ref = refs[:count], refs[count:-1], refs[-1]
    _, _, width, samples = panel_ref.shape
    rows = []
    for block in sorted({block for piece in pieces for block, _, _ in piece}):
        for level in range(levels):
            for a in range(panel_ref.shape[0]):
                real_part, imag_part = 0.0, 0.0
                for i, piece in enumerate(pieces):
                    partner = partner_refs[level * len(pieces) + i]
                    for (b, first, last), (start, end) in zip(piece, columns(piece)):
                        if b != block:
                            continue
                        x_re, x_im = panel_ref[a, 0, :, first:last], panel_ref[a, 1, :, first:last]
                        y_re = partner[:width, start:end]
                        y_im = partner[width : 2 * width, start:end]
                        real_part = real_part + (product(x_re, y_re) + product(x_im, y_im))
                        imag_part = imag_part + (product(x_im, y_re) - product(x_re, y_im))
                rows.append(lag_rows(jnp.stack([real_part, imag_part])) * (1.0 / samples))
    sums = add_lags(rows, pick_ref, sums_ref)
    for more_ref in more_refs:
        terms = partner_refs[-1][2 * width :, :].astype(jnp.float32)
        half = terms.shape[0] // 2
        sums = sums + group_sums(more_ref[...], terms[:half] + terms[half:])
    out_ref[...] = sums


def last_kernel(levels, samples, pick_ref, sums_ref, panel_ref, *refs):
    partner_refs, out_refs = refs[:levels], refs[levels:]
    blocks, rows_both, _ = panel_ref.shape
    width = rows_both // 2
    rows = []
    for partner_ref in partner_refs:
        for a in range(blocks):
            tiles = product(panel_ref[a], partner_ref[...]).reshape(2, width, width)
            rows += sheared_eights(tiles)
    terms = split_rows(jnp.concatenate(rows, axis=0) * (1.0 / samples))
    terms = jnp.concatenate([terms, turn_lags(terms)], axis=0).astype(jnp.bfloat16)
    sums = sums_ref[...] + jnp.dot(pick_ref[...], terms, preferred_element_type=jnp.float32)
    share = sums.shape[0] // len(out_refs)
    for place, out_ref in enumerate(out_refs):
        out_ref[...] = sums[place * share : (place + 1) * share]


def pair_call(kernel, inputs, work, shares=1):
    rows, width = inputs[1].shape
    return pl.pallas_call(
        kernel,
        out_shape=[jax.ShapeDtypeStruct((rows // shares, width), jnp.float32)] * shares,
        in_specs=[WHOLE] * len(inputs),
        out_specs=[WHOLE] * shares,
        compiler_params=pltpu.CompilerParams(vmem_limit_bytes=16 << 20),
        cost_estimate=pl.CostEstimate(flops=work, bytes_accessed=4 << 20, transcendentals=0),
        name="pair_level",
    )(*inputs)


def finish_kernel(levels, *refs):
    part_refs, out_ref = refs[:-1], refs[-1]
    mine = parity(lax.axis_index("inp"), levels)
    groups, channels, parts, lags = out_ref.shape
    sums = [None, None]
    for distance, part_ref in enumerate(reversed(part_refs)):
        side = distance.bit_count() % 2
        sums[side] = part_ref[...] if sums[side] is None else sums[side] + part_ref[...]
    for f in range(channels):
        total = jnp.where(mine == f, sums[0], sums[1])
        for g in range(groups):
            out_ref[g, f] = total[g * parts : (g + 1) * parts, :lags]


def finish(parts, levels, lags):
    return pl.pallas_call(
        functools.partial(finish_kernel, levels),
        out_shape=jax.ShapeDtypeStruct((RG_DEV, 2, 2, lags), jnp.float32),
        in_specs=[WHOLE] * len(parts),
        out_specs=WHOLE,
        compiler_params=pltpu.CompilerParams(vmem_limit_bytes=8 << 20),
        name="finish",
    )(*parts)


def on_device(volts, position_input, tile_group):
    blocks, width = position_input.shape
    samples = volts.shape[3]
    devices = lax.axis_size("inp")
    levels = devices.bit_length() - 1
    out_rows = devices * RG_DEV * 2
    eighth = samples // 8
    head = [(0, 0, 2 * eighth)]
    rest = [(0, 2 * eighth, samples), (1, 0, 2 * eighth)]
    tail = [(1, 2 * eighth, 6 * eighth)]
    last = (1, 6 * eighth, samples)
    by_block = tile_group.transpose(0, 2, 1)
    partner_of = [functools.partial(xor_permute, axis="inp", distance=1 << l) for l in range(levels)]
    sent, second = early_pieces(position_input, volts, by_block, head, rest, levels)
    head_arrived = [send(sent) for send in partner_of]
    rest_arrived = [send(second) for send in partner_of]
    panel, sums, neighbour, both, single, eights, *sent = own_level(
        by_block, position_input, volts, head_arrived, tail, last, out_rows
    )
    head_ordered, (more, piece, last_piece, last_panel) = sent[:levels], sent[levels:]
    tail_arrived = [send(piece) for send in partner_of[:-1]] + [partner_of[-1](more)]
    last_arrived = [send(last_piece) for send in partner_of]

    flops = 8 * levels * blocks * width * width
    arrived = [piece for pair in zip(head_ordered, rest_arrived) for piece in pair]
    (sums,) = pair_call(
        functools.partial(pair_kernel, levels, [head, rest]),
        [both, sums, panel, *arrived],
        flops * 10 * eighth,
    )
    (sums,) = pair_call(
        functools.partial(pair_kernel, levels, [tail]),
        [single, sums, panel, *tail_arrived, neighbour],
        flops * 4 * eighth,
    )
    parts = pair_call(
        functools.partial(last_kernel, levels, samples),
        [eights, sums, last_panel, *last_arrived],
        flops * 2 * eighth,
        devices,
    )
    parts = [
        xor_permute(parts[distance], "inp", distance) for distance in reversed(range(1, devices))
    ] + [parts[0]]
    return finish(parts, levels, 2 * width - 1)


def solution(mesh):
    return jax.shard_map(
        on_device,
        mesh=mesh,
        in_specs=(P("freq", None, "inp", None), P("inp", None), P("inp", None, None)),
        out_specs=P("inp", "freq", None, None),
        check_vma=False,
    )
```

```python
import functools

import jax
import jax.numpy as jnp
from jax import lax
from jax.experimental import pallas as pl
from jax.experimental.pallas import tpu as pltpu
from jax.sharding import PartitionSpec as P

RG_DEV = 8
GROUP_ROWS = 16
HBM = pl.BlockSpec(memory_space=pltpu.HBM)
WHOLE = pl.BlockSpec(memory_space=pltpu.VMEM)


def xor_permute(x, axis, distance):
    return lax.ppermute(x, axis, [(i, i ^ distance) for i in range(lax.axis_size(axis))])


def parity(index, levels):
    bits = index & 1
    for level in range(1, levels):
        bits = bits ^ ((index >> level) & 1)
    return bits


def order_matrix(position_row):
    width = position_row.shape[-1]
    by_position = jnp.transpose(jnp.broadcast_to(position_row, (width, width)))
    inputs = lax.broadcasted_iota(jnp.int32, (width, width), 1)
    return (by_position == inputs).astype(jnp.float32).astype(jnp.bfloat16)


def product(x, y):
    return lax.dot_general(x, y, (((1,), (1,)), ((), ())), preferred_element_type=jnp.float32)


def lag_rows(tiles):
    count, width, _ = tiles.shape
    half = width // 2
    low, high = tiles[:, :half], tiles[:, half:]
    sheared = jnp.concatenate(
        [
            high[:, :, :half],
            high[:, :, half:] + low[:, :, :half],
            low[:, :, half:],
            jnp.zeros((count, half, half), jnp.float32),
        ],
        axis=2,
    )
    rows = half
    while rows > 8:
        rows //= 2
        upper = sheared[:, :rows].reshape(count * rows, 2 * width)
        upper = pltpu.roll(upper, rows, 1).reshape(count, rows, 2 * width)
        sheared = upper + sheared[:, rows:]
    flat = sheared.reshape(count * rows, 2 * width)
    sublane = lax.broadcasted_iota(jnp.int32, flat.shape, 0) % 8
    while rows > 1:
        rows //= 2
        flat = jnp.where((sublane & rows) == 0, pltpu.roll(flat, rows, 1), flat)
    return jnp.sum(flat.reshape(count, 8, 2 * width), axis=1)


def tile_lags(x_re, x_im, y_re, y_im, samples):
    real_part = product(x_re, y_re) + product(x_im, y_im)
    imag_part = product(x_im, y_re) - product(x_re, y_im)
    return lag_rows(jnp.stack([real_part, imag_part])) * (1.0 / samples)


def split_rows(x):
    first = x.astype(jnp.bfloat16).astype(jnp.float32)
    rest = x - first
    second = rest.astype(jnp.bfloat16).astype(jnp.float32)
    return jnp.concatenate([first, second, rest - second], axis=0)


def anti_identity(size):
    place = lax.broadcasted_iota(jnp.int32, (size, size), 0) + lax.broadcasted_iota(
        jnp.int32, (size, size), 1
    )
    return (place == size - 1).astype(jnp.float32).astype(jnp.bfloat16)


def turn_lags(terms):
    count, width = terms.shape
    lanes = 128
    spans = range(0, width, lanes)
    terms = jnp.concatenate([terms[:, first : first + lanes] for first in spans], axis=0)
    terms = jnp.dot(
        terms.astype(jnp.bfloat16), anti_identity(lanes), preferred_element_type=jnp.float32
    )
    blocks = [terms[count * i : count * (i + 1)] for i in reversed(range(len(spans)))]
    return pltpu.roll(jnp.concatenate(blocks, axis=1), width - 1, 1)


def conjugate_lags(lags):
    count = lags.shape[0]
    turned = turn_lags(split_rows(lags))
    turned = turned[:count] + turned[count : 2 * count] + turned[2 * count :]
    odd = lax.broadcasted_iota(jnp.int32, turned.shape, 0) % 2 == 1
    return jnp.where(odd, -turned, turned)


def reversed_lags(lags):
    count, width = lags.shape
    lanes = 128
    rows = jnp.pad(lags, ((0, -count % 8), (0, 0)))
    index = lanes - 1 - lax.broadcasted_iota(jnp.int32, (rows.shape[0], lanes), 1)
    blocks = [
        jnp.take_along_axis(
            rows[:, first : first + lanes], index, axis=1, mode="promise_in_bounds"
        )
        for first in reversed(range(0, width, lanes))
    ]
    return pltpu.roll(jnp.concatenate(blocks, axis=1), width - 1, 1)[:count]


def sheared_eights(tiles):
    count, width, _ = tiles.shape
    half = width // 2
    low, high = tiles[:, :half], tiles[:, half:]
    sheared = jnp.concatenate(
        [
            low[:, :, :half],
            low[:, :, half:] + high[:, :, :half],
            high[:, :, half:],
            jnp.zeros((count, half, half), jnp.float32),
        ],
        axis=2,
    )
    rows = half
    while rows > 8:
        rows //= 2
        lower = sheared[:, rows:].reshape(count * rows, 2 * width)
        lower = pltpu.roll(lower, rows, 1).reshape(count, rows, 2 * width)
        sheared = sheared[:, :rows] + lower
    return [pltpu.roll(sheared[i], 0, 1, stride=1, stride_axis=0) for i in range(count)]


def group_block(groups, columns=128):
    rows = jnp.concatenate([groups[b] for b in range(groups.shape[0])], axis=0)
    lines, lanes = rows.shape
    return jnp.pad(rows, ((0, GROUP_ROWS - lines), (0, columns - lanes)))


def target_rows(groups):
    me = lax.axis_index("inp")
    bits = RG_DEV.bit_length() - 1
    return (((groups >> bits) ^ me) << (bits + 1)) + ((groups & (RG_DEV - 1)) << 1)


def pick_matrix(entries, rows):
    count = len(entries)
    shape = (rows, 3 * count)
    row = lax.broadcasted_iota(jnp.int32, shape, 0)
    column = lax.broadcasted_iota(jnp.int32, shape, 1) % count
    pick = jnp.zeros(shape, jnp.float32)
    for j, (targets, line, lane, part, _) in enumerate(entries):
        target = jnp.broadcast_to(targets[line : line + 1, lane : lane + 1] + part, shape)
        pick = jnp.where(jnp.logical_and(column == j, row == target), 1.0, pick)
    return pick.astype(jnp.bfloat16)


def row_masks(entries, rows):
    row = lax.broadcasted_iota(jnp.int32, (rows, 128), 0)
    masks = []
    for targets, line, lane, part, sign in entries:
        target = jnp.broadcast_to(targets[line : line + 1, lane : lane + 1] + part, row.shape)
        masks.append(jnp.where(row == target, sign, 0.0))
    return jnp.stack(masks)


def pick_matrices(groups, heads, blocks, out_rows):
    own = target_rows(group_block(groups))
    others = [target_rows(head.astype(jnp.float32).astype(jnp.int32)) for head in heads]

    def pairs(b):
        order = [(level, a, p) for level in range(len(heads)) for a in range(blocks) for p in range(2)]
        forward = [(own, a * blocks + b, level + 1, p, 1.0) for level, a, p in order]
        turned = [(others[level], b * blocks + a, level + 1, p, 1.0) for level, a, p in order]
        return forward, turned

    forward, turned = zip(*[pairs(b) for b in range(blocks)])
    tiles = [
        [(targets, line, 0, p, 1.0) for line in range(blocks * blocks) for p in range(2)]
        for targets in (own, others[-1])
    ]
    both = [entry for side in (forward, turned) for block in side for entry in block]
    signed = [entry[:4] + (-1.0 if i % 2 else 1.0,) for i, entry in enumerate(turned[-1])]
    return [
        pick_matrix(tiles[0], out_rows),
        pick_matrix(tiles[1], out_rows),
        pick_matrix(both, out_rows),
        pick_matrix(forward[-1] + turned[-1], out_rows),
        row_masks(forward[-1] + signed, out_rows),
    ]


def group_sums(pick, lags):
    terms = split_rows(lags).astype(jnp.bfloat16)
    return jnp.dot(pick, terms, preferred_element_type=jnp.float32)


def columns(piece):
    spans, start = [], 0
    for _, first, last in piece:
        spans.append((start, start + last - first))
        start += last - first
    return spans


def piece_shape(piece, width, more):
    return jax.ShapeDtypeStruct((2 * width + more, columns(piece)[-1][1]), jnp.bfloat16)


def load_piece(piece, other, width, volts_ref, raw, in_sem):
    blocks = sorted({block for block, _, _ in piece})
    loads = []
    for i, block in enumerate(blocks):
        start = min(first for b, first, _ in piece if b == block)
        end = max(last for b, _, last in piece if b == block)
        for c in range(2):
            load = pltpu.make_async_copy(
                volts_ref.at[other, c, pl.ds(block * width, width), pl.ds(start, end - start)],
                raw.at[i, c, :, pl.ds(start, end - start)],
                in_sem.at[i, c],
            )
            load.start()
            loads.append((i, block, c, load))
    return loads


def order_piece(piece, loads, position, raw, out_ref):
    width = position.shape[1]
    orders = {
        block: order_matrix(position[block : block + 1, :]) for block in sorted({l[1] for l in loads})
    }
    for i, block, c, load in loads:
        load.wait()
        for (b, first, last), (start, end) in zip(piece, columns(piece)):
            if b == block:
                out_ref[c * width : (c + 1) * width, start:end] = jnp.dot(
                    orders[block], raw[i, c, :, first:last], preferred_element_type=jnp.float32
                ).astype(jnp.bfloat16)


def head_kernel(levels, piece, position_ref, volts_ref, group_ref, head_ref, *scratch):
    position, groups, small_sem, in_sem = scratch
    other = 1 - parity(lax.axis_index("inp"), levels)
    width = position.shape[1]
    ((block, first, last),) = piece
    smalls = [
        pltpu.make_async_copy(position_ref, position, small_sem.at[0]),
        pltpu.make_async_copy(group_ref, groups, small_sem.at[1]),
    ]
    loads = [
        pltpu.make_async_copy(
            volts_ref.at[other, c, pl.ds(block * width, width), pl.ds(first, last - first)],
            head_ref.at[pl.ds(c * width, width), :],
            in_sem.at[c],
        )
        for c in range(2)
    ]
    for copy in smalls + loads:
        copy.start()
    for copy in smalls:
        copy.wait()
    rows = group_block(groups[...], last - first)
    line = lax.broadcasted_iota(jnp.int32, rows.shape, 0)
    own_row = jnp.broadcast_to(position[block : block + 1, :], rows.shape)
    rows = jnp.where(line == groups.shape[0] ** 2, own_row, rows)
    head_ref[2 * width :, :] = rows.astype(jnp.float32).astype(jnp.bfloat16)
    for copy in loads:
        copy.wait()


def rest_kernel(levels, piece, position_ref, volts_ref, _, out_ref, position, raw, small_sem, in_sem):
    other = 1 - parity(lax.axis_index("inp"), levels)
    load_position = pltpu.make_async_copy(position_ref, position, small_sem)
    load_position.start()
    loads = load_piece(piece, other, position.shape[1], volts_ref, raw, in_sem)
    load_position.wait()
    order_piece(piece, loads, position, raw, out_ref)


def early_pieces(position_input, volts, groups, head, rest, levels):
    blocks, width = position_input.shape
    samples = volts.shape[3]
    assert columns(head)[-1][1] == width
    in_hbm = [pltpu.with_memory_space_constraint(x, pltpu.HBM) for x in (position_input, volts)]
    position = pltpu.VMEM(position_input.shape, jnp.int32)
    semaphore = pltpu.SemaphoreType.DMA
    sent = pl.pallas_call(
        functools.partial(head_kernel, levels, head),
        out_shape=piece_shape(head, width, GROUP_ROWS),
        in_specs=[HBM] * 3,
        out_specs=WHOLE,
        scratch_shapes=[
            position,
            pltpu.VMEM(groups.shape, jnp.int32),
            semaphore((2,)),
            semaphore((2,)),
        ],
        compiler_params=pltpu.CompilerParams(vmem_limit_bytes=8 << 20),
        cost_estimate=pl.CostEstimate(flops=0, bytes_accessed=1 << 20, transcendentals=0),
        name="first_piece",
    )(*in_hbm, pltpu.with_memory_space_constraint(groups, pltpu.HBM))
    second = pl.pallas_call(
        functools.partial(rest_kernel, levels, rest),
        out_shape=piece_shape(rest, width, 0),
        in_specs=[HBM, HBM, pl.BlockSpec(memory_space=pl.ANY)],
        out_specs=WHOLE,
        scratch_shapes=[
            position,
            pltpu.VMEM((blocks, 2, width, samples), jnp.bfloat16),
            semaphore(()),
            semaphore((blocks, 2)),
        ],
        compiler_params=pltpu.CompilerParams(vmem_limit_bytes=16 << 20),
        cost_estimate=pl.CostEstimate(
            flops=4 * width * width * columns(rest)[-1][1],
            bytes_accessed=4 << 20,
            transcendentals=0,
        ),
        name="second_piece",
    )(*in_hbm, sent)
    return sent, second


def own_kernel(levels, piece, last, group_ref, position_ref, volts_ref, *refs):
    head_refs, refs = refs[:levels], refs[levels:]
    panel_ref, sums_ref, *refs, raw, other_panel, lags_ref, in_sem = refs
    pick_refs, ordered_refs, refs = refs[:4], refs[4 : 4 + levels], refs[4 + levels :]
    more_ref, piece_ref, last_ref, last_panel_ref = refs
    blocks, _, width, _ = panel_ref.shape
    mine = parity(lax.axis_index("inp"), levels)
    channels = (mine, 1 - mine)
    loads = [
        [
            [
                pltpu.make_async_copy(
                    volts_ref.at[channels[f], c, pl.ds(b * width, width)],
                    raw.at[f, b, c],
                    in_sem.at[f, b, c],
                )
                for c in range(2)
            ]
            for b in range(blocks)
        ]
        for f in range(2)
    ]
    for f in range(2):
        for b in range(blocks):
            for c in range(2):
                loads[f][b][c].start()
    orders = [order_matrix(position_ref[b : b + 1, :]) for b in range(blocks)]
    for f, panel in enumerate((panel_ref, other_panel)):
        for b in range(blocks):
            for c in range(2):
                loads[f][b][c].wait()
                panel[b, c] = jnp.dot(
                    orders[b], raw[f, b, c], preferred_element_type=jnp.float32
                ).astype(jnp.bfloat16)

        def one_tile(index, carry, panel=panel, f=f):
            a = index // blocks
            b = index % blocks
            lags = tile_lags(panel[a, 0], panel[a, 1], panel[b, 0], panel[b, 1], panel.shape[3])
            center = lax.broadcasted_iota(jnp.int32, lags.shape, 1) == width - 1
            lags_ref[f * blocks * blocks + index] = jnp.where(
                jnp.logical_and(center, a == b), 0.0, lags
            )
            return carry

        lax.fori_loop(0, blocks * blocks, one_tile, 0)
    tiles = blocks * blocks
    lags = jnp.concatenate([lags_ref[i] for i in range(tiles)], axis=0)
    heads = [head_ref[2 * width :, :] for head_ref in head_refs]
    for head, head_ref, ordered_ref in zip(heads, head_refs, ordered_refs):
        positions = head.astype(jnp.float32).astype(jnp.int32)[blocks**2 : blocks**2 + 1]
        order = order_matrix(positions)
        for c in range(2):
            rows = head_ref[c * width : (c + 1) * width, :]
            rows = jnp.dot(order, rows, preferred_element_type=jnp.float32)
            ordered_ref[c * width : (c + 1) * width, :] = rows.astype(jnp.bfloat16)
    own_pick, *picks = pick_matrices(group_ref[...], heads, blocks, sums_ref.shape[0])
    for pick_ref, pick in zip(pick_refs, picks):
        pick_ref[...] = pick
    sums_ref[...] = group_sums(own_pick, lags)
    for (block, first, end), (start, stop) in zip(piece, columns(piece)):
        for c in range(2):
            rows = other_panel[block, c, :, first:end]
            piece_ref[c * width : (c + 1) * width, start:stop] = rows
            more_ref[c * width : (c + 1) * width, start:stop] = rows
    lags = jnp.concatenate([lags_ref[tiles + i] for i in range(tiles)], axis=0)
    high = lags.astype(jnp.bfloat16).astype(jnp.float32)
    terms = jnp.concatenate([high, lags - high], axis=0)
    more_ref[2 * width :, :] = terms.astype(jnp.bfloat16)
    block, first, end = last
    depth = end - first
    for c in range(2):
        last_ref[:, c * depth : (c + 1) * depth] = other_panel[block, c, :, first:end]
    turn = anti_identity(width)
    for a in range(blocks):
        real_part, imag_part = [
            jnp.dot(turn, panel_ref[a, c, :, first:end], preferred_element_type=jnp.float32)
            for c in range(2)
        ]
        last_panel_ref[a, :width, :depth] = real_part.astype(jnp.bfloat16)
        last_panel_ref[a, :width, depth:] = imag_part.astype(jnp.bfloat16)
        last_panel_ref[a, width:, :depth] = imag_part.astype(jnp.bfloat16)
        last_panel_ref[a, width:, depth:] = (-real_part).astype(jnp.bfloat16)


def own_level(groups, position_input, volts, heads, piece, last, out_rows):
    levels = len(heads)
    blocks, width = position_input.shape
    samples = volts.shape[3]
    pairs = 4 * levels * blocks
    tiles = 2 * blocks * blocks
    counts = (3 * tiles, 3 * pairs * blocks, 3 * pairs)
    depth = last[2] - last[1]
    return pl.pallas_call(
        functools.partial(own_kernel, levels, piece, last),
        out_shape=(
            jax.ShapeDtypeStruct((blocks, 2, width, samples), jnp.bfloat16),
            jax.ShapeDtypeStruct((out_rows, 2 * width), jnp.float32),
            *[jax.ShapeDtypeStruct((out_rows, n), jnp.bfloat16) for n in counts],
            jax.ShapeDtypeStruct((pairs, out_rows, 128), jnp.float32),
            *[jax.ShapeDtypeStruct((2 * width, head.shape[1]), jnp.bfloat16) for head in heads],
            piece_shape(piece, width, 2 * tiles),
            piece_shape(piece, width, 0),
            jax.ShapeDtypeStruct((width, 2 * depth), jnp.bfloat16),
            jax.ShapeDtypeStruct((blocks, 2 * width, 2 * depth), jnp.bfloat16),
        ),
        in_specs=[WHOLE, WHOLE, HBM] + [WHOLE] * levels,
        out_specs=(WHOLE,) * (7 + len(counts) + levels),
        scratch_shapes=[
            pltpu.VMEM((2, blocks, 2, width, samples), jnp.bfloat16),
            pltpu.VMEM((blocks, 2, width, samples), jnp.bfloat16),
            pltpu.VMEM((2 * blocks * blocks, 2, 2 * width), jnp.float32),
            pltpu.SemaphoreType.DMA((2, blocks, 2)),
        ],
        compiler_params=pltpu.CompilerParams(vmem_limit_bytes=16 << 20),
        cost_estimate=pl.CostEstimate(
            flops=64 * blocks * blocks * width * width * samples,
            bytes_accessed=12 * blocks * width * samples,
            transcendentals=0,
        ),
        name="own_level",
    )(groups, position_input, pltpu.with_memory_space_constraint(volts, pltpu.HBM), *heads)


def add_lags(rows, pick_ref, sums_ref):
    lags = jnp.concatenate(rows, axis=0)
    lags = jnp.concatenate([lags, conjugate_lags(lags)], axis=0)
    return sums_ref[...] + group_sums(pick_ref[...], lags)


def pair_kernel(levels, pieces, pick_ref, sums_ref, panel_ref, *refs):
    count = levels * len(pieces)
    partner_refs, more_refs, out_ref = refs[:count], refs[count:-1], refs[-1]
    _, _, width, samples = panel_ref.shape
    rows = []
    for block in sorted({block for piece in pieces for block, _, _ in piece}):
        for level in range(levels):
            for a in range(panel_ref.shape[0]):
                real_part, imag_part = 0.0, 0.0
                for i, piece in enumerate(pieces):
                    partner = partner_refs[level * len(pieces) + i]
                    for (b, first, last), (start, end) in zip(piece, columns(piece)):
                        if b != block:
                            continue
                        x_re, x_im = panel_ref[a, 0, :, first:last], panel_ref[a, 1, :, first:last]
                        y_re = partner[:width, start:end]
                        y_im = partner[width : 2 * width, start:end]
                        real_part = real_part + (product(x_re, y_re) + product(x_im, y_im))
                        imag_part = imag_part + (product(x_im, y_re) - product(x_re, y_im))
                rows.append(lag_rows(jnp.stack([real_part, imag_part])) * (1.0 / samples))
    sums = add_lags(rows, pick_ref, sums_ref)
    for more_ref in more_refs:
        terms = partner_refs[-1][2 * width :, :].astype(jnp.float32)
        half = terms.shape[0] // 2
        sums = sums + group_sums(more_ref[...], terms[:half] + terms[half:])
    out_ref[...] = sums


def rows_of(x):
    return [x[i : i + 1] for i in range(x.shape[0])]


def last_kernel(levels, samples, mask_ref, sums_ref, panel_ref, *refs):
    partner_refs, out_refs = refs[:levels], refs[levels:]
    blocks, rows_both, _ = panel_ref.shape
    width = rows_both // 2
    rows = []
    for partner_ref in partner_refs:
        for a in range(blocks):
            tiles = product(panel_ref[a], partner_ref[...]).reshape(2, width, width)
            rows += sheared_eights(tiles)
    lags = jnp.sum(jnp.stack(rows), axis=1) * (1.0 / samples)
    sums = sums_ref[...]
    blocks_wide = sums.shape[1] // 128
    for i, row in enumerate([*rows_of(lags), *rows_of(reversed_lags(lags))]):
        mask = jnp.concatenate([mask_ref[i]] * blocks_wide, axis=1)
        sums = sums + mask * row
    share = sums.shape[0] // len(out_refs)
    for place, out_ref in enumerate(out_refs):
        out_ref[...] = sums[place * share : (place + 1) * share]


def pair_call(kernel, inputs, work, shares=1):
    rows, width = inputs[1].shape
    return pl.pallas_call(
        kernel,
        out_shape=[jax.ShapeDtypeStruct((rows // shares, width), jnp.float32)] * shares,
        in_specs=[WHOLE] * len(inputs),
        out_specs=[WHOLE] * shares,
        compiler_params=pltpu.CompilerParams(vmem_limit_bytes=16 << 20),
        cost_estimate=pl.CostEstimate(flops=work, bytes_accessed=4 << 20, transcendentals=0),
        name="pair_level",
    )(*inputs)


def finish_kernel(levels, *refs):
    part_refs, out_ref = refs[:-1], refs[-1]
    mine = parity(lax.axis_index("inp"), levels)
    groups, channels, parts, lags = out_ref.shape
    sums = [None, None]
    for distance, part_ref in enumerate(reversed(part_refs)):
        side = distance.bit_count() % 2
        sums[side] = part_ref[...] if sums[side] is None else sums[side] + part_ref[...]
    for f in range(channels):
        total = jnp.where(mine == f, sums[0], sums[1])
        for g in range(groups):
            out_ref[g, f] = total[g * parts : (g + 1) * parts, :lags]


def finish(parts, levels, lags):
    return pl.pallas_call(
        functools.partial(finish_kernel, levels),
        out_shape=jax.ShapeDtypeStruct((RG_DEV, 2, 2, lags), jnp.float32),
        in_specs=[WHOLE] * len(parts),
        out_specs=WHOLE,
        compiler_params=pltpu.CompilerParams(vmem_limit_bytes=8 << 20),
        name="finish",
    )(*parts)


def on_device(volts, position_input, tile_group):
    blocks, width = position_input.shape
    samples = volts.shape[3]
    devices = lax.axis_size("inp")
    levels = devices.bit_length() - 1
    out_rows = devices * RG_DEV * 2
    eighth = samples // 8
    head = [(0, 0, 2 * eighth)]
    rest = [(0, 2 * eighth, samples), (1, 0, 2 * eighth)]
    tail = [(1, 2 * eighth, 6 * eighth)]
    last = (1, 6 * eighth, samples)
    by_block = tile_group.transpose(0, 2, 1)
    partner_of = [functools.partial(xor_permute, axis="inp", distance=1 << l) for l in range(levels)]
    sent, second = early_pieces(position_input, volts, by_block, head, rest, levels)
    head_arrived = [send(sent) for send in partner_of]
    rest_arrived = [send(second) for send in partner_of]
    panel, sums, neighbour, both, single, masks, *sent = own_level(
        by_block, position_input, volts, head_arrived, tail, last, out_rows
    )
    head_ordered, (more, piece, last_piece, last_panel) = sent[:levels], sent[levels:]
    tail_arrived = [send(piece) for send in partner_of[:-1]] + [partner_of[-1](more)]
    last_arrived = [send(last_piece) for send in partner_of]

    flops = 8 * levels * blocks * width * width
    arrived = [piece for pair in zip(head_ordered, rest_arrived) for piece in pair]
    (sums,) = pair_call(
        functools.partial(pair_kernel, levels, [head, rest]),
        [both, sums, panel, *arrived],
        flops * 10 * eighth,
    )
    (sums,) = pair_call(
        functools.partial(pair_kernel, levels, [tail]),
        [single, sums, panel, *tail_arrived, neighbour],
        flops * 4 * eighth,
    )
    parts = pair_call(
        functools.partial(last_kernel, levels, samples),
        [masks, sums, last_panel, *last_arrived],
        flops * 2 * eighth,
        devices,
    )
    parts = [
        xor_permute(parts[distance], "inp", distance) for distance in reversed(range(1, devices))
    ] + [parts[0]]
    return finish(parts, levels, 2 * width - 1)


def solution(mesh):
    return jax.shard_map(
        on_device,
        mesh=mesh,
        in_specs=(P("freq", None, "inp", None), P("inp", None), P("inp", None, None)),
        out_specs=P("inp", "freq", None, None),
        check_vma=False,
    )
```

```python
import functools

import jax
import jax.numpy as jnp
from jax import lax
from jax.experimental import pallas as pl
from jax.experimental.pallas import tpu as pltpu
from jax.sharding import PartitionSpec as P

RG_DEV = 8
GROUP_ROWS = 16
HBM = pl.BlockSpec(memory_space=pltpu.HBM)
WHOLE = pl.BlockSpec(memory_space=pltpu.VMEM)


def xor_permute(x, axis, distance):
    return lax.ppermute(x, axis, [(i, i ^ distance) for i in range(lax.axis_size(axis))])


def parity(index, levels):
    bits = index & 1
    for level in range(1, levels):
        bits = bits ^ ((index >> level) & 1)
    return bits


def order_matrix(position_row):
    width = position_row.shape[-1]
    by_position = jnp.transpose(jnp.broadcast_to(position_row, (width, width)))
    inputs = lax.broadcasted_iota(jnp.int32, (width, width), 1)
    return (by_position == inputs).astype(jnp.float32).astype(jnp.bfloat16)


def product(x, y):
    return lax.dot_general(x, y, (((1,), (1,)), ((), ())), preferred_element_type=jnp.float32)


def lag_rows(tiles):
    count, width, _ = tiles.shape
    half = width // 2
    low, high = tiles[:, :half], tiles[:, half:]
    sheared = jnp.concatenate(
        [
            high[:, :, :half],
            high[:, :, half:] + low[:, :, :half],
            low[:, :, half:],
            jnp.zeros((count, half, half), jnp.float32),
        ],
        axis=2,
    )
    rows = half
    while rows > 8:
        rows //= 2
        upper = sheared[:, :rows].reshape(count * rows, 2 * width)
        upper = pltpu.roll(upper, rows, 1).reshape(count, rows, 2 * width)
        sheared = upper + sheared[:, rows:]
    flat = sheared.reshape(count * rows, 2 * width)
    sublane = lax.broadcasted_iota(jnp.int32, flat.shape, 0) % 8
    while rows > 1:
        rows //= 2
        flat = jnp.where((sublane & rows) == 0, pltpu.roll(flat, rows, 1), flat)
    return jnp.sum(flat.reshape(count, 8, 2 * width), axis=1)


def tile_lags(x_re, x_im, y_re, y_im, samples):
    real_part = product(x_re, y_re) + product(x_im, y_im)
    imag_part = product(x_im, y_re) - product(x_re, y_im)
    return lag_rows(jnp.stack([real_part, imag_part])) * (1.0 / samples)


def split_rows(x):
    first = x.astype(jnp.bfloat16).astype(jnp.float32)
    rest = x - first
    second = rest.astype(jnp.bfloat16).astype(jnp.float32)
    return jnp.concatenate([first, second, rest - second], axis=0)


def anti_identity(size):
    place = lax.broadcasted_iota(jnp.int32, (size, size), 0) + lax.broadcasted_iota(
        jnp.int32, (size, size), 1
    )
    return (place == size - 1).astype(jnp.float32).astype(jnp.bfloat16)


def turn_lags(terms):
    count, width = terms.shape
    lanes = 128
    spans = range(0, width, lanes)
    terms = jnp.concatenate([terms[:, first : first + lanes] for first in spans], axis=0)
    terms = jnp.dot(
        terms.astype(jnp.bfloat16), anti_identity(lanes), preferred_element_type=jnp.float32
    )
    blocks = [terms[count * i : count * (i + 1)] for i in reversed(range(len(spans)))]
    return pltpu.roll(jnp.concatenate(blocks, axis=1), width - 1, 1)


def conjugate_lags(lags):
    count = lags.shape[0]
    turned = turn_lags(split_rows(lags))
    turned = turned[:count] + turned[count : 2 * count] + turned[2 * count :]
    odd = lax.broadcasted_iota(jnp.int32, turned.shape, 0) % 2 == 1
    return jnp.where(odd, -turned, turned)


def reversed_lags(lags):
    count, width = lags.shape
    lanes = 128
    rows = jnp.pad(lags, ((0, -count % 8), (0, 0)))
    index = lanes - 1 - lax.broadcasted_iota(jnp.int32, (rows.shape[0], lanes), 1)
    blocks = [
        jnp.take_along_axis(
            rows[:, first : first + lanes], index, axis=1, mode="promise_in_bounds"
        )
        for first in reversed(range(0, width, lanes))
    ]
    return pltpu.roll(jnp.concatenate(blocks, axis=1), width - 1, 1)[:count]


def sheared_eights(tiles):
    count, width, _ = tiles.shape
    half = width // 2
    low, high = tiles[:, :half], tiles[:, half:]
    sheared = jnp.concatenate(
        [
            low[:, :, :half],
            low[:, :, half:] + high[:, :, :half],
            high[:, :, half:],
            jnp.zeros((count, half, half), jnp.float32),
        ],
        axis=2,
    )
    rows = half
    while rows > 8:
        rows //= 2
        lower = sheared[:, rows:].reshape(count * rows, 2 * width)
        lower = pltpu.roll(lower, rows, 1).reshape(count, rows, 2 * width)
        sheared = sheared[:, :rows] + lower
    return [pltpu.roll(sheared[i], 0, 1, stride=1, stride_axis=0) for i in range(count)]


def group_block(groups, columns=128):
    rows = jnp.concatenate([groups[b] for b in range(groups.shape[0])], axis=0)
    lines, lanes = rows.shape
    return jnp.pad(rows, ((0, GROUP_ROWS - lines), (0, columns - lanes)))


def target_rows(groups):
    return groups ^ (lax.axis_index("inp") * RG_DEV)


def pick_matrix(entries, rows):
    count = len(entries)
    shape = (rows, 3 * count)
    row = lax.broadcasted_iota(jnp.int32, shape, 0)
    column = lax.broadcasted_iota(jnp.int32, shape, 1) % count
    pick = jnp.zeros(shape, jnp.float32)
    for j, (targets, line, lane, part) in enumerate(entries):
        target = targets[line : line + 1, lane : lane + 1] + part * (rows // 2)
        target = jnp.broadcast_to(target, shape)
        pick = jnp.where(jnp.logical_and(column == j, row == target), 1.0, pick)
    return pick.astype(jnp.bfloat16)


def row_masks(entries, rows):
    row = lax.broadcasted_iota(jnp.int32, (rows, 128), 0)
    masks = []
    for targets, line, lane, _ in entries:
        target = jnp.broadcast_to(targets[line : line + 1, lane : lane + 1], row.shape)
        masks.append((row == target).astype(jnp.float32))
    return jnp.stack(masks)


def pick_matrices(groups, heads, blocks, out_rows):
    own = target_rows(group_block(groups))
    others = [target_rows(head.astype(jnp.float32).astype(jnp.int32)) for head in heads]
    groups_all = out_rows // 2

    def pairs(b):
        order = [(level, a, p) for level in range(len(heads)) for a in range(blocks) for p in range(2)]
        forward = [(own, a * blocks + b, level + 1, p) for level, a, p in order]
        turned = [(others[level], b * blocks + a, level + 1, p) for level, a, p in order]
        return forward, turned

    forward, turned = zip(*[pairs(b) for b in range(blocks)])
    tiles = [
        [(targets, line, 0, p) for line in range(blocks * blocks) for p in range(2)]
        for targets in (own, others[-1])
    ]
    both = [entry for side in (forward, turned) for block in side for entry in block]
    return [
        pick_matrix(tiles[0], out_rows),
        pick_matrix(tiles[1], out_rows),
        pick_matrix(both, out_rows),
        pick_matrix(forward[-1] + turned[-1], out_rows),
        row_masks(forward[-1][::2] + turned[-1][::2], groups_all),
    ]


def group_sums(pick, lags):
    terms = split_rows(lags).astype(jnp.bfloat16)
    return jnp.dot(pick, terms, preferred_element_type=jnp.float32)


def columns(piece):
    spans, start = [], 0
    for _, first, last in piece:
        spans.append((start, start + last - first))
        start += last - first
    return spans


def piece_shape(piece, width, more):
    return jax.ShapeDtypeStruct((2 * width + more, columns(piece)[-1][1]), jnp.bfloat16)


def load_piece(piece, other, width, volts_ref, raw, in_sem):
    blocks = sorted({block for block, _, _ in piece})
    loads = []
    for i, block in enumerate(blocks):
        start = min(first for b, first, _ in piece if b == block)
        end = max(last for b, _, last in piece if b == block)
        for c in range(2):
            load = pltpu.make_async_copy(
                volts_ref.at[other, c, pl.ds(block * width, width), pl.ds(start, end - start)],
                raw.at[i, c, :, pl.ds(start, end - start)],
                in_sem.at[i, c],
            )
            load.start()
            loads.append((i, block, c, load))
    return loads


def order_piece(piece, loads, position, raw, out_ref):
    width = position.shape[1]
    orders = {
        block: order_matrix(position[block : block + 1, :]) for block in sorted({l[1] for l in loads})
    }
    for i, block, c, load in loads:
        load.wait()
        for (b, first, last), (start, end) in zip(piece, columns(piece)):
            if b == block:
                out_ref[c * width : (c + 1) * width, start:end] = jnp.dot(
                    orders[block], raw[i, c, :, first:last], preferred_element_type=jnp.float32
                ).astype(jnp.bfloat16)


def head_kernel(levels, piece, position_ref, volts_ref, group_ref, head_ref, *scratch):
    position, groups, small_sem, in_sem = scratch
    other = 1 - parity(lax.axis_index("inp"), levels)
    width = position.shape[1]
    ((block, first, last),) = piece
    smalls = [
        pltpu.make_async_copy(position_ref, position, small_sem.at[0]),
        pltpu.make_async_copy(group_ref, groups, small_sem.at[1]),
    ]
    loads = [
        pltpu.make_async_copy(
            volts_ref.at[other, c, pl.ds(block * width, width), pl.ds(first, last - first)],
            head_ref.at[pl.ds(c * width, width), :],
            in_sem.at[c],
        )
        for c in range(2)
    ]
    for copy in smalls + loads:
        copy.start()
    for copy in smalls:
        copy.wait()
    rows = group_block(groups[...], last - first)
    line = lax.broadcasted_iota(jnp.int32, rows.shape, 0)
    own_row = jnp.broadcast_to(position[block : block + 1, :], rows.shape)
    rows = jnp.where(line == groups.shape[0] ** 2, own_row, rows)
    head_ref[2 * width :, :] = rows.astype(jnp.float32).astype(jnp.bfloat16)
    for copy in loads:
        copy.wait()


def rest_kernel(levels, piece, position_ref, volts_ref, _, out_ref, position, raw, small_sem, in_sem):
    other = 1 - parity(lax.axis_index("inp"), levels)
    load_position = pltpu.make_async_copy(position_ref, position, small_sem)
    load_position.start()
    loads = load_piece(piece, other, position.shape[1], volts_ref, raw, in_sem)
    load_position.wait()
    order_piece(piece, loads, position, raw, out_ref)


def early_pieces(position_input, volts, groups, head, rest, levels):
    blocks, width = position_input.shape
    samples = volts.shape[3]
    assert columns(head)[-1][1] == width
    in_hbm = [pltpu.with_memory_space_constraint(x, pltpu.HBM) for x in (position_input, volts)]
    position = pltpu.VMEM(position_input.shape, jnp.int32)
    semaphore = pltpu.SemaphoreType.DMA
    sent = pl.pallas_call(
        functools.partial(head_kernel, levels, head),
        out_shape=piece_shape(head, width, GROUP_ROWS),
        in_specs=[HBM] * 3,
        out_specs=WHOLE,
        scratch_shapes=[
            position,
            pltpu.VMEM(groups.shape, jnp.int32),
            semaphore((2,)),
            semaphore((2,)),
        ],
        compiler_params=pltpu.CompilerParams(vmem_limit_bytes=8 << 20),
        cost_estimate=pl.CostEstimate(flops=0, bytes_accessed=1 << 20, transcendentals=0),
        name="first_piece",
    )(*in_hbm, pltpu.with_memory_space_constraint(groups, pltpu.HBM))
    second = pl.pallas_call(
        functools.partial(rest_kernel, levels, rest),
        out_shape=piece_shape(rest, width, 0),
        in_specs=[HBM, HBM, pl.BlockSpec(memory_space=pl.ANY)],
        out_specs=WHOLE,
        scratch_shapes=[
            position,
            pltpu.VMEM((blocks, 2, width, samples), jnp.bfloat16),
            semaphore(()),
            semaphore((blocks, 2)),
        ],
        compiler_params=pltpu.CompilerParams(vmem_limit_bytes=16 << 20),
        cost_estimate=pl.CostEstimate(
            flops=4 * width * width * columns(rest)[-1][1],
            bytes_accessed=4 << 20,
            transcendentals=0,
        ),
        name="second_piece",
    )(*in_hbm, sent)
    return sent, second


def own_kernel(levels, piece, last, group_ref, position_ref, volts_ref, *refs):
    head_refs, refs = refs[:levels], refs[levels:]
    panel_ref, sums_ref, *refs, raw, other_panel, lags_ref, in_sem = refs
    pick_refs, ordered_refs, refs = refs[:4], refs[4 : 4 + levels], refs[4 + levels :]
    more_ref, piece_ref, *last_refs, last_panel_ref = refs
    blocks, _, width, _ = panel_ref.shape
    mine = parity(lax.axis_index("inp"), levels)
    channels = (mine, 1 - mine)
    loads = [
        [
            [
                pltpu.make_async_copy(
                    volts_ref.at[channels[f], c, pl.ds(b * width, width)],
                    raw.at[f, b, c],
                    in_sem.at[f, b, c],
                )
                for c in range(2)
            ]
            for b in range(blocks)
        ]
        for f in range(2)
    ]
    for f in range(2):
        for b in range(blocks):
            for c in range(2):
                loads[f][b][c].start()
    orders = [order_matrix(position_ref[b : b + 1, :]) for b in range(blocks)]
    for f, panel in enumerate((panel_ref, other_panel)):
        for b in range(blocks):
            for c in range(2):
                loads[f][b][c].wait()
                panel[b, c] = jnp.dot(
                    orders[b], raw[f, b, c], preferred_element_type=jnp.float32
                ).astype(jnp.bfloat16)

        def one_tile(index, carry, panel=panel, f=f):
            a = index // blocks
            b = index % blocks
            lags = tile_lags(panel[a, 0], panel[a, 1], panel[b, 0], panel[b, 1], panel.shape[3])
            center = lax.broadcasted_iota(jnp.int32, lags.shape, 1) == width - 1
            lags_ref[f * blocks * blocks + index] = jnp.where(
                jnp.logical_and(center, a == b), 0.0, lags
            )
            return carry

        lax.fori_loop(0, blocks * blocks, one_tile, 0)
    tiles = blocks * blocks
    lags = jnp.concatenate([lags_ref[i] for i in range(tiles)], axis=0)
    heads = [head_ref[2 * width :, :] for head_ref in head_refs]
    for head, head_ref, ordered_ref in zip(heads, head_refs, ordered_refs):
        positions = head.astype(jnp.float32).astype(jnp.int32)[blocks**2 : blocks**2 + 1]
        order = order_matrix(positions)
        for c in range(2):
            rows = head_ref[c * width : (c + 1) * width, :]
            rows = jnp.dot(order, rows, preferred_element_type=jnp.float32)
            ordered_ref[c * width : (c + 1) * width, :] = rows.astype(jnp.bfloat16)
    own_pick, *picks = pick_matrices(group_ref[...], heads, blocks, sums_ref.shape[0])
    for pick_ref, pick in zip(pick_refs, picks):
        pick_ref[...] = pick
    sums_ref[...] = group_sums(own_pick, lags)
    for (block, first, end), (start, stop) in zip(piece, columns(piece)):
        for c in range(2):
            rows = other_panel[block, c, :, first:end]
            piece_ref[c * width : (c + 1) * width, start:stop] = rows
            more_ref[c * width : (c + 1) * width, start:stop] = rows
    lags = jnp.concatenate([lags_ref[tiles + i] for i in range(tiles)], axis=0)
    high = lags.astype(jnp.bfloat16).astype(jnp.float32)
    terms = jnp.concatenate([high, lags - high], axis=0)
    more_ref[2 * width :, :] = terms.astype(jnp.bfloat16)
    for (block, first, end), last_ref in zip(last, last_refs):
        for c in range(2):
            depth = end - first
            last_ref[:, c * depth : (c + 1) * depth] = other_panel[block, c, :, first:end]
    turn = anti_identity(width)
    for a in range(blocks):
        start = 0
        for _, first, end in last:
            real_part, imag_part = [
                jnp.dot(turn, panel_ref[a, c, :, first:end], preferred_element_type=jnp.float32)
                for c in range(2)
            ]
            middle, stop = start + end - first, start + 2 * (end - first)
            last_panel_ref[a, :width, start:middle] = real_part.astype(jnp.bfloat16)
            last_panel_ref[a, :width, middle:stop] = imag_part.astype(jnp.bfloat16)
            last_panel_ref[a, width:, start:middle] = imag_part.astype(jnp.bfloat16)
            last_panel_ref[a, width:, middle:stop] = (-real_part).astype(jnp.bfloat16)
            start = stop


def own_level(groups, position_input, volts, heads, piece, last, out_rows):
    levels = len(heads)
    blocks, width = position_input.shape
    samples = volts.shape[3]
    pairs = 4 * levels * blocks
    tiles = 2 * blocks * blocks
    counts = (3 * tiles, 3 * pairs * blocks, 3 * pairs)
    depths = [2 * (end - first) for _, first, end in last]
    return pl.pallas_call(
        functools.partial(own_kernel, levels, piece, last),
        out_shape=(
            jax.ShapeDtypeStruct((blocks, 2, width, samples), jnp.bfloat16),
            jax.ShapeDtypeStruct((out_rows, 2 * width), jnp.float32),
            *[jax.ShapeDtypeStruct((out_rows, n), jnp.bfloat16) for n in counts],
            jax.ShapeDtypeStruct((pairs // 2, out_rows // 2, 128), jnp.float32),
            *[jax.ShapeDtypeStruct((2 * width, head.shape[1]), jnp.bfloat16) for head in heads],
            piece_shape(piece, width, 2 * tiles),
            piece_shape(piece, width, 0),
            *[jax.ShapeDtypeStruct((width, depth), jnp.bfloat16) for depth in depths],
            jax.ShapeDtypeStruct((blocks, 2 * width, sum(depths)), jnp.bfloat16),
        ),
        in_specs=[WHOLE, WHOLE, HBM] + [WHOLE] * levels,
        out_specs=(WHOLE,) * (6 + len(counts) + levels + len(last)),
        scratch_shapes=[
            pltpu.VMEM((2, blocks, 2, width, samples), jnp.bfloat16),
            pltpu.VMEM((blocks, 2, width, samples), jnp.bfloat16),
            pltpu.VMEM((2 * blocks * blocks, 2, 2 * width), jnp.float32),
            pltpu.SemaphoreType.DMA((2, blocks, 2)),
        ],
        compiler_params=pltpu.CompilerParams(vmem_limit_bytes=16 << 20),
        cost_estimate=pl.CostEstimate(
            flops=64 * blocks * blocks * width * width * samples,
            bytes_accessed=12 * blocks * width * samples,
            transcendentals=0,
        ),
        name="own_level",
    )(groups, position_input, pltpu.with_memory_space_constraint(volts, pltpu.HBM), *heads)


def add_lags(rows, pick_ref, sums_ref):
    lags = jnp.concatenate(rows, axis=0)
    lags = jnp.concatenate([lags, conjugate_lags(lags)], axis=0)
    return sums_ref[...] + group_sums(pick_ref[...], lags)


def pair_kernel(levels, pieces, passed, pick_ref, sums_ref, panel_ref, *refs):
    count = levels * len(pieces)
    out_ref = refs[-1 - passed]
    partner_refs, more_refs = refs[:count], refs[count : len(refs) - 1 - 2 * passed]
    _, _, width, samples = panel_ref.shape
    rows = []
    for block in sorted({block for piece in pieces for block, _, _ in piece}):
        for level in range(levels):
            for a in range(panel_ref.shape[0]):
                real_part, imag_part = 0.0, 0.0
                for i, piece in enumerate(pieces):
                    partner = partner_refs[level * len(pieces) + i]
                    for (b, first, last), (start, end) in zip(piece, columns(piece)):
                        if b != block:
                            continue
                        x_re, x_im = panel_ref[a, 0, :, first:last], panel_ref[a, 1, :, first:last]
                        y_re = partner[:width, start:end]
                        y_im = partner[width : 2 * width, start:end]
                        real_part = real_part + (product(x_re, y_re) + product(x_im, y_im))
                        imag_part = imag_part + (product(x_im, y_re) - product(x_re, y_im))
                rows.append(lag_rows(jnp.stack([real_part, imag_part])) * (1.0 / samples))
    sums = add_lags(rows, pick_ref, sums_ref)
    for more_ref in more_refs:
        terms = partner_refs[-1][2 * width :, :].astype(jnp.float32)
        half = terms.shape[0] // 2
        sums = sums + group_sums(more_ref[...], terms[:half] + terms[half:])
    out_ref[...] = sums


def last_kernel(levels, samples, cut, mask_ref, sums_ref, panel_ref, *refs):
    partner_refs, out_refs = refs[:levels], refs[levels:]
    blocks, rows_both, _ = panel_ref.shape
    width = rows_both // 2
    rows = []
    for partner_ref in partner_refs:
        for a in range(blocks):
            tiles = product(panel_ref[a, :, cut[0] : cut[1]], partner_ref[...])
            rows += sheared_eights(tiles.reshape(2, width, width))
    lags = jnp.sum(jnp.stack(rows), axis=1) * (1.0 / samples)
    turned = reversed_lags(lags)
    half = sums_ref.shape[0] // 2
    sums = [sums_ref[:half, :], sums_ref[half:, :]]
    count = lags.shape[0] // 2
    for i in range(count):
        forward = jnp.concatenate([mask_ref[i]] * (sums_ref.shape[1] // 128), axis=1)
        back = jnp.concatenate([mask_ref[count + i]] * (sums_ref.shape[1] // 128), axis=1)
        re, im = 2 * i, 2 * i + 1
        sums[0] = sums[0] + forward * lags[re : re + 1] + back * turned[re : re + 1]
        sums[1] = sums[1] + forward * lags[im : im + 1] - back * turned[im : im + 1]
    share = half // len(out_refs)
    for place, out_ref in enumerate(out_refs):
        for part in range(2):
            rows = sums[part][place * share : (place + 1) * share]
            out_ref[part * share : (part + 1) * share, :] = rows


def pair_call(kernel, inputs, work, shares=1, passed=()):
    rows, width = inputs[1].shape
    any_space = [pl.BlockSpec(memory_space=pl.ANY)] * len(passed)
    return pl.pallas_call(
        kernel,
        out_shape=[jax.ShapeDtypeStruct((rows // shares, width), jnp.float32)] * shares
        + [jax.ShapeDtypeStruct(x.shape, x.dtype) for x in passed],
        in_specs=[WHOLE] * len(inputs) + any_space,
        out_specs=[WHOLE] * shares + any_space,
        input_output_aliases={len(inputs) + i: shares + i for i in range(len(passed))},
        compiler_params=pltpu.CompilerParams(vmem_limit_bytes=16 << 20),
        cost_estimate=pl.CostEstimate(flops=work, bytes_accessed=4 << 20, transcendentals=0),
        name="pair_level",
    )(*inputs, *passed)


def finish_kernel(levels, *refs):
    part_refs, out_ref = refs[:-1], refs[-1]
    mine = parity(lax.axis_index("inp"), levels)
    groups, channels, parts, lags = out_ref.shape
    sums = [None, None]
    for distance, part_ref in enumerate(reversed(part_refs)):
        side = distance.bit_count() % 2
        sums[side] = part_ref[...] if sums[side] is None else sums[side] + part_ref[...]
    for f in range(channels):
        total = jnp.where(mine == f, sums[0], sums[1])
        for g in range(groups):
            for part in range(parts):
                row = part * groups + g
                out_ref[g, f, part : part + 1] = total[row : row + 1, :lags]


def finish(parts, levels, lags):
    return pl.pallas_call(
        functools.partial(finish_kernel, levels),
        out_shape=jax.ShapeDtypeStruct((RG_DEV, 2, 2, lags), jnp.float32),
        in_specs=[WHOLE] * len(parts),
        out_specs=WHOLE,
        compiler_params=pltpu.CompilerParams(vmem_limit_bytes=8 << 20),
        name="finish",
    )(*parts)


def on_device(volts, position_input, tile_group):
    blocks, width = position_input.shape
    samples = volts.shape[3]
    devices = lax.axis_size("inp")
    levels = devices.bit_length() - 1
    out_rows = devices * RG_DEV * 2
    eighth = samples // 8
    head = [(0, 0, 2 * eighth)]
    rest = [(0, 2 * eighth, samples), (1, 0, 2 * eighth)]
    tail = [(1, 2 * eighth, 6 * eighth)]
    last = [(1, 6 * eighth, 7 * eighth), (1, 7 * eighth, samples)]
    by_block = tile_group.transpose(0, 2, 1)
    partner_of = [functools.partial(xor_permute, axis="inp", distance=1 << l) for l in range(levels)]
    sent, second = early_pieces(position_input, volts, by_block, head, rest, levels)
    head_arrived = [send(sent) for send in partner_of]
    rest_arrived = [send(second) for send in partner_of]
    panel, sums, neighbour, both, single, masks, *sent = own_level(
        by_block, position_input, volts, head_arrived, tail, last, out_rows
    )
    head_ordered, (more, piece, *last_pieces, last_panel) = sent[:levels], sent[levels:]
    tail_arrived = [send(piece) for send in partner_of[:-1]] + [partner_of[-1](more)]

    flops = 8 * levels * blocks * width * width
    arrived = [piece for pair in zip(head_ordered, rest_arrived) for piece in pair]
    sums, *last_pieces = pair_call(
        functools.partial(pair_kernel, levels, [head, rest], len(last_pieces)),
        [both, sums, panel, *arrived],
        flops * 10 * eighth,
        passed=last_pieces,
    )
    last_arrived = [[send(piece) for send in partner_of] for piece in last_pieces]
    (sums,) = pair_call(
        functools.partial(pair_kernel, levels, [tail], 0),
        [single, sums, panel, *tail_arrived, neighbour],
        flops * 4 * eighth,
    )
    for i, arrived in enumerate(last_arrived):
        cut = (2 * eighth * i, 2 * eighth * (i + 1))
        parts = pair_call(
            functools.partial(last_kernel, levels, samples, cut),
            [masks, sums, last_panel, *arrived],
            flops * eighth,
            devices if i == len(last_arrived) - 1 else 1,
        )
        sums = parts[0]
    parts = [
        xor_permute(parts[distance], "inp", distance) for distance in reversed(range(1, devices))
    ] + [parts[0]]
    return finish(parts, levels, 2 * width - 1)


def solution(mesh):
    return jax.shard_map(
        on_device,
        mesh=mesh,
        in_specs=(P("freq", None, "inp", None), P("inp", None), P("inp", None, None)),
        out_specs=P("inp", "freq", None, None),
        check_vma=False,
    )
```

```python
import functools

import jax
import jax.numpy as jnp
from jax import lax
from jax.experimental import pallas as pl
from jax.experimental.pallas import tpu as pltpu
from jax.sharding import PartitionSpec as P

RG_DEV = 8
GROUP_ROWS = 16
HBM = pl.BlockSpec(memory_space=pltpu.HBM)
WHOLE = pl.BlockSpec(memory_space=pltpu.VMEM)


def xor_permute(x, axis, distance):
    return lax.ppermute(x, axis, [(i, i ^ distance) for i in range(lax.axis_size(axis))])


def parity(index, levels):
    bits = index & 1
    for level in range(1, levels):
        bits = bits ^ ((index >> level) & 1)
    return bits


def order_matrix(position_row):
    width = position_row.shape[-1]
    by_position = jnp.transpose(jnp.broadcast_to(position_row, (width, width)))
    inputs = lax.broadcasted_iota(jnp.int32, (width, width), 1)
    return (by_position == inputs).astype(jnp.float32).astype(jnp.bfloat16)


def product(x, y):
    return lax.dot_general(x, y, (((1,), (1,)), ((), ())), preferred_element_type=jnp.float32)


def lag_rows(tiles):
    count, width, _ = tiles.shape
    half = width // 2
    low, high = tiles[:, :half], tiles[:, half:]
    sheared = jnp.concatenate(
        [
            high[:, :, :half],
            high[:, :, half:] + low[:, :, :half],
            low[:, :, half:],
            jnp.zeros((count, half, half), jnp.float32),
        ],
        axis=2,
    )
    rows = half
    while rows > 8:
        rows //= 2
        upper = sheared[:, :rows].reshape(count * rows, 2 * width)
        upper = pltpu.roll(upper, rows, 1).reshape(count, rows, 2 * width)
        sheared = upper + sheared[:, rows:]
    flat = sheared.reshape(count * rows, 2 * width)
    sublane = lax.broadcasted_iota(jnp.int32, flat.shape, 0) % 8
    while rows > 1:
        rows //= 2
        flat = jnp.where((sublane & rows) == 0, pltpu.roll(flat, rows, 1), flat)
    return jnp.sum(flat.reshape(count, 8, 2 * width), axis=1)


def tile_lags(x_re, x_im, y_re, y_im, samples):
    real_part = product(x_re, y_re) + product(x_im, y_im)
    imag_part = product(x_im, y_re) - product(x_re, y_im)
    return lag_rows(jnp.stack([real_part, imag_part])) * (1.0 / samples)


def split_rows(x):
    first = x.astype(jnp.bfloat16).astype(jnp.float32)
    rest = x - first
    second = rest.astype(jnp.bfloat16).astype(jnp.float32)
    return jnp.concatenate([first, second, rest - second], axis=0)


def anti_identity(size):
    place = lax.broadcasted_iota(jnp.int32, (size, size), 0) + lax.broadcasted_iota(
        jnp.int32, (size, size), 1
    )
    return (place == size - 1).astype(jnp.float32).astype(jnp.bfloat16)


def turn_lags(terms):
    count, width = terms.shape
    lanes = 128
    spans = range(0, width, lanes)
    terms = jnp.concatenate([terms[:, first : first + lanes] for first in spans], axis=0)
    terms = jnp.dot(
        terms.astype(jnp.bfloat16), anti_identity(lanes), preferred_element_type=jnp.float32
    )
    blocks = [terms[count * i : count * (i + 1)] for i in reversed(range(len(spans)))]
    return pltpu.roll(jnp.concatenate(blocks, axis=1), width - 1, 1)


def conjugate_lags(lags):
    count = lags.shape[0]
    turned = turn_lags(split_rows(lags))
    turned = turned[:count] + turned[count : 2 * count] + turned[2 * count :]
    odd = lax.broadcasted_iota(jnp.int32, turned.shape, 0) % 2 == 1
    return jnp.where(odd, -turned, turned)


def reversed_lags(lags):
    count, width = lags.shape
    lanes = 128
    rows = jnp.pad(lags, ((0, -count % 8), (0, 0)))
    index = lanes - 1 - lax.broadcasted_iota(jnp.int32, (rows.shape[0], lanes), 1)
    blocks = [
        jnp.take_along_axis(
            rows[:, first : first + lanes], index, axis=1, mode="promise_in_bounds"
        )
        for first in reversed(range(0, width, lanes))
    ]
    return pltpu.roll(jnp.concatenate(blocks, axis=1), width - 1, 1)[:count]


def sheared_eights(tiles):
    count, width, _ = tiles.shape
    half = width // 2
    low, high = tiles[:, :half], tiles[:, half:]
    sheared = jnp.concatenate(
        [
            low[:, :, :half],
            low[:, :, half:] + high[:, :, :half],
            high[:, :, half:],
            jnp.zeros((count, half, half), jnp.float32),
        ],
        axis=2,
    )
    rows = half
    while rows > 8:
        rows //= 2
        lower = sheared[:, rows:].reshape(count * rows, 2 * width)
        lower = pltpu.roll(lower, rows, 1).reshape(count, rows, 2 * width)
        sheared = sheared[:, :rows] + lower
    return [pltpu.roll(sheared[i], 0, 1, stride=1, stride_axis=0) for i in range(count)]


def group_block(groups, columns=128):
    rows = jnp.concatenate([groups[b] for b in range(groups.shape[0])], axis=0)
    lines, lanes = rows.shape
    return jnp.pad(rows, ((0, GROUP_ROWS - lines), (0, columns - lanes)))


def target_rows(groups):
    return groups ^ (lax.axis_index("inp") * RG_DEV)


def pick_matrix(entries, rows):
    count = len(entries)
    shape = (rows, 3 * count)
    row = lax.broadcasted_iota(jnp.int32, shape, 0)
    column = lax.broadcasted_iota(jnp.int32, shape, 1) % count
    pick = jnp.zeros(shape, jnp.float32)
    for j, (targets, line, lane, part) in enumerate(entries):
        target = targets[line : line + 1, lane : lane + 1] + part * (rows // 2)
        target = jnp.broadcast_to(target, shape)
        pick = jnp.where(jnp.logical_and(column == j, row == target), 1.0, pick)
    return pick.astype(jnp.bfloat16)


def row_masks(entries, rows):
    row = lax.broadcasted_iota(jnp.int32, (rows, 128), 0)
    masks = []
    for targets, line, lane, _ in entries:
        target = jnp.broadcast_to(targets[line : line + 1, lane : lane + 1], row.shape)
        masks.append((row == target).astype(jnp.float32))
    return jnp.stack(masks)


def pick_matrices(groups, heads, blocks, out_rows):
    own = target_rows(group_block(groups))
    others = [target_rows(head.astype(jnp.float32).astype(jnp.int32)) for head in heads]
    groups_all = out_rows // 2

    def pairs(b):
        order = [(level, a, p) for level in range(len(heads)) for a in range(blocks) for p in range(2)]
        forward = [(own, a * blocks + b, level + 1, p) for level, a, p in order]
        turned = [(others[level], b * blocks + a, level + 1, p) for level, a, p in order]
        return forward, turned

    forward, turned = zip(*[pairs(b) for b in range(blocks)])
    tiles = [
        [(targets, line, 0, p) for line in range(blocks * blocks) for p in range(2)]
        for targets in (own, others[-1])
    ]
    both = [entry for side in (forward, turned) for block in side for entry in block]
    return [
        pick_matrix(tiles[0], out_rows),
        pick_matrix(tiles[1], out_rows),
        pick_matrix(both, out_rows),
        pick_matrix(forward[-1] + turned[-1], out_rows),
        row_masks(forward[-1][::2] + turned[-1][::2], groups_all),
    ]


def group_sums(pick, lags):
    terms = split_rows(lags).astype(jnp.bfloat16)
    return jnp.dot(pick, terms, preferred_element_type=jnp.float32)


def columns(piece):
    spans, start = [], 0
    for _, first, last in piece:
        spans.append((start, start + last - first))
        start += last - first
    return spans


def piece_shape(piece, width, more):
    return jax.ShapeDtypeStruct((2 * width + more, columns(piece)[-1][1]), jnp.bfloat16)


def load_piece(piece, other, width, volts_ref, raw, in_sem):
    blocks = sorted({block for block, _, _ in piece})
    loads = []
    for i, block in enumerate(blocks):
        start = min(first for b, first, _ in piece if b == block)
        end = max(last for b, _, last in piece if b == block)
        for c in range(2):
            load = pltpu.make_async_copy(
                volts_ref.at[other, c, pl.ds(block * width, width), pl.ds(start, end - start)],
                raw.at[i, c, :, pl.ds(start, end - start)],
                in_sem.at[i, c],
            )
            load.start()
            loads.append((i, block, c, load))
    return loads


def order_piece(piece, loads, position, raw, out_ref):
    width = position.shape[1]
    orders = {
        block: order_matrix(position[block : block + 1, :]) for block in sorted({l[1] for l in loads})
    }
    for i, block, c, load in loads:
        load.wait()
        for (b, first, last), (start, end) in zip(piece, columns(piece)):
            if b == block:
                out_ref[c * width : (c + 1) * width, start:end] = jnp.dot(
                    orders[block], raw[i, c, :, first:last], preferred_element_type=jnp.float32
                ).astype(jnp.bfloat16)


def head_kernel(levels, piece, position_ref, volts_ref, group_ref, head_ref, *scratch):
    position, groups, small_sem, in_sem = scratch
    other = 1 - parity(lax.axis_index("inp"), levels)
    width = position.shape[1]
    ((block, first, last),) = piece
    smalls = [
        pltpu.make_async_copy(position_ref, position, small_sem.at[0]),
        pltpu.make_async_copy(group_ref, groups, small_sem.at[1]),
    ]
    loads = [
        pltpu.make_async_copy(
            volts_ref.at[other, c, pl.ds(block * width, width), pl.ds(first, last - first)],
            head_ref.at[pl.ds(c * width, width), :],
            in_sem.at[c],
        )
        for c in range(2)
    ]
    for copy in smalls + loads:
        copy.start()
    for copy in smalls:
        copy.wait()
    rows = group_block(groups[...], last - first)
    line = lax.broadcasted_iota(jnp.int32, rows.shape, 0)
    own_row = jnp.broadcast_to(position[block : block + 1, :], rows.shape)
    rows = jnp.where(line == groups.shape[0] ** 2, own_row, rows)
    head_ref[2 * width :, :] = rows.astype(jnp.float32).astype(jnp.bfloat16)
    for copy in loads:
        copy.wait()


def rest_kernel(levels, piece, position_ref, volts_ref, _, out_ref, position, raw, small_sem, in_sem):
    other = 1 - parity(lax.axis_index("inp"), levels)
    load_position = pltpu.make_async_copy(position_ref, position, small_sem)
    load_position.start()
    loads = load_piece(piece, other, position.shape[1], volts_ref, raw, in_sem)
    load_position.wait()
    order_piece(piece, loads, position, raw, out_ref)


def early_pieces(position_input, volts, groups, head, rest, levels):
    blocks, width = position_input.shape
    samples = volts.shape[3]
    assert columns(head)[-1][1] == width
    in_hbm = [pltpu.with_memory_space_constraint(x, pltpu.HBM) for x in (position_input, volts)]
    position = pltpu.VMEM(position_input.shape, jnp.int32)
    semaphore = pltpu.SemaphoreType.DMA
    sent = pl.pallas_call(
        functools.partial(head_kernel, levels, head),
        out_shape=piece_shape(head, width, GROUP_ROWS),
        in_specs=[HBM] * 3,
        out_specs=WHOLE,
        scratch_shapes=[
            position,
            pltpu.VMEM(groups.shape, jnp.int32),
            semaphore((2,)),
            semaphore((2,)),
        ],
        compiler_params=pltpu.CompilerParams(vmem_limit_bytes=8 << 20),
        cost_estimate=pl.CostEstimate(flops=0, bytes_accessed=1 << 20, transcendentals=0),
        name="first_piece",
    )(*in_hbm, pltpu.with_memory_space_constraint(groups, pltpu.HBM))
    second = pl.pallas_call(
        functools.partial(rest_kernel, levels, rest),
        out_shape=piece_shape(rest, width, 0),
        in_specs=[HBM, HBM, pl.BlockSpec(memory_space=pl.ANY)],
        out_specs=WHOLE,
        scratch_shapes=[
            position,
            pltpu.VMEM((blocks, 2, width, samples), jnp.bfloat16),
            semaphore(()),
            semaphore((blocks, 2)),
        ],
        compiler_params=pltpu.CompilerParams(vmem_limit_bytes=16 << 20),
        cost_estimate=pl.CostEstimate(
            flops=4 * width * width * columns(rest)[-1][1],
            bytes_accessed=4 << 20,
            transcendentals=0,
        ),
        name="second_piece",
    )(*in_hbm, sent)
    return sent, second


def own_kernel(levels, piece, last, group_ref, position_ref, volts_ref, *refs):
    head_refs, refs = refs[:levels], refs[levels:]
    panel_ref, sums_ref, *refs, raw, other_panel, lags_ref, in_sem = refs
    pick_refs, ordered_refs, refs = refs[:4], refs[4 : 4 + levels], refs[4 + levels :]
    more_ref, piece_ref, *last_refs, joined_ref, last_panel_ref = refs
    blocks, _, width, _ = panel_ref.shape
    mine = parity(lax.axis_index("inp"), levels)
    channels = (mine, 1 - mine)
    loads = [
        [
            [
                pltpu.make_async_copy(
                    volts_ref.at[channels[f], c, pl.ds(b * width, width)],
                    raw.at[f, b, c],
                    in_sem.at[f, b, c],
                )
                for c in range(2)
            ]
            for b in range(blocks)
        ]
        for f in range(2)
    ]
    for f in range(2):
        for b in range(blocks):
            for c in range(2):
                loads[f][b][c].start()
    orders = [order_matrix(position_ref[b : b + 1, :]) for b in range(blocks)]
    for f, panel in enumerate((panel_ref, other_panel)):
        for b in range(blocks):
            for c in range(2):
                loads[f][b][c].wait()
                panel[b, c] = jnp.dot(
                    orders[b], raw[f, b, c], preferred_element_type=jnp.float32
                ).astype(jnp.bfloat16)

        def one_tile(index, carry, panel=panel, f=f):
            a = index // blocks
            b = index % blocks
            lags = tile_lags(panel[a, 0], panel[a, 1], panel[b, 0], panel[b, 1], panel.shape[3])
            center = lax.broadcasted_iota(jnp.int32, lags.shape, 1) == width - 1
            lags_ref[f * blocks * blocks + index] = jnp.where(
                jnp.logical_and(center, a == b), 0.0, lags
            )
            return carry

        lax.fori_loop(0, blocks * blocks, one_tile, 0)
    tiles = blocks * blocks
    lags = jnp.concatenate([lags_ref[i] for i in range(tiles)], axis=0)
    heads = [head_ref[2 * width :, :] for head_ref in head_refs]
    for head, head_ref, ordered_ref in zip(heads, head_refs, ordered_refs):
        positions = head.astype(jnp.float32).astype(jnp.int32)[blocks**2 : blocks**2 + 1]
        order = order_matrix(positions)
        for c in range(2):
            rows = head_ref[c * width : (c + 1) * width, :]
            rows = jnp.dot(order, rows, preferred_element_type=jnp.float32)
            ordered_ref[c * width : (c + 1) * width, :] = rows.astype(jnp.bfloat16)
    own_pick, *picks = pick_matrices(group_ref[...], heads, blocks, sums_ref.shape[0])
    for pick_ref, pick in zip(pick_refs, picks):
        pick_ref[...] = pick
    sums_ref[...] = group_sums(own_pick, lags)
    for (block, first, end), (start, stop) in zip(piece, columns(piece)):
        for c in range(2):
            rows = other_panel[block, c, :, first:end]
            piece_ref[c * width : (c + 1) * width, start:stop] = rows
            more_ref[c * width : (c + 1) * width, start:stop] = rows
    lags = jnp.concatenate([lags_ref[tiles + i] for i in range(tiles)], axis=0)
    high = lags.astype(jnp.bfloat16).astype(jnp.float32)
    terms = jnp.concatenate([high, lags - high], axis=0)
    more_ref[2 * width :, :] = terms.astype(jnp.bfloat16)
    start = 0
    for (block, first, end), last_ref in zip(last, last_refs):
        for c in range(2):
            depth = end - first
            rows = other_panel[block, c, :, first:end]
            last_ref[:, c * depth : (c + 1) * depth] = rows
            joined_ref[:, start : start + depth] = rows
            start += depth
    turn = anti_identity(width)
    for a in range(blocks):
        start = 0
        for _, first, end in last:
            real_part, imag_part = [
                jnp.dot(turn, panel_ref[a, c, :, first:end], preferred_element_type=jnp.float32)
                for c in range(2)
            ]
            middle, stop = start + end - first, start + 2 * (end - first)
            last_panel_ref[a, :width, start:middle] = real_part.astype(jnp.bfloat16)
            last_panel_ref[a, :width, middle:stop] = imag_part.astype(jnp.bfloat16)
            last_panel_ref[a, width:, start:middle] = imag_part.astype(jnp.bfloat16)
            last_panel_ref[a, width:, middle:stop] = (-real_part).astype(jnp.bfloat16)
            start = stop


def own_level(groups, position_input, volts, heads, piece, last, out_rows):
    levels = len(heads)
    blocks, width = position_input.shape
    samples = volts.shape[3]
    pairs = 4 * levels * blocks
    tiles = 2 * blocks * blocks
    counts = (3 * tiles, 3 * pairs * blocks, 3 * pairs)
    depths = [2 * (end - first) for _, first, end in last]
    return pl.pallas_call(
        functools.partial(own_kernel, levels, piece, last),
        out_shape=(
            jax.ShapeDtypeStruct((blocks, 2, width, samples), jnp.bfloat16),
            jax.ShapeDtypeStruct((out_rows, 2 * width), jnp.float32),
            *[jax.ShapeDtypeStruct((out_rows, n), jnp.bfloat16) for n in counts],
            jax.ShapeDtypeStruct((pairs // 2, out_rows // 2, 128), jnp.float32),
            *[jax.ShapeDtypeStruct((2 * width, head.shape[1]), jnp.bfloat16) for head in heads],
            piece_shape(piece, width, 2 * tiles),
            piece_shape(piece, width, 0),
            *[jax.ShapeDtypeStruct((width, depth), jnp.bfloat16) for depth in depths],
            jax.ShapeDtypeStruct((width, sum(depths)), jnp.bfloat16),
            jax.ShapeDtypeStruct((blocks, 2 * width, sum(depths)), jnp.bfloat16),
        ),
        in_specs=[WHOLE, WHOLE, HBM] + [WHOLE] * levels,
        out_specs=(WHOLE,) * (7 + len(counts) + levels + len(last)),
        scratch_shapes=[
            pltpu.VMEM((2, blocks, 2, width, samples), jnp.bfloat16),
            pltpu.VMEM((blocks, 2, width, samples), jnp.bfloat16),
            pltpu.VMEM((2 * blocks * blocks, 2, 2 * width), jnp.float32),
            pltpu.SemaphoreType.DMA((2, blocks, 2)),
        ],
        compiler_params=pltpu.CompilerParams(vmem_limit_bytes=16 << 20),
        cost_estimate=pl.CostEstimate(
            flops=64 * blocks * blocks * width * width * samples,
            bytes_accessed=12 * blocks * width * samples,
            transcendentals=0,
        ),
        name="own_level",
    )(groups, position_input, pltpu.with_memory_space_constraint(volts, pltpu.HBM), *heads)


def add_lags(rows, pick_ref, sums_ref):
    lags = jnp.concatenate(rows, axis=0)
    lags = jnp.concatenate([lags, conjugate_lags(lags)], axis=0)
    return sums_ref[...] + group_sums(pick_ref[...], lags)


def pair_kernel(levels, pieces, passed, pick_ref, sums_ref, panel_ref, *refs):
    count = levels * len(pieces)
    out_ref = refs[-1 - passed]
    partner_refs, more_refs = refs[:count], refs[count : len(refs) - 1 - 2 * passed]
    _, _, width, samples = panel_ref.shape
    rows = []
    for block in sorted({block for piece in pieces for block, _, _ in piece}):
        for level in range(levels):
            for a in range(panel_ref.shape[0]):
                real_part, imag_part = 0.0, 0.0
                for i, piece in enumerate(pieces):
                    partner = partner_refs[level * len(pieces) + i]
                    for (b, first, last), (start, end) in zip(piece, columns(piece)):
                        if b != block:
                            continue
                        x_re, x_im = panel_ref[a, 0, :, first:last], panel_ref[a, 1, :, first:last]
                        y_re = partner[:width, start:end]
                        y_im = partner[width : 2 * width, start:end]
                        real_part = real_part + (product(x_re, y_re) + product(x_im, y_im))
                        imag_part = imag_part + (product(x_im, y_re) - product(x_re, y_im))
                rows.append(lag_rows(jnp.stack([real_part, imag_part])) * (1.0 / samples))
    sums = add_lags(rows, pick_ref, sums_ref)
    for more_ref in more_refs:
        terms = partner_refs[-1][2 * width :, :].astype(jnp.float32)
        half = terms.shape[0] // 2
        sums = sums + group_sums(more_ref[...], terms[:half] + terms[half:])
    out_ref[...] = sums


def last_kernel(parts, samples, mask_ref, sums_ref, panel_ref, *refs):
    partner_refs, out_refs = refs[: len(parts)], refs[len(parts) :]
    blocks, rows_both, _ = panel_ref.shape
    width = rows_both // 2
    rows, tiles_at = [], []
    for (level, first, last), partner_ref in zip(parts, partner_refs):
        for a in range(blocks):
            tiles = product(panel_ref[a, :, first:last], partner_ref[...])
            rows += sheared_eights(tiles.reshape(2, width, width))
            tiles_at.append(level * blocks + a)
    lags = jnp.sum(jnp.stack(rows), axis=1) * (1.0 / samples)
    turned = reversed_lags(lags)
    half = sums_ref.shape[0] // 2
    sums = [sums_ref[:half, :], sums_ref[half:, :]]
    count = mask_ref.shape[0] // 2
    for i, tile in enumerate(tiles_at):
        forward = jnp.concatenate([mask_ref[tile]] * (sums_ref.shape[1] // 128), axis=1)
        back = jnp.concatenate([mask_ref[count + tile]] * (sums_ref.shape[1] // 128), axis=1)
        re, im = 2 * i, 2 * i + 1
        sums[0] = sums[0] + forward * lags[re : re + 1] + back * turned[re : re + 1]
        sums[1] = sums[1] + forward * lags[im : im + 1] - back * turned[im : im + 1]
    share = half // len(out_refs)
    for place, out_ref in enumerate(out_refs):
        for part in range(2):
            rows = sums[part][place * share : (place + 1) * share]
            out_ref[part * share : (part + 1) * share, :] = rows


def pair_call(kernel, inputs, work, shares=1, passed=()):
    rows, width = inputs[1].shape
    any_space = [pl.BlockSpec(memory_space=pl.ANY)] * len(passed)
    return pl.pallas_call(
        kernel,
        out_shape=[jax.ShapeDtypeStruct((rows // shares, width), jnp.float32)] * shares
        + [jax.ShapeDtypeStruct(x.shape, x.dtype) for x in passed],
        in_specs=[WHOLE] * len(inputs) + any_space,
        out_specs=[WHOLE] * shares + any_space,
        input_output_aliases={len(inputs) + i: shares + i for i in range(len(passed))},
        compiler_params=pltpu.CompilerParams(vmem_limit_bytes=16 << 20),
        cost_estimate=pl.CostEstimate(flops=work, bytes_accessed=4 << 20, transcendentals=0),
        name="pair_level",
    )(*inputs, *passed)


def finish_kernel(levels, *refs):
    part_refs, out_ref = refs[:-1], refs[-1]
    mine = parity(lax.axis_index("inp"), levels)
    groups, channels, parts, lags = out_ref.shape
    sums = [None, None]
    for distance, part_ref in enumerate(reversed(part_refs)):
        side = distance.bit_count() % 2
        sums[side] = part_ref[...] if sums[side] is None else sums[side] + part_ref[...]
    for f in range(channels):
        total = jnp.where(mine == f, sums[0], sums[1])
        for g in range(groups):
            for part in range(parts):
                row = part * groups + g
                out_ref[g, f, part : part + 1] = total[row : row + 1, :lags]


def finish(parts, levels, lags):
    return pl.pallas_call(
        functools.partial(finish_kernel, levels),
        out_shape=jax.ShapeDtypeStruct((RG_DEV, 2, 2, lags), jnp.float32),
        in_specs=[WHOLE] * len(parts),
        out_specs=WHOLE,
        compiler_params=pltpu.CompilerParams(vmem_limit_bytes=8 << 20),
        name="finish",
    )(*parts)


def on_device(volts, position_input, tile_group):
    blocks, width = position_input.shape
    samples = volts.shape[3]
    devices = lax.axis_size("inp")
    levels = devices.bit_length() - 1
    out_rows = devices * RG_DEV * 2
    eighth = samples // 8
    head = [(0, 0, 2 * eighth)]
    rest = [(0, 2 * eighth, samples), (1, 0, 2 * eighth)]
    tail = [(1, 2 * eighth, 6 * eighth)]
    last = [(1, 6 * eighth, 7 * eighth), (1, 7 * eighth, samples)]
    by_block = tile_group.transpose(0, 2, 1)
    partner_of = [functools.partial(xor_permute, axis="inp", distance=1 << l) for l in range(levels)]
    sent, second = early_pieces(position_input, volts, by_block, head, rest, levels)
    head_arrived = [send(sent) for send in partner_of]
    rest_arrived = [send(second) for send in partner_of]
    panel, sums, neighbour, both, single, masks, *sent = own_level(
        by_block, position_input, volts, head_arrived, tail, last, out_rows
    )
    head_ordered, (more, piece, *last_pieces, last_panel) = sent[:levels], sent[levels:]
    tail_arrived = [send(piece) for send in partner_of[:-1]] + [partner_of[-1](more)]

    flops = 8 * levels * blocks * width * width
    arrived = [piece for pair in zip(head_ordered, rest_arrived) for piece in pair]
    sums, *last_pieces = pair_call(
        functools.partial(pair_kernel, levels, [head, rest], len(last_pieces)),
        [both, sums, panel, *arrived],
        flops * 10 * eighth,
        passed=last_pieces,
    )
    *last_pieces, joined = last_pieces
    last_arrived = [[send(piece) for send in partner_of[:-1]] for piece in last_pieces]
    last_arrived[-1].append(partner_of[-1](joined))
    (sums,) = pair_call(
        functools.partial(pair_kernel, levels, [tail], 0),
        [single, sums, panel, *tail_arrived, neighbour],
        flops * 4 * eighth,
    )
    for i, arrived in enumerate(last_arrived):
        final = i == len(last_arrived) - 1
        columns_of = [(2 * eighth * i, 2 * eighth * (i + 1))] * (levels - 1)
        if final:
            columns_of.append((0, joined.shape[1]))
        parts = pair_call(
            functools.partial(
                last_kernel, [(level, *cut) for level, cut in enumerate(columns_of)], samples
            ),
            [masks, sums, last_panel, *arrived],
            flops * eighth,
            devices if final else 1,
        )
        sums = parts[0]
    parts = [
        xor_permute(parts[distance], "inp", distance) for distance in reversed(range(1, devices))
    ] + [parts[0]]
    return finish(parts, levels, 2 * width - 1)


def solution(mesh):
    return jax.shard_map(
        on_device,
        mesh=mesh,
        in_specs=(P("freq", None, "inp", None), P("inp", None), P("inp", None, None)),
        out_specs=P("inp", "freq", None, None),
        check_vma=False,
    )
```

```python
import functools

import jax
import jax.numpy as jnp
from jax import lax
from jax.experimental import pallas as pl
from jax.experimental.pallas import tpu as pltpu
from jax.sharding import PartitionSpec as P

RG_DEV = 8
GROUP_ROWS = 16
HBM = pl.BlockSpec(memory_space=pltpu.HBM)
WHOLE = pl.BlockSpec(memory_space=pltpu.VMEM)


def xor_permute(x, axis, distance):
    return lax.ppermute(x, axis, [(i, i ^ distance) for i in range(lax.axis_size(axis))])


def parity(index, levels):
    bits = index & 1
    for level in range(1, levels):
        bits = bits ^ ((index >> level) & 1)
    return bits


def order_matrix(position_row):
    width = position_row.shape[-1]
    by_position = jnp.transpose(jnp.broadcast_to(position_row, (width, width)))
    inputs = lax.broadcasted_iota(jnp.int32, (width, width), 1)
    return (by_position == inputs).astype(jnp.float32).astype(jnp.bfloat16)


def product(x, y):
    return lax.dot_general(x, y, (((1,), (1,)), ((), ())), preferred_element_type=jnp.float32)


def lag_rows(tiles):
    count, width, _ = tiles.shape
    half = width // 2
    low, high = tiles[:, :half], tiles[:, half:]
    sheared = jnp.concatenate(
        [
            high[:, :, :half],
            high[:, :, half:] + low[:, :, :half],
            low[:, :, half:],
            jnp.zeros((count, half, half), jnp.float32),
        ],
        axis=2,
    )
    rows = half
    while rows > 8:
        rows //= 2
        upper = sheared[:, :rows].reshape(count * rows, 2 * width)
        upper = pltpu.roll(upper, rows, 1).reshape(count, rows, 2 * width)
        sheared = upper + sheared[:, rows:]
    flat = sheared.reshape(count * rows, 2 * width)
    sublane = lax.broadcasted_iota(jnp.int32, flat.shape, 0) % 8
    while rows > 1:
        rows //= 2
        flat = jnp.where((sublane & rows) == 0, pltpu.roll(flat, rows, 1), flat)
    return jnp.sum(flat.reshape(count, 8, 2 * width), axis=1)


def tile_lags(x_re, x_im, y_re, y_im, samples):
    real_part = product(x_re, y_re) + product(x_im, y_im)
    imag_part = product(x_im, y_re) - product(x_re, y_im)
    return lag_rows(jnp.stack([real_part, imag_part])) * (1.0 / samples)


def split_rows(x):
    first = x.astype(jnp.bfloat16).astype(jnp.float32)
    rest = x - first
    second = rest.astype(jnp.bfloat16).astype(jnp.float32)
    return jnp.concatenate([first, second, rest - second], axis=0)


def anti_identity(size):
    place = lax.broadcasted_iota(jnp.int32, (size, size), 0) + lax.broadcasted_iota(
        jnp.int32, (size, size), 1
    )
    return (place == size - 1).astype(jnp.float32).astype(jnp.bfloat16)


def turn_lags(terms):
    count, width = terms.shape
    lanes = 128
    spans = range(0, width, lanes)
    terms = jnp.concatenate([terms[:, first : first + lanes] for first in spans], axis=0)
    terms = jnp.dot(
        terms.astype(jnp.bfloat16), anti_identity(lanes), preferred_element_type=jnp.float32
    )
    blocks = [terms[count * i : count * (i + 1)] for i in reversed(range(len(spans)))]
    return pltpu.roll(jnp.concatenate(blocks, axis=1), width - 1, 1)


def conjugate_lags(lags):
    count = lags.shape[0]
    turned = turn_lags(split_rows(lags))
    turned = turned[:count] + turned[count : 2 * count] + turned[2 * count :]
    odd = lax.broadcasted_iota(jnp.int32, turned.shape, 0) % 2 == 1
    return jnp.where(odd, -turned, turned)


def reversed_lags(lags):
    count, width = lags.shape
    lanes = 128
    rows = jnp.pad(lags, ((0, -count % 8), (0, 0)))
    index = lanes - 1 - lax.broadcasted_iota(jnp.int32, (rows.shape[0], lanes), 1)
    blocks = [
        jnp.take_along_axis(
            rows[:, first : first + lanes], index, axis=1, mode="promise_in_bounds"
        )
        for first in reversed(range(0, width, lanes))
    ]
    return pltpu.roll(jnp.concatenate(blocks, axis=1), width - 1, 1)[:count]


def sheared_eights(tiles):
    count, width, _ = tiles.shape
    half = width // 2
    low, high = tiles[:, :half], tiles[:, half:]
    sheared = jnp.concatenate(
        [
            low[:, :, :half],
            low[:, :, half:] + high[:, :, :half],
            high[:, :, half:],
            jnp.zeros((count, half, half), jnp.float32),
        ],
        axis=2,
    )
    rows = half
    while rows > 8:
        rows //= 2
        lower = sheared[:, rows:].reshape(count * rows, 2 * width)
        lower = pltpu.roll(lower, rows, 1).reshape(count, rows, 2 * width)
        sheared = sheared[:, :rows] + lower
    return [pltpu.roll(sheared[i], 0, 1, stride=1, stride_axis=0) for i in range(count)]


def group_block(groups, columns=128):
    rows = jnp.concatenate([groups[b] for b in range(groups.shape[0])], axis=0)
    lines, lanes = rows.shape
    return jnp.pad(rows, ((0, GROUP_ROWS - lines), (0, columns - lanes)))


def target_rows(groups):
    return groups ^ (lax.axis_index("inp") * RG_DEV)


def pick_matrix(entries, rows):
    count = len(entries)
    shape = (rows, 3 * count)
    row = lax.broadcasted_iota(jnp.int32, shape, 0)
    column = lax.broadcasted_iota(jnp.int32, shape, 1) % count
    pick = jnp.zeros(shape, jnp.float32)
    for j, (targets, line, lane, part) in enumerate(entries):
        target = targets[line : line + 1, lane : lane + 1] + part * (rows // 2)
        target = jnp.broadcast_to(target, shape)
        pick = jnp.where(jnp.logical_and(column == j, row == target), 1.0, pick)
    return pick.astype(jnp.bfloat16)


def row_masks(entries, rows):
    row = lax.broadcasted_iota(jnp.int32, (rows, 128), 0)
    masks = []
    for targets, line, lane, _ in entries:
        target = jnp.broadcast_to(targets[line : line + 1, lane : lane + 1], row.shape)
        masks.append((row == target).astype(jnp.float32))
    return jnp.stack(masks)


def pick_matrices(groups, heads, blocks, out_rows):
    own = target_rows(group_block(groups))
    others = [target_rows(head.astype(jnp.float32).astype(jnp.int32)) for head in heads]
    groups_all = out_rows // 2

    def pairs(b):
        order = [(level, a, p) for level in range(len(heads)) for a in range(blocks) for p in range(2)]
        forward = [(own, a * blocks + b, level + 1, p) for level, a, p in order]
        turned = [(others[level], b * blocks + a, level + 1, p) for level, a, p in order]
        return forward, turned

    forward, turned = zip(*[pairs(b) for b in range(blocks)])
    tiles = [
        [(targets, line, 0, p) for line in range(blocks * blocks) for p in range(2)]
        for targets in (own, others[-1])
    ]
    both = [entry for side in (forward, turned) for block in side for entry in block]
    return [
        pick_matrix(tiles[0], out_rows),
        pick_matrix(tiles[1], out_rows),
        pick_matrix(both, out_rows),
        pick_matrix(forward[-1] + turned[-1], out_rows),
        row_masks(forward[-1][::2] + turned[-1][::2], groups_all),
    ]


def group_sums(pick, lags):
    terms = split_rows(lags).astype(jnp.bfloat16)
    return jnp.dot(pick, terms, preferred_element_type=jnp.float32)


def columns(piece):
    spans, start = [], 0
    for _, first, last in piece:
        spans.append((start, start + last - first))
        start += last - first
    return spans


def piece_shape(piece, width, more):
    return jax.ShapeDtypeStruct((2 * width + more, columns(piece)[-1][1]), jnp.bfloat16)


def load_piece(piece, other, width, volts_ref, raw, in_sem):
    blocks = sorted({block for block, _, _ in piece})
    loads = []
    for i, block in enumerate(blocks):
        start = min(first for b, first, _ in piece if b == block)
        end = max(last for b, _, last in piece if b == block)
        for c in range(2):
            load = pltpu.make_async_copy(
                volts_ref.at[other, c, pl.ds(block * width, width), pl.ds(start, end - start)],
                raw.at[i, c, :, pl.ds(start, end - start)],
                in_sem.at[i, c],
            )
            load.start()
            loads.append((i, block, c, load))
    return loads


def order_piece(piece, loads, position, raw, out_ref):
    width = position.shape[1]
    orders = {
        block: order_matrix(position[block : block + 1, :]) for block in sorted({l[1] for l in loads})
    }
    for i, block, c, load in loads:
        load.wait()
        for (b, first, last), (start, end) in zip(piece, columns(piece)):
            if b == block:
                out_ref[c * width : (c + 1) * width, start:end] = jnp.dot(
                    orders[block], raw[i, c, :, first:last], preferred_element_type=jnp.float32
                ).astype(jnp.bfloat16)


def head_kernel(levels, piece, position_ref, volts_ref, group_ref, head_ref, *scratch):
    position, groups, small_sem, in_sem = scratch
    other = 1 - parity(lax.axis_index("inp"), levels)
    width = position.shape[1]
    ((block, first, last),) = piece
    smalls = [
        pltpu.make_async_copy(position_ref, position, small_sem.at[0]),
        pltpu.make_async_copy(group_ref, groups, small_sem.at[1]),
    ]
    loads = [
        pltpu.make_async_copy(
            volts_ref.at[other, c, pl.ds(block * width, width), pl.ds(first, last - first)],
            head_ref.at[pl.ds(c * width, width), :],
            in_sem.at[c],
        )
        for c in range(2)
    ]
    for copy in smalls + loads:
        copy.start()
    for copy in smalls:
        copy.wait()
    rows = group_block(groups[...], last - first)
    line = lax.broadcasted_iota(jnp.int32, rows.shape, 0)
    own_row = jnp.broadcast_to(position[block : block + 1, :], rows.shape)
    rows = jnp.where(line == groups.shape[0] ** 2, own_row, rows)
    head_ref[2 * width :, :] = rows.astype(jnp.float32).astype(jnp.bfloat16)
    for copy in loads:
        copy.wait()


def on_odd_core():
    return lax.axis_index("freq") % 2 == 1


def load_channel(channel, volts_ref, raw, in_sem):
    blocks, _, width, _ = raw.shape
    loads = []
    for b in range(blocks):
        for c in range(2):
            load = pltpu.make_async_copy(
                volts_ref.at[channel, c, pl.ds(b * width, width)], raw.at[b, c], in_sem.at[b, c]
            )
            load.start()
            loads.append((b, c, load))
    return loads


def own_tiles(loads, position_ref, raw, panel, lags_ref, start):
    blocks, _, width, samples = raw.shape
    orders = [order_matrix(position_ref[b : b + 1, :]) for b in range(blocks)]
    for b, c, load in loads:
        load.wait()
        rows = jnp.dot(orders[b], raw[b, c], preferred_element_type=jnp.float32)
        panel[b, c] = rows.astype(jnp.bfloat16)

    def one_tile(index, carry):
        a = index // blocks
        b = index % blocks
        lags = tile_lags(panel[a, 0], panel[a, 1], panel[b, 0], panel[b, 1], samples)
        center = lax.broadcasted_iota(jnp.int32, lags.shape, 1) == width - 1
        lags_ref[start + index] = jnp.where(jnp.logical_and(center, a == b), 0.0, lags)
        return carry

    lax.fori_loop(0, blocks * blocks, one_tile, 0)


def rest_kernel(levels, piece, position_ref, volts_ref, _, out_ref, panel_ref, lags_ref, *scratch):
    position, raw, small_sem, in_sem = scratch
    mine = parity(lax.axis_index("inp"), levels)
    load_position = pltpu.make_async_copy(position_ref, position, small_sem)
    load_position.start()
    load_position.wait()

    @pl.when(on_odd_core())
    def _():
        loads = load_channel(mine, volts_ref, raw, in_sem)
        own_tiles(loads, position, raw, panel_ref, lags_ref, 0)

    loads = load_piece(piece, 1 - mine, position.shape[1], volts_ref, raw, in_sem)
    order_piece(piece, loads, position, raw, out_ref)


def early_pieces(position_input, volts, groups, head, rest, levels):
    blocks, width = position_input.shape
    samples = volts.shape[3]
    assert columns(head)[-1][1] == width
    in_hbm = [pltpu.with_memory_space_constraint(x, pltpu.HBM) for x in (position_input, volts)]
    position = pltpu.VMEM(position_input.shape, jnp.int32)
    semaphore = pltpu.SemaphoreType.DMA
    sent = pl.pallas_call(
        functools.partial(head_kernel, levels, head),
        out_shape=piece_shape(head, width, GROUP_ROWS),
        in_specs=[HBM] * 3,
        out_specs=WHOLE,
        scratch_shapes=[
            position,
            pltpu.VMEM(groups.shape, jnp.int32),
            semaphore((2,)),
            semaphore((2,)),
        ],
        compiler_params=pltpu.CompilerParams(vmem_limit_bytes=8 << 20),
        cost_estimate=pl.CostEstimate(flops=0, bytes_accessed=1 << 20, transcendentals=0),
        name="first_piece",
    )(*in_hbm, pltpu.with_memory_space_constraint(groups, pltpu.HBM))
    second, early_panel, early_lags = pl.pallas_call(
        functools.partial(rest_kernel, levels, rest),
        out_shape=[
            piece_shape(rest, width, 0),
            jax.ShapeDtypeStruct((blocks, 2, width, samples), jnp.bfloat16),
            jax.ShapeDtypeStruct((blocks * blocks, 2, 2 * width), jnp.float32),
        ],
        in_specs=[HBM, HBM, pl.BlockSpec(memory_space=pl.ANY)],
        out_specs=[WHOLE] * 3,
        scratch_shapes=[
            position,
            pltpu.VMEM((blocks, 2, width, samples), jnp.bfloat16),
            semaphore(()),
            semaphore((blocks, 2)),
        ],
        compiler_params=pltpu.CompilerParams(vmem_limit_bytes=16 << 20),
        cost_estimate=pl.CostEstimate(
            flops=4 * width * width * columns(rest)[-1][1],
            bytes_accessed=4 << 20,
            transcendentals=0,
        ),
        name="second_piece",
    )(*in_hbm, sent)
    return sent, second, early_panel, early_lags


def own_kernel(levels, piece, last, group_ref, position_ref, volts_ref, *refs):
    head_refs, refs = refs[:levels][::-1], refs[levels:]
    early_panel_ref, early_lags_ref, *refs = refs
    panel_ref, sums_ref, *refs, raw, other_raw, other_panel, lags_ref, in_sem, other_sem = refs
    pick_refs, ordered_refs, refs = refs[:4], refs[4 : 4 + levels], refs[4 + levels :]
    more_ref, piece_ref, *last_refs, joined_ref, last_panel_ref = refs
    blocks, _, width, _ = panel_ref.shape
    mine = parity(lax.axis_index("inp"), levels)
    other_loads = load_channel(1 - mine, volts_ref, other_raw, other_sem)

    @pl.when(jnp.logical_not(on_odd_core()))
    def _():
        loads = load_channel(mine, volts_ref, raw, in_sem)
        own_tiles(loads, position_ref, raw, panel_ref, lags_ref, 0)

    @pl.when(on_odd_core())
    def _():
        for b in range(blocks):
            for c in range(2):
                panel_ref[b, c] = early_panel_ref[b, c]
        for i in range(blocks * blocks):
            lags_ref[i] = early_lags_ref[i]

    own_tiles(other_loads, position_ref, other_raw, other_panel, lags_ref, blocks * blocks)
    tiles = blocks * blocks
    lags = jnp.concatenate([lags_ref[i] for i in range(tiles)], axis=0)
    heads = [head_ref[2 * width :, :] for head_ref in head_refs]
    for head, head_ref, ordered_ref in zip(heads, head_refs, ordered_refs):
        positions = head.astype(jnp.float32).astype(jnp.int32)[blocks**2 : blocks**2 + 1]
        order = order_matrix(positions)
        for c in range(2):
            rows = head_ref[c * width : (c + 1) * width, :]
            rows = jnp.dot(order, rows, preferred_element_type=jnp.float32)
            ordered_ref[c * width : (c + 1) * width, :] = rows.astype(jnp.bfloat16)
    own_pick, *picks = pick_matrices(group_ref[...], heads, blocks, sums_ref.shape[0])
    for pick_ref, pick in zip(pick_refs, picks):
        pick_ref[...] = pick
    sums_ref[...] = group_sums(own_pick, lags)
    for (block, first, end), (start, stop) in zip(piece, columns(piece)):
        for c in range(2):
            rows = other_panel[block, c, :, first:end]
            piece_ref[c * width : (c + 1) * width, start:stop] = rows
            more_ref[c * width : (c + 1) * width, start:stop] = rows
    lags = jnp.concatenate([lags_ref[tiles + i] for i in range(tiles)], axis=0)
    high = lags.astype(jnp.bfloat16).astype(jnp.float32)
    terms = jnp.concatenate([high, lags - high], axis=0)
    more_ref[2 * width :, :] = terms.astype(jnp.bfloat16)
    start = 0
    for (block, first, end), last_ref in zip(last, last_refs):
        for c in range(2):
            depth = end - first
            rows = other_panel[block, c, :, first:end]
            last_ref[:, c * depth : (c + 1) * depth] = rows
            joined_ref[:, start : start + depth] = rows
            start += depth
    turn = anti_identity(width)
    for a in range(blocks):
        start = 0
        for _, first, end in last:
            real_part, imag_part = [
                jnp.dot(turn, panel_ref[a, c, :, first:end], preferred_element_type=jnp.float32)
                for c in range(2)
            ]
            middle, stop = start + end - first, start + 2 * (end - first)
            last_panel_ref[a, :width, start:middle] = real_part.astype(jnp.bfloat16)
            last_panel_ref[a, :width, middle:stop] = imag_part.astype(jnp.bfloat16)
            last_panel_ref[a, width:, start:middle] = imag_part.astype(jnp.bfloat16)
            last_panel_ref[a, width:, middle:stop] = (-real_part).astype(jnp.bfloat16)
            start = stop


def own_level(groups, position_input, volts, early, heads, piece, last, out_rows):
    levels = len(heads)
    blocks, width = position_input.shape
    samples = volts.shape[3]
    pairs = 4 * levels * blocks
    tiles = 2 * blocks * blocks
    counts = (3 * tiles, 3 * pairs * blocks, 3 * pairs)
    depths = [2 * (end - first) for _, first, end in last]
    return pl.pallas_call(
        functools.partial(own_kernel, levels, piece, last),
        out_shape=(
            jax.ShapeDtypeStruct((blocks, 2, width, samples), jnp.bfloat16),
            jax.ShapeDtypeStruct((out_rows, 2 * width), jnp.float32),
            *[jax.ShapeDtypeStruct((out_rows, n), jnp.bfloat16) for n in counts],
            jax.ShapeDtypeStruct((pairs // 2, out_rows // 2, 128), jnp.float32),
            *[jax.ShapeDtypeStruct((2 * width, head.shape[1]), jnp.bfloat16) for head in heads],
            piece_shape(piece, width, 2 * tiles),
            piece_shape(piece, width, 0),
            *[jax.ShapeDtypeStruct((width, depth), jnp.bfloat16) for depth in depths],
            jax.ShapeDtypeStruct((width, sum(depths)), jnp.bfloat16),
            jax.ShapeDtypeStruct((blocks, 2 * width, sum(depths)), jnp.bfloat16),
        ),
        in_specs=[WHOLE, WHOLE, HBM] + [WHOLE] * (len(early) + levels),
        out_specs=(WHOLE,) * (7 + len(counts) + levels + len(last)),
        scratch_shapes=[
            pltpu.VMEM((blocks, 2, width, samples), jnp.bfloat16),
            pltpu.VMEM((blocks, 2, width, samples), jnp.bfloat16),
            pltpu.VMEM((blocks, 2, width, samples), jnp.bfloat16),
            pltpu.VMEM((2 * blocks * blocks, 2, 2 * width), jnp.float32),
            pltpu.SemaphoreType.DMA((blocks, 2)),
            pltpu.SemaphoreType.DMA((blocks, 2)),
        ],
        compiler_params=pltpu.CompilerParams(vmem_limit_bytes=16 << 20),
        cost_estimate=pl.CostEstimate(
            flops=64 * blocks * blocks * width * width * samples,
            bytes_accessed=12 * blocks * width * samples,
            transcendentals=0,
        ),
        name="own_level",
    )(groups, position_input, pltpu.with_memory_space_constraint(volts, pltpu.HBM), *heads[::-1], *early)


def add_lags(rows, pick_ref, sums_ref):
    lags = jnp.concatenate(rows, axis=0)
    lags = jnp.concatenate([lags, conjugate_lags(lags)], axis=0)
    return sums_ref[...] + group_sums(pick_ref[...], lags)


def pair_kernel(levels, pieces, passed, pick_ref, sums_ref, panel_ref, *refs):
    count = levels * len(pieces)
    out_ref = refs[-1 - passed]
    partner_refs, more_refs = refs[:count], refs[count : len(refs) - 1 - 2 * passed]
    _, _, width, samples = panel_ref.shape
    rows = []
    for block in sorted({block for piece in pieces for block, _, _ in piece}):
        for level in range(levels):
            for a in range(panel_ref.shape[0]):
                real_part, imag_part = 0.0, 0.0
                for i, piece in enumerate(pieces):
                    partner = partner_refs[level * len(pieces) + i]
                    for (b, first, last), (start, end) in zip(piece, columns(piece)):
                        if b != block:
                            continue
                        x_re, x_im = panel_ref[a, 0, :, first:last], panel_ref[a, 1, :, first:last]
                        y_re = partner[:width, start:end]
                        y_im = partner[width : 2 * width, start:end]
                        real_part = real_part + (product(x_re, y_re) + product(x_im, y_im))
                        imag_part = imag_part + (product(x_im, y_re) - product(x_re, y_im))
                rows.append(lag_rows(jnp.stack([real_part, imag_part])) * (1.0 / samples))
    sums = add_lags(rows, pick_ref, sums_ref)
    for more_ref in more_refs:
        terms = partner_refs[-1][2 * width :, :].astype(jnp.float32)
        half = terms.shape[0] // 2
        sums = sums + group_sums(more_ref[...], terms[:half] + terms[half:])
    out_ref[...] = sums


def last_kernel(parts, samples, mask_ref, sums_ref, panel_ref, *refs):
    partner_refs, out_refs = refs[: len(parts)], refs[len(parts) :]
    blocks, rows_both, _ = panel_ref.shape
    width = rows_both // 2
    rows, tiles_at = [], []
    for (level, first, last), partner_ref in zip(parts, partner_refs):
        for a in range(blocks):
            tiles = product(panel_ref[a, :, first:last], partner_ref[...])
            rows += sheared_eights(tiles.reshape(2, width, width))
            tiles_at.append(level * blocks + a)
    lags = jnp.sum(jnp.stack(rows), axis=1) * (1.0 / samples)
    turned = reversed_lags(lags)
    half = sums_ref.shape[0] // 2
    sums = [sums_ref[:half, :], sums_ref[half:, :]]
    count = mask_ref.shape[0] // 2
    for i, tile in enumerate(tiles_at):
        forward = jnp.concatenate([mask_ref[tile]] * (sums_ref.shape[1] // 128), axis=1)
        back = jnp.concatenate([mask_ref[count + tile]] * (sums_ref.shape[1] // 128), axis=1)
        re, im = 2 * i, 2 * i + 1
        sums[0] = sums[0] + forward * lags[re : re + 1] + back * turned[re : re + 1]
        sums[1] = sums[1] + forward * lags[im : im + 1] - back * turned[im : im + 1]
    share = half // len(out_refs)
    for place, out_ref in enumerate(out_refs):
        for part in range(2):
            rows = sums[part][place * share : (place + 1) * share]
            out_ref[part * share : (part + 1) * share, :] = rows


def pair_call(kernel, inputs, work, shares=1, passed=()):
    rows, width = inputs[1].shape
    any_space = [pl.BlockSpec(memory_space=pl.ANY)] * len(passed)
    return pl.pallas_call(
        kernel,
        out_shape=[jax.ShapeDtypeStruct((rows // shares, width), jnp.float32)] * shares
        + [jax.ShapeDtypeStruct(x.shape, x.dtype) for x in passed],
        in_specs=[WHOLE] * len(inputs) + any_space,
        out_specs=[WHOLE] * shares + any_space,
        input_output_aliases={len(inputs) + i: shares + i for i in range(len(passed))},
        compiler_params=pltpu.CompilerParams(vmem_limit_bytes=16 << 20),
        cost_estimate=pl.CostEstimate(flops=work, bytes_accessed=4 << 20, transcendentals=0),
        name="pair_level",
    )(*inputs, *passed)


def finish_kernel(levels, distances, *refs):
    part_refs, out_ref = refs[:-1], refs[-1]
    mine = parity(lax.axis_index("inp"), levels)
    groups, channels, parts, lags = out_ref.shape
    sums = [None, None]
    for distance, part_ref in zip(distances, part_refs):
        side = distance.bit_count() % 2
        sums[side] = part_ref[...] if sums[side] is None else sums[side] + part_ref[...]
    for f in range(channels):
        total = jnp.where(mine == f, sums[0], sums[1])
        for g in range(groups):
            for part in range(parts):
                row = part * groups + g
                out_ref[g, f, part : part + 1] = total[row : row + 1, :lags]


def finish(parts, distances, levels, lags):
    return pl.pallas_call(
        functools.partial(finish_kernel, levels, distances),
        out_shape=jax.ShapeDtypeStruct((RG_DEV, 2, 2, lags), jnp.float32),
        in_specs=[WHOLE] * len(parts),
        out_specs=WHOLE,
        compiler_params=pltpu.CompilerParams(vmem_limit_bytes=8 << 20),
        name="finish",
    )(*parts)


def on_device(volts, position_input, tile_group):
    blocks, width = position_input.shape
    samples = volts.shape[3]
    devices = lax.axis_size("inp")
    levels = devices.bit_length() - 1
    out_rows = devices * RG_DEV * 2
    eighth = samples // 8
    head = [(0, 0, 2 * eighth)]
    rest = [(0, 2 * eighth, samples), (1, 0, 2 * eighth)]
    tail = [(1, 2 * eighth, 6 * eighth)]
    last = [(1, 6 * eighth, 7 * eighth), (1, 7 * eighth, samples)]
    by_block = tile_group.transpose(0, 2, 1)
    partner_of = [functools.partial(xor_permute, axis="inp", distance=1 << l) for l in range(levels)]
    sent, second, *early = early_pieces(position_input, volts, by_block, head, rest, levels)
    head_arrived = [send(sent) for send in partner_of]
    rest_arrived = [send(second) for send in partner_of]
    panel, sums, neighbour, both, single, masks, *sent = own_level(
        by_block, position_input, volts, early, head_arrived, tail, last, out_rows
    )
    head_ordered, (more, piece, *last_pieces, last_panel) = sent[:levels], sent[levels:]
    tail_arrived = [send(piece) for send in partner_of[:-1]] + [partner_of[-1](more)]

    flops = 8 * levels * blocks * width * width
    arrived = [piece for pair in zip(head_ordered, rest_arrived) for piece in pair]
    sums, *last_pieces = pair_call(
        functools.partial(pair_kernel, levels, [head, rest], len(last_pieces)),
        [both, sums, panel, *arrived],
        flops * 10 * eighth,
        passed=last_pieces,
    )
    *last_pieces, joined = last_pieces
    last_arrived = [[send(piece) for send in partner_of[:-1]] for piece in last_pieces]
    last_arrived[-1].append(partner_of[-1](joined))
    (sums,) = pair_call(
        functools.partial(pair_kernel, levels, [tail], 0),
        [single, sums, panel, *tail_arrived, neighbour],
        flops * 4 * eighth,
    )
    for i, arrived in enumerate(last_arrived):
        final = i == len(last_arrived) - 1
        columns_of = [(2 * eighth * i, 2 * eighth * (i + 1))] * (levels - 1)
        if final:
            columns_of.append((0, joined.shape[1]))
        parts = pair_call(
            functools.partial(
                last_kernel, [(level, *cut) for level, cut in enumerate(columns_of)], samples
            ),
            [masks, sums, last_panel, *arrived],
            flops * eighth,
            devices if final else 1,
        )
        sums = parts[0]
    distances = [1, *range(devices - 1, 1, -1), 0]
    parts = [
        xor_permute(parts[distance], "inp", distance) if distance else parts[0]
        for distance in distances
    ]
    return finish(parts, distances, levels, 2 * width - 1)


def solution(mesh):
    return jax.shard_map(
        on_device,
        mesh=mesh,
        in_specs=(P("freq", None, "inp", None), P("inp", None), P("inp", None, None)),
        out_specs=P("inp", "freq", None, None),
        check_vma=False,
    )
```

```python
import functools

import jax
import jax.numpy as jnp
from jax import lax
from jax.experimental import pallas as pl
from jax.experimental.pallas import tpu as pltpu
from jax.sharding import PartitionSpec as P

RG_DEV = 8
GROUP_ROWS = 16
EARLY_TILES = 3
HBM = pl.BlockSpec(memory_space=pltpu.HBM)
WHOLE = pl.BlockSpec(memory_space=pltpu.VMEM)


def xor_permute(x, axis, distance):
    return lax.ppermute(x, axis, [(i, i ^ distance) for i in range(lax.axis_size(axis))])


def parity(index, levels):
    bits = index & 1
    for level in range(1, levels):
        bits = bits ^ ((index >> level) & 1)
    return bits


def order_matrix(position_row):
    width = position_row.shape[-1]
    by_position = jnp.transpose(jnp.broadcast_to(position_row, (width, width)))
    inputs = lax.broadcasted_iota(jnp.int32, (width, width), 1)
    return (by_position == inputs).astype(jnp.float32).astype(jnp.bfloat16)


def product(x, y):
    return lax.dot_general(x, y, (((1,), (1,)), ((), ())), preferred_element_type=jnp.float32)


def lag_rows(tiles):
    count, width, _ = tiles.shape
    half = width // 2
    low, high = tiles[:, :half], tiles[:, half:]
    sheared = jnp.concatenate(
        [
            high[:, :, :half],
            high[:, :, half:] + low[:, :, :half],
            low[:, :, half:],
            jnp.zeros((count, half, half), jnp.float32),
        ],
        axis=2,
    )
    rows = half
    while rows > 8:
        rows //= 2
        upper = sheared[:, :rows].reshape(count * rows, 2 * width)
        upper = pltpu.roll(upper, rows, 1).reshape(count, rows, 2 * width)
        sheared = upper + sheared[:, rows:]
    flat = sheared.reshape(count * rows, 2 * width)
    sublane = lax.broadcasted_iota(jnp.int32, flat.shape, 0) % 8
    while rows > 1:
        rows //= 2
        flat = jnp.where((sublane & rows) == 0, pltpu.roll(flat, rows, 1), flat)
    return jnp.sum(flat.reshape(count, 8, 2 * width), axis=1)


def tile_lags(x_re, x_im, y_re, y_im, samples):
    real_part = product(x_re, y_re) + product(x_im, y_im)
    imag_part = product(x_im, y_re) - product(x_re, y_im)
    return lag_rows(jnp.stack([real_part, imag_part])) * (1.0 / samples)


def split_rows(x):
    first = x.astype(jnp.bfloat16).astype(jnp.float32)
    rest = x - first
    second = rest.astype(jnp.bfloat16).astype(jnp.float32)
    return jnp.concatenate([first, second, rest - second], axis=0)


def anti_identity(size):
    place = lax.broadcasted_iota(jnp.int32, (size, size), 0) + lax.broadcasted_iota(
        jnp.int32, (size, size), 1
    )
    return (place == size - 1).astype(jnp.float32).astype(jnp.bfloat16)


def turn_lags(terms):
    count, width = terms.shape
    lanes = 128
    spans = range(0, width, lanes)
    terms = jnp.concatenate([terms[:, first : first + lanes] for first in spans], axis=0)
    terms = jnp.dot(
        terms.astype(jnp.bfloat16), anti_identity(lanes), preferred_element_type=jnp.float32
    )
    blocks = [terms[count * i : count * (i + 1)] for i in reversed(range(len(spans)))]
    return pltpu.roll(jnp.concatenate(blocks, axis=1), width - 1, 1)


def conjugate_lags(lags):
    count = lags.shape[0]
    turned = turn_lags(split_rows(lags))
    turned = turned[:count] + turned[count : 2 * count] + turned[2 * count :]
    odd = lax.broadcasted_iota(jnp.int32, turned.shape, 0) % 2 == 1
    return jnp.where(odd, -turned, turned)


def reversed_lags(lags):
    count, width = lags.shape
    lanes = 128
    rows = jnp.pad(lags, ((0, -count % 8), (0, 0)))
    index = lanes - 1 - lax.broadcasted_iota(jnp.int32, (rows.shape[0], lanes), 1)
    blocks = [
        jnp.take_along_axis(
            rows[:, first : first + lanes], index, axis=1, mode="promise_in_bounds"
        )
        for first in reversed(range(0, width, lanes))
    ]
    return pltpu.roll(jnp.concatenate(blocks, axis=1), width - 1, 1)[:count]


def sheared_eights(tiles):
    count, width, _ = tiles.shape
    half = width // 2
    low, high = tiles[:, :half], tiles[:, half:]
    sheared = jnp.concatenate(
        [
            low[:, :, :half],
            low[:, :, half:] + high[:, :, :half],
            high[:, :, half:],
            jnp.zeros((count, half, half), jnp.float32),
        ],
        axis=2,
    )
    rows = half
    while rows > 8:
        rows //= 2
        lower = sheared[:, rows:].reshape(count * rows, 2 * width)
        lower = pltpu.roll(lower, rows, 1).reshape(count, rows, 2 * width)
        sheared = sheared[:, :rows] + lower
    return [pltpu.roll(sheared[i], 0, 1, stride=1, stride_axis=0) for i in range(count)]


def group_block(groups, columns=128):
    rows = jnp.concatenate([groups[b] for b in range(groups.shape[0])], axis=0)
    lines, lanes = rows.shape
    return jnp.pad(rows, ((0, GROUP_ROWS - lines), (0, columns - lanes)))


def target_rows(groups):
    return groups ^ (lax.axis_index("inp") * RG_DEV)


def pick_matrix(entries, rows):
    count = len(entries)
    shape = (rows, 3 * count)
    row = lax.broadcasted_iota(jnp.int32, shape, 0)
    column = lax.broadcasted_iota(jnp.int32, shape, 1) % count
    pick = jnp.zeros(shape, jnp.float32)
    for j, (targets, line, lane, part) in enumerate(entries):
        target = targets[line : line + 1, lane : lane + 1] + part * (rows // 2)
        target = jnp.broadcast_to(target, shape)
        pick = jnp.where(jnp.logical_and(column == j, row == target), 1.0, pick)
    return pick.astype(jnp.bfloat16)


def row_masks(entries, rows):
    row = lax.broadcasted_iota(jnp.int32, (rows, 128), 0)
    masks = []
    for targets, line, lane, _ in entries:
        target = jnp.broadcast_to(targets[line : line + 1, lane : lane + 1], row.shape)
        masks.append((row == target).astype(jnp.float32))
    return jnp.stack(masks)


def pick_matrices(groups, heads, blocks, out_rows):
    own = target_rows(group_block(groups))
    others = [target_rows(head.astype(jnp.float32).astype(jnp.int32)) for head in heads]
    groups_all = out_rows // 2

    def pairs(b):
        order = [(level, a, p) for level in range(len(heads)) for a in range(blocks) for p in range(2)]
        forward = [(own, a * blocks + b, level + 1, p) for level, a, p in order]
        turned = [(others[level], b * blocks + a, level + 1, p) for level, a, p in order]
        return forward, turned

    forward, turned = zip(*[pairs(b) for b in range(blocks)])
    tiles = [
        [(targets, line, 0, p) for line in range(blocks * blocks) for p in range(2)]
        for targets in (own, others[-1])
    ]
    both = [entry for side in (forward, turned) for block in side for entry in block]
    return [
        pick_matrix(tiles[0], out_rows),
        pick_matrix(tiles[1], out_rows),
        pick_matrix(both, out_rows),
        pick_matrix(forward[-1] + turned[-1], out_rows),
        row_masks(forward[-1][::2] + turned[-1][::2], groups_all),
    ]


def group_sums(pick, lags):
    terms = split_rows(lags).astype(jnp.bfloat16)
    return jnp.dot(pick, terms, preferred_element_type=jnp.float32)


def columns(piece):
    spans, start = [], 0
    for _, first, last in piece:
        spans.append((start, start + last - first))
        start += last - first
    return spans


def piece_shape(piece, width, more):
    return jax.ShapeDtypeStruct((2 * width + more, columns(piece)[-1][1]), jnp.bfloat16)


def load_piece(piece, other, width, volts_ref, raw, in_sem):
    blocks = sorted({block for block, _, _ in piece})
    loads = []
    for i, block in enumerate(blocks):
        start = min(first for b, first, _ in piece if b == block)
        end = max(last for b, _, last in piece if b == block)
        for c in range(2):
            load = pltpu.make_async_copy(
                volts_ref.at[other, c, pl.ds(block * width, width), pl.ds(start, end - start)],
                raw.at[i, c, :, pl.ds(start, end - start)],
                in_sem.at[i, c],
            )
            load.start()
            loads.append((i, block, c, load))
    return loads


def order_piece(piece, loads, position, raw, out_ref):
    width = position.shape[1]
    orders = {
        block: order_matrix(position[block : block + 1, :]) for block in sorted({l[1] for l in loads})
    }
    for i, block, c, load in loads:
        load.wait()
        for (b, first, last), (start, end) in zip(piece, columns(piece)):
            if b == block:
                out_ref[c * width : (c + 1) * width, start:end] = jnp.dot(
                    orders[block], raw[i, c, :, first:last], preferred_element_type=jnp.float32
                ).astype(jnp.bfloat16)


def head_kernel(levels, piece, position_ref, volts_ref, group_ref, head_ref, *scratch):
    position, groups, small_sem, in_sem = scratch
    other = 1 - parity(lax.axis_index("inp"), levels)
    width = position.shape[1]
    ((block, first, last),) = piece
    smalls = [
        pltpu.make_async_copy(position_ref, position, small_sem.at[0]),
        pltpu.make_async_copy(group_ref, groups, small_sem.at[1]),
    ]
    loads = [
        pltpu.make_async_copy(
            volts_ref.at[other, c, pl.ds(block * width, width), pl.ds(first, last - first)],
            head_ref.at[pl.ds(c * width, width), :],
            in_sem.at[c],
        )
        for c in range(2)
    ]
    for copy in smalls + loads:
        copy.start()
    for copy in smalls:
        copy.wait()
    rows = group_block(groups[...], last - first)
    line = lax.broadcasted_iota(jnp.int32, rows.shape, 0)
    own_row = jnp.broadcast_to(position[block : block + 1, :], rows.shape)
    rows = jnp.where(line == groups.shape[0] ** 2, own_row, rows)
    head_ref[2 * width :, :] = rows.astype(jnp.float32).astype(jnp.bfloat16)
    for copy in loads:
        copy.wait()


def on_odd_core():
    return lax.axis_index("freq") % 2 == 1


def load_channel(channel, volts_ref, raw, in_sem):
    blocks, _, width, _ = raw.shape
    loads = []
    for b in range(blocks):
        for c in range(2):
            load = pltpu.make_async_copy(
                volts_ref.at[channel, c, pl.ds(b * width, width)], raw.at[b, c], in_sem.at[b, c]
            )
            load.start()
            loads.append((b, c, load))
    return loads


def order_channel(loads, position_ref, raw, panel):
    blocks = raw.shape[0]
    orders = [order_matrix(position_ref[b : b + 1, :]) for b in range(blocks)]
    for b, c, load in loads:
        load.wait()
        rows = jnp.dot(orders[b], raw[b, c], preferred_element_type=jnp.float32)
        panel[b, c] = rows.astype(jnp.bfloat16)


def own_tiles(panel, lags_ref, start, first, last):
    blocks, _, width, samples = panel.shape

    def one_tile(index, carry):
        a = index // blocks
        b = index % blocks
        lags = tile_lags(panel[a, 0], panel[a, 1], panel[b, 0], panel[b, 1], samples)
        center = lax.broadcasted_iota(jnp.int32, lags.shape, 1) == width - 1
        lags_ref[start + index] = jnp.where(jnp.logical_and(center, a == b), 0.0, lags)
        return carry

    lax.fori_loop(first, last, one_tile, 0)


def rest_kernel(levels, piece, position_ref, volts_ref, _, out_ref, panel_ref, lags_ref, *scratch):
    position, raw, small_sem, in_sem = scratch
    mine = parity(lax.axis_index("inp"), levels)
    load_position = pltpu.make_async_copy(position_ref, position, small_sem)
    load_position.start()
    load_position.wait()

    @pl.when(on_odd_core())
    def _():
        loads = load_channel(mine, volts_ref, raw, in_sem)
        order_channel(loads, position, raw, panel_ref)
        own_tiles(panel_ref, lags_ref, 0, 0, EARLY_TILES)

    loads = load_piece(piece, 1 - mine, position.shape[1], volts_ref, raw, in_sem)
    order_piece(piece, loads, position, raw, out_ref)


def early_pieces(position_input, volts, groups, head, rest, levels):
    blocks, width = position_input.shape
    samples = volts.shape[3]
    assert columns(head)[-1][1] == width
    in_hbm = [pltpu.with_memory_space_constraint(x, pltpu.HBM) for x in (position_input, volts)]
    position = pltpu.VMEM(position_input.shape, jnp.int32)
    semaphore = pltpu.SemaphoreType.DMA
    sent = pl.pallas_call(
        functools.partial(head_kernel, levels, head),
        out_shape=piece_shape(head, width, GROUP_ROWS),
        in_specs=[HBM] * 3,
        out_specs=WHOLE,
        scratch_shapes=[
            position,
            pltpu.VMEM(groups.shape, jnp.int32),
            semaphore((2,)),
            semaphore((2,)),
        ],
        compiler_params=pltpu.CompilerParams(vmem_limit_bytes=8 << 20),
        cost_estimate=pl.CostEstimate(flops=0, bytes_accessed=1 << 20, transcendentals=0),
        name="first_piece",
    )(*in_hbm, pltpu.with_memory_space_constraint(groups, pltpu.HBM))
    second, early_panel, early_lags = pl.pallas_call(
        functools.partial(rest_kernel, levels, rest),
        out_shape=[
            piece_shape(rest, width, 0),
            jax.ShapeDtypeStruct((blocks, 2, width, samples), jnp.bfloat16),
            jax.ShapeDtypeStruct((blocks * blocks, 2, 2 * width), jnp.float32),
        ],
        in_specs=[HBM, HBM, pl.BlockSpec(memory_space=pl.ANY)],
        out_specs=[WHOLE] * 3,
        scratch_shapes=[
            position,
            pltpu.VMEM((blocks, 2, width, samples), jnp.bfloat16),
            semaphore(()),
            semaphore((blocks, 2)),
        ],
        compiler_params=pltpu.CompilerParams(vmem_limit_bytes=16 << 20),
        cost_estimate=pl.CostEstimate(
            flops=4 * width * width * columns(rest)[-1][1],
            bytes_accessed=4 << 20,
            transcendentals=0,
        ),
        name="second_piece",
    )(*in_hbm, sent)
    return sent, second, early_panel, early_lags


def own_kernel(levels, piece, last, group_ref, position_ref, volts_ref, *refs):
    head_refs, refs = refs[:levels][::-1], refs[levels:]
    early_panel_ref, early_lags_ref, *refs = refs
    panel_ref, sums_ref, *refs, raw, other_raw, other_panel, lags_ref, in_sem, other_sem = refs
    pick_refs, ordered_refs, refs = refs[:4], refs[4 : 4 + levels], refs[4 + levels :]
    more_ref, piece_ref, *last_refs, joined_ref, last_panel_ref = refs
    blocks, _, width, _ = panel_ref.shape
    mine = parity(lax.axis_index("inp"), levels)
    other_loads = load_channel(1 - mine, volts_ref, other_raw, other_sem)

    @pl.when(jnp.logical_not(on_odd_core()))
    def _():
        loads = load_channel(mine, volts_ref, raw, in_sem)
        order_channel(loads, position_ref, raw, panel_ref)
        own_tiles(panel_ref, lags_ref, 0, 0, EARLY_TILES)

    @pl.when(on_odd_core())
    def _():
        for b in range(blocks):
            for c in range(2):
                panel_ref[b, c] = early_panel_ref[b, c]
        for i in range(EARLY_TILES):
            lags_ref[i] = early_lags_ref[i]

    tiles = blocks * blocks
    own_tiles(panel_ref, lags_ref, 0, EARLY_TILES, tiles)
    order_channel(other_loads, position_ref, other_raw, other_panel)
    own_tiles(other_panel, lags_ref, tiles, 0, tiles)
    lags = jnp.concatenate([lags_ref[i] for i in range(tiles)], axis=0)
    heads = [head_ref[2 * width :, :] for head_ref in head_refs]
    for head, head_ref, ordered_ref in zip(heads, head_refs, ordered_refs):
        positions = head.astype(jnp.float32).astype(jnp.int32)[blocks**2 : blocks**2 + 1]
        order = order_matrix(positions)
        for c in range(2):
            rows = head_ref[c * width : (c + 1) * width, :]
            rows = jnp.dot(order, rows, preferred_element_type=jnp.float32)
            ordered_ref[c * width : (c + 1) * width, :] = rows.astype(jnp.bfloat16)
    own_pick, *picks = pick_matrices(group_ref[...], heads, blocks, sums_ref.shape[0])
    for pick_ref, pick in zip(pick_refs, picks):
        pick_ref[...] = pick
    sums_ref[...] = group_sums(own_pick, lags)
    for (block, first, end), (start, stop) in zip(piece, columns(piece)):
        for c in range(2):
            rows = other_panel[block, c, :, first:end]
            piece_ref[c * width : (c + 1) * width, start:stop] = rows
            more_ref[c * width : (c + 1) * width, start:stop] = rows
    lags = jnp.concatenate([lags_ref[tiles + i] for i in range(tiles)], axis=0)
    high = lags.astype(jnp.bfloat16).astype(jnp.float32)
    terms = jnp.concatenate([high, lags - high], axis=0)
    more_ref[2 * width :, :] = terms.astype(jnp.bfloat16)
    start = 0
    for (block, first, end), last_ref in zip(last, last_refs):
        for c in range(2):
            depth = end - first
            rows = other_panel[block, c, :, first:end]
            last_ref[:, c * depth : (c + 1) * depth] = rows
            joined_ref[:, start : start + depth] = rows
            start += depth
    turn = anti_identity(width)
    for a in range(blocks):
        start = 0
        for _, first, end in last:
            real_part, imag_part = [
                jnp.dot(turn, panel_ref[a, c, :, first:end], preferred_element_type=jnp.float32)
                for c in range(2)
            ]
            middle, stop = start + end - first, start + 2 * (end - first)
            last_panel_ref[a, :width, start:middle] = real_part.astype(jnp.bfloat16)
            last_panel_ref[a, :width, middle:stop] = imag_part.astype(jnp.bfloat16)
            last_panel_ref[a, width:, start:middle] = imag_part.astype(jnp.bfloat16)
            last_panel_ref[a, width:, middle:stop] = (-real_part).astype(jnp.bfloat16)
            start = stop


def own_level(groups, position_input, volts, early, heads, piece, last, out_rows):
    levels = len(heads)
    blocks, width = position_input.shape
    samples = volts.shape[3]
    pairs = 4 * levels * blocks
    tiles = 2 * blocks * blocks
    counts = (3 * tiles, 3 * pairs * blocks, 3 * pairs)
    depths = [2 * (end - first) for _, first, end in last]
    return pl.pallas_call(
        functools.partial(own_kernel, levels, piece, last),
        out_shape=(
            jax.ShapeDtypeStruct((blocks, 2, width, samples), jnp.bfloat16),
            jax.ShapeDtypeStruct((out_rows, 2 * width), jnp.float32),
            *[jax.ShapeDtypeStruct((out_rows, n), jnp.bfloat16) for n in counts],
            jax.ShapeDtypeStruct((pairs // 2, out_rows // 2, 128), jnp.float32),
            *[jax.ShapeDtypeStruct((2 * width, head.shape[1]), jnp.bfloat16) for head in heads],
            piece_shape(piece, width, 2 * tiles),
            piece_shape(piece, width, 0),
            *[jax.ShapeDtypeStruct((width, depth), jnp.bfloat16) for depth in depths],
            jax.ShapeDtypeStruct((width, sum(depths)), jnp.bfloat16),
            jax.ShapeDtypeStruct((blocks, 2 * width, sum(depths)), jnp.bfloat16),
        ),
        in_specs=[WHOLE, WHOLE, HBM] + [WHOLE] * (len(early) + levels),
        out_specs=(WHOLE,) * (7 + len(counts) + levels + len(last)),
        scratch_shapes=[
            pltpu.VMEM((blocks, 2, width, samples), jnp.bfloat16),
            pltpu.VMEM((blocks, 2, width, samples), jnp.bfloat16),
            pltpu.VMEM((blocks, 2, width, samples), jnp.bfloat16),
            pltpu.VMEM((2 * blocks * blocks, 2, 2 * width), jnp.float32),
            pltpu.SemaphoreType.DMA((blocks, 2)),
            pltpu.SemaphoreType.DMA((blocks, 2)),
        ],
        compiler_params=pltpu.CompilerParams(vmem_limit_bytes=16 << 20),
        cost_estimate=pl.CostEstimate(
            flops=64 * blocks * blocks * width * width * samples,
            bytes_accessed=12 * blocks * width * samples,
            transcendentals=0,
        ),
        name="own_level",
    )(groups, position_input, pltpu.with_memory_space_constraint(volts, pltpu.HBM), *heads[::-1], *early)


def add_lags(rows, pick_ref, sums_ref):
    lags = jnp.concatenate(rows, axis=0)
    lags = jnp.concatenate([lags, conjugate_lags(lags)], axis=0)
    return sums_ref[...] + group_sums(pick_ref[...], lags)


def pair_kernel(levels, pieces, passed, pick_ref, sums_ref, panel_ref, *refs):
    count = levels * len(pieces)
    out_ref = refs[-1 - passed]
    partner_refs, more_refs = refs[:count], refs[count : len(refs) - 1 - 2 * passed]
    _, _, width, samples = panel_ref.shape
    rows = []
    for block in sorted({block for piece in pieces for block, _, _ in piece}):
        for level in range(levels):
            for a in range(panel_ref.shape[0]):
                real_part, imag_part = 0.0, 0.0
                for i, piece in enumerate(pieces):
                    partner = partner_refs[level * len(pieces) + i]
                    for (b, first, last), (start, end) in zip(piece, columns(piece)):
                        if b != block:
                            continue
                        x_re, x_im = panel_ref[a, 0, :, first:last], panel_ref[a, 1, :, first:last]
                        y_re = partner[:width, start:end]
                        y_im = partner[width : 2 * width, start:end]
                        real_part = real_part + (product(x_re, y_re) + product(x_im, y_im))
                        imag_part = imag_part + (product(x_im, y_re) - product(x_re, y_im))
                rows.append(lag_rows(jnp.stack([real_part, imag_part])) * (1.0 / samples))
    sums = add_lags(rows, pick_ref, sums_ref)
    for more_ref in more_refs:
        terms = partner_refs[-1][2 * width :, :].astype(jnp.float32)
        half = terms.shape[0] // 2
        sums = sums + group_sums(more_ref[...], terms[:half] + terms[half:])
    out_ref[...] = sums


def last_kernel(parts, samples, mask_ref, sums_ref, panel_ref, *refs):
    partner_refs, out_refs = refs[: len(parts)], refs[len(parts) :]
    blocks, rows_both, _ = panel_ref.shape
    width = rows_both // 2
    rows, tiles_at = [], []
    for (level, first, last), partner_ref in zip(parts, partner_refs):
        for a in range(blocks):
            tiles = product(panel_ref[a, :, first:last], partner_ref[...])
            rows += sheared_eights(tiles.reshape(2, width, width))
            tiles_at.append(level * blocks + a)
    lags = jnp.sum(jnp.stack(rows), axis=1) * (1.0 / samples)
    turned = reversed_lags(lags)
    half = sums_ref.shape[0] // 2
    sums = [sums_ref[:half, :], sums_ref[half:, :]]
    count = mask_ref.shape[0] // 2
    for i, tile in enumerate(tiles_at):
        forward = jnp.concatenate([mask_ref[tile]] * (sums_ref.shape[1] // 128), axis=1)
        back = jnp.concatenate([mask_ref[count + tile]] * (sums_ref.shape[1] // 128), axis=1)
        re, im = 2 * i, 2 * i + 1
        sums[0] = sums[0] + forward * lags[re : re + 1] + back * turned[re : re + 1]
        sums[1] = sums[1] + forward * lags[im : im + 1] - back * turned[im : im + 1]
    share = half // len(out_refs)
    for place, out_ref in enumerate(out_refs):
        for part in range(2):
            rows = sums[part][place * share : (place + 1) * share]
            out_ref[part * share : (part + 1) * share, :] = rows


def pair_call(kernel, inputs, work, shares=1, passed=()):
    rows, width = inputs[1].shape
    any_space = [pl.BlockSpec(memory_space=pl.ANY)] * len(passed)
    return pl.pallas_call(
        kernel,
        out_shape=[jax.ShapeDtypeStruct((rows // shares, width), jnp.float32)] * shares
        + [jax.ShapeDtypeStruct(x.shape, x.dtype) for x in passed],
        in_specs=[WHOLE] * len(inputs) + any_space,
        out_specs=[WHOLE] * shares + any_space,
        input_output_aliases={len(inputs) + i: shares + i for i in range(len(passed))},
        compiler_params=pltpu.CompilerParams(vmem_limit_bytes=16 << 20),
        cost_estimate=pl.CostEstimate(flops=work, bytes_accessed=4 << 20, transcendentals=0),
        name="pair_level",
    )(*inputs, *passed)


def finish_kernel(levels, distances, *refs):
    part_refs, out_ref = refs[:-1], refs[-1]
    mine = parity(lax.axis_index("inp"), levels)
    groups, channels, parts, lags = out_ref.shape
    sums = [None, None]
    for distance, part_ref in zip(distances, part_refs):
        side = distance.bit_count() % 2
        sums[side] = part_ref[...] if sums[side] is None else sums[side] + part_ref[...]
    for f in range(channels):
        total = jnp.where(mine == f, sums[0], sums[1])
        for g in range(groups):
            for part in range(parts):
                row = part * groups + g
                out_ref[g, f, part : part + 1] = total[row : row + 1, :lags]


def finish(parts, distances, levels, lags):
    return pl.pallas_call(
        functools.partial(finish_kernel, levels, distances),
        out_shape=jax.ShapeDtypeStruct((RG_DEV, 2, 2, lags), jnp.float32),
        in_specs=[WHOLE] * len(parts),
        out_specs=WHOLE,
        compiler_params=pltpu.CompilerParams(vmem_limit_bytes=8 << 20),
        name="finish",
    )(*parts)


def on_device(volts, position_input, tile_group):
    blocks, width = position_input.shape
    samples = volts.shape[3]
    devices = lax.axis_size("inp")
    levels = devices.bit_length() - 1
    out_rows = devices * RG_DEV * 2
    eighth = samples // 8
    head = [(0, 0, 2 * eighth)]
    rest = [(0, 2 * eighth, samples), (1, 0, 2 * eighth)]
    tail = [(1, 2 * eighth, 6 * eighth)]
    last = [(1, 6 * eighth, 7 * eighth), (1, 7 * eighth, samples)]
    by_block = tile_group.transpose(0, 2, 1)
    partner_of = [functools.partial(xor_permute, axis="inp", distance=1 << l) for l in range(levels)]
    sent, second, *early = early_pieces(position_input, volts, by_block, head, rest, levels)
    head_arrived = [send(sent) for send in partner_of]
    rest_arrived = [send(second) for send in partner_of]
    panel, sums, neighbour, both, single, masks, *sent = own_level(
        by_block, position_input, volts, early, head_arrived, tail, last, out_rows
    )
    head_ordered, (more, piece, *last_pieces, last_panel) = sent[:levels], sent[levels:]
    tail_arrived = [send(piece) for send in partner_of[:-1]] + [partner_of[-1](more)]

    flops = 8 * levels * blocks * width * width
    arrived = [piece for pair in zip(head_ordered, rest_arrived) for piece in pair]
    sums, *last_pieces = pair_call(
        functools.partial(pair_kernel, levels, [head, rest], len(last_pieces)),
        [both, sums, panel, *arrived],
        flops * 10 * eighth,
        passed=last_pieces,
    )
    *last_pieces, joined = last_pieces
    last_arrived = [[send(piece) for send in partner_of[:-1]] for piece in last_pieces]
    last_arrived[-1].append(partner_of[-1](joined))
    (sums,) = pair_call(
        functools.partial(pair_kernel, levels, [tail], 0),
        [single, sums, panel, *tail_arrived, neighbour],
        flops * 4 * eighth,
    )
    for i, arrived in enumerate(last_arrived):
        final = i == len(last_arrived) - 1
        columns_of = [(2 * eighth * i, 2 * eighth * (i + 1))] * (levels - 1)
        if final:
            columns_of.append((0, joined.shape[1]))
        parts = pair_call(
            functools.partial(
                last_kernel, [(level, *cut) for level, cut in enumerate(columns_of)], samples
            ),
            [masks, sums, last_panel, *arrived],
            flops * eighth,
            devices if final else 1,
        )
        sums = parts[0]
    distances = [1, *range(devices - 1, 1, -1), 0]
    parts = [
        xor_permute(parts[distance], "inp", distance) if distance else parts[0]
        for distance in distances
    ]
    return finish(parts, distances, levels, 2 * width - 1)


def solution(mesh):
    return jax.shard_map(
        on_device,
        mesh=mesh,
        in_specs=(P("freq", None, "inp", None), P("inp", None), P("inp", None, None)),
        out_specs=P("inp", "freq", None, None),
        check_vma=False,
    )
```

```python
import functools

import jax
import jax.numpy as jnp
from jax import lax
from jax.experimental import pallas as pl
from jax.experimental.pallas import tpu as pltpu
from jax.sharding import PartitionSpec as P

RG_DEV = 8
GROUP_ROWS = 16
EARLY_TILES = 2
HBM = pl.BlockSpec(memory_space=pltpu.HBM)
WHOLE = pl.BlockSpec(memory_space=pltpu.VMEM)


def xor_permute(x, axis, distance):
    return lax.ppermute(x, axis, [(i, i ^ distance) for i in range(lax.axis_size(axis))])


def parity(index, levels):
    bits = index & 1
    for level in range(1, levels):
        bits = bits ^ ((index >> level) & 1)
    return bits


def order_matrix(position_row):
    width = position_row.shape[-1]
    by_position = jnp.transpose(jnp.broadcast_to(position_row, (width, width)))
    inputs = lax.broadcasted_iota(jnp.int32, (width, width), 1)
    return (by_position == inputs).astype(jnp.float32).astype(jnp.bfloat16)


def product(x, y):
    return lax.dot_general(x, y, (((1,), (1,)), ((), ())), preferred_element_type=jnp.float32)


def lag_rows(tiles):
    count, width, _ = tiles.shape
    half = width // 2
    low, high = tiles[:, :half], tiles[:, half:]
    sheared = jnp.concatenate(
        [
            high[:, :, :half],
            high[:, :, half:] + low[:, :, :half],
            low[:, :, half:],
            jnp.zeros((count, half, half), jnp.float32),
        ],
        axis=2,
    )
    rows = half
    while rows > 8:
        rows //= 2
        upper = sheared[:, :rows].reshape(count * rows, 2 * width)
        upper = pltpu.roll(upper, rows, 1).reshape(count, rows, 2 * width)
        sheared = upper + sheared[:, rows:]
    flat = sheared.reshape(count * rows, 2 * width)
    sublane = lax.broadcasted_iota(jnp.int32, flat.shape, 0) % 8
    while rows > 1:
        rows //= 2
        flat = jnp.where((sublane & rows) == 0, pltpu.roll(flat, rows, 1), flat)
    return jnp.sum(flat.reshape(count, 8, 2 * width), axis=1)


def tile_lags(x_re, x_im, y_re, y_im, samples):
    real_part = product(x_re, y_re) + product(x_im, y_im)
    imag_part = product(x_im, y_re) - product(x_re, y_im)
    return lag_rows(jnp.stack([real_part, imag_part])) * (1.0 / samples)


def split_rows(x):
    first = x.astype(jnp.bfloat16).astype(jnp.float32)
    rest = x - first
    second = rest.astype(jnp.bfloat16).astype(jnp.float32)
    return jnp.concatenate([first, second, rest - second], axis=0)


def anti_identity(size):
    place = lax.broadcasted_iota(jnp.int32, (size, size), 0) + lax.broadcasted_iota(
        jnp.int32, (size, size), 1
    )
    return (place == size - 1).astype(jnp.float32).astype(jnp.bfloat16)


def turn_lags(terms):
    count, width = terms.shape
    lanes = 128
    spans = range(0, width, lanes)
    terms = jnp.concatenate([terms[:, first : first + lanes] for first in spans], axis=0)
    terms = jnp.dot(
        terms.astype(jnp.bfloat16), anti_identity(lanes), preferred_element_type=jnp.float32
    )
    blocks = [terms[count * i : count * (i + 1)] for i in reversed(range(len(spans)))]
    return pltpu.roll(jnp.concatenate(blocks, axis=1), width - 1, 1)


def conjugate_lags(lags):
    count = lags.shape[0]
    turned = turn_lags(split_rows(lags))
    turned = turned[:count] + turned[count : 2 * count] + turned[2 * count :]
    odd = lax.broadcasted_iota(jnp.int32, turned.shape, 0) % 2 == 1
    return jnp.where(odd, -turned, turned)


def reversed_lags(lags):
    count, width = lags.shape
    lanes = 128
    rows = jnp.pad(lags, ((0, -count % 8), (0, 0)))
    index = lanes - 1 - lax.broadcasted_iota(jnp.int32, (rows.shape[0], lanes), 1)
    blocks = [
        jnp.take_along_axis(
            rows[:, first : first + lanes], index, axis=1, mode="promise_in_bounds"
        )
        for first in reversed(range(0, width, lanes))
    ]
    return pltpu.roll(jnp.concatenate(blocks, axis=1), width - 1, 1)[:count]


def sheared_eights(tiles):
    count, width, _ = tiles.shape
    half = width // 2
    low, high = tiles[:, :half], tiles[:, half:]
    sheared = jnp.concatenate(
        [
            low[:, :, :half],
            low[:, :, half:] + high[:, :, :half],
            high[:, :, half:],
            jnp.zeros((count, half, half), jnp.float32),
        ],
        axis=2,
    )
    rows = half
    while rows > 8:
        rows //= 2
        lower = sheared[:, rows:].reshape(count * rows, 2 * width)
        lower = pltpu.roll(lower, rows, 1).reshape(count, rows, 2 * width)
        sheared = sheared[:, :rows] + lower
    return [pltpu.roll(sheared[i], 0, 1, stride=1, stride_axis=0) for i in range(count)]


def group_block(groups, columns=128):
    rows = jnp.concatenate([groups[b] for b in range(groups.shape[0])], axis=0)
    lines, lanes = rows.shape
    return jnp.pad(rows, ((0, GROUP_ROWS - lines), (0, columns - lanes)))


def target_rows(groups):
    return groups ^ (lax.axis_index("inp") * RG_DEV)


def pick_matrix(entries, rows):
    count = len(entries)
    shape = (rows, 3 * count)
    row = lax.broadcasted_iota(jnp.int32, shape, 0)
    column = lax.broadcasted_iota(jnp.int32, shape, 1) % count
    pick = jnp.zeros(shape, jnp.float32)
    for j, (targets, line, lane, part) in enumerate(entries):
        target = targets[line : line + 1, lane : lane + 1] + part * (rows // 2)
        target = jnp.broadcast_to(target, shape)
        pick = jnp.where(jnp.logical_and(column == j, row == target), 1.0, pick)
    return pick.astype(jnp.bfloat16)


def row_masks(entries, rows):
    row = lax.broadcasted_iota(jnp.int32, (rows, 128), 0)
    masks = []
    for targets, line, lane, _ in entries:
        target = jnp.broadcast_to(targets[line : line + 1, lane : lane + 1], row.shape)
        masks.append((row == target).astype(jnp.float32))
    return jnp.stack(masks)


def pick_matrices(groups, heads, blocks, out_rows):
    own = target_rows(group_block(groups))
    others = [target_rows(head.astype(jnp.float32).astype(jnp.int32)) for head in heads]
    groups_all = out_rows // 2

    def pairs(b):
        order = [(level, a, p) for level in range(len(heads)) for a in range(blocks) for p in range(2)]
        forward = [(own, a * blocks + b, level + 1, p) for level, a, p in order]
        turned = [(others[level], b * blocks + a, level + 1, p) for level, a, p in order]
        return forward, turned

    forward, turned = zip(*[pairs(b) for b in range(blocks)])
    tiles = [
        [(targets, line, 0, p) for line in range(blocks * blocks) for p in range(2)]
        for targets in (own, others[-1])
    ]
    both = [entry for side in (forward, turned) for block in side for entry in block]
    return [
        pick_matrix(tiles[0], out_rows),
        pick_matrix(tiles[1], out_rows),
        pick_matrix(both, out_rows),
        pick_matrix(forward[-1] + turned[-1], out_rows),
        row_masks(forward[-1][::2] + turned[-1][::2], groups_all),
    ]


def group_sums(pick, lags):
    terms = split_rows(lags).astype(jnp.bfloat16)
    return jnp.dot(pick, terms, preferred_element_type=jnp.float32)


def columns(piece):
    spans, start = [], 0
    for _, first, last in piece:
        spans.append((start, start + last - first))
        start += last - first
    return spans


def piece_shape(piece, width, more):
    return jax.ShapeDtypeStruct((2 * width + more, columns(piece)[-1][1]), jnp.bfloat16)


def load_piece(piece, other, width, volts_ref, raw, in_sem):
    blocks = sorted({block for block, _, _ in piece})
    loads = []
    for i, block in enumerate(blocks):
        start = min(first for b, first, _ in piece if b == block)
        end = max(last for b, _, last in piece if b == block)
        for c in range(2):
            load = pltpu.make_async_copy(
                volts_ref.at[other, c, pl.ds(block * width, width), pl.ds(start, end - start)],
                raw.at[i, c, :, pl.ds(start, end - start)],
                in_sem.at[i, c],
            )
            load.start()
            loads.append((i, block, c, load))
    return loads


def order_piece(piece, loads, position, raw, out_ref):
    width = position.shape[1]
    orders = {
        block: order_matrix(position[block : block + 1, :]) for block in sorted({l[1] for l in loads})
    }
    for i, block, c, load in loads:
        load.wait()
        for (b, first, last), (start, end) in zip(piece, columns(piece)):
            if b == block:
                out_ref[c * width : (c + 1) * width, start:end] = jnp.dot(
                    orders[block], raw[i, c, :, first:last], preferred_element_type=jnp.float32
                ).astype(jnp.bfloat16)


def head_kernel(levels, piece, position_ref, volts_ref, group_ref, head_ref, *scratch):
    position, groups, small_sem, in_sem = scratch
    other = 1 - parity(lax.axis_index("inp"), levels)
    width = position.shape[1]
    ((block, first, last),) = piece
    smalls = [
        pltpu.make_async_copy(position_ref, position, small_sem.at[0]),
        pltpu.make_async_copy(group_ref, groups, small_sem.at[1]),
    ]
    loads = [
        pltpu.make_async_copy(
            volts_ref.at[other, c, pl.ds(block * width, width), pl.ds(first, last - first)],
            head_ref.at[pl.ds(c * width, width), :],
            in_sem.at[c],
        )
        for c in range(2)
    ]
    for copy in smalls + loads:
        copy.start()
    for copy in smalls:
        copy.wait()
    rows = group_block(groups[...], last - first)
    line = lax.broadcasted_iota(jnp.int32, rows.shape, 0)
    own_row = jnp.broadcast_to(position[block : block + 1, :], rows.shape)
    rows = jnp.where(line == groups.shape[0] ** 2, own_row, rows)
    head_ref[2 * width :, :] = rows.astype(jnp.float32).astype(jnp.bfloat16)
    for copy in loads:
        copy.wait()


def on_odd_core():
    return lax.axis_index("freq") % 2 == 1


def load_channel(channel, volts_ref, raw, in_sem):
    blocks, _, width, _ = raw.shape
    loads = []
    for b in range(blocks):
        for c in range(2):
            load = pltpu.make_async_copy(
                volts_ref.at[channel, c, pl.ds(b * width, width)], raw.at[b, c], in_sem.at[b, c]
            )
            load.start()
            loads.append((b, c, load))
    return loads


def order_channel(loads, position_ref, raw, panel):
    blocks = raw.shape[0]
    orders = [order_matrix(position_ref[b : b + 1, :]) for b in range(blocks)]
    for b, c, load in loads:
        load.wait()
        rows = jnp.dot(orders[b], raw[b, c], preferred_element_type=jnp.float32)
        panel[b, c] = rows.astype(jnp.bfloat16)


def own_tiles(panel, lags_ref, start, first, last):
    blocks, _, width, samples = panel.shape

    def one_tile(index, carry):
        a = index // blocks
        b = index % blocks
        lags = tile_lags(panel[a, 0], panel[a, 1], panel[b, 0], panel[b, 1], samples)
        center = lax.broadcasted_iota(jnp.int32, lags.shape, 1) == width - 1
        lags_ref[start + index] = jnp.where(jnp.logical_and(center, a == b), 0.0, lags)
        return carry

    lax.fori_loop(first, last, one_tile, 0)


def rest_kernel(levels, piece, position_ref, volts_ref, _, out_ref, panel_ref, lags_ref, *scratch):
    position, raw, small_sem, in_sem = scratch
    mine = parity(lax.axis_index("inp"), levels)
    load_position = pltpu.make_async_copy(position_ref, position, small_sem)
    load_position.start()
    load_position.wait()

    @pl.when(on_odd_core())
    def _():
        loads = load_channel(mine, volts_ref, raw, in_sem)
        order_channel(loads, position, raw, panel_ref)
        own_tiles(panel_ref, lags_ref, 0, 0, EARLY_TILES)

    loads = load_piece(piece, 1 - mine, position.shape[1], volts_ref, raw, in_sem)
    order_piece(piece, loads, position, raw, out_ref)


def early_pieces(position_input, volts, groups, head, rest, levels):
    blocks, width = position_input.shape
    samples = volts.shape[3]
    assert columns(head)[-1][1] == width
    in_hbm = [pltpu.with_memory_space_constraint(x, pltpu.HBM) for x in (position_input, volts)]
    position = pltpu.VMEM(position_input.shape, jnp.int32)
    semaphore = pltpu.SemaphoreType.DMA
    sent = pl.pallas_call(
        functools.partial(head_kernel, levels, head),
        out_shape=piece_shape(head, width, GROUP_ROWS),
        in_specs=[HBM] * 3,
        out_specs=WHOLE,
        scratch_shapes=[
            position,
            pltpu.VMEM(groups.shape, jnp.int32),
            semaphore((2,)),
            semaphore((2,)),
        ],
        compiler_params=pltpu.CompilerParams(vmem_limit_bytes=8 << 20),
        cost_estimate=pl.CostEstimate(flops=0, bytes_accessed=1 << 20, transcendentals=0),
        name="first_piece",
    )(*in_hbm, pltpu.with_memory_space_constraint(groups, pltpu.HBM))
    second, early_panel, early_lags = pl.pallas_call(
        functools.partial(rest_kernel, levels, rest),
        out_shape=[
            piece_shape(rest, width, 0),
            jax.ShapeDtypeStruct((blocks, 2, width, samples), jnp.bfloat16),
            jax.ShapeDtypeStruct((blocks * blocks, 2, 2 * width), jnp.float32),
        ],
        in_specs=[HBM, HBM, pl.BlockSpec(memory_space=pl.ANY)],
        out_specs=[WHOLE] * 3,
        scratch_shapes=[
            position,
            pltpu.VMEM((blocks, 2, width, samples), jnp.bfloat16),
            semaphore(()),
            semaphore((blocks, 2)),
        ],
        compiler_params=pltpu.CompilerParams(vmem_limit_bytes=16 << 20),
        cost_estimate=pl.CostEstimate(
            flops=4 * width * width * columns(rest)[-1][1],
            bytes_accessed=4 << 20,
            transcendentals=0,
        ),
        name="second_piece",
    )(*in_hbm, sent)
    return sent, second, early_panel, early_lags


def own_kernel(levels, piece, last, group_ref, position_ref, volts_ref, *refs):
    head_refs, refs = refs[:levels][::-1], refs[levels:]
    early_panel_ref, early_lags_ref, *refs = refs
    panel_ref, sums_ref, *refs, raw, other_raw, other_panel, lags_ref, in_sem, other_sem = refs
    pick_refs, ordered_refs, refs = refs[:4], refs[4 : 4 + levels], refs[4 + levels :]
    more_ref, piece_ref, *last_refs, joined_ref, last_panel_ref = refs
    blocks, _, width, _ = panel_ref.shape
    mine = parity(lax.axis_index("inp"), levels)
    other_loads = load_channel(1 - mine, volts_ref, other_raw, other_sem)

    @pl.when(jnp.logical_not(on_odd_core()))
    def _():
        loads = load_channel(mine, volts_ref, raw, in_sem)
        order_channel(loads, position_ref, raw, panel_ref)
        own_tiles(panel_ref, lags_ref, 0, 0, EARLY_TILES)

    @pl.when(on_odd_core())
    def _():
        for b in range(blocks):
            for c in range(2):
                panel_ref[b, c] = early_panel_ref[b, c]
        for i in range(EARLY_TILES):
            lags_ref[i] = early_lags_ref[i]

    tiles = blocks * blocks
    own_tiles(panel_ref, lags_ref, 0, EARLY_TILES, tiles)
    order_channel(other_loads, position_ref, other_raw, other_panel)
    own_tiles(other_panel, lags_ref, tiles, 0, tiles)
    lags = jnp.concatenate([lags_ref[i] for i in range(tiles)], axis=0)
    heads = [head_ref[2 * width :, :] for head_ref in head_refs]
    for head, head_ref, ordered_ref in zip(heads, head_refs, ordered_refs):
        positions = head.astype(jnp.float32).astype(jnp.int32)[blocks**2 : blocks**2 + 1]
        order = order_matrix(positions)
        for c in range(2):
            rows = head_ref[c * width : (c + 1) * width, :]
            rows = jnp.dot(order, rows, preferred_element_type=jnp.float32)
            ordered_ref[c * width : (c + 1) * width, :] = rows.astype(jnp.bfloat16)
    own_pick, *picks = pick_matrices(group_ref[...], heads, blocks, sums_ref.shape[0])
    for pick_ref, pick in zip(pick_refs, picks):
        pick_ref[...] = pick
    sums_ref[...] = group_sums(own_pick, lags)
    for (block, first, end), (start, stop) in zip(piece, columns(piece)):
        for c in range(2):
            rows = other_panel[block, c, :, first:end]
            piece_ref[c * width : (c + 1) * width, start:stop] = rows
            more_ref[c * width : (c + 1) * width, start:stop] = rows
    lags = jnp.concatenate([lags_ref[tiles + i] for i in range(tiles)], axis=0)
    high = lags.astype(jnp.bfloat16).astype(jnp.float32)
    terms = jnp.concatenate([high, lags - high], axis=0)
    more_ref[2 * width :, :] = terms.astype(jnp.bfloat16)
    start = 0
    for (block, first, end), last_ref in zip(last, last_refs):
        for c in range(2):
            depth = end - first
            rows = other_panel[block, c, :, first:end]
            last_ref[:, c * depth : (c + 1) * depth] = rows
            joined_ref[:, start : start + depth] = rows
            start += depth
    turn = anti_identity(width)
    for a in range(blocks):
        start = 0
        for _, first, end in last:
            real_part, imag_part = [
                jnp.dot(turn, panel_ref[a, c, :, first:end], preferred_element_type=jnp.float32)
                for c in range(2)
            ]
            middle, stop = start + end - first, start + 2 * (end - first)
            last_panel_ref[a, :width, start:middle] = real_part.astype(jnp.bfloat16)
            last_panel_ref[a, :width, middle:stop] = imag_part.astype(jnp.bfloat16)
            last_panel_ref[a, width:, start:middle] = imag_part.astype(jnp.bfloat16)
            last_panel_ref[a, width:, middle:stop] = (-real_part).astype(jnp.bfloat16)
            start = stop


def own_level(groups, position_input, volts, early, heads, piece, last, out_rows):
    levels = len(heads)
    blocks, width = position_input.shape
    samples = volts.shape[3]
    pairs = 4 * levels * blocks
    tiles = 2 * blocks * blocks
    counts = (3 * tiles, 3 * pairs * blocks, 3 * pairs)
    depths = [2 * (end - first) for _, first, end in last]
    return pl.pallas_call(
        functools.partial(own_kernel, levels, piece, last),
        out_shape=(
            jax.ShapeDtypeStruct((blocks, 2, width, samples), jnp.bfloat16),
            jax.ShapeDtypeStruct((out_rows, 2 * width), jnp.float32),
            *[jax.ShapeDtypeStruct((out_rows, n), jnp.bfloat16) for n in counts],
            jax.ShapeDtypeStruct((pairs // 2, out_rows // 2, 128), jnp.float32),
            *[jax.ShapeDtypeStruct((2 * width, head.shape[1]), jnp.bfloat16) for head in heads],
            piece_shape(piece, width, 2 * tiles),
            piece_shape(piece, width, 0),
            *[jax.ShapeDtypeStruct((width, depth), jnp.bfloat16) for depth in depths],
            jax.ShapeDtypeStruct((width, sum(depths)), jnp.bfloat16),
            jax.ShapeDtypeStruct((blocks, 2 * width, sum(depths)), jnp.bfloat16),
        ),
        in_specs=[WHOLE, WHOLE, HBM] + [WHOLE] * (len(early) + levels),
        out_specs=(WHOLE,) * (7 + len(counts) + levels + len(last)),
        scratch_shapes=[
            pltpu.VMEM((blocks, 2, width, samples), jnp.bfloat16),
            pltpu.VMEM((blocks, 2, width, samples), jnp.bfloat16),
            pltpu.VMEM((blocks, 2, width, samples), jnp.bfloat16),
            pltpu.VMEM((2 * blocks * blocks, 2, 2 * width), jnp.float32),
            pltpu.SemaphoreType.DMA((blocks, 2)),
            pltpu.SemaphoreType.DMA((blocks, 2)),
        ],
        compiler_params=pltpu.CompilerParams(vmem_limit_bytes=16 << 20),
        cost_estimate=pl.CostEstimate(
            flops=64 * blocks * blocks * width * width * samples,
            bytes_accessed=12 * blocks * width * samples,
            transcendentals=0,
        ),
        name="own_level",
    )(groups, position_input, pltpu.with_memory_space_constraint(volts, pltpu.HBM), *heads[::-1], *early)


def add_lags(rows, pick_ref, sums_ref):
    lags = jnp.concatenate(rows, axis=0)
    lags = jnp.concatenate([lags, conjugate_lags(lags)], axis=0)
    return sums_ref[...] + group_sums(pick_ref[...], lags)


def pair_kernel(levels, pieces, passed, pick_ref, sums_ref, panel_ref, *refs):
    count = levels * len(pieces)
    out_ref = refs[-1 - passed]
    partner_refs, more_refs = refs[:count], refs[count : len(refs) - 1 - 2 * passed]
    _, _, width, samples = panel_ref.shape
    rows = []
    for block in sorted({block for piece in pieces for block, _, _ in piece}):
        for level in range(levels):
            for a in range(panel_ref.shape[0]):
                real_part, imag_part = 0.0, 0.0
                for i, piece in enumerate(pieces):
                    partner = partner_refs[level * len(pieces) + i]
                    for (b, first, last), (start, end) in zip(piece, columns(piece)):
                        if b != block:
                            continue
                        x_re, x_im = panel_ref[a, 0, :, first:last], panel_ref[a, 1, :, first:last]
                        y_re = partner[:width, start:end]
                        y_im = partner[width : 2 * width, start:end]
                        real_part = real_part + (product(x_re, y_re) + product(x_im, y_im))
                        imag_part = imag_part + (product(x_im, y_re) - product(x_re, y_im))
                rows.append(lag_rows(jnp.stack([real_part, imag_part])) * (1.0 / samples))
    sums = add_lags(rows, pick_ref, sums_ref)
    for more_ref in more_refs:
        terms = partner_refs[-1][2 * width :, :].astype(jnp.float32)
        half = terms.shape[0] // 2
        sums = sums + group_sums(more_ref[...], terms[:half] + terms[half:])
    out_ref[...] = sums


def last_kernel(parts, samples, mask_ref, sums_ref, panel_ref, *refs):
    partner_refs, out_refs = refs[: len(parts)], refs[len(parts) :]
    blocks, rows_both, _ = panel_ref.shape
    width = rows_both // 2
    rows, tiles_at = [], []
    for (level, first, last), partner_ref in zip(parts, partner_refs):
        for a in range(blocks):
            tiles = product(panel_ref[a, :, first:last], partner_ref[...])
            rows += sheared_eights(tiles.reshape(2, width, width))
            tiles_at.append(level * blocks + a)
    lags = jnp.sum(jnp.stack(rows), axis=1) * (1.0 / samples)
    turned = reversed_lags(lags)
    half = sums_ref.shape[0] // 2
    sums = [sums_ref[:half, :], sums_ref[half:, :]]
    count = mask_ref.shape[0] // 2
    for i, tile in enumerate(tiles_at):
        forward = jnp.concatenate([mask_ref[tile]] * (sums_ref.shape[1] // 128), axis=1)
        back = jnp.concatenate([mask_ref[count + tile]] * (sums_ref.shape[1] // 128), axis=1)
        re, im = 2 * i, 2 * i + 1
        sums[0] = sums[0] + forward * lags[re : re + 1] + back * turned[re : re + 1]
        sums[1] = sums[1] + forward * lags[im : im + 1] - back * turned[im : im + 1]
    share = half // len(out_refs)
    for place, out_ref in enumerate(out_refs):
        for part in range(2):
            rows = sums[part][place * share : (place + 1) * share]
            out_ref[part * share : (part + 1) * share, :] = rows


def pair_call(kernel, inputs, work, shares=1, passed=()):
    rows, width = inputs[1].shape
    any_space = [pl.BlockSpec(memory_space=pl.ANY)] * len(passed)
    return pl.pallas_call(
        kernel,
        out_shape=[jax.ShapeDtypeStruct((rows // shares, width), jnp.float32)] * shares
        + [jax.ShapeDtypeStruct(x.shape, x.dtype) for x in passed],
        in_specs=[WHOLE] * len(inputs) + any_space,
        out_specs=[WHOLE] * shares + any_space,
        input_output_aliases={len(inputs) + i: shares + i for i in range(len(passed))},
        compiler_params=pltpu.CompilerParams(vmem_limit_bytes=16 << 20),
        cost_estimate=pl.CostEstimate(flops=work, bytes_accessed=4 << 20, transcendentals=0),
        name="pair_level",
    )(*inputs, *passed)


def finish_kernel(levels, distances, *refs):
    part_refs, out_ref = refs[:-1], refs[-1]
    mine = parity(lax.axis_index("inp"), levels)
    groups, channels, parts, lags = out_ref.shape
    sums = [None, None]
    for distance, part_ref in zip(distances, part_refs):
        side = distance.bit_count() % 2
        sums[side] = part_ref[...] if sums[side] is None else sums[side] + part_ref[...]
    for f in range(channels):
        total = jnp.where(mine == f, sums[0], sums[1])
        for g in range(groups):
            for part in range(parts):
                row = part * groups + g
                out_ref[g, f, part : part + 1] = total[row : row + 1, :lags]


def finish(parts, distances, levels, lags):
    return pl.pallas_call(
        functools.partial(finish_kernel, levels, distances),
        out_shape=jax.ShapeDtypeStruct((RG_DEV, 2, 2, lags), jnp.float32),
        in_specs=[WHOLE] * len(parts),
        out_specs=WHOLE,
        compiler_params=pltpu.CompilerParams(vmem_limit_bytes=8 << 20),
        name="finish",
    )(*parts)


def on_device(volts, position_input, tile_group):
    blocks, width = position_input.shape
    samples = volts.shape[3]
    devices = lax.axis_size("inp")
    levels = devices.bit_length() - 1
    out_rows = devices * RG_DEV * 2
    eighth = samples // 8
    head = [(0, 0, 2 * eighth)]
    rest = [(0, 2 * eighth, samples), (1, 0, 2 * eighth)]
    tail = [(1, 2 * eighth, 6 * eighth)]
    last = [(1, 6 * eighth, 7 * eighth), (1, 7 * eighth, samples)]
    by_block = tile_group.transpose(0, 2, 1)
    partner_of = [functools.partial(xor_permute, axis="inp", distance=1 << l) for l in range(levels)]
    sent, second, *early = early_pieces(position_input, volts, by_block, head, rest, levels)
    head_arrived = [send(sent) for send in partner_of]
    rest_arrived = [send(second) for send in partner_of]
    panel, sums, neighbour, both, single, masks, *sent = own_level(
        by_block, position_input, volts, early, head_arrived, tail, last, out_rows
    )
    head_ordered, (more, piece, *last_pieces, last_panel) = sent[:levels], sent[levels:]
    tail_arrived = [send(piece) for send in partner_of[:-1]] + [partner_of[-1](more)]

    flops = 8 * levels * blocks * width * width
    arrived = [piece for pair in zip(head_ordered, rest_arrived) for piece in pair]
    sums, *last_pieces = pair_call(
        functools.partial(pair_kernel, levels, [head, rest], len(last_pieces)),
        [both, sums, panel, *arrived],
        flops * 10 * eighth,
        passed=last_pieces,
    )
    *last_pieces, joined = last_pieces
    last_arrived = [[send(piece) for send in partner_of[:-1]] for piece in last_pieces]
    last_arrived[-1].append(partner_of[-1](joined))
    (sums,) = pair_call(
        functools.partial(pair_kernel, levels, [tail], 0),
        [single, sums, panel, *tail_arrived, neighbour],
        flops * 4 * eighth,
    )
    for i, arrived in enumerate(last_arrived):
        final = i == len(last_arrived) - 1
        columns_of = [(2 * eighth * i, 2 * eighth * (i + 1))] * (levels - 1)
        if final:
            columns_of.append((0, joined.shape[1]))
        parts = pair_call(
            functools.partial(
                last_kernel, [(level, *cut) for level, cut in enumerate(columns_of)], samples
            ),
            [masks, sums, last_panel, *arrived],
            flops * eighth,
            devices if final else 1,
        )
        sums = parts[0]
    distances = [1, *range(devices - 1, 1, -1), 0]
    parts = [
        xor_permute(parts[distance], "inp", distance) if distance else parts[0]
        for distance in distances
    ]
    return finish(parts, distances, levels, 2 * width - 1)


def solution(mesh):
    return jax.shard_map(
        on_device,
        mesh=mesh,
        in_specs=(P("freq", None, "inp", None), P("inp", None), P("inp", None, None)),
        out_specs=P("inp", "freq", None, None),
        check_vma=False,
    )
```

```python
import functools

import jax
import jax.numpy as jnp
from jax import lax
from jax.experimental import pallas as pl
from jax.experimental.pallas import tpu as pltpu
from jax.sharding import PartitionSpec as P

RG_DEV = 8
GROUP_ROWS = 16
EARLY_TILES = 3
HBM = pl.BlockSpec(memory_space=pltpu.HBM)
WHOLE = pl.BlockSpec(memory_space=pltpu.VMEM)


def xor_permute(x, axis, distance):
    return lax.ppermute(x, axis, [(i, i ^ distance) for i in range(lax.axis_size(axis))])


def parity(index, levels):
    bits = index & 1
    for level in range(1, levels):
        bits = bits ^ ((index >> level) & 1)
    return bits


def order_matrix(position_row):
    width = position_row.shape[-1]
    by_position = jnp.transpose(jnp.broadcast_to(position_row, (width, width)))
    inputs = lax.broadcasted_iota(jnp.int32, (width, width), 1)
    return (by_position == inputs).astype(jnp.float32).astype(jnp.bfloat16)


def product(x, y):
    return lax.dot_general(x, y, (((1,), (1,)), ((), ())), preferred_element_type=jnp.float32)


def lag_rows(tiles):
    count, width, _ = tiles.shape
    half = width // 2
    low, high = tiles[:, :half], tiles[:, half:]
    sheared = jnp.concatenate(
        [
            high[:, :, :half],
            high[:, :, half:] + low[:, :, :half],
            low[:, :, half:],
            jnp.zeros((count, half, half), jnp.float32),
        ],
        axis=2,
    )
    rows = half
    while rows > 8:
        rows //= 2
        upper = sheared[:, :rows].reshape(count * rows, 2 * width)
        upper = pltpu.roll(upper, rows, 1).reshape(count, rows, 2 * width)
        sheared = upper + sheared[:, rows:]
    flat = sheared.reshape(count * rows, 2 * width)
    sublane = lax.broadcasted_iota(jnp.int32, flat.shape, 0) % 8
    while rows > 1:
        rows //= 2
        flat = jnp.where((sublane & rows) == 0, pltpu.roll(flat, rows, 1), flat)
    return jnp.sum(flat.reshape(count, 8, 2 * width), axis=1)


def tile_lags(x_re, x_im, y_re, y_im, samples):
    real_part = product(x_re, y_re) + product(x_im, y_im)
    imag_part = product(x_im, y_re) - product(x_re, y_im)
    return lag_rows(jnp.stack([real_part, imag_part])) * (1.0 / samples)


def split_rows(x):
    first = x.astype(jnp.bfloat16).astype(jnp.float32)
    rest = x - first
    second = rest.astype(jnp.bfloat16).astype(jnp.float32)
    return jnp.concatenate([first, second, rest - second], axis=0)


def anti_identity(size):
    place = lax.broadcasted_iota(jnp.int32, (size, size), 0) + lax.broadcasted_iota(
        jnp.int32, (size, size), 1
    )
    return (place == size - 1).astype(jnp.float32).astype(jnp.bfloat16)


def turn_lags(terms):
    count, width = terms.shape
    lanes = 128
    spans = range(0, width, lanes)
    terms = jnp.concatenate([terms[:, first : first + lanes] for first in spans], axis=0)
    terms = jnp.dot(
        terms.astype(jnp.bfloat16), anti_identity(lanes), preferred_element_type=jnp.float32
    )
    blocks = [terms[count * i : count * (i + 1)] for i in reversed(range(len(spans)))]
    return pltpu.roll(jnp.concatenate(blocks, axis=1), width - 1, 1)


def conjugate_lags(lags):
    count = lags.shape[0]
    turned = turn_lags(split_rows(lags))
    turned = turned[:count] + turned[count : 2 * count] + turned[2 * count :]
    odd = lax.broadcasted_iota(jnp.int32, turned.shape, 0) % 2 == 1
    return jnp.where(odd, -turned, turned)


def reversed_lags(lags):
    count, width = lags.shape
    lanes = 128
    rows = jnp.pad(lags, ((0, -count % 8), (0, 0)))
    index = lanes - 1 - lax.broadcasted_iota(jnp.int32, (rows.shape[0], lanes), 1)
    blocks = [
        jnp.take_along_axis(
            rows[:, first : first + lanes], index, axis=1, mode="promise_in_bounds"
        )
        for first in reversed(range(0, width, lanes))
    ]
    return pltpu.roll(jnp.concatenate(blocks, axis=1), width - 1, 1)[:count]


def sheared_eights(tiles):
    count, width, _ = tiles.shape
    half = width // 2
    low, high = tiles[:, :half], tiles[:, half:]
    sheared = jnp.concatenate(
        [
            low[:, :, :half],
            low[:, :, half:] + high[:, :, :half],
            high[:, :, half:],
            jnp.zeros((count, half, half), jnp.float32),
        ],
        axis=2,
    )
    rows = half
    while rows > 8:
        rows //= 2
        lower = sheared[:, rows:].reshape(count * rows, 2 * width)
        lower = pltpu.roll(lower, rows, 1).reshape(count, rows, 2 * width)
        sheared = sheared[:, :rows] + lower
    return [pltpu.roll(sheared[i], 0, 1, stride=1, stride_axis=0) for i in range(count)]


def group_block(groups, columns=128):
    rows = jnp.concatenate([groups[b] for b in range(groups.shape[0])], axis=0)
    lines, lanes = rows.shape
    return jnp.pad(rows, ((0, GROUP_ROWS - lines), (0, columns - lanes)))


def target_rows(groups):
    return groups ^ (lax.axis_index("inp") * RG_DEV)


def pick_matrix(entries, rows):
    count = len(entries)
    shape = (rows, 3 * count)
    row = lax.broadcasted_iota(jnp.int32, shape, 0)
    column = lax.broadcasted_iota(jnp.int32, shape, 1) % count
    pick = jnp.zeros(shape, jnp.float32)
    for j, (targets, line, lane, part) in enumerate(entries):
        target = targets[line : line + 1, lane : lane + 1] + part * (rows // 2)
        target = jnp.broadcast_to(target, shape)
        pick = jnp.where(jnp.logical_and(column == j, row == target), 1.0, pick)
    return pick.astype(jnp.bfloat16)


def row_masks(entries, rows):
    row = lax.broadcasted_iota(jnp.int32, (rows, 128), 0)
    masks = []
    for targets, line, lane, _ in entries:
        target = jnp.broadcast_to(targets[line : line + 1, lane : lane + 1], row.shape)
        masks.append((row == target).astype(jnp.float32))
    return jnp.stack(masks)


def pick_matrices(groups, heads, blocks, out_rows):
    own = target_rows(group_block(groups))
    others = [target_rows(head.astype(jnp.float32).astype(jnp.int32)) for head in heads]
    groups_all = out_rows // 2

    def pairs(b):
        order = [(level, a, p) for level in range(len(heads)) for a in range(blocks) for p in range(2)]
        forward = [(own, a * blocks + b, level + 1, p) for level, a, p in order]
        turned = [(others[level], b * blocks + a, level + 1, p) for level, a, p in order]
        return forward, turned

    forward, turned = zip(*[pairs(b) for b in range(blocks)])
    tiles = [
        [(targets, line, 0, p) for line in range(blocks * blocks) for p in range(2)]
        for targets in (own, others[-1])
    ]
    both = [entry for side in (forward, turned) for block in side for entry in block]
    return [
        pick_matrix(tiles[0], out_rows),
        pick_matrix(tiles[1], out_rows),
        pick_matrix(both, out_rows),
        row_masks(forward[-1][::2] + turned[-1][::2], groups_all),
    ]


def group_sums(pick, lags):
    terms = split_rows(lags).astype(jnp.bfloat16)
    return jnp.dot(pick, terms, preferred_element_type=jnp.float32)


def columns(piece):
    spans, start = [], 0
    for _, first, last in piece:
        spans.append((start, start + last - first))
        start += last - first
    return spans


def piece_shape(piece, width, more):
    return jax.ShapeDtypeStruct((2 * width + more, columns(piece)[-1][1]), jnp.bfloat16)


def load_piece(piece, other, width, volts_ref, raw, in_sem):
    blocks = sorted({block for block, _, _ in piece})
    loads = []
    for i, block in enumerate(blocks):
        start = min(first for b, first, _ in piece if b == block)
        end = max(last for b, _, last in piece if b == block)
        for c in range(2):
            load = pltpu.make_async_copy(
                volts_ref.at[other, c, pl.ds(block * width, width), pl.ds(start, end - start)],
                raw.at[i, c, :, pl.ds(start, end - start)],
                in_sem.at[i, c],
            )
            load.start()
            loads.append((i, block, c, load))
    return loads


def order_piece(piece, loads, position, raw, out_ref):
    width = position.shape[1]
    orders = {
        block: order_matrix(position[block : block + 1, :]) for block in sorted({l[1] for l in loads})
    }
    for i, block, c, load in loads:
        load.wait()
        for (b, first, last), (start, end) in zip(piece, columns(piece)):
            if b == block:
                out_ref[c * width : (c + 1) * width, start:end] = jnp.dot(
                    orders[block], raw[i, c, :, first:last], preferred_element_type=jnp.float32
                ).astype(jnp.bfloat16)


def head_kernel(levels, piece, position_ref, volts_ref, group_ref, head_ref, *scratch):
    position, groups, small_sem, in_sem = scratch
    other = 1 - parity(lax.axis_index("inp"), levels)
    width = position.shape[1]
    ((block, first, last),) = piece
    smalls = [
        pltpu.make_async_copy(position_ref, position, small_sem.at[0]),
        pltpu.make_async_copy(group_ref, groups, small_sem.at[1]),
    ]
    loads = [
        pltpu.make_async_copy(
            volts_ref.at[other, c, pl.ds(block * width, width), pl.ds(first, last - first)],
            head_ref.at[pl.ds(c * width, width), :],
            in_sem.at[c],
        )
        for c in range(2)
    ]
    for copy in smalls + loads:
        copy.start()
    for copy in smalls:
        copy.wait()
    rows = group_block(groups[...], last - first)
    line = lax.broadcasted_iota(jnp.int32, rows.shape, 0)
    own_row = jnp.broadcast_to(position[block : block + 1, :], rows.shape)
    rows = jnp.where(line == groups.shape[0] ** 2, own_row, rows)
    head_ref[2 * width :, :] = rows.astype(jnp.float32).astype(jnp.bfloat16)
    for copy in loads:
        copy.wait()


def on_odd_core():
    return lax.axis_index("freq") % 2 == 1


def load_channel(channel, volts_ref, raw, in_sem):
    blocks, _, width, _ = raw.shape
    loads = []
    for b in range(blocks):
        for c in range(2):
            load = pltpu.make_async_copy(
                volts_ref.at[channel, c, pl.ds(b * width, width)], raw.at[b, c], in_sem.at[b, c]
            )
            load.start()
            loads.append((b, c, load))
    return loads


def order_channel(loads, position_ref, raw, panel):
    blocks = raw.shape[0]
    orders = [order_matrix(position_ref[b : b + 1, :]) for b in range(blocks)]
    for b, c, load in loads:
        load.wait()
        rows = jnp.dot(orders[b], raw[b, c], preferred_element_type=jnp.float32)
        panel[b, c] = rows.astype(jnp.bfloat16)


def own_tiles(panel, lags_ref, start, first, last):
    blocks, _, width, samples = panel.shape

    def one_tile(index, carry):
        a = index // blocks
        b = index % blocks
        lags = tile_lags(panel[a, 0], panel[a, 1], panel[b, 0], panel[b, 1], samples)
        center = lax.broadcasted_iota(jnp.int32, lags.shape, 1) == width - 1
        lags_ref[start + index] = jnp.where(jnp.logical_and(center, a == b), 0.0, lags)
        return carry

    lax.fori_loop(first, last, one_tile, 0)


def rest_kernel(levels, piece, position_ref, volts_ref, _, out_ref, panel_ref, lags_ref, *scratch):
    position, raw, small_sem, in_sem = scratch
    mine = parity(lax.axis_index("inp"), levels)
    load_position = pltpu.make_async_copy(position_ref, position, small_sem)
    load_position.start()
    load_position.wait()

    @pl.when(on_odd_core())
    def _():
        loads = load_channel(mine, volts_ref, raw, in_sem)
        order_channel(loads, position, raw, panel_ref)
        own_tiles(panel_ref, lags_ref, 0, 0, EARLY_TILES)

    loads = load_piece(piece, 1 - mine, position.shape[1], volts_ref, raw, in_sem)
    order_piece(piece, loads, position, raw, out_ref)


def early_pieces(position_input, volts, groups, head, rest, levels):
    blocks, width = position_input.shape
    samples = volts.shape[3]
    assert columns(head)[-1][1] == width
    in_hbm = [pltpu.with_memory_space_constraint(x, pltpu.HBM) for x in (position_input, volts)]
    position = pltpu.VMEM(position_input.shape, jnp.int32)
    semaphore = pltpu.SemaphoreType.DMA
    sent = pl.pallas_call(
        functools.partial(head_kernel, levels, head),
        out_shape=piece_shape(head, width, GROUP_ROWS),
        in_specs=[HBM] * 3,
        out_specs=WHOLE,
        scratch_shapes=[
            position,
            pltpu.VMEM(groups.shape, jnp.int32),
            semaphore((2,)),
            semaphore((2,)),
        ],
        compiler_params=pltpu.CompilerParams(vmem_limit_bytes=8 << 20),
        cost_estimate=pl.CostEstimate(flops=0, bytes_accessed=1 << 20, transcendentals=0),
        name="first_piece",
    )(*in_hbm, pltpu.with_memory_space_constraint(groups, pltpu.HBM))
    second, early_panel, early_lags = pl.pallas_call(
        functools.partial(rest_kernel, levels, rest),
        out_shape=[
            piece_shape(rest, width, 0),
            jax.ShapeDtypeStruct((blocks, 2, width, samples), jnp.bfloat16),
            jax.ShapeDtypeStruct((blocks * blocks, 2, 2 * width), jnp.float32),
        ],
        in_specs=[HBM, HBM, pl.BlockSpec(memory_space=pl.ANY)],
        out_specs=[WHOLE] * 3,
        scratch_shapes=[
            position,
            pltpu.VMEM((blocks, 2, width, samples), jnp.bfloat16),
            semaphore(()),
            semaphore((blocks, 2)),
        ],
        compiler_params=pltpu.CompilerParams(vmem_limit_bytes=16 << 20),
        cost_estimate=pl.CostEstimate(
            flops=4 * width * width * columns(rest)[-1][1],
            bytes_accessed=4 << 20,
            transcendentals=0,
        ),
        name="second_piece",
    )(*in_hbm, sent)
    return sent, second, early_panel, early_lags


def own_kernel(levels, piece, last, group_ref, position_ref, volts_ref, *refs):
    head_refs, refs = refs[:levels][::-1], refs[levels:]
    early_panel_ref, early_lags_ref, *refs = refs
    panel_ref, sums_ref, *refs, raw, other_raw, other_panel, lags_ref, in_sem, other_sem = refs
    pick_refs, ordered_refs, refs = refs[:3], refs[3 : 3 + levels], refs[3 + levels :]
    more_ref, piece_ref, *last_refs, joined_ref, last_panel_ref = refs
    blocks, _, width, _ = panel_ref.shape
    mine = parity(lax.axis_index("inp"), levels)
    other_loads = load_channel(1 - mine, volts_ref, other_raw, other_sem)

    @pl.when(jnp.logical_not(on_odd_core()))
    def _():
        loads = load_channel(mine, volts_ref, raw, in_sem)
        order_channel(loads, position_ref, raw, panel_ref)
        own_tiles(panel_ref, lags_ref, 0, 0, EARLY_TILES)

    @pl.when(on_odd_core())
    def _():
        for b in range(blocks):
            for c in range(2):
                panel_ref[b, c] = early_panel_ref[b, c]
        for i in range(EARLY_TILES):
            lags_ref[i] = early_lags_ref[i]

    tiles = blocks * blocks
    own_tiles(panel_ref, lags_ref, 0, EARLY_TILES, tiles)
    order_channel(other_loads, position_ref, other_raw, other_panel)
    own_tiles(other_panel, lags_ref, tiles, 0, tiles)
    lags = jnp.concatenate([lags_ref[i] for i in range(tiles)], axis=0)
    heads = [head_ref[2 * width :, :] for head_ref in head_refs]
    for head, head_ref, ordered_ref in zip(heads, head_refs, ordered_refs):
        positions = head.astype(jnp.float32).astype(jnp.int32)[blocks**2 : blocks**2 + 1]
        order = order_matrix(positions)
        for c in range(2):
            rows = head_ref[c * width : (c + 1) * width, :]
            rows = jnp.dot(order, rows, preferred_element_type=jnp.float32)
            ordered_ref[c * width : (c + 1) * width, :] = rows.astype(jnp.bfloat16)
    own_pick, *picks = pick_matrices(group_ref[...], heads, blocks, sums_ref.shape[0])
    for pick_ref, pick in zip(pick_refs, picks):
        pick_ref[...] = pick
    sums_ref[...] = group_sums(own_pick, lags)
    for (block, first, end), (start, stop) in zip(piece, columns(piece)):
        for c in range(2):
            rows = other_panel[block, c, :, first:end]
            piece_ref[c * width : (c + 1) * width, start:stop] = rows
            more_ref[c * width : (c + 1) * width, start:stop] = rows
    lags = jnp.concatenate([lags_ref[tiles + i] for i in range(tiles)], axis=0)
    high = lags.astype(jnp.bfloat16).astype(jnp.float32)
    terms = jnp.concatenate([high, lags - high], axis=0)
    more_ref[2 * width :, :] = terms.astype(jnp.bfloat16)
    start = 0
    for (block, first, end), last_ref in zip(last, last_refs):
        for c in range(2):
            depth = end - first
            rows = other_panel[block, c, :, first:end]
            last_ref[:, c * depth : (c + 1) * depth] = rows
            joined_ref[:, start : start + depth] = rows
            start += depth
    turn = anti_identity(width)
    for a in range(blocks):
        start = 0
        for _, first, end in last:
            real_part, imag_part = [
                jnp.dot(turn, panel_ref[a, c, :, first:end], preferred_element_type=jnp.float32)
                for c in range(2)
            ]
            middle, stop = start + end - first, start + 2 * (end - first)
            last_panel_ref[a, :width, start:middle] = real_part.astype(jnp.bfloat16)
            last_panel_ref[a, :width, middle:stop] = imag_part.astype(jnp.bfloat16)
            last_panel_ref[a, width:, start:middle] = imag_part.astype(jnp.bfloat16)
            last_panel_ref[a, width:, middle:stop] = (-real_part).astype(jnp.bfloat16)
            start = stop


def own_level(groups, position_input, volts, early, heads, piece, last, out_rows):
    levels = len(heads)
    blocks, width = position_input.shape
    samples = volts.shape[3]
    pairs = 4 * levels * blocks
    tiles = 2 * blocks * blocks
    counts = (3 * tiles, 3 * pairs * blocks)
    depths = [2 * (end - first) for _, first, end in last]
    return pl.pallas_call(
        functools.partial(own_kernel, levels, piece, last),
        out_shape=(
            jax.ShapeDtypeStruct((blocks, 2, width, samples), jnp.bfloat16),
            jax.ShapeDtypeStruct((out_rows, 2 * width), jnp.float32),
            *[jax.ShapeDtypeStruct((out_rows, n), jnp.bfloat16) for n in counts],
            jax.ShapeDtypeStruct((pairs // 2, out_rows // 2, 128), jnp.float32),
            *[jax.ShapeDtypeStruct((2 * width, head.shape[1]), jnp.bfloat16) for head in heads],
            piece_shape(piece, width, 2 * tiles),
            piece_shape(piece, width, 0),
            *[jax.ShapeDtypeStruct((width, depth), jnp.bfloat16) for depth in depths],
            jax.ShapeDtypeStruct((width, sum(depths)), jnp.bfloat16),
            jax.ShapeDtypeStruct((blocks, 2 * width, sum(depths)), jnp.bfloat16),
        ),
        in_specs=[WHOLE, WHOLE, HBM] + [WHOLE] * (len(early) + levels),
        out_specs=(WHOLE,) * (7 + len(counts) + levels + len(last)),
        scratch_shapes=[
            pltpu.VMEM((blocks, 2, width, samples), jnp.bfloat16),
            pltpu.VMEM((blocks, 2, width, samples), jnp.bfloat16),
            pltpu.VMEM((blocks, 2, width, samples), jnp.bfloat16),
            pltpu.VMEM((2 * blocks * blocks, 2, 2 * width), jnp.float32),
            pltpu.SemaphoreType.DMA((blocks, 2)),
            pltpu.SemaphoreType.DMA((blocks, 2)),
        ],
        compiler_params=pltpu.CompilerParams(vmem_limit_bytes=16 << 20),
        cost_estimate=pl.CostEstimate(
            flops=64 * blocks * blocks * width * width * samples,
            bytes_accessed=12 * blocks * width * samples,
            transcendentals=0,
        ),
        name="own_level",
    )(groups, position_input, pltpu.with_memory_space_constraint(volts, pltpu.HBM), *heads[::-1], *early)


def add_lags(rows, pick_ref, sums_ref):
    lags = jnp.concatenate(rows, axis=0)
    lags = jnp.concatenate([lags, conjugate_lags(lags)], axis=0)
    return sums_ref[...] + group_sums(pick_ref[...], lags)


def add_masked(lags, tiles_at, mask_ref, sums_ref):
    turned = reversed_lags(lags)
    half, count = sums_ref.shape[0] // 2, mask_ref.shape[0] // 2
    sums = [sums_ref[:half, :], sums_ref[half:, :]]
    for i, tile in enumerate(tiles_at):
        forward = jnp.concatenate([mask_ref[tile]] * (sums_ref.shape[1] // 128), axis=1)
        back = jnp.concatenate([mask_ref[count + tile]] * (sums_ref.shape[1] // 128), axis=1)
        re, im = 2 * i, 2 * i + 1
        sums[0] = sums[0] + forward * lags[re : re + 1] + back * turned[re : re + 1]
        sums[1] = sums[1] + forward * lags[im : im + 1] - back * turned[im : im + 1]
    return sums


def pair_kernel(levels, pieces, passed, pick_ref, sums_ref, panel_ref, *refs):
    count = levels * len(pieces)
    out_ref = refs[-1 - passed]
    partner_refs, more_refs = refs[:count], refs[count : len(refs) - 1 - 2 * passed]
    _, _, width, samples = panel_ref.shape
    rows = []
    for block in sorted({block for piece in pieces for block, _, _ in piece}):
        for level in range(levels):
            for a in range(panel_ref.shape[0]):
                real_part, imag_part = 0.0, 0.0
                for i, piece in enumerate(pieces):
                    partner = partner_refs[level * len(pieces) + i]
                    for (b, first, last), (start, end) in zip(piece, columns(piece)):
                        if b != block:
                            continue
                        x_re, x_im = panel_ref[a, 0, :, first:last], panel_ref[a, 1, :, first:last]
                        y_re = partner[:width, start:end]
                        y_im = partner[width : 2 * width, start:end]
                        real_part = real_part + (product(x_re, y_re) + product(x_im, y_im))
                        imag_part = imag_part + (product(x_im, y_re) - product(x_re, y_im))
                rows.append(lag_rows(jnp.stack([real_part, imag_part])) * (1.0 / samples))
    if len(pick_ref.shape) == 3:
        sums = add_masked(jnp.concatenate(rows, axis=0), range(len(rows)), pick_ref, sums_ref)
        sums = jnp.concatenate(sums, axis=0)
    else:
        sums = add_lags(rows, pick_ref, sums_ref)
    for more_ref in more_refs:
        terms = partner_refs[-1][2 * width :, :].astype(jnp.float32)
        half = terms.shape[0] // 2
        sums = sums + group_sums(more_ref[...], terms[:half] + terms[half:])
    out_ref[...] = sums


def last_kernel(parts, samples, mask_ref, sums_ref, panel_ref, *refs):
    partner_refs, out_refs = refs[: len(parts)], refs[len(parts) :]
    blocks, rows_both, _ = panel_ref.shape
    width = rows_both // 2
    rows, tiles_at = [], []
    for (level, first, last), partner_ref in zip(parts, partner_refs):
        for a in range(blocks):
            tiles = product(panel_ref[a, :, first:last], partner_ref[...])
            rows += sheared_eights(tiles.reshape(2, width, width))
            tiles_at.append(level * blocks + a)
    lags = jnp.sum(jnp.stack(rows), axis=1) * (1.0 / samples)
    sums = add_masked(lags, tiles_at, mask_ref, sums_ref)
    half = sums_ref.shape[0] // 2
    share = half // len(out_refs)
    for place, out_ref in enumerate(out_refs):
        for part in range(2):
            rows = sums[part][place * share : (place + 1) * share]
            out_ref[part * share : (part + 1) * share, :] = rows


def pair_call(kernel, inputs, work, shares=1, passed=()):
    rows, width = inputs[1].shape
    any_space = [pl.BlockSpec(memory_space=pl.ANY)] * len(passed)
    return pl.pallas_call(
        kernel,
        out_shape=[jax.ShapeDtypeStruct((rows // shares, width), jnp.float32)] * shares
        + [jax.ShapeDtypeStruct(x.shape, x.dtype) for x in passed],
        in_specs=[WHOLE] * len(inputs) + any_space,
        out_specs=[WHOLE] * shares + any_space,
        input_output_aliases={len(inputs) + i: shares + i for i in range(len(passed))},
        compiler_params=pltpu.CompilerParams(vmem_limit_bytes=16 << 20),
        cost_estimate=pl.CostEstimate(flops=work, bytes_accessed=4 << 20, transcendentals=0),
        name="pair_level",
    )(*inputs, *passed)


def finish_kernel(levels, distances, *refs):
    part_refs, out_ref = refs[:-1], refs[-1]
    mine = parity(lax.axis_index("inp"), levels)
    groups, channels, parts, lags = out_ref.shape
    sums = [None, None]
    for distance, part_ref in zip(distances, part_refs):
        side = distance.bit_count() % 2
        sums[side] = part_ref[...] if sums[side] is None else sums[side] + part_ref[...]
    for f in range(channels):
        total = jnp.where(mine == f, sums[0], sums[1])
        for g in range(groups):
            for part in range(parts):
                row = part * groups + g
                out_ref[g, f, part : part + 1] = total[row : row + 1, :lags]


def finish(parts, distances, levels, lags):
    return pl.pallas_call(
        functools.partial(finish_kernel, levels, distances),
        out_shape=jax.ShapeDtypeStruct((RG_DEV, 2, 2, lags), jnp.float32),
        in_specs=[WHOLE] * len(parts),
        out_specs=WHOLE,
        compiler_params=pltpu.CompilerParams(vmem_limit_bytes=8 << 20),
        name="finish",
    )(*parts)


def on_device(volts, position_input, tile_group):
    blocks, width = position_input.shape
    samples = volts.shape[3]
    devices = lax.axis_size("inp")
    levels = devices.bit_length() - 1
    out_rows = devices * RG_DEV * 2
    eighth = samples // 8
    head = [(0, 0, 2 * eighth)]
    rest = [(0, 2 * eighth, samples), (1, 0, 2 * eighth)]
    tail = [(1, 2 * eighth, 6 * eighth)]
    last = [(1, 6 * eighth, 7 * eighth), (1, 7 * eighth, samples)]
    by_block = tile_group.transpose(0, 2, 1)
    partner_of = [functools.partial(xor_permute, axis="inp", distance=1 << l) for l in range(levels)]
    sent, second, *early = early_pieces(position_input, volts, by_block, head, rest, levels)
    head_arrived = [send(sent) for send in partner_of]
    rest_arrived = [send(second) for send in partner_of]
    panel, sums, neighbour, both, masks, *sent = own_level(
        by_block, position_input, volts, early, head_arrived, tail, last, out_rows
    )
    head_ordered, (more, piece, *last_pieces, last_panel) = sent[:levels], sent[levels:]
    tail_arrived = [send(piece) for send in partner_of[:-1]] + [partner_of[-1](more)]

    flops = 8 * levels * blocks * width * width
    arrived = [piece for pair in zip(head_ordered, rest_arrived) for piece in pair]
    sums, *last_pieces = pair_call(
        functools.partial(pair_kernel, levels, [head, rest], len(last_pieces)),
        [both, sums, panel, *arrived],
        flops * 10 * eighth,
        passed=last_pieces,
    )
    *last_pieces, joined = last_pieces
    last_arrived = [[send(piece) for send in partner_of[:-1]] for piece in last_pieces]
    last_arrived[-1].append(partner_of[-1](joined))
    (sums,) = pair_call(
        functools.partial(pair_kernel, levels, [tail], 0),
        [masks, sums, panel, *tail_arrived, neighbour],
        flops * 4 * eighth,
    )
    for i, arrived in enumerate(last_arrived):
        final = i == len(last_arrived) - 1
        columns_of = [(2 * eighth * i, 2 * eighth * (i + 1))] * (levels - 1)
        if final:
            columns_of.append((0, joined.shape[1]))
        parts = pair_call(
            functools.partial(
                last_kernel, [(level, *cut) for level, cut in enumerate(columns_of)], samples
            ),
            [masks, sums, last_panel, *arrived],
            flops * eighth,
            devices if final else 1,
        )
        sums = parts[0]
    distances = [1, *range(devices - 1, 1, -1), 0]
    parts = [
        xor_permute(parts[distance], "inp", distance) if distance else parts[0]
        for distance in distances
    ]
    return finish(parts, distances, levels, 2 * width - 1)


def solution(mesh):
    return jax.shard_map(
        on_device,
        mesh=mesh,
        in_specs=(P("freq", None, "inp", None), P("inp", None), P("inp", None, None)),
        out_specs=P("inp", "freq", None, None),
        check_vma=False,
    )
```

```python
import functools

import jax
import jax.numpy as jnp
from jax import lax
from jax.experimental import pallas as pl
from jax.experimental.pallas import tpu as pltpu
from jax.sharding import PartitionSpec as P

RG_DEV = 8
GROUP_ROWS = 16
EARLY_TILES = 1
HBM = pl.BlockSpec(memory_space=pltpu.HBM)
WHOLE = pl.BlockSpec(memory_space=pltpu.VMEM)


def xor_permute(x, axis, distance):
    return lax.ppermute(x, axis, [(i, i ^ distance) for i in range(lax.axis_size(axis))])


def parity(index, levels):
    bits = index & 1
    for level in range(1, levels):
        bits = bits ^ ((index >> level) & 1)
    return bits


def order_matrix(position_row):
    width = position_row.shape[-1]
    by_position = jnp.transpose(jnp.broadcast_to(position_row, (width, width)))
    inputs = lax.broadcasted_iota(jnp.int32, (width, width), 1)
    return (by_position == inputs).astype(jnp.float32).astype(jnp.bfloat16)


def product(x, y):
    return lax.dot_general(x, y, (((1,), (1,)), ((), ())), preferred_element_type=jnp.float32)


def lag_rows(tiles):
    count, width, _ = tiles.shape
    half = width // 2
    low, high = tiles[:, :half], tiles[:, half:]
    sheared = jnp.concatenate(
        [
            high[:, :, :half],
            high[:, :, half:] + low[:, :, :half],
            low[:, :, half:],
            jnp.zeros((count, half, half), jnp.float32),
        ],
        axis=2,
    )
    rows = half
    while rows > 8:
        rows //= 2
        upper = sheared[:, :rows].reshape(count * rows, 2 * width)
        upper = pltpu.roll(upper, rows, 1).reshape(count, rows, 2 * width)
        sheared = upper + sheared[:, rows:]
    flat = sheared.reshape(count * rows, 2 * width)
    sublane = lax.broadcasted_iota(jnp.int32, flat.shape, 0) % 8
    while rows > 1:
        rows //= 2
        flat = jnp.where((sublane & rows) == 0, pltpu.roll(flat, rows, 1), flat)
    return jnp.sum(flat.reshape(count, 8, 2 * width), axis=1)


def tile_lags(x_re, x_im, y_re, y_im, samples):
    real_part = product(x_re, y_re) + product(x_im, y_im)
    imag_part = product(x_im, y_re) - product(x_re, y_im)
    return lag_rows(jnp.stack([real_part, imag_part])) * (1.0 / samples)


def split_rows(x):
    first = x.astype(jnp.bfloat16).astype(jnp.float32)
    rest = x - first
    second = rest.astype(jnp.bfloat16).astype(jnp.float32)
    return jnp.concatenate([first, second, rest - second], axis=0)


def anti_identity(size):
    place = lax.broadcasted_iota(jnp.int32, (size, size), 0) + lax.broadcasted_iota(
        jnp.int32, (size, size), 1
    )
    return (place == size - 1).astype(jnp.float32).astype(jnp.bfloat16)


def turn_lags(terms):
    count, width = terms.shape
    lanes = 128
    spans = range(0, width, lanes)
    terms = jnp.concatenate([terms[:, first : first + lanes] for first in spans], axis=0)
    terms = jnp.dot(
        terms.astype(jnp.bfloat16), anti_identity(lanes), preferred_element_type=jnp.float32
    )
    blocks = [terms[count * i : count * (i + 1)] for i in reversed(range(len(spans)))]
    return pltpu.roll(jnp.concatenate(blocks, axis=1), width - 1, 1)


def conjugate_lags(lags):
    count = lags.shape[0]
    turned = turn_lags(split_rows(lags))
    turned = turned[:count] + turned[count : 2 * count] + turned[2 * count :]
    odd = lax.broadcasted_iota(jnp.int32, turned.shape, 0) % 2 == 1
    return jnp.where(odd, -turned, turned)


def reversed_lags(lags):
    count, width = lags.shape
    lanes = 128
    rows = jnp.pad(lags, ((0, -count % 8), (0, 0)))
    index = lanes - 1 - lax.broadcasted_iota(jnp.int32, (rows.shape[0], lanes), 1)
    blocks = [
        jnp.take_along_axis(
            rows[:, first : first + lanes], index, axis=1, mode="promise_in_bounds"
        )
        for first in reversed(range(0, width, lanes))
    ]
    return pltpu.roll(jnp.concatenate(blocks, axis=1), width - 1, 1)[:count]


def sheared_eights(tiles):
    count, width, _ = tiles.shape
    half = width // 2
    low, high = tiles[:, :half], tiles[:, half:]
    sheared = jnp.concatenate(
        [
            low[:, :, :half],
            low[:, :, half:] + high[:, :, :half],
            high[:, :, half:],
            jnp.zeros((count, half, half), jnp.float32),
        ],
        axis=2,
    )
    rows = half
    while rows > 8:
        rows //= 2
        lower = sheared[:, rows:].reshape(count * rows, 2 * width)
        lower = pltpu.roll(lower, rows, 1).reshape(count, rows, 2 * width)
        sheared = sheared[:, :rows] + lower
    return [pltpu.roll(sheared[i], 0, 1, stride=1, stride_axis=0) for i in range(count)]


def group_block(groups, columns=128):
    rows = jnp.concatenate([groups[b] for b in range(groups.shape[0])], axis=0)
    lines, lanes = rows.shape
    return jnp.pad(rows, ((0, GROUP_ROWS - lines), (0, columns - lanes)))


def target_rows(groups):
    return groups ^ (lax.axis_index("inp") * RG_DEV)


def pick_matrix(entries, rows):
    count = len(entries)
    shape = (rows, 3 * count)
    row = lax.broadcasted_iota(jnp.int32, shape, 0)
    column = lax.broadcasted_iota(jnp.int32, shape, 1) % count
    pick = jnp.zeros(shape, jnp.float32)
    for j, (targets, line, lane, part) in enumerate(entries):
        target = targets[line : line + 1, lane : lane + 1] + part * (rows // 2)
        target = jnp.broadcast_to(target, shape)
        pick = jnp.where(jnp.logical_and(column == j, row == target), 1.0, pick)
    return pick.astype(jnp.bfloat16)


def row_masks(entries, rows):
    row = lax.broadcasted_iota(jnp.int32, (rows, 128), 0)
    masks = []
    for targets, line, lane, _ in entries:
        target = jnp.broadcast_to(targets[line : line + 1, lane : lane + 1], row.shape)
        masks.append((row == target).astype(jnp.float32))
    return jnp.stack(masks)


def pick_matrices(groups, heads, blocks, out_rows):
    own = target_rows(group_block(groups))
    others = [target_rows(head.astype(jnp.float32).astype(jnp.int32)) for head in heads]
    groups_all = out_rows // 2

    def pairs(b):
        order = [(level, a, p) for level in range(len(heads)) for a in range(blocks) for p in range(2)]
        forward = [(own, a * blocks + b, level + 1, p) for level, a, p in order]
        turned = [(others[level], b * blocks + a, level + 1, p) for level, a, p in order]
        return forward, turned

    forward, turned = zip(*[pairs(b) for b in range(blocks)])
    tiles = [
        [(targets, line, 0, p) for line in range(blocks * blocks) for p in range(2)]
        for targets in (own, others[-1])
    ]
    both = [entry for side in (forward, turned) for block in side for entry in block]
    return [
        pick_matrix(tiles[0], out_rows),
        pick_matrix(tiles[1], out_rows),
        pick_matrix(both, out_rows),
        row_masks(forward[-1][::2] + turned[-1][::2], groups_all),
    ]


def group_sums(pick, lags):
    terms = split_rows(lags).astype(jnp.bfloat16)
    return jnp.dot(pick, terms, preferred_element_type=jnp.float32)


def columns(piece):
    spans, start = [], 0
    for _, first, last in piece:
        spans.append((start, start + last - first))
        start += last - first
    return spans


def piece_shape(piece, width, more):
    return jax.ShapeDtypeStruct((2 * width + more, columns(piece)[-1][1]), jnp.bfloat16)


def load_piece(piece, other, width, volts_ref, raw, in_sem):
    blocks = sorted({block for block, _, _ in piece})
    loads = []
    for i, block in enumerate(blocks):
        start = min(first for b, first, _ in piece if b == block)
        end = max(last for b, _, last in piece if b == block)
        for c in range(2):
            load = pltpu.make_async_copy(
                volts_ref.at[other, c, pl.ds(block * width, width), pl.ds(start, end - start)],
                raw.at[i, c, :, pl.ds(start, end - start)],
                in_sem.at[i, c],
            )
            load.start()
            loads.append((i, block, c, load))
    return loads


def order_piece(piece, loads, position, raw, out_ref):
    width = position.shape[1]
    orders = {
        block: order_matrix(position[block : block + 1, :]) for block in sorted({l[1] for l in loads})
    }
    for i, block, c, load in loads:
        load.wait()
        for (b, first, last), (start, end) in zip(piece, columns(piece)):
            if b == block:
                out_ref[c * width : (c + 1) * width, start:end] = jnp.dot(
                    orders[block], raw[i, c, :, first:last], preferred_element_type=jnp.float32
                ).astype(jnp.bfloat16)


def head_kernel(levels, piece, position_ref, volts_ref, group_ref, head_ref, *scratch):
    position, groups, small_sem, in_sem = scratch
    other = 1 - parity(lax.axis_index("inp"), levels)
    width = position.shape[1]
    ((block, first, last),) = piece
    smalls = [
        pltpu.make_async_copy(position_ref, position, small_sem.at[0]),
        pltpu.make_async_copy(group_ref, groups, small_sem.at[1]),
    ]
    loads = [
        pltpu.make_async_copy(
            volts_ref.at[other, c, pl.ds(block * width, width), pl.ds(first, last - first)],
            head_ref.at[pl.ds(c * width, width), :],
            in_sem.at[c],
        )
        for c in range(2)
    ]
    for copy in smalls + loads:
        copy.start()
    for copy in smalls:
        copy.wait()
    rows = group_block(groups[...], last - first)
    line = lax.broadcasted_iota(jnp.int32, rows.shape, 0)
    own_row = jnp.broadcast_to(position[block : block + 1, :], rows.shape)
    rows = jnp.where(line == groups.shape[0] ** 2, own_row, rows)
    head_ref[2 * width :, :] = rows.astype(jnp.float32).astype(jnp.bfloat16)
    for copy in loads:
        copy.wait()


def on_odd_core():
    return lax.axis_index("freq") % 2 == 1


def load_channel(channel, volts_ref, raw, in_sem):
    blocks, _, width, _ = raw.shape
    loads = []
    for b in range(blocks):
        for c in range(2):
            load = pltpu.make_async_copy(
                volts_ref.at[channel, c, pl.ds(b * width, width)], raw.at[b, c], in_sem.at[b, c]
            )
            load.start()
            loads.append((b, c, load))
    return loads


def order_channel(loads, position_ref, raw, panel):
    blocks = raw.shape[0]
    orders = [order_matrix(position_ref[b : b + 1, :]) for b in range(blocks)]
    for b, c, load in loads:
        load.wait()
        rows = jnp.dot(orders[b], raw[b, c], preferred_element_type=jnp.float32)
        panel[b, c] = rows.astype(jnp.bfloat16)


def own_tiles(panel, lags_ref, start, first, last):
    blocks, _, width, samples = panel.shape

    def one_tile(index, carry):
        a = index // blocks
        b = index % blocks
        lags = tile_lags(panel[a, 0], panel[a, 1], panel[b, 0], panel[b, 1], samples)
        center = lax.broadcasted_iota(jnp.int32, lags.shape, 1) == width - 1
        lags_ref[start + index] = jnp.where(jnp.logical_and(center, a == b), 0.0, lags)
        return carry

    lax.fori_loop(first, last, one_tile, 0)


def rest_kernel(levels, piece, position_ref, volts_ref, _, out_ref, panel_ref, lags_ref, *scratch):
    position, raw, small_sem, in_sem = scratch
    mine = parity(lax.axis_index("inp"), levels)
    load_position = pltpu.make_async_copy(position_ref, position, small_sem)
    load_position.start()
    load_position.wait()

    @pl.when(on_odd_core())
    def _():
        loads = load_channel(mine, volts_ref, raw, in_sem)
        order_channel(loads, position, raw, panel_ref)
        own_tiles(panel_ref, lags_ref, 0, 0, EARLY_TILES)

    loads = load_piece(piece, 1 - mine, position.shape[1], volts_ref, raw, in_sem)
    order_piece(piece, loads, position, raw, out_ref)


def early_pieces(position_input, volts, groups, head, rest, levels):
    blocks, width = position_input.shape
    samples = volts.shape[3]
    assert columns(head)[-1][1] == width
    in_hbm = [pltpu.with_memory_space_constraint(x, pltpu.HBM) for x in (position_input, volts)]
    position = pltpu.VMEM(position_input.shape, jnp.int32)
    semaphore = pltpu.SemaphoreType.DMA
    sent = pl.pallas_call(
        functools.partial(head_kernel, levels, head),
        out_shape=piece_shape(head, width, GROUP_ROWS),
        in_specs=[HBM] * 3,
        out_specs=WHOLE,
        scratch_shapes=[
            position,
            pltpu.VMEM(groups.shape, jnp.int32),
            semaphore((2,)),
            semaphore((2,)),
        ],
        compiler_params=pltpu.CompilerParams(vmem_limit_bytes=8 << 20),
        cost_estimate=pl.CostEstimate(flops=0, bytes_accessed=1 << 20, transcendentals=0),
        name="first_piece",
    )(*in_hbm, pltpu.with_memory_space_constraint(groups, pltpu.HBM))
    second, early_panel, early_lags = pl.pallas_call(
        functools.partial(rest_kernel, levels, rest),
        out_shape=[
            piece_shape(rest, width, 0),
            jax.ShapeDtypeStruct((blocks, 2, width, samples), jnp.bfloat16),
            jax.ShapeDtypeStruct((blocks * blocks, 2, 2 * width), jnp.float32),
        ],
        in_specs=[HBM, HBM, pl.BlockSpec(memory_space=pl.ANY)],
        out_specs=[WHOLE] * 3,
        scratch_shapes=[
            position,
            pltpu.VMEM((blocks, 2, width, samples), jnp.bfloat16),
            semaphore(()),
            semaphore((blocks, 2)),
        ],
        compiler_params=pltpu.CompilerParams(vmem_limit_bytes=16 << 20),
        cost_estimate=pl.CostEstimate(
            flops=4 * width * width * columns(rest)[-1][1],
            bytes_accessed=4 << 20,
            transcendentals=0,
        ),
        name="second_piece",
    )(*in_hbm, sent)
    return sent, second, early_panel, early_lags


def own_kernel(levels, piece, last, group_ref, position_ref, volts_ref, *refs):
    head_refs, refs = refs[:levels][::-1], refs[levels:]
    early_panel_ref, early_lags_ref, *refs = refs
    panel_ref, sums_ref, *refs, raw, other_raw, other_panel, lags_ref, in_sem, other_sem = refs
    pick_refs, ordered_refs, refs = refs[:3], refs[3 : 3 + levels], refs[3 + levels :]
    more_ref, piece_ref, *last_refs, joined_ref, last_panel_ref = refs
    blocks, _, width, _ = panel_ref.shape
    mine = parity(lax.axis_index("inp"), levels)
    other_loads = load_channel(1 - mine, volts_ref, other_raw, other_sem)

    @pl.when(jnp.logical_not(on_odd_core()))
    def _():
        loads = load_channel(mine, volts_ref, raw, in_sem)
        order_channel(loads, position_ref, raw, panel_ref)
        own_tiles(panel_ref, lags_ref, 0, 0, EARLY_TILES)

    @pl.when(on_odd_core())
    def _():
        for b in range(blocks):
            for c in range(2):
                panel_ref[b, c] = early_panel_ref[b, c]
        for i in range(EARLY_TILES):
            lags_ref[i] = early_lags_ref[i]

    tiles = blocks * blocks
    own_tiles(panel_ref, lags_ref, 0, EARLY_TILES, tiles)
    order_channel(other_loads, position_ref, other_raw, other_panel)
    own_tiles(other_panel, lags_ref, tiles, 0, tiles)
    lags = jnp.concatenate([lags_ref[i] for i in range(tiles)], axis=0)
    heads = [head_ref[2 * width :, :] for head_ref in head_refs]
    for head, head_ref, ordered_ref in zip(heads, head_refs, ordered_refs):
        positions = head.astype(jnp.float32).astype(jnp.int32)[blocks**2 : blocks**2 + 1]
        order = order_matrix(positions)
        for c in range(2):
            rows = head_ref[c * width : (c + 1) * width, :]
            rows = jnp.dot(order, rows, preferred_element_type=jnp.float32)
            ordered_ref[c * width : (c + 1) * width, :] = rows.astype(jnp.bfloat16)
    own_pick, *picks = pick_matrices(group_ref[...], heads, blocks, sums_ref.shape[0])
    for pick_ref, pick in zip(pick_refs, picks):
        pick_ref[...] = pick
    sums_ref[...] = group_sums(own_pick, lags)
    for (block, first, end), (start, stop) in zip(piece, columns(piece)):
        for c in range(2):
            rows = other_panel[block, c, :, first:end]
            piece_ref[c * width : (c + 1) * width, start:stop] = rows
            more_ref[c * width : (c + 1) * width, start:stop] = rows
    lags = jnp.concatenate([lags_ref[tiles + i] for i in range(tiles)], axis=0)
    high = lags.astype(jnp.bfloat16).astype(jnp.float32)
    terms = jnp.concatenate([high, lags - high], axis=0)
    more_ref[2 * width :, :] = terms.astype(jnp.bfloat16)
    start = 0
    for (block, first, end), last_ref in zip(last, last_refs):
        for c in range(2):
            depth = end - first
            rows = other_panel[block, c, :, first:end]
            last_ref[:, c * depth : (c + 1) * depth] = rows
            joined_ref[:, start : start + depth] = rows
            start += depth
    turn = anti_identity(width)
    for a in range(blocks):
        start = 0
        for _, first, end in last:
            real_part, imag_part = [
                jnp.dot(turn, panel_ref[a, c, :, first:end], preferred_element_type=jnp.float32)
                for c in range(2)
            ]
            middle, stop = start + end - first, start + 2 * (end - first)
            last_panel_ref[a, :width, start:middle] = real_part.astype(jnp.bfloat16)
            last_panel_ref[a, :width, middle:stop] = imag_part.astype(jnp.bfloat16)
            last_panel_ref[a, width:, start:middle] = imag_part.astype(jnp.bfloat16)
            last_panel_ref[a, width:, middle:stop] = (-real_part).astype(jnp.bfloat16)
            start = stop


def own_level(groups, position_input, volts, early, heads, piece, last, out_rows):
    levels = len(heads)
    blocks, width = position_input.shape
    samples = volts.shape[3]
    pairs = 4 * levels * blocks
    tiles = 2 * blocks * blocks
    counts = (3 * tiles, 3 * pairs * blocks)
    depths = [2 * (end - first) for _, first, end in last]
    return pl.pallas_call(
        functools.partial(own_kernel, levels, piece, last),
        out_shape=(
            jax.ShapeDtypeStruct((blocks, 2, width, samples), jnp.bfloat16),
            jax.ShapeDtypeStruct((out_rows, 2 * width), jnp.float32),
            *[jax.ShapeDtypeStruct((out_rows, n), jnp.bfloat16) for n in counts],
            jax.ShapeDtypeStruct((pairs // 2, out_rows // 2, 128), jnp.float32),
            *[jax.ShapeDtypeStruct((2 * width, head.shape[1]), jnp.bfloat16) for head in heads],
            piece_shape(piece, width, 2 * tiles),
            piece_shape(piece, width, 0),
            *[jax.ShapeDtypeStruct((width, depth), jnp.bfloat16) for depth in depths],
            jax.ShapeDtypeStruct((width, sum(depths)), jnp.bfloat16),
            jax.ShapeDtypeStruct((blocks, 2 * width, sum(depths)), jnp.bfloat16),
        ),
        in_specs=[WHOLE, WHOLE, HBM] + [WHOLE] * (len(early) + levels),
        out_specs=(WHOLE,) * (7 + len(counts) + levels + len(last)),
        scratch_shapes=[
            pltpu.VMEM((blocks, 2, width, samples), jnp.bfloat16),
            pltpu.VMEM((blocks, 2, width, samples), jnp.bfloat16),
            pltpu.VMEM((blocks, 2, width, samples), jnp.bfloat16),
            pltpu.VMEM((2 * blocks * blocks, 2, 2 * width), jnp.float32),
            pltpu.SemaphoreType.DMA((blocks, 2)),
            pltpu.SemaphoreType.DMA((blocks, 2)),
        ],
        compiler_params=pltpu.CompilerParams(vmem_limit_bytes=16 << 20),
        cost_estimate=pl.CostEstimate(
            flops=64 * blocks * blocks * width * width * samples,
            bytes_accessed=12 * blocks * width * samples,
            transcendentals=0,
        ),
        name="own_level",
    )(groups, position_input, pltpu.with_memory_space_constraint(volts, pltpu.HBM), *heads[::-1], *early)


def add_lags(rows, pick_ref, sums_ref):
    lags = jnp.concatenate(rows, axis=0)
    lags = jnp.concatenate([lags, conjugate_lags(lags)], axis=0)
    return sums_ref[...] + group_sums(pick_ref[...], lags)


def add_masked(lags, tiles_at, mask_ref, sums_ref):
    turned = reversed_lags(lags)
    half, count = sums_ref.shape[0] // 2, mask_ref.shape[0] // 2
    sums = [sums_ref[:half, :], sums_ref[half:, :]]
    for i, tile in enumerate(tiles_at):
        forward = jnp.concatenate([mask_ref[tile]] * (sums_ref.shape[1] // 128), axis=1)
        back = jnp.concatenate([mask_ref[count + tile]] * (sums_ref.shape[1] // 128), axis=1)
        re, im = 2 * i, 2 * i + 1
        sums[0] = sums[0] + forward * lags[re : re + 1] + back * turned[re : re + 1]
        sums[1] = sums[1] + forward * lags[im : im + 1] - back * turned[im : im + 1]
    return sums


def pair_kernel(levels, pieces, passed, pick_ref, sums_ref, panel_ref, *refs):
    count = levels * len(pieces)
    out_ref = refs[-1 - passed]
    partner_refs, more_refs = refs[:count], refs[count : len(refs) - 1 - 2 * passed]
    _, _, width, samples = panel_ref.shape
    rows = []
    for block in sorted({block for piece in pieces for block, _, _ in piece}):
        for level in range(levels):
            for a in range(panel_ref.shape[0]):
                real_part, imag_part = 0.0, 0.0
                for i, piece in enumerate(pieces):
                    partner = partner_refs[level * len(pieces) + i]
                    for (b, first, last), (start, end) in zip(piece, columns(piece)):
                        if b != block:
                            continue
                        x_re, x_im = panel_ref[a, 0, :, first:last], panel_ref[a, 1, :, first:last]
                        y_re = partner[:width, start:end]
                        y_im = partner[width : 2 * width, start:end]
                        real_part = real_part + (product(x_re, y_re) + product(x_im, y_im))
                        imag_part = imag_part + (product(x_im, y_re) - product(x_re, y_im))
                rows.append(lag_rows(jnp.stack([real_part, imag_part])) * (1.0 / samples))
    if len(pick_ref.shape) == 3:
        sums = add_masked(jnp.concatenate(rows, axis=0), range(len(rows)), pick_ref, sums_ref)
        sums = jnp.concatenate(sums, axis=0)
    else:
        sums = add_lags(rows, pick_ref, sums_ref)
    for more_ref in more_refs:
        terms = partner_refs[-1][2 * width :, :].astype(jnp.float32)
        half = terms.shape[0] // 2
        sums = sums + group_sums(more_ref[...], terms[:half] + terms[half:])
    out_ref[...] = sums


def last_kernel(parts, samples, mask_ref, sums_ref, panel_ref, *refs):
    partner_refs, out_refs = refs[: len(parts)], refs[len(parts) :]
    blocks, rows_both, _ = panel_ref.shape
    width = rows_both // 2
    rows, tiles_at = [], []
    for (level, first, last), partner_ref in zip(parts, partner_refs):
        for a in range(blocks):
            tiles = product(panel_ref[a, :, first:last], partner_ref[...])
            rows += sheared_eights(tiles.reshape(2, width, width))
            tiles_at.append(level * blocks + a)
    lags = jnp.sum(jnp.stack(rows), axis=1) * (1.0 / samples)
    sums = add_masked(lags, tiles_at, mask_ref, sums_ref)
    half = sums_ref.shape[0] // 2
    share = half // len(out_refs)
    for place, out_ref in enumerate(out_refs):
        for part in range(2):
            rows = sums[part][place * share : (place + 1) * share]
            out_ref[part * share : (part + 1) * share, :] = rows


def pair_call(kernel, inputs, work, shares=1, passed=()):
    rows, width = inputs[1].shape
    any_space = [pl.BlockSpec(memory_space=pl.ANY)] * len(passed)
    return pl.pallas_call(
        kernel,
        out_shape=[jax.ShapeDtypeStruct((rows // shares, width), jnp.float32)] * shares
        + [jax.ShapeDtypeStruct(x.shape, x.dtype) for x in passed],
        in_specs=[WHOLE] * len(inputs) + any_space,
        out_specs=[WHOLE] * shares + any_space,
        input_output_aliases={len(inputs) + i: shares + i for i in range(len(passed))},
        compiler_params=pltpu.CompilerParams(vmem_limit_bytes=16 << 20),
        cost_estimate=pl.CostEstimate(flops=work, bytes_accessed=4 << 20, transcendentals=0),
        name="pair_level",
    )(*inputs, *passed)


def finish_kernel(levels, distances, *refs):
    part_refs, out_ref = refs[:-1], refs[-1]
    mine = parity(lax.axis_index("inp"), levels)
    groups, channels, parts, lags = out_ref.shape
    sums = [None, None]
    for distance, part_ref in zip(distances, part_refs):
        side = distance.bit_count() % 2
        sums[side] = part_ref[...] if sums[side] is None else sums[side] + part_ref[...]
    for f in range(channels):
        total = jnp.where(mine == f, sums[0], sums[1])
        for g in range(groups):
            for part in range(parts):
                row = part * groups + g
                out_ref[g, f, part : part + 1] = total[row : row + 1, :lags]


def finish(parts, distances, levels, lags):
    return pl.pallas_call(
        functools.partial(finish_kernel, levels, distances),
        out_shape=jax.ShapeDtypeStruct((RG_DEV, 2, 2, lags), jnp.float32),
        in_specs=[WHOLE] * len(parts),
        out_specs=WHOLE,
        compiler_params=pltpu.CompilerParams(vmem_limit_bytes=8 << 20),
        name="finish",
    )(*parts)


def on_device(volts, position_input, tile_group):
    blocks, width = position_input.shape
    samples = volts.shape[3]
    devices = lax.axis_size("inp")
    levels = devices.bit_length() - 1
    out_rows = devices * RG_DEV * 2
    eighth = samples // 8
    head = [(0, 0, 2 * eighth)]
    rest = [(0, 2 * eighth, samples), (1, 0, 2 * eighth)]
    tail = [(1, 2 * eighth, 6 * eighth)]
    last = [(1, 6 * eighth, 7 * eighth), (1, 7 * eighth, samples)]
    by_block = tile_group.transpose(0, 2, 1)
    partner_of = [functools.partial(xor_permute, axis="inp", distance=1 << l) for l in range(levels)]
    sent, second, *early = early_pieces(position_input, volts, by_block, head, rest, levels)
    head_arrived = [send(sent) for send in partner_of]
    rest_arrived = [send(second) for send in partner_of]
    panel, sums, neighbour, both, masks, *sent = own_level(
        by_block, position_input, volts, early, head_arrived, tail, last, out_rows
    )
    head_ordered, (more, piece, *last_pieces, last_panel) = sent[:levels], sent[levels:]
    tail_arrived = [send(piece) for send in partner_of[:-1]] + [partner_of[-1](more)]

    flops = 8 * levels * blocks * width * width
    arrived = [piece for pair in zip(head_ordered, rest_arrived) for piece in pair]
    sums, *last_pieces = pair_call(
        functools.partial(pair_kernel, levels, [head, rest], len(last_pieces)),
        [both, sums, panel, *arrived],
        flops * 10 * eighth,
        passed=last_pieces,
    )
    *last_pieces, joined = last_pieces
    last_arrived = [[send(piece) for send in partner_of[:-1]] for piece in last_pieces]
    last_arrived[-1].append(partner_of[-1](joined))
    (sums,) = pair_call(
        functools.partial(pair_kernel, levels, [tail], 0),
        [masks, sums, panel, *tail_arrived, neighbour],
        flops * 4 * eighth,
    )
    for i, arrived in enumerate(last_arrived):
        final = i == len(last_arrived) - 1
        columns_of = [(2 * eighth * i, 2 * eighth * (i + 1))] * (levels - 1)
        if final:
            columns_of.append((0, joined.shape[1]))
        parts = pair_call(
            functools.partial(
                last_kernel, [(level, *cut) for level, cut in enumerate(columns_of)], samples
            ),
            [masks, sums, last_panel, *arrived],
            flops * eighth,
            devices if final else 1,
        )
        sums = parts[0]
    distances = [1, *range(devices - 1, 1, -1), 0]
    parts = [
        xor_permute(parts[distance], "inp", distance) if distance else parts[0]
        for distance in distances
    ]
    return finish(parts, distances, levels, 2 * width - 1)


def solution(mesh):
    return jax.shard_map(
        on_device,
        mesh=mesh,
        in_specs=(P("freq", None, "inp", None), P("inp", None), P("inp", None, None)),
        out_specs=P("inp", "freq", None, None),
        check_vma=False,
    )
```

```python
import functools

import jax
import jax.numpy as jnp
from jax import lax
from jax.experimental import pallas as pl
from jax.experimental.pallas import tpu as pltpu
from jax.sharding import PartitionSpec as P

RG_DEV = 8
GROUP_ROWS = 16
EARLY_TILES = 3
HBM = pl.BlockSpec(memory_space=pltpu.HBM)
WHOLE = pl.BlockSpec(memory_space=pltpu.VMEM)


def xor_permute(x, axis, distance):
    return lax.ppermute(x, axis, [(i, i ^ distance) for i in range(lax.axis_size(axis))])


def parity(index, levels):
    bits = index & 1
    for level in range(1, levels):
        bits = bits ^ ((index >> level) & 1)
    return bits


def order_matrix(position_row):
    width = position_row.shape[-1]
    by_position = jnp.transpose(jnp.broadcast_to(position_row, (width, width)))
    inputs = lax.broadcasted_iota(jnp.int32, (width, width), 1)
    return (by_position == inputs).astype(jnp.float32).astype(jnp.bfloat16)


def product(x, y):
    return lax.dot_general(x, y, (((1,), (1,)), ((), ())), preferred_element_type=jnp.float32)


def lag_rows(tiles):
    count, width, _ = tiles.shape
    half = width // 2
    low, high = tiles[:, :half], tiles[:, half:]
    sheared = jnp.concatenate(
        [
            high[:, :, :half],
            high[:, :, half:] + low[:, :, :half],
            low[:, :, half:],
            jnp.zeros((count, half, half), jnp.float32),
        ],
        axis=2,
    )
    rows = half
    while rows > 8:
        rows //= 2
        upper = sheared[:, :rows].reshape(count * rows, 2 * width)
        upper = pltpu.roll(upper, rows, 1).reshape(count, rows, 2 * width)
        sheared = upper + sheared[:, rows:]
    flat = sheared.reshape(count * rows, 2 * width)
    sublane = lax.broadcasted_iota(jnp.int32, flat.shape, 0) % 8
    while rows > 1:
        rows //= 2
        flat = jnp.where((sublane & rows) == 0, pltpu.roll(flat, rows, 1), flat)
    return jnp.sum(flat.reshape(count, 8, 2 * width), axis=1)


def tile_lags(x_re, x_im, y_re, y_im, samples):
    real_part = product(x_re, y_re) + product(x_im, y_im)
    imag_part = product(x_im, y_re) - product(x_re, y_im)
    return lag_rows(jnp.stack([real_part, imag_part])) * (1.0 / samples)


def split_rows(x):
    first = x.astype(jnp.bfloat16).astype(jnp.float32)
    rest = x - first
    second = rest.astype(jnp.bfloat16).astype(jnp.float32)
    return jnp.concatenate([first, second, rest - second], axis=0)


def anti_identity(size):
    place = lax.broadcasted_iota(jnp.int32, (size, size), 0) + lax.broadcasted_iota(
        jnp.int32, (size, size), 1
    )
    return (place == size - 1).astype(jnp.float32).astype(jnp.bfloat16)


def turn_lags(terms):
    count, width = terms.shape
    lanes = 128
    spans = range(0, width, lanes)
    terms = jnp.concatenate([terms[:, first : first + lanes] for first in spans], axis=0)
    terms = jnp.dot(
        terms.astype(jnp.bfloat16), anti_identity(lanes), preferred_element_type=jnp.float32
    )
    blocks = [terms[count * i : count * (i + 1)] for i in reversed(range(len(spans)))]
    return pltpu.roll(jnp.concatenate(blocks, axis=1), width - 1, 1)


def conjugate_lags(lags):
    count = lags.shape[0]
    turned = turn_lags(split_rows(lags))
    turned = turned[:count] + turned[count : 2 * count] + turned[2 * count :]
    odd = lax.broadcasted_iota(jnp.int32, turned.shape, 0) % 2 == 1
    return jnp.where(odd, -turned, turned)


def reversed_lags(lags):
    count, width = lags.shape
    lanes = 128
    rows = jnp.pad(lags, ((0, -count % 8), (0, 0)))
    index = lanes - 1 - lax.broadcasted_iota(jnp.int32, (rows.shape[0], lanes), 1)
    blocks = [
        jnp.take_along_axis(
            rows[:, first : first + lanes], index, axis=1, mode="promise_in_bounds"
        )
        for first in reversed(range(0, width, lanes))
    ]
    return pltpu.roll(jnp.concatenate(blocks, axis=1), width - 1, 1)[:count]


def sheared_eights(tiles):
    count, width, _ = tiles.shape
    half = width // 2
    low, high = tiles[:, :half], tiles[:, half:]
    sheared = jnp.concatenate(
        [
            low[:, :, :half],
            low[:, :, half:] + high[:, :, :half],
            high[:, :, half:],
            jnp.zeros((count, half, half), jnp.float32),
        ],
        axis=2,
    )
    rows = half
    while rows > 8:
        rows //= 2
        lower = sheared[:, rows:].reshape(count * rows, 2 * width)
        lower = pltpu.roll(lower, rows, 1).reshape(count, rows, 2 * width)
        sheared = sheared[:, :rows] + lower
    return [pltpu.roll(sheared[i], 0, 1, stride=1, stride_axis=0) for i in range(count)]


def group_block(groups, columns=128):
    rows = jnp.concatenate([groups[b] for b in range(groups.shape[0])], axis=0)
    lines, lanes = rows.shape
    return jnp.pad(rows, ((0, GROUP_ROWS - lines), (0, columns - lanes)))


def target_rows(groups):
    return groups ^ (lax.axis_index("inp") * RG_DEV)


def pick_matrix(entries, rows):
    count = len(entries)
    shape = (rows, 3 * count)
    row = lax.broadcasted_iota(jnp.int32, shape, 0)
    column = lax.broadcasted_iota(jnp.int32, shape, 1) % count
    pick = jnp.zeros(shape, jnp.float32)
    for j, (targets, line, lane, part) in enumerate(entries):
        target = targets[line : line + 1, lane : lane + 1] + part * (rows // 2)
        target = jnp.broadcast_to(target, shape)
        pick = jnp.where(jnp.logical_and(column == j, row == target), 1.0, pick)
    return pick.astype(jnp.bfloat16)


def row_masks(entries, rows):
    row = lax.broadcasted_iota(jnp.int32, (rows, 128), 0)
    masks = []
    for targets, line, lane, _ in entries:
        target = jnp.broadcast_to(targets[line : line + 1, lane : lane + 1], row.shape)
        masks.append((row == target).astype(jnp.float32))
    return jnp.stack(masks)


def pick_matrices(groups, heads, blocks, out_rows):
    own = target_rows(group_block(groups))
    others = [target_rows(head.astype(jnp.float32).astype(jnp.int32)) for head in heads]
    groups_all = out_rows // 2

    def pairs(b):
        order = [(level, a, p) for level in range(len(heads)) for a in range(blocks) for p in range(2)]
        forward = [(own, a * blocks + b, level + 1, p) for level, a, p in order]
        turned = [(others[level], b * blocks + a, level + 1, p) for level, a, p in order]
        return forward, turned

    forward, turned = zip(*[pairs(b) for b in range(blocks)])
    tiles = [
        [(targets, line, 0, p) for line in range(blocks * blocks) for p in range(2)]
        for targets in (own, others[-1])
    ]
    both = [entry for side in (forward, turned) for block in side for entry in block]
    return [
        pick_matrix(tiles[0], out_rows),
        pick_matrix(tiles[1], out_rows),
        pick_matrix(both, out_rows),
        pick_matrix(forward[-1] + turned[-1], out_rows),
        row_masks(forward[-1][::2] + turned[-1][::2], groups_all),
    ]


def group_sums(pick, lags):
    terms = split_rows(lags).astype(jnp.bfloat16)
    return jnp.dot(pick, terms, preferred_element_type=jnp.float32)


def columns(piece):
    spans, start = [], 0
    for _, first, last in piece:
        spans.append((start, start + last - first))
        start += last - first
    return spans


def piece_shape(piece, width, more):
    return jax.ShapeDtypeStruct((2 * width + more, columns(piece)[-1][1]), jnp.bfloat16)


def load_piece(piece, other, width, volts_ref, raw, in_sem):
    blocks = sorted({block for block, _, _ in piece})
    loads = []
    for i, block in enumerate(blocks):
        start = min(first for b, first, _ in piece if b == block)
        end = max(last for b, _, last in piece if b == block)
        for c in range(2):
            load = pltpu.make_async_copy(
                volts_ref.at[other, c, pl.ds(block * width, width), pl.ds(start, end - start)],
                raw.at[i, c, :, pl.ds(start, end - start)],
                in_sem.at[i, c],
            )
            load.start()
            loads.append((i, block, c, load))
    return loads


def order_piece(piece, loads, position, raw, out_ref):
    width = position.shape[1]
    orders = {
        block: order_matrix(position[block : block + 1, :]) for block in sorted({l[1] for l in loads})
    }
    for i, block, c, load in loads:
        load.wait()
        for (b, first, last), (start, end) in zip(piece, columns(piece)):
            if b == block:
                out_ref[c * width : (c + 1) * width, start:end] = jnp.dot(
                    orders[block], raw[i, c, :, first:last], preferred_element_type=jnp.float32
                ).astype(jnp.bfloat16)


def head_kernel(levels, piece, position_ref, volts_ref, group_ref, head_ref, *scratch):
    position, groups, small_sem, in_sem = scratch
    other = 1 - parity(lax.axis_index("inp"), levels)
    width = position.shape[1]
    ((block, first, last),) = piece
    smalls = [
        pltpu.make_async_copy(position_ref, position, small_sem.at[0]),
        pltpu.make_async_copy(group_ref, groups, small_sem.at[1]),
    ]
    loads = [
        pltpu.make_async_copy(
            volts_ref.at[other, c, pl.ds(block * width, width), pl.ds(first, last - first)],
            head_ref.at[pl.ds(c * width, width), :],
            in_sem.at[c],
        )
        for c in range(2)
    ]
    for copy in smalls + loads:
        copy.start()
    for copy in smalls:
        copy.wait()
    rows = group_block(groups[...], last - first)
    line = lax.broadcasted_iota(jnp.int32, rows.shape, 0)
    own_row = jnp.broadcast_to(position[block : block + 1, :], rows.shape)
    rows = jnp.where(line == groups.shape[0] ** 2, own_row, rows)
    head_ref[2 * width :, :] = rows.astype(jnp.float32).astype(jnp.bfloat16)
    for copy in loads:
        copy.wait()


def on_odd_core():
    return lax.axis_index("freq") % 2 == 1


def load_channel(channel, volts_ref, raw, in_sem):
    blocks, _, width, _ = raw.shape
    loads = []
    for b in range(blocks):
        for c in range(2):
            load = pltpu.make_async_copy(
                volts_ref.at[channel, c, pl.ds(b * width, width)], raw.at[b, c], in_sem.at[b, c]
            )
            load.start()
            loads.append((b, c, load))
    return loads


def order_channel(loads, position_ref, raw, panel):
    blocks = raw.shape[0]
    orders = [order_matrix(position_ref[b : b + 1, :]) for b in range(blocks)]
    for b, c, load in loads:
        load.wait()
        rows = jnp.dot(orders[b], raw[b, c], preferred_element_type=jnp.float32)
        panel[b, c] = rows.astype(jnp.bfloat16)


def own_tiles(panel, lags_ref, start, first, last):
    blocks, _, width, samples = panel.shape

    def one_tile(index, carry):
        a = index // blocks
        b = index % blocks
        lags = tile_lags(panel[a, 0], panel[a, 1], panel[b, 0], panel[b, 1], samples)
        center = lax.broadcasted_iota(jnp.int32, lags.shape, 1) == width - 1
        lags_ref[start + index] = jnp.where(jnp.logical_and(center, a == b), 0.0, lags)
        return carry

    lax.fori_loop(first, last, one_tile, 0)


def rest_kernel(levels, piece, position_ref, volts_ref, _, out_ref, panel_ref, lags_ref, *scratch):
    position, raw, own_raw, small_sem, in_sem, own_sem = scratch
    mine = parity(lax.axis_index("inp"), levels)
    load_position = pltpu.make_async_copy(position_ref, position, small_sem)
    load_position.start()
    piece_loads = load_piece(piece, 1 - mine, position.shape[1], volts_ref, raw, in_sem)
    load_position.wait()

    @pl.when(on_odd_core())
    def _():
        loads = load_channel(mine, volts_ref, own_raw, own_sem)
        order_channel(loads, position, own_raw, panel_ref)
        own_tiles(panel_ref, lags_ref, 0, 0, EARLY_TILES)

    order_piece(piece, piece_loads, position, raw, out_ref)


def early_pieces(position_input, volts, groups, head, rest, levels):
    blocks, width = position_input.shape
    samples = volts.shape[3]
    assert columns(head)[-1][1] == width
    in_hbm = [pltpu.with_memory_space_constraint(x, pltpu.HBM) for x in (position_input, volts)]
    position = pltpu.VMEM(position_input.shape, jnp.int32)
    semaphore = pltpu.SemaphoreType.DMA
    sent = pl.pallas_call(
        functools.partial(head_kernel, levels, head),
        out_shape=piece_shape(head, width, GROUP_ROWS),
        in_specs=[HBM] * 3,
        out_specs=WHOLE,
        scratch_shapes=[
            position,
            pltpu.VMEM(groups.shape, jnp.int32),
            semaphore((2,)),
            semaphore((2,)),
        ],
        compiler_params=pltpu.CompilerParams(vmem_limit_bytes=8 << 20),
        cost_estimate=pl.CostEstimate(flops=0, bytes_accessed=1 << 20, transcendentals=0),
        name="first_piece",
    )(*in_hbm, pltpu.with_memory_space_constraint(groups, pltpu.HBM))
    second, early_panel, early_lags = pl.pallas_call(
        functools.partial(rest_kernel, levels, rest),
        out_shape=[
            piece_shape(rest, width, 0),
            jax.ShapeDtypeStruct((blocks, 2, width, samples), jnp.bfloat16),
            jax.ShapeDtypeStruct((blocks * blocks, 2, 2 * width), jnp.float32),
        ],
        in_specs=[HBM, HBM, pl.BlockSpec(memory_space=pl.ANY)],
        out_specs=[WHOLE] * 3,
        scratch_shapes=[
            position,
            pltpu.VMEM((blocks, 2, width, samples), jnp.bfloat16),
            pltpu.VMEM((blocks, 2, width, samples), jnp.bfloat16),
            semaphore(()),
            semaphore((blocks, 2)),
            semaphore((blocks, 2)),
        ],
        compiler_params=pltpu.CompilerParams(vmem_limit_bytes=16 << 20),
        cost_estimate=pl.CostEstimate(
            flops=4 * width * width * columns(rest)[-1][1],
            bytes_accessed=4 << 20,
            transcendentals=0,
        ),
        name="second_piece",
    )(*in_hbm, sent)
    return sent, second, early_panel, early_lags


def own_kernel(levels, piece, last, group_ref, position_ref, volts_ref, *refs):
    head_refs, refs = refs[:levels][::-1], refs[levels:]
    early_panel_ref, early_lags_ref, *refs = refs
    panel_ref, sums_ref, *refs, raw, other_raw, other_panel, lags_ref, in_sem, other_sem = refs
    pick_refs, ordered_refs, refs = refs[:4], refs[4 : 4 + levels], refs[4 + levels :]
    more_ref, piece_ref, *last_refs, joined_ref, last_panel_ref = refs
    blocks, _, width, _ = panel_ref.shape
    mine = parity(lax.axis_index("inp"), levels)
    other_loads = load_channel(1 - mine, volts_ref, other_raw, other_sem)

    @pl.when(jnp.logical_not(on_odd_core()))
    def _():
        loads = load_channel(mine, volts_ref, raw, in_sem)
        order_channel(loads, position_ref, raw, panel_ref)
        own_tiles(panel_ref, lags_ref, 0, 0, EARLY_TILES)

    @pl.when(on_odd_core())
    def _():
        for b in range(blocks):
            for c in range(2):
                panel_ref[b, c] = early_panel_ref[b, c]
        for i in range(EARLY_TILES):
            lags_ref[i] = early_lags_ref[i]

    tiles = blocks * blocks
    own_tiles(panel_ref, lags_ref, 0, EARLY_TILES, tiles)
    order_channel(other_loads, position_ref, other_raw, other_panel)
    own_tiles(other_panel, lags_ref, tiles, 0, tiles)
    lags = jnp.concatenate([lags_ref[i] for i in range(tiles)], axis=0)
    heads = [head_ref[2 * width :, :] for head_ref in head_refs]
    for head, head_ref, ordered_ref in zip(heads, head_refs, ordered_refs):
        positions = head.astype(jnp.float32).astype(jnp.int32)[blocks**2 : blocks**2 + 1]
        order = order_matrix(positions)
        for c in range(2):
            rows = head_ref[c * width : (c + 1) * width, :]
            rows = jnp.dot(order, rows, preferred_element_type=jnp.float32)
            ordered_ref[c * width : (c + 1) * width, :] = rows.astype(jnp.bfloat16)
    own_pick, *picks = pick_matrices(group_ref[...], heads, blocks, sums_ref.shape[0])
    for pick_ref, pick in zip(pick_refs, picks):
        pick_ref[...] = pick
    sums_ref[...] = group_sums(own_pick, lags)
    for (block, first, end), (start, stop) in zip(piece, columns(piece)):
        for c in range(2):
            rows = other_panel[block, c, :, first:end]
            piece_ref[c * width : (c + 1) * width, start:stop] = rows
            more_ref[c * width : (c + 1) * width, start:stop] = rows
    lags = jnp.concatenate([lags_ref[tiles + i] for i in range(tiles)], axis=0)
    high = lags.astype(jnp.bfloat16).astype(jnp.float32)
    terms = jnp.concatenate([high, lags - high], axis=0)
    more_ref[2 * width :, :] = terms.astype(jnp.bfloat16)
    start = 0
    for (block, first, end), last_ref in zip(last, last_refs):
        for c in range(2):
            depth = end - first
            rows = other_panel[block, c, :, first:end]
            last_ref[:, c * depth : (c + 1) * depth] = rows
            joined_ref[:, start : start + depth] = rows
            start += depth
    turn = anti_identity(width)
    for a in range(blocks):
        start = 0
        for _, first, end in last:
            real_part, imag_part = [
                jnp.dot(turn, panel_ref[a, c, :, first:end], preferred_element_type=jnp.float32)
                for c in range(2)
            ]
            middle, stop = start + end - first, start + 2 * (end - first)
            last_panel_ref[a, :width, start:middle] = real_part.astype(jnp.bfloat16)
            last_panel_ref[a, :width, middle:stop] = imag_part.astype(jnp.bfloat16)
            last_panel_ref[a, width:, start:middle] = imag_part.astype(jnp.bfloat16)
            last_panel_ref[a, width:, middle:stop] = (-real_part).astype(jnp.bfloat16)
            start = stop


def own_level(groups, position_input, volts, early, heads, piece, last, out_rows):
    levels = len(heads)
    blocks, width = position_input.shape
    samples = volts.shape[3]
    pairs = 4 * levels * blocks
    tiles = 2 * blocks * blocks
    counts = (3 * tiles, 3 * pairs * blocks, 3 * pairs)
    depths = [2 * (end - first) for _, first, end in last]
    return pl.pallas_call(
        functools.partial(own_kernel, levels, piece, last),
        out_shape=(
            jax.ShapeDtypeStruct((blocks, 2, width, samples), jnp.bfloat16),
            jax.ShapeDtypeStruct((out_rows, 2 * width), jnp.float32),
            *[jax.ShapeDtypeStruct((out_rows, n), jnp.bfloat16) for n in counts],
            jax.ShapeDtypeStruct((pairs // 2, out_rows // 2, 128), jnp.float32),
            *[jax.ShapeDtypeStruct((2 * width, head.shape[1]), jnp.bfloat16) for head in heads],
            piece_shape(piece, width, 2 * tiles),
            piece_shape(piece, width, 0),
            *[jax.ShapeDtypeStruct((width, depth), jnp.bfloat16) for depth in depths],
            jax.ShapeDtypeStruct((width, sum(depths)), jnp.bfloat16),
            jax.ShapeDtypeStruct((blocks, 2 * width, sum(depths)), jnp.bfloat16),
        ),
        in_specs=[WHOLE, WHOLE, HBM] + [WHOLE] * (len(early) + levels),
        out_specs=(WHOLE,) * (7 + len(counts) + levels + len(last)),
        scratch_shapes=[
            pltpu.VMEM((blocks, 2, width, samples), jnp.bfloat16),
            pltpu.VMEM((blocks, 2, width, samples), jnp.bfloat16),
            pltpu.VMEM((blocks, 2, width, samples), jnp.bfloat16),
            pltpu.VMEM((2 * blocks * blocks, 2, 2 * width), jnp.float32),
            pltpu.SemaphoreType.DMA((blocks, 2)),
            pltpu.SemaphoreType.DMA((blocks, 2)),
        ],
        compiler_params=pltpu.CompilerParams(vmem_limit_bytes=16 << 20),
        cost_estimate=pl.CostEstimate(
            flops=64 * blocks * blocks * width * width * samples,
            bytes_accessed=12 * blocks * width * samples,
            transcendentals=0,
        ),
        name="own_level",
    )(groups, position_input, pltpu.with_memory_space_constraint(volts, pltpu.HBM), *heads[::-1], *early)


def add_lags(rows, pick_ref, sums_ref):
    lags = jnp.concatenate(rows, axis=0)
    lags = jnp.concatenate([lags, conjugate_lags(lags)], axis=0)
    return sums_ref[...] + group_sums(pick_ref[...], lags)


def pair_kernel(levels, pieces, passed, pick_ref, sums_ref, panel_ref, *refs):
    count = levels * len(pieces)
    out_ref = refs[-1 - passed]
    partner_refs, more_refs = refs[:count], refs[count : len(refs) - 1 - 2 * passed]
    _, _, width, samples = panel_ref.shape
    rows = []
    for block in sorted({block for piece in pieces for block, _, _ in piece}):
        for level in range(levels):
            for a in range(panel_ref.shape[0]):
                real_part, imag_part = 0.0, 0.0
                for i, piece in enumerate(pieces):
                    partner = partner_refs[level * len(pieces) + i]
                    for (b, first, last), (start, end) in zip(piece, columns(piece)):
                        if b != block:
                            continue
                        x_re, x_im = panel_ref[a, 0, :, first:last], panel_ref[a, 1, :, first:last]
                        y_re = partner[:width, start:end]
                        y_im = partner[width : 2 * width, start:end]
                        real_part = real_part + (product(x_re, y_re) + product(x_im, y_im))
                        imag_part = imag_part + (product(x_im, y_re) - product(x_re, y_im))
                rows.append(lag_rows(jnp.stack([real_part, imag_part])) * (1.0 / samples))
    sums = add_lags(rows, pick_ref, sums_ref)
    for more_ref in more_refs:
        terms = partner_refs[-1][2 * width :, :].astype(jnp.float32)
        half = terms.shape[0] // 2
        sums = sums + group_sums(more_ref[...], terms[:half] + terms[half:])
    out_ref[...] = sums


def last_kernel(parts, samples, mask_ref, sums_ref, panel_ref, *refs):
    partner_refs, out_refs = refs[: len(parts)], refs[len(parts) :]
    blocks, rows_both, _ = panel_ref.shape
    width = rows_both // 2
    rows, tiles_at = [], []
    for (level, first, last), partner_ref in zip(parts, partner_refs):
        for a in range(blocks):
            tiles = product(panel_ref[a, :, first:last], partner_ref[...])
            rows += sheared_eights(tiles.reshape(2, width, width))
            tiles_at.append(level * blocks + a)
    lags = jnp.sum(jnp.stack(rows), axis=1) * (1.0 / samples)
    turned = reversed_lags(lags)
    half = sums_ref.shape[0] // 2
    sums = [sums_ref[:half, :], sums_ref[half:, :]]
    count = mask_ref.shape[0] // 2
    for i, tile in enumerate(tiles_at):
        forward = jnp.concatenate([mask_ref[tile]] * (sums_ref.shape[1] // 128), axis=1)
        back = jnp.concatenate([mask_ref[count + tile]] * (sums_ref.shape[1] // 128), axis=1)
        re, im = 2 * i, 2 * i + 1
        sums[0] = sums[0] + forward * lags[re : re + 1] + back * turned[re : re + 1]
        sums[1] = sums[1] + forward * lags[im : im + 1] - back * turned[im : im + 1]
    share = half // len(out_refs)
    for place, out_ref in enumerate(out_refs):
        for part in range(2):
            rows = sums[part][place * share : (place + 1) * share]
            out_ref[part * share : (part + 1) * share, :] = rows


def pair_call(kernel, inputs, work, shares=1, passed=()):
    rows, width = inputs[1].shape
    any_space = [pl.BlockSpec(memory_space=pl.ANY)] * len(passed)
    return pl.pallas_call(
        kernel,
        out_shape=[jax.ShapeDtypeStruct((rows // shares, width), jnp.float32)] * shares
        + [jax.ShapeDtypeStruct(x.shape, x.dtype) for x in passed],
        in_specs=[WHOLE] * len(inputs) + any_space,
        out_specs=[WHOLE] * shares + any_space,
        input_output_aliases={len(inputs) + i: shares + i for i in range(len(passed))},
        compiler_params=pltpu.CompilerParams(vmem_limit_bytes=16 << 20),
        cost_estimate=pl.CostEstimate(flops=work, bytes_accessed=4 << 20, transcendentals=0),
        name="pair_level",
    )(*inputs, *passed)


def finish_kernel(levels, distances, *refs):
    part_refs, out_ref = refs[:-1], refs[-1]
    mine = parity(lax.axis_index("inp"), levels)
    groups, channels, parts, lags = out_ref.shape
    sums = [None, None]
    for distance, part_ref in zip(distances, part_refs):
        side = distance.bit_count() % 2
        sums[side] = part_ref[...] if sums[side] is None else sums[side] + part_ref[...]
    for f in range(channels):
        total = jnp.where(mine == f, sums[0], sums[1])
        for g in range(groups):
            for part in range(parts):
                row = part * groups + g
                out_ref[g, f, part : part + 1] = total[row : row + 1, :lags]


def finish(parts, distances, levels, lags):
    return pl.pallas_call(
        functools.partial(finish_kernel, levels, distances),
        out_shape=jax.ShapeDtypeStruct((RG_DEV, 2, 2, lags), jnp.float32),
        in_specs=[WHOLE] * len(parts),
        out_specs=WHOLE,
        compiler_params=pltpu.CompilerParams(vmem_limit_bytes=8 << 20),
        name="finish",
    )(*parts)


def on_device(volts, position_input, tile_group):
    blocks, width = position_input.shape
    samples = volts.shape[3]
    devices = lax.axis_size("inp")
    levels = devices.bit_length() - 1
    out_rows = devices * RG_DEV * 2
    eighth = samples // 8
    head = [(0, 0, 2 * eighth)]
    rest = [(0, 2 * eighth, samples), (1, 0, 2 * eighth)]
    tail = [(1, 2 * eighth, 6 * eighth)]
    last = [(1, 6 * eighth, 7 * eighth), (1, 7 * eighth, samples)]
    by_block = tile_group.transpose(0, 2, 1)
    partner_of = [functools.partial(xor_permute, axis="inp", distance=1 << l) for l in range(levels)]
    sent, second, *early = early_pieces(position_input, volts, by_block, head, rest, levels)
    head_arrived = [send(sent) for send in partner_of]
    rest_arrived = [send(second) for send in partner_of]
    panel, sums, neighbour, both, single, masks, *sent = own_level(
        by_block, position_input, volts, early, head_arrived, tail, last, out_rows
    )
    head_ordered, (more, piece, *last_pieces, last_panel) = sent[:levels], sent[levels:]
    tail_arrived = [send(piece) for send in partner_of[:-1]] + [partner_of[-1](more)]

    flops = 8 * levels * blocks * width * width
    arrived = [piece for pair in zip(head_ordered, rest_arrived) for piece in pair]
    sums, *last_pieces = pair_call(
        functools.partial(pair_kernel, levels, [head, rest], len(last_pieces)),
        [both, sums, panel, *arrived],
        flops * 10 * eighth,
        passed=last_pieces,
    )
    *last_pieces, joined = last_pieces
    last_arrived = [[send(piece) for send in partner_of[:-1]] for piece in last_pieces]
    last_arrived[-1].append(partner_of[-1](joined))
    (sums,) = pair_call(
        functools.partial(pair_kernel, levels, [tail], 0),
        [single, sums, panel, *tail_arrived, neighbour],
        flops * 4 * eighth,
    )
    for i, arrived in enumerate(last_arrived):
        final = i == len(last_arrived) - 1
        columns_of = [(2 * eighth * i, 2 * eighth * (i + 1))] * (levels - 1)
        if final:
            columns_of.append((0, joined.shape[1]))
        parts = pair_call(
            functools.partial(
                last_kernel, [(level, *cut) for level, cut in enumerate(columns_of)], samples
            ),
            [masks, sums, last_panel, *arrived],
            flops * eighth,
            devices if final else 1,
        )
        sums = parts[0]
    distances = [1, *range(devices - 1, 1, -1), 0]
    parts = [
        xor_permute(parts[distance], "inp", distance) if distance else parts[0]
        for distance in distances
    ]
    return finish(parts, distances, levels, 2 * width - 1)


def solution(mesh):
    return jax.shard_map(
        on_device,
        mesh=mesh,
        in_specs=(P("freq", None, "inp", None), P("inp", None), P("inp", None, None)),
        out_specs=P("inp", "freq", None, None),
        check_vma=False,
    )
```

```python
import functools

import jax
import jax.numpy as jnp
from jax import lax
from jax.experimental import pallas as pl
from jax.experimental.pallas import tpu as pltpu
from jax.sharding import PartitionSpec as P

RG_DEV = 8
GROUP_ROWS = 16
EARLY_TILES = 3
HBM = pl.BlockSpec(memory_space=pltpu.HBM)
WHOLE = pl.BlockSpec(memory_space=pltpu.VMEM)


def xor_permute(x, axis, distance):
    return lax.ppermute(x, axis, [(i, i ^ distance) for i in range(lax.axis_size(axis))])


def parity(index, levels):
    bits = index & 1
    for level in range(1, levels):
        bits = bits ^ ((index >> level) & 1)
    return bits


def order_matrix(position_row):
    width = position_row.shape[-1]
    by_position = jnp.transpose(jnp.broadcast_to(position_row, (width, width)))
    inputs = lax.broadcasted_iota(jnp.int32, (width, width), 1)
    return (by_position == inputs).astype(jnp.float32).astype(jnp.bfloat16)


def product(x, y):
    return lax.dot_general(x, y, (((1,), (1,)), ((), ())), preferred_element_type=jnp.float32)


def lag_rows(tiles):
    count, width, _ = tiles.shape
    half = width // 2
    low, high = tiles[:, :half], tiles[:, half:]
    sheared = jnp.concatenate(
        [
            high[:, :, :half],
            high[:, :, half:] + low[:, :, :half],
            low[:, :, half:],
            jnp.zeros((count, half, half), jnp.float32),
        ],
        axis=2,
    )
    rows = half
    while rows > 8:
        rows //= 2
        upper = sheared[:, :rows].reshape(count * rows, 2 * width)
        upper = pltpu.roll(upper, rows, 1).reshape(count, rows, 2 * width)
        sheared = upper + sheared[:, rows:]
    flat = sheared.reshape(count * rows, 2 * width)
    sublane = lax.broadcasted_iota(jnp.int32, flat.shape, 0) % 8
    while rows > 1:
        rows //= 2
        flat = jnp.where((sublane & rows) == 0, pltpu.roll(flat, rows, 1), flat)
    return jnp.sum(flat.reshape(count, 8, 2 * width), axis=1)


def tile_lags(x_re, x_im, y_re, y_im, samples):
    real_part = product(x_re, y_re) + product(x_im, y_im)
    imag_part = product(x_im, y_re) - product(x_re, y_im)
    return lag_rows(jnp.stack([real_part, imag_part])) * (1.0 / samples)


def split_rows(x):
    first = x.astype(jnp.bfloat16).astype(jnp.float32)
    rest = x - first
    second = rest.astype(jnp.bfloat16).astype(jnp.float32)
    return jnp.concatenate([first, second, rest - second], axis=0)


def anti_identity(size):
    place = lax.broadcasted_iota(jnp.int32, (size, size), 0) + lax.broadcasted_iota(
        jnp.int32, (size, size), 1
    )
    return (place == size - 1).astype(jnp.float32).astype(jnp.bfloat16)


def turn_lags(terms):
    count, width = terms.shape
    lanes = 128
    spans = range(0, width, lanes)
    terms = jnp.concatenate([terms[:, first : first + lanes] for first in spans], axis=0)
    terms = jnp.dot(
        terms.astype(jnp.bfloat16), anti_identity(lanes), preferred_element_type=jnp.float32
    )
    blocks = [terms[count * i : count * (i + 1)] for i in reversed(range(len(spans)))]
    return pltpu.roll(jnp.concatenate(blocks, axis=1), width - 1, 1)


def conjugate_lags(lags):
    count = lags.shape[0]
    turned = turn_lags(split_rows(lags))
    turned = turned[:count] + turned[count : 2 * count] + turned[2 * count :]
    odd = lax.broadcasted_iota(jnp.int32, turned.shape, 0) % 2 == 1
    return jnp.where(odd, -turned, turned)


def reversed_lags(lags):
    count, width = lags.shape
    lanes = 128
    rows = jnp.pad(lags, ((0, -count % 8), (0, 0)))
    index = lanes - 1 - lax.broadcasted_iota(jnp.int32, (rows.shape[0], lanes), 1)
    blocks = [
        jnp.take_along_axis(
            rows[:, first : first + lanes], index, axis=1, mode="promise_in_bounds"
        )
        for first in reversed(range(0, width, lanes))
    ]
    return pltpu.roll(jnp.concatenate(blocks, axis=1), width - 1, 1)[:count]


def sheared_eights(tiles):
    count, width, _ = tiles.shape
    half = width // 2
    low, high = tiles[:, :half], tiles[:, half:]
    sheared = jnp.concatenate(
        [
            low[:, :, :half],
            low[:, :, half:] + high[:, :, :half],
            high[:, :, half:],
            jnp.zeros((count, half, half), jnp.float32),
        ],
        axis=2,
    )
    rows = half
    while rows > 8:
        rows //= 2
        lower = sheared[:, rows:].reshape(count * rows, 2 * width)
        lower = pltpu.roll(lower, rows, 1).reshape(count, rows, 2 * width)
        sheared = sheared[:, :rows] + lower
    return [pltpu.roll(sheared[i], 0, 1, stride=1, stride_axis=0) for i in range(count)]


def group_block(groups, columns=128):
    rows = jnp.concatenate([groups[b] for b in range(groups.shape[0])], axis=0)
    lines, lanes = rows.shape
    return jnp.pad(rows, ((0, GROUP_ROWS - lines), (0, columns - lanes)))


def target_rows(groups):
    return groups ^ (lax.axis_index("inp") * RG_DEV)


def pick_matrix(entries, rows):
    count = len(entries)
    shape = (rows, 3 * count)
    row = lax.broadcasted_iota(jnp.int32, shape, 0)
    column = lax.broadcasted_iota(jnp.int32, shape, 1) % count
    pick = jnp.zeros(shape, jnp.float32)
    for j, (targets, line, lane, part) in enumerate(entries):
        target = targets[line : line + 1, lane : lane + 1] + part * (rows // 2)
        target = jnp.broadcast_to(target, shape)
        pick = jnp.where(jnp.logical_and(column == j, row == target), 1.0, pick)
    return pick.astype(jnp.bfloat16)


def row_masks(entries, rows):
    row = lax.broadcasted_iota(jnp.int32, (rows, 128), 0)
    masks = []
    for targets, line, lane, _ in entries:
        target = jnp.broadcast_to(targets[line : line + 1, lane : lane + 1], row.shape)
        masks.append((row == target).astype(jnp.float32))
    return jnp.stack(masks)


def pick_matrices(groups, heads, blocks, out_rows):
    own = target_rows(group_block(groups))
    others = [target_rows(head.astype(jnp.float32).astype(jnp.int32)) for head in heads]
    groups_all = out_rows // 2

    def pairs(b):
        order = [(level, a, p) for level in range(len(heads)) for a in range(blocks) for p in range(2)]
        forward = [(own, a * blocks + b, level + 1, p) for level, a, p in order]
        turned = [(others[level], b * blocks + a, level + 1, p) for level, a, p in order]
        return forward, turned

    forward, turned = zip(*[pairs(b) for b in range(blocks)])
    tiles = [
        [(targets, line, 0, p) for line in range(blocks * blocks) for p in range(2)]
        for targets in (own, others[-1])
    ]
    both = [entry for side in (forward, turned) for block in side for entry in block]
    return [
        pick_matrix(tiles[0], out_rows),
        pick_matrix(tiles[1], out_rows),
        pick_matrix(both, out_rows),
        row_masks(forward[-1][::2] + turned[-1][::2], groups_all),
    ]


def group_sums(pick, lags):
    terms = split_rows(lags).astype(jnp.bfloat16)
    return jnp.dot(pick, terms, preferred_element_type=jnp.float32)


def columns(piece):
    spans, start = [], 0
    for _, first, last in piece:
        spans.append((start, start + last - first))
        start += last - first
    return spans


def piece_shape(piece, width, more):
    return jax.ShapeDtypeStruct((2 * width + more, columns(piece)[-1][1]), jnp.bfloat16)


def load_piece(piece, other, width, volts_ref, raw, in_sem):
    blocks = sorted({block for block, _, _ in piece})
    loads = []
    for i, block in enumerate(blocks):
        start = min(first for b, first, _ in piece if b == block)
        end = max(last for b, _, last in piece if b == block)
        for c in range(2):
            load = pltpu.make_async_copy(
                volts_ref.at[other, c, pl.ds(block * width, width), pl.ds(start, end - start)],
                raw.at[i, c, :, pl.ds(start, end - start)],
                in_sem.at[i, c],
            )
            load.start()
            loads.append((i, block, c, load))
    return loads


def order_piece(piece, loads, position, raw, out_ref):
    width = position.shape[1]
    orders = {
        block: order_matrix(position[block : block + 1, :]) for block in sorted({l[1] for l in loads})
    }
    for i, block, c, load in loads:
        load.wait()
        for (b, first, last), (start, end) in zip(piece, columns(piece)):
            if b == block:
                out_ref[c * width : (c + 1) * width, start:end] = jnp.dot(
                    orders[block], raw[i, c, :, first:last], preferred_element_type=jnp.float32
                ).astype(jnp.bfloat16)


def head_kernel(levels, piece, position_ref, volts_ref, group_ref, head_ref, *scratch):
    position, groups, small_sem, in_sem = scratch
    other = 1 - parity(lax.axis_index("inp"), levels)
    width = position.shape[1]
    ((block, first, last),) = piece
    smalls = [
        pltpu.make_async_copy(position_ref, position, small_sem.at[0]),
        pltpu.make_async_copy(group_ref, groups, small_sem.at[1]),
    ]
    loads = [
        pltpu.make_async_copy(
            volts_ref.at[other, c, pl.ds(block * width, width), pl.ds(first, last - first)],
            head_ref.at[pl.ds(c * width, width), :],
            in_sem.at[c],
        )
        for c in range(2)
    ]
    for copy in smalls + loads:
        copy.start()
    for copy in smalls:
        copy.wait()
    rows = group_block(groups[...], last - first)
    line = lax.broadcasted_iota(jnp.int32, rows.shape, 0)
    own_row = jnp.broadcast_to(position[block : block + 1, :], rows.shape)
    rows = jnp.where(line == groups.shape[0] ** 2, own_row, rows)
    head_ref[2 * width :, :] = rows.astype(jnp.float32).astype(jnp.bfloat16)
    for copy in loads:
        copy.wait()


def on_odd_core():
    return lax.axis_index("freq") % 2 == 1


def load_channel(channel, volts_ref, raw, in_sem):
    blocks, _, width, _ = raw.shape
    loads = []
    for b in range(blocks):
        for c in range(2):
            load = pltpu.make_async_copy(
                volts_ref.at[channel, c, pl.ds(b * width, width)], raw.at[b, c], in_sem.at[b, c]
            )
            load.start()
            loads.append((b, c, load))
    return loads


def order_channel(loads, position_ref, raw, panel):
    blocks = raw.shape[0]
    orders = [order_matrix(position_ref[b : b + 1, :]) for b in range(blocks)]
    for b, c, load in loads:
        load.wait()
        rows = jnp.dot(orders[b], raw[b, c], preferred_element_type=jnp.float32)
        panel[b, c] = rows.astype(jnp.bfloat16)


def own_tiles(panel, lags_ref, start, first, last):
    blocks, _, width, samples = panel.shape

    def one_tile(index, carry):
        a = index // blocks
        b = index % blocks
        lags = tile_lags(panel[a, 0], panel[a, 1], panel[b, 0], panel[b, 1], samples)
        center = lax.broadcasted_iota(jnp.int32, lags.shape, 1) == width - 1
        lags_ref[start + index] = jnp.where(jnp.logical_and(center, a == b), 0.0, lags)
        return carry

    lax.fori_loop(first, last, one_tile, 0)


def rest_kernel(levels, piece, position_ref, volts_ref, _, out_ref, panel_ref, lags_ref, *scratch):
    position, raw, own_raw, small_sem, in_sem, own_sem = scratch
    mine = parity(lax.axis_index("inp"), levels)
    load_position = pltpu.make_async_copy(position_ref, position, small_sem)
    load_position.start()
    piece_loads = load_piece(piece, 1 - mine, position.shape[1], volts_ref, raw, in_sem)
    load_position.wait()

    @pl.when(on_odd_core())
    def _():
        loads = load_channel(mine, volts_ref, own_raw, own_sem)
        order_channel(loads, position, own_raw, panel_ref)
        own_tiles(panel_ref, lags_ref, 0, 0, EARLY_TILES)

    order_piece(piece, piece_loads, position, raw, out_ref)


def early_pieces(position_input, volts, groups, head, rest, levels):
    blocks, width = position_input.shape
    samples = volts.shape[3]
    assert columns(head)[-1][1] == width
    in_hbm = [pltpu.with_memory_space_constraint(x, pltpu.HBM) for x in (position_input, volts)]
    position = pltpu.VMEM(position_input.shape, jnp.int32)
    semaphore = pltpu.SemaphoreType.DMA
    sent = pl.pallas_call(
        functools.partial(head_kernel, levels, head),
        out_shape=piece_shape(head, width, GROUP_ROWS),
        in_specs=[HBM] * 3,
        out_specs=WHOLE,
        scratch_shapes=[
            position,
            pltpu.VMEM(groups.shape, jnp.int32),
            semaphore((2,)),
            semaphore((2,)),
        ],
        compiler_params=pltpu.CompilerParams(vmem_limit_bytes=8 << 20),
        cost_estimate=pl.CostEstimate(flops=0, bytes_accessed=1 << 20, transcendentals=0),
        name="first_piece",
    )(*in_hbm, pltpu.with_memory_space_constraint(groups, pltpu.HBM))
    second, early_panel, early_lags = pl.pallas_call(
        functools.partial(rest_kernel, levels, rest),
        out_shape=[
            piece_shape(rest, width, 0),
            jax.ShapeDtypeStruct((blocks, 2, width, samples), jnp.bfloat16),
            jax.ShapeDtypeStruct((blocks * blocks, 2, 2 * width), jnp.float32),
        ],
        in_specs=[HBM, HBM, pl.BlockSpec(memory_space=pl.ANY)],
        out_specs=[WHOLE] * 3,
        scratch_shapes=[
            position,
            pltpu.VMEM((blocks, 2, width, samples), jnp.bfloat16),
            pltpu.VMEM((blocks, 2, width, samples), jnp.bfloat16),
            semaphore(()),
            semaphore((blocks, 2)),
            semaphore((blocks, 2)),
        ],
        compiler_params=pltpu.CompilerParams(vmem_limit_bytes=16 << 20),
        cost_estimate=pl.CostEstimate(
            flops=4 * width * width * columns(rest)[-1][1],
            bytes_accessed=4 << 20,
            transcendentals=0,
        ),
        name="second_piece",
    )(*in_hbm, sent)
    return sent, second, early_panel, early_lags


def own_kernel(levels, piece, last, group_ref, position_ref, volts_ref, *refs):
    head_refs, refs = refs[:levels][::-1], refs[levels:]
    early_panel_ref, early_lags_ref, *refs = refs
    panel_ref, sums_ref, *refs, raw, other_raw, other_panel, lags_ref, in_sem, other_sem = refs
    pick_refs, ordered_refs, refs = refs[:3], refs[3 : 3 + levels], refs[3 + levels :]
    more_ref, piece_ref, *last_refs, joined_ref, last_panel_ref = refs
    blocks, _, width, _ = panel_ref.shape
    mine = parity(lax.axis_index("inp"), levels)
    other_loads = load_channel(1 - mine, volts_ref, other_raw, other_sem)

    @pl.when(jnp.logical_not(on_odd_core()))
    def _():
        loads = load_channel(mine, volts_ref, raw, in_sem)
        order_channel(loads, position_ref, raw, panel_ref)
        own_tiles(panel_ref, lags_ref, 0, 0, EARLY_TILES)

    @pl.when(on_odd_core())
    def _():
        for b in range(blocks):
            for c in range(2):
                panel_ref[b, c] = early_panel_ref[b, c]
        for i in range(EARLY_TILES):
            lags_ref[i] = early_lags_ref[i]

    tiles = blocks * blocks
    own_tiles(panel_ref, lags_ref, 0, EARLY_TILES, tiles)
    order_channel(other_loads, position_ref, other_raw, other_panel)
    own_tiles(other_panel, lags_ref, tiles, 0, tiles)
    lags = jnp.concatenate([lags_ref[i] for i in range(tiles)], axis=0)
    heads = [head_ref[2 * width :, :] for head_ref in head_refs]
    for head, head_ref, ordered_ref in zip(heads, head_refs, ordered_refs):
        positions = head.astype(jnp.float32).astype(jnp.int32)[blocks**2 : blocks**2 + 1]
        order = order_matrix(positions)
        for c in range(2):
            rows = head_ref[c * width : (c + 1) * width, :]
            rows = jnp.dot(order, rows, preferred_element_type=jnp.float32)
            ordered_ref[c * width : (c + 1) * width, :] = rows.astype(jnp.bfloat16)
    own_pick, *picks = pick_matrices(group_ref[...], heads, blocks, sums_ref.shape[0])
    for pick_ref, pick in zip(pick_refs, picks):
        pick_ref[...] = pick
    sums_ref[...] = group_sums(own_pick, lags)
    for (block, first, end), (start, stop) in zip(piece, columns(piece)):
        for c in range(2):
            rows = other_panel[block, c, :, first:end]
            piece_ref[c * width : (c + 1) * width, start:stop] = rows
            more_ref[c * width : (c + 1) * width, start:stop] = rows
    lags = jnp.concatenate([lags_ref[tiles + i] for i in range(tiles)], axis=0)
    high = lags.astype(jnp.bfloat16).astype(jnp.float32)
    terms = jnp.concatenate([high, lags - high], axis=0)
    more_ref[2 * width :, :] = terms.astype(jnp.bfloat16)
    start = 0
    for (block, first, end), last_ref in zip(last, last_refs):
        for c in range(2):
            depth = end - first
            rows = other_panel[block, c, :, first:end]
            last_ref[:, c * depth : (c + 1) * depth] = rows
            joined_ref[:, start : start + depth] = rows
            start += depth
    turn = anti_identity(width)
    for a in range(blocks):
        start = 0
        for _, first, end in last:
            real_part, imag_part = [
                jnp.dot(turn, panel_ref[a, c, :, first:end], preferred_element_type=jnp.float32)
                for c in range(2)
            ]
            middle, stop = start + end - first, start + 2 * (end - first)
            last_panel_ref[a, :width, start:middle] = real_part.astype(jnp.bfloat16)
            last_panel_ref[a, :width, middle:stop] = imag_part.astype(jnp.bfloat16)
            last_panel_ref[a, width:, start:middle] = imag_part.astype(jnp.bfloat16)
            last_panel_ref[a, width:, middle:stop] = (-real_part).astype(jnp.bfloat16)
            start = stop


def own_level(groups, position_input, volts, early, heads, piece, last, out_rows):
    levels = len(heads)
    blocks, width = position_input.shape
    samples = volts.shape[3]
    pairs = 4 * levels * blocks
    tiles = 2 * blocks * blocks
    counts = (3 * tiles, 3 * pairs * blocks)
    depths = [2 * (end - first) for _, first, end in last]
    return pl.pallas_call(
        functools.partial(own_kernel, levels, piece, last),
        out_shape=(
            jax.ShapeDtypeStruct((blocks, 2, width, samples), jnp.bfloat16),
            jax.ShapeDtypeStruct((out_rows, 2 * width), jnp.float32),
            *[jax.ShapeDtypeStruct((out_rows, n), jnp.bfloat16) for n in counts],
            jax.ShapeDtypeStruct((pairs // 2, out_rows // 2, 128), jnp.float32),
            *[jax.ShapeDtypeStruct((2 * width, head.shape[1]), jnp.bfloat16) for head in heads],
            piece_shape(piece, width, 2 * tiles),
            piece_shape(piece, width, 0),
            *[jax.ShapeDtypeStruct((width, depth), jnp.bfloat16) for depth in depths],
            jax.ShapeDtypeStruct((width, sum(depths)), jnp.bfloat16),
            jax.ShapeDtypeStruct((blocks, 2 * width, sum(depths)), jnp.bfloat16),
        ),
        in_specs=[WHOLE, WHOLE, HBM] + [WHOLE] * (len(early) + levels),
        out_specs=(WHOLE,) * (7 + len(counts) + levels + len(last)),
        scratch_shapes=[
            pltpu.VMEM((blocks, 2, width, samples), jnp.bfloat16),
            pltpu.VMEM((blocks, 2, width, samples), jnp.bfloat16),
            pltpu.VMEM((blocks, 2, width, samples), jnp.bfloat16),
            pltpu.VMEM((2 * blocks * blocks, 2, 2 * width), jnp.float32),
            pltpu.SemaphoreType.DMA((blocks, 2)),
            pltpu.SemaphoreType.DMA((blocks, 2)),
        ],
        compiler_params=pltpu.CompilerParams(vmem_limit_bytes=16 << 20),
        cost_estimate=pl.CostEstimate(
            flops=64 * blocks * blocks * width * width * samples,
            bytes_accessed=12 * blocks * width * samples,
            transcendentals=0,
        ),
        name="own_level",
    )(groups, position_input, pltpu.with_memory_space_constraint(volts, pltpu.HBM), *heads[::-1], *early)


def add_lags(rows, pick_ref, sums_ref):
    lags = jnp.concatenate(rows, axis=0)
    lags = jnp.concatenate([lags, conjugate_lags(lags)], axis=0)
    return sums_ref[...] + group_sums(pick_ref[...], lags)


def add_masked(lags, tiles_at, mask_ref, sums_ref):
    turned = reversed_lags(lags)
    half, count = sums_ref.shape[0] // 2, mask_ref.shape[0] // 2
    sums = [sums_ref[:half, :], sums_ref[half:, :]]
    for i, tile in enumerate(tiles_at):
        forward = jnp.concatenate([mask_ref[tile]] * (sums_ref.shape[1] // 128), axis=1)
        back = jnp.concatenate([mask_ref[count + tile]] * (sums_ref.shape[1] // 128), axis=1)
        re, im = 2 * i, 2 * i + 1
        sums[0] = sums[0] + forward * lags[re : re + 1] + back * turned[re : re + 1]
        sums[1] = sums[1] + forward * lags[im : im + 1] - back * turned[im : im + 1]
    return sums


def pair_kernel(levels, pieces, passed, pick_ref, sums_ref, panel_ref, *refs):
    count = levels * len(pieces)
    out_ref = refs[-1 - passed]
    partner_refs, more_refs = refs[:count], refs[count : len(refs) - 1 - 2 * passed]
    _, _, width, samples = panel_ref.shape
    rows = []
    for block in sorted({block for piece in pieces for block, _, _ in piece}):
        for level in range(levels):
            for a in range(panel_ref.shape[0]):
                real_part, imag_part = 0.0, 0.0
                for i, piece in enumerate(pieces):
                    partner = partner_refs[level * len(pieces) + i]
                    for (b, first, last), (start, end) in zip(piece, columns(piece)):
                        if b != block:
                            continue
                        x_re, x_im = panel_ref[a, 0, :, first:last], panel_ref[a, 1, :, first:last]
                        y_re = partner[:width, start:end]
                        y_im = partner[width : 2 * width, start:end]
                        real_part = real_part + (product(x_re, y_re) + product(x_im, y_im))
                        imag_part = imag_part + (product(x_im, y_re) - product(x_re, y_im))
                rows.append(lag_rows(jnp.stack([real_part, imag_part])) * (1.0 / samples))
    if len(pick_ref.shape) == 3:
        sums = add_masked(jnp.concatenate(rows, axis=0), range(len(rows)), pick_ref, sums_ref)
        sums = jnp.concatenate(sums, axis=0)
    else:
        sums = add_lags(rows, pick_ref, sums_ref)
    for more_ref in more_refs:
        terms = partner_refs[-1][2 * width :, :].astype(jnp.float32)
        half = terms.shape[0] // 2
        sums = sums + group_sums(more_ref[...], terms[:half] + terms[half:])
    out_ref[...] = sums


def last_kernel(parts, samples, mask_ref, sums_ref, panel_ref, *refs):
    partner_refs, out_refs = refs[: len(parts)], refs[len(parts) :]
    blocks, rows_both, _ = panel_ref.shape
    width = rows_both // 2
    rows, tiles_at = [], []
    for (level, first, last), partner_ref in zip(parts, partner_refs):
        for a in range(blocks):
            tiles = product(panel_ref[a, :, first:last], partner_ref[...])
            rows += sheared_eights(tiles.reshape(2, width, width))
            tiles_at.append(level * blocks + a)
    lags = jnp.sum(jnp.stack(rows), axis=1) * (1.0 / samples)
    sums = add_masked(lags, tiles_at, mask_ref, sums_ref)
    half = sums_ref.shape[0] // 2
    share = half // len(out_refs)
    for place, out_ref in enumerate(out_refs):
        for part in range(2):
            rows = sums[part][place * share : (place + 1) * share]
            out_ref[part * share : (part + 1) * share, :] = rows


def pair_call(kernel, inputs, work, shares=1, passed=()):
    rows, width = inputs[1].shape
    any_space = [pl.BlockSpec(memory_space=pl.ANY)] * len(passed)
    return pl.pallas_call(
        kernel,
        out_shape=[jax.ShapeDtypeStruct((rows // shares, width), jnp.float32)] * shares
        + [jax.ShapeDtypeStruct(x.shape, x.dtype) for x in passed],
        in_specs=[WHOLE] * len(inputs) + any_space,
        out_specs=[WHOLE] * shares + any_space,
        input_output_aliases={len(inputs) + i: shares + i for i in range(len(passed))},
        compiler_params=pltpu.CompilerParams(vmem_limit_bytes=16 << 20),
        cost_estimate=pl.CostEstimate(flops=work, bytes_accessed=4 << 20, transcendentals=0),
        name="pair_level",
    )(*inputs, *passed)


def finish_kernel(levels, distances, *refs):
    part_refs, out_ref = refs[:-1], refs[-1]
    mine = parity(lax.axis_index("inp"), levels)
    groups, channels, parts, lags = out_ref.shape
    sums = [None, None]
    for distance, part_ref in zip(distances, part_refs):
        side = distance.bit_count() % 2
        sums[side] = part_ref[...] if sums[side] is None else sums[side] + part_ref[...]
    for f in range(channels):
        total = jnp.where(mine == f, sums[0], sums[1])
        for g in range(groups):
            for part in range(parts):
                row = part * groups + g
                out_ref[g, f, part : part + 1] = total[row : row + 1, :lags]


def finish(parts, distances, levels, lags):
    return pl.pallas_call(
        functools.partial(finish_kernel, levels, distances),
        out_shape=jax.ShapeDtypeStruct((RG_DEV, 2, 2, lags), jnp.float32),
        in_specs=[WHOLE] * len(parts),
        out_specs=WHOLE,
        compiler_params=pltpu.CompilerParams(vmem_limit_bytes=8 << 20),
        name="finish",
    )(*parts)


def on_device(volts, position_input, tile_group):
    blocks, width = position_input.shape
    samples = volts.shape[3]
    devices = lax.axis_size("inp")
    levels = devices.bit_length() - 1
    out_rows = devices * RG_DEV * 2
    eighth = samples // 8
    head = [(0, 0, 2 * eighth)]
    rest = [(0, 2 * eighth, samples), (1, 0, 2 * eighth)]
    tail = [(1, 2 * eighth, 6 * eighth)]
    last = [(1, 6 * eighth, 7 * eighth), (1, 7 * eighth, samples)]
    by_block = tile_group.transpose(0, 2, 1)
    partner_of = [functools.partial(xor_permute, axis="inp", distance=1 << l) for l in range(levels)]
    sent, second, *early = early_pieces(position_input, volts, by_block, head, rest, levels)
    head_arrived = [send(sent) for send in partner_of]
    rest_arrived = [send(second) for send in partner_of]
    panel, sums, neighbour, both, masks, *sent = own_level(
        by_block, position_input, volts, early, head_arrived, tail, last, out_rows
    )
    head_ordered, (more, piece, *last_pieces, last_panel) = sent[:levels], sent[levels:]
    tail_arrived = [send(piece) for send in partner_of[:-1]] + [partner_of[-1](more)]

    flops = 8 * levels * blocks * width * width
    arrived = [piece for pair in zip(head_ordered, rest_arrived) for piece in pair]
    sums, *last_pieces = pair_call(
        functools.partial(pair_kernel, levels, [head, rest], len(last_pieces)),
        [both, sums, panel, *arrived],
        flops * 10 * eighth,
        passed=last_pieces,
    )
    *last_pieces, joined = last_pieces
    last_arrived = [[send(piece) for send in partner_of[:-1]] for piece in last_pieces]
    last_arrived[-1].append(partner_of[-1](joined))
    (sums,) = pair_call(
        functools.partial(pair_kernel, levels, [tail], 0),
        [masks, sums, panel, *tail_arrived, neighbour],
        flops * 4 * eighth,
    )
    for i, arrived in enumerate(last_arrived):
        final = i == len(last_arrived) - 1
        columns_of = [(2 * eighth * i, 2 * eighth * (i + 1))] * (levels - 1)
        if final:
            columns_of.append((0, joined.shape[1]))
        parts = pair_call(
            functools.partial(
                last_kernel, [(level, *cut) for level, cut in enumerate(columns_of)], samples
            ),
            [masks, sums, last_panel, *arrived],
            flops * eighth,
            devices if final else 1,
        )
        sums = parts[0]
    distances = [1, *range(devices - 1, 1, -1), 0]
    parts = [
        xor_permute(parts[distance], "inp", distance) if distance else parts[0]
        for distance in distances
    ]
    return finish(parts, distances, levels, 2 * width - 1)


def solution(mesh):
    return jax.shard_map(
        on_device,
        mesh=mesh,
        in_specs=(P("freq", None, "inp", None), P("inp", None), P("inp", None, None)),
        out_specs=P("inp", "freq", None, None),
        check_vma=False,
    )
```
